32 devices in a mesh: parts: 2 (over x), space: 8 (over z, y), member: 2 (over core).
Axes of the slice: x: 2, y: 2, z: 4, core: 2. Of those that a mesh axis runs over, the one named last changes fastest.
Arguments:
- densities: float32 [4096, 4, 4096], P('space', ('parts', 'member')), parts along dimension 1, may hold values from 0.05 to 40, as said below
- scaling: float32 [4096, 4, 4096], P('space', ('parts', 'member')), parts along dimension 1, may hold values from 0.25 to 4
- weights: float32 [4], P('parts'), parts along dimension 0, may hold values from 0.5 to 2
- band: float32 [32, 3, 128, 128], replicated, may hold values from 0 to 0.009375, as said below
Outputs:
- barycenter: float32 [8192, 4096], P(('parts', 'space')), parts along dimension 0
- new_scaling: float32 [4096, 4, 4096], P('space', ('parts', 'member')), parts along dimension 1
The draws below stay inside these ranges and needn't reach their ends.
There are 2 independent parts, one for each index of `parts`. The reference program is written for one: setup_inputs(seed, part) draws one part's arguments, and reference() takes and returns one part's arrays. A program takes and returns all parts, laid end to end along the dimension named above; an argument that names none is the same for every part. Nothing has to cross between parts.
Inputs may be any that keep to these rules, and one draw needn't show every extreme that they name: Positive densities. `band`: positive entries.
All inputs are finite; a program needn't handle non-finite values.
Results may differ from the reference program's by a relative error of at most 0.0001.
Values sent between devices are 32-bit elements; how exact they have to be, the bound alone decides.
No kernel may reach another device: no remote copies, remote signals or barrier semaphores. Data moves between devices by JAX's collectives and lax.ppermute only.
A program may use at most 192 MiB of HBM per device.

```python
import math
import jax
import jax.numpy as jnp
from jax import lax

BLK = 128
N = 4096
NBLK = 32
MEMBERS = 2


def draw_band(key, part):
    key = jax.random.fold_in(key, 11)
    rough = jax.random.uniform(key, (NBLK, 3, BLK, BLK), jnp.float32, 0.5, 1.5)
    offsets = jnp.arange(3).reshape(1, 3, 1, 1)
    rowpos = jnp.arange(BLK).reshape(1, 1, BLK, 1)
    colpos = jnp.arange(BLK).reshape(1, 1, 1, BLK)
    distance = ((offsets - 1) * BLK + colpos - rowpos).astype(jnp.float32)
    spread = BLK / 2.0
    return rough * jnp.exp(-distance * distance / (2.0 * spread * spread)) / (spread * 2.5066)


def draw_densities(key, part):
    key = jax.random.fold_in(key, 5)
    ramp = (1.0 + 2.0 * jnp.arange(N).astype(jnp.float32) / (N - 1)).reshape(N, 1, 1)
    base = jnp.exp(0.6 * jax.random.truncated_normal(key, -4.0, 4.0, (N, MEMBERS, N), jnp.float32))
    return base * ramp


def levels(own_key, shape, cuts, low, high):
    def one(axis_at, blocks):
        draws = jax.random.uniform(jax.random.fold_in(jax.random.fold_in(own_key, 6), axis_at), (blocks,), jnp.float32, low / len(cuts), high / len(cuts))
        return jnp.repeat(jnp.exp(draws), shape[axis_at] // blocks).reshape((-1,) + (1,) * (len(shape) - axis_at - 1))

    factor_of = one(*cuts[0])
    for cut in cuts[1:]:
        factor_of = factor_of * one(*cut)
    return factor_of


def setup_inputs(seed: int = 0, part: int = 0) -> dict:
    arg_keys = jax.random.split(jax.random.key(seed), 5)
    part_splits = jax.random.split(jax.random.fold_in(arg_keys[4], part), 5)
    densities = draw_densities(jax.random.fold_in(jax.random.fold_in(arg_keys[4], part), 71), part)
    scaling = jnp.clip(jnp.exp(math.log(4.0) - 2.7725887 * jax.random.uniform(part_splits[1], (N, MEMBERS, N), jnp.float32) ** levels(part_splits[1], (N, MEMBERS, N), ((0, 8), (1, 2)), -0.2, 0.2)), 0.25, 4.0)
    weights = jnp.clip(jnp.exp(jax.random.uniform(part_splits[2], (MEMBERS,), jnp.float32, math.log(0.5), math.log(2.0))), 0.5, 2.0)
    band = draw_band(jax.random.fold_in(arg_keys[4], 71), part)
    return {"densities": densities, "scaling": scaling, "weights": weights, "band": band}


def row_pass(field, band):
    nblocks, _, width, _ = band.shape
    lead = field.shape[:-1]
    blocks = field.reshape(lead + (nblocks, width))
    padding = [(0, 0)] * len(lead) + [(1, 1), (0, 0)]
    padded = jnp.pad(blocks, padding)
    total = jnp.zeros(blocks.shape, jnp.float32)
    for offset in range(3):
        window = lax.slice_in_dim(padded, offset, offset + nblocks, axis=len(lead))
        total = total + jnp.einsum("...bq,bpq->...bp", window, band[:, offset], precision=lax.Precision.HIGHEST)
    return total.reshape(field.shape)


def col_pass(field, band):
    nblocks, _, width, _ = band.shape
    blocks = field.reshape(nblocks, width, field.shape[1])
    padded = jnp.pad(blocks, ((1, 1), (0, 0), (0, 0)))
    total = jnp.zeros(blocks.shape, jnp.float32)
    for offset in range(3):
        total = total + jnp.einsum("bpq,bqc->bpc", band[:, offset], padded[offset:offset + nblocks], precision=lax.Precision.HIGHEST)
    return total.reshape(field.shape)


def blur_maps(field, band):
    rows_all = field.shape[0]
    passed = row_pass(field, band)
    return col_pass(passed.reshape(rows_all, -1), band).reshape(field.shape)


def reference(densities, scaling, weights, band):
    shares = weights / jnp.sum(weights)
    blurred = blur_maps(scaling, band)
    ratio = densities / blurred
    smeared = blur_maps(ratio, band)
    logmean = jnp.sum(shares[None, :, None] * jnp.log(scaling * smeared), axis=1)
    raw = jnp.exp(logmean)
    mass = jnp.sum(raw)
    barycenter = raw * (float(N * N) / mass)
    new_scaling = barycenter[:, None, :] / smeared
    return barycenter, new_scaling
```

```python
import functools

import jax
import jax.numpy as jnp
from jax import lax
from jax.experimental import pallas as pl
from jax.experimental.pallas import tpu as pltpu
from jax.sharding import PartitionSpec as P

F32 = jnp.float32
BF16 = jnp.bfloat16
VMEM_LIMIT = 56 * 1024 * 1024
ANY = pl.BlockSpec(memory_space=pl.ANY)
INVMEM = pl.BlockSpec(memory_space=pltpu.VMEM)
INSMEM = pl.BlockSpec(memory_space=pltpu.SMEM)


def split(x):
    high = x.astype(BF16)
    return high, (x - high.astype(F32)).astype(BF16)


def dot3(a, b, dims):
    one = functools.partial(lax.dot_general, dimension_numbers=(dims, ((), ())), preferred_element_type=F32)
    return one(a[0], b[0]) + (one(a[0], b[1]) + one(a[1], b[0]))


def params():
    return pltpu.CompilerParams(vmem_limit_bytes=VMEM_LIMIT)


def weight_kernel(nblocks, band_ref, high_ref, low_ref):
    pair = pl.program_id(0)
    width = band_ref.shape[2]
    zero = jnp.zeros((width, width), F32)
    for o in range(2):
        for i in range(4):
            j = i - o
            value = band_ref[o, j] if 0 <= j <= 2 else zero
            if (o, j) == (0, 0):
                value = jnp.where(pair > 0, value, 0.0)
            if (o, j) == (1, 2):
                value = jnp.where(pair < nblocks // 2 - 1, value, 0.0)
            high, low = split(value)
            rows, columns = slice(o * width, (o + 1) * width), slice(i * width, (i + 1) * width)
            high_ref[0, rows, columns] = high
            low_ref[0, rows, columns] = low


def row_weights(band):
    nblocks, _, width, _ = band.shape
    shape = jax.ShapeDtypeStruct((nblocks // 2, 2 * width, 4 * width), BF16)
    out_spec = pl.BlockSpec((1, 2 * width, 4 * width), lambda t: (t, 0, 0))
    return pl.pallas_call(
        functools.partial(weight_kernel, nblocks),
        grid=(nblocks // 2,),
        in_specs=[pl.BlockSpec((2, 3, width, width), lambda t: (t, 0, 0, 0))],
        out_specs=(out_spec, out_spec),
        out_shape=(shape, shape),
        name="row_weights",
    )(band)


def blur_kernel(plan, *refs):
    pieces, narrays, groups, extra, first, last, nblocks, width, final = plan
    arrays = refs[:narrays]
    a_ref, high_ref, low_ref, extra_ref = refs[narrays : narrays + 4]
    rest = refs[narrays + 4 :]
    if final:
        share_ref, rest = rest[0], rest[1:]
    nouts = 2 if final else len(groups)
    outs = rest[:nouts]
    field, yhigh, ylow, whigh, wlow, other, sems = rest[nouts:]

    copies = []
    for k, (which, row, block, rows, blocks, to_row, to_block) in enumerate(pieces):
        copies.append(
            pltpu.make_async_copy(
                arrays[which].at[pl.ds(row, rows), pl.ds(block * width, blocks * width)],
                field.at[pl.ds(to_row, rows), pl.ds(to_block * width, blocks * width)],
                sems.at[k],
            )
        )
    count = len(pieces)
    late = []
    pairs = (last - first) // 2
    for src, dst in ((high_ref, whigh), (low_ref, wlow)):
        late.append(pltpu.make_async_copy(src.at[pl.ds(first // 2, pairs)], dst, sems.at[count]))
        count += 1
    at = 0
    for row, rows in extra:
        late.append(
            pltpu.make_async_copy(
                extra_ref.at[pl.ds(row, rows), pl.ds(first * width, (last - first) * width)],
                other.at[pl.ds(at, rows)],
                sems.at[count],
            )
        )
        count += 1
        at += rows
    for copy in copies + late:
        copy.start()
    if first == 0:
        field[:, :width] = jnp.zeros((field.shape[0], width), F32)
    if last == nblocks:
        field[:, field.shape[1] - width :] = jnp.zeros((field.shape[0], width), F32)
    bands = [split(a_ref[to : to + m, :k]) for _, k, to, m in groups]
    for copy in copies:
        copy.wait()

    def columns_pass(i, carry):
        at = pl.ds(pl.multiple_of(i * 2 * width, 2 * width), 2 * width)
        for (row, k, to, m), a in zip(groups, bands):
            y = dot3(a, split(field[row : row + k, at]), ((1,), (0,)))
            high, low = split(y)
            yhigh[to : to + m, at] = high
            ylow[to : to + m, at] = low
        return carry

    lax.fori_loop(0, pairs + 1, columns_pass, 0)
    for copy in late:
        copy.wait()

    def rows_pass(t, carry):
        source = pl.ds(pl.multiple_of(t * 2 * width, 2 * width), 4 * width)
        at = pl.ds(pl.multiple_of(t * 2 * width, 2 * width), 2 * width)
        value = dot3((yhigh[:, source], ylow[:, source]), (whigh[t], wlow[t]), ((1,), (1,)))
        if final:
            outs[0][:, at] = share_ref[0] * jnp.log(other[:, at] * value)
            outs[1][:, at] = value
        else:
            ratio = other[:, at] / value
            for out, (_, _, to, m) in zip(outs, groups):
                out[:, at] = ratio[to : to + m]
        return carry

    lax.fori_loop(0, pairs, rows_pass, 0)


def blur(name, arrays, pieces, groups, extra, first, last, a, weights, other, share=None):
    width = weights[0].shape[1] // 2
    nblocks = weights[0].shape[0] * 2
    total = sum(m for _, _, _, m in groups)
    depth = max(row + k for row, k, _, _ in groups)
    columns = (last - first) * width
    final = share is not None
    plan = (pieces, len(arrays), groups, extra, first, last, nblocks, width, final)
    if final:
        shapes = [jax.ShapeDtypeStruct((total, columns), F32)] * 2
    else:
        shapes = [jax.ShapeDtypeStruct((m, columns), F32) for _, _, _, m in groups]
    pairs = (last - first) // 2
    work = 3 * 2 * total * columns * (depth + 4 * width)
    moved = 4 * (depth + 3 * total) * columns + pairs * 2 * 2 * 8 * width * width
    return pl.pallas_call(
        functools.partial(blur_kernel, plan),
        in_specs=[ANY] * len(arrays) + [INVMEM, ANY, ANY, ANY] + [INSMEM] * final,
        out_specs=[INVMEM] * len(shapes),
        out_shape=shapes,
        scratch_shapes=[
            pltpu.VMEM((depth, columns + 2 * width), F32),
            pltpu.VMEM((total, columns + 2 * width), BF16),
            pltpu.VMEM((total, columns + 2 * width), BF16),
            pltpu.VMEM((pairs, 2 * width, 4 * width), BF16),
            pltpu.VMEM((pairs, 2 * width, 4 * width), BF16),
            pltpu.VMEM((total, columns), F32),
            pltpu.SemaphoreType.DMA((len(pieces) + 2 + len(extra),)),
        ],
        compiler_params=params(),
        cost_estimate=pl.CostEstimate(flops=work, bytes_accessed=moved, transcendentals=0),
        name=name,
    )(*arrays, a, *weights, other, *([share] if final else []))


def raw_kernel(plan, t_ref, peer_ref, m_ref, *refs):
    extra, column, fresh = plan
    if fresh:
        raw_all, quotient_all, mass_ref, raw, quotient, sems = refs
    else:
        _, _, before_ref, raw_all, quotient_all, mass_ref, raw, quotient, sems = refs
    raw[...] = jnp.exp(t_ref[...] + peer_ref[...])
    quotient[...] = raw[...] / m_ref[...]
    copies = []
    at = 0
    for row, rows in extra:
        for src, dst in ((raw, raw_all), (quotient, quotient_all)):
            copies.append(
                pltpu.make_async_copy(
                    src.at[pl.ds(at, rows)],
                    dst.at[pl.ds(row, rows), pl.ds(column, raw.shape[1])],
                    sems.at[len(copies)],
                )
            )
        at += rows
    for copy in copies:
        copy.start()
    mass = jnp.sum(raw[...])
    mass_ref[0] = mass if fresh else mass + before_ref[0]
    for copy in copies:
        copy.wait()


def raw_piece(name, t, peer, m, extra, column, whole, so_far):
    fresh = so_far is None
    shape = jax.ShapeDtypeStruct(whole, F32)
    return pl.pallas_call(
        functools.partial(raw_kernel, (extra, column, fresh)),
        in_specs=[INVMEM] * 3 + ([] if fresh else [ANY, ANY, INSMEM]),
        out_specs=(ANY, ANY, INSMEM),
        out_shape=(shape, shape, jax.ShapeDtypeStruct((1,), F32)),
        scratch_shapes=[
            pltpu.VMEM(t.shape, F32),
            pltpu.VMEM(t.shape, F32),
            pltpu.SemaphoreType.DMA((2 * len(extra),)),
        ],
        input_output_aliases={} if fresh else {3: 0, 4: 1},
        compiler_params=params(),
        cost_estimate=pl.CostEstimate(flops=4 * t.size, bytes_accessed=20 * t.size, transcendentals=2 * t.size),
        name=name,
    )(t, peer, m, *([] if fresh else so_far))


def output_kernel(raw_ref, quotient_ref, scale_ref, barycenter_ref, scaling_ref):
    scale = scale_ref[0]
    barycenter_ref[...] = raw_ref[...] * scale
    width = scaling_ref.shape[2]
    for b in range(scaling_ref.shape[1]):
        scaling_ref[:, b, :] = quotient_ref[:, b * width : (b + 1) * width] * scale


def outputs(raw, quotient, scale, width):
    rows, columns = raw.shape
    tile = 64
    flat = pl.BlockSpec((tile, columns), lambda i: (i, 0))
    return pl.pallas_call(
        output_kernel,
        grid=(rows // tile,),
        in_specs=[flat, flat, INSMEM],
        out_specs=(flat, pl.BlockSpec((tile, columns // width, width), lambda i: (i, 0, 0))),
        out_shape=(
            jax.ShapeDtypeStruct((rows, columns), F32),
            jax.ShapeDtypeStruct((rows, columns // width, width), F32),
        ),
        compiler_params=params(),
        name="outputs",
    )(raw, quotient, scale)


def local(densities, scaling, weights, band):
    rows_here, maps_here, cols_all = densities.shape
    nblocks, _, width, _ = band.shape
    nlocal = rows_here // width
    count = lax.axis_size("space")
    members = lax.axis_size("member")
    forward = [(i, i + 1) for i in range(count - 1)]
    backward = [(i + 1, i) for i in range(count - 1)]
    swap = [(0, 1), (1, 0)]
    assert maps_here == 1 and members == 2

    cuts1 = [0, nblocks // 2 + 2, nblocks]
    cuts2 = [0, nblocks // 2, nblocks]
    cuts3 = [0, nblocks // 2 - 2, nblocks]
    chunks = len(cuts1) - 1

    halo1 = []
    for c in range(chunks):
        start, stop = cuts1[c] * width, cuts1[c + 1] * width
        bottom = scaling[rows_here - width :, 0, start:stop]
        top = scaling[:width, 0, start:stop]
        halo1.append((lax.ppermute(bottom, "space", forward), lax.ppermute(top, "space", backward)))

    shares = weights / jnp.sum(weights)
    share = lax.dynamic_slice_in_dim(shares, lax.axis_index("member"), 1)
    own = scaling.reshape(rows_here, cols_all)
    dens = densities.reshape(rows_here, cols_all)
    wts = row_weights(band)
    mine = lax.dynamic_slice_in_dim(band, lax.axis_index("space") * nlocal, nlocal, 0)
    mine = mine.transpose(0, 2, 1, 3).reshape(nlocal, width, 3 * width)

    edges = sorted({0, nlocal - 1})
    inner = nlocal - 2
    a_edge = jnp.concatenate([mine[e] for e in edges], axis=0)
    edge_rows = tuple((e * width, width) for e in edges)
    edge_groups = tuple((g * 3 * width, 3 * width, g * width, width) for g in range(len(edges)))
    if inner > 0:
        a_inner = jnp.concatenate(
            [jnp.pad(mine[1 + i], ((0, 0), (i * width, (inner - 1 - i) * width))) for i in range(inner)], axis=0
        )
        inner_rows = ((width, inner * width),)
        inner_groups = ((0, nlocal * width, 0, inner * width),)

    def needs(blocks):
        return [(g * 3 * width + j * width, e - 1 + j) for g, e in enumerate(edges) for j in range(3)]

    def chunk_pieces(ids, to_row, cuts, first, last, row=0):
        found = []
        low, high = max(first - 1, 0), min(last + 1, nblocks)
        for c, which in enumerate(ids):
            a, b = max(low, cuts[c]), min(high, cuts[c + 1])
            if a < b:
                found.append((which, row, a - cuts[c], width, b - a, to_row, a - (first - 1)))
        return found

    if inner > 0:
        (ratio_inner,) = blur(
            "ratio_inner", [own], ((0, 0, 0, nlocal * width, nblocks, 0, 1),), inner_groups, inner_rows,
            0, nblocks, a_inner, wts, dens,
        )
    ratio_edges = []
    halo2 = []
    for c in range(chunks):
        first, last = cuts2[c], cuts2[c + 1]
        tops = [h[0] for h in halo1[: c + 1]]
        bottoms = [h[1] for h in halo1[: c + 1]]
        arrays = [own] + tops + bottoms
        pieces = []
        for to_row, b in needs(edges):
            if b < 0:
                pieces += chunk_pieces(range(1, c + 2), to_row, cuts1, first, last)
            elif b >= nlocal:
                pieces += chunk_pieces(range(c + 2, 2 * c + 3), to_row, cuts1, first, last)
            else:
                pieces += chunk_pieces([0], to_row, [0, nblocks], first, last, row=b * width)
        got = blur(
            f"ratio_edges_{c}", arrays, tuple(pieces), edge_groups, edge_rows, first, last, a_edge, wts, dens
        )
        ratio_edges.append(got)
        halo2.append((lax.ppermute(got[-1], "space", forward), lax.ppermute(got[0], "space", backward)))

    state = None
    whole = (rows_here, cols_all)
    if inner > 0:
        arrays = [ratio_inner] + [r[0] for r in ratio_edges] + [r[-1] for r in ratio_edges]
        pieces = [(0, 0, 0, inner * width, nblocks, width, 1)]
        pieces += chunk_pieces(range(1, chunks + 1), 0, cuts2, 0, nblocks)
        pieces += chunk_pieces(range(chunks + 1, 2 * chunks + 1), (nlocal - 1) * width, cuts2, 0, nblocks)
        t, m = blur(
            "logs_inner", arrays, tuple(pieces), inner_groups, inner_rows, 0, nblocks, a_inner, wts, own, share
        )
        state = raw_piece("raw_inner", t, lax.ppermute(t, "member", swap), m, inner_rows, 0, whole, state)
    for c in range(chunks):
        first, last = cuts3[c], cuts3[c + 1]
        arrays = [ratio_inner] if inner > 0 else []
        base = len(arrays)
        arrays += [h[0] for h in halo2[: c + 1]] + [h[1] for h in halo2[: c + 1]]
        arrays += [r[0] for r in ratio_edges[: c + 1]] + [r[-1] for r in ratio_edges[: c + 1]]
        ids = lambda part: range(base + part * (c + 1), base + (part + 1) * (c + 1))
        pieces = []
        for to_row, b in needs(edges):
            if b < 0:
                pieces += chunk_pieces(ids(0), to_row, cuts2, first, last)
            elif b >= nlocal:
                pieces += chunk_pieces(ids(1), to_row, cuts2, first, last)
            elif b == 0:
                pieces += chunk_pieces(ids(2), to_row, cuts2, first, last)
            elif b == nlocal - 1:
                pieces += chunk_pieces(ids(3), to_row, cuts2, first, last)
            else:
                pieces += chunk_pieces([0], to_row, [0, nblocks], first, last, row=(b - 1) * width)
        t, m = blur(
            f"logs_edges_{c}", arrays, tuple(pieces), edge_groups, edge_rows, first, last, a_edge, wts, own, share
        )
        state = raw_piece(
            f"raw_edges_{c}", t, lax.ppermute(t, "member", swap), m, edge_rows, first * width, whole, state
        )

    raw, quotient, mass = state
    mass = lax.psum(mass, "space")
    barycenter, new_scaling = outputs(raw, quotient, float(cols_all * cols_all) / mass, width)
    return barycenter, new_scaling.reshape(rows_here, 1, cols_all)


def solution(mesh):
    return jax.shard_map(
        local,
        mesh=mesh,
        in_specs=(
            P("space", ("parts", "member"), None),
            P("space", ("parts", "member"), None),
            P("parts"),
            P(),
        ),
        out_specs=(P(("parts", "space"), None), P("space", ("parts", "member"), None)),
        check_vma=False,
    )
```

```python
import functools

import jax
import jax.numpy as jnp
from jax import lax
from jax.experimental import pallas as pl
from jax.experimental.pallas import tpu as pltpu
from jax.sharding import PartitionSpec as P

F32 = jnp.float32
BF16 = jnp.bfloat16
VMEM_LIMIT = 48 * 1024 * 1024
GROUPS = 4
ANY = pl.BlockSpec(memory_space=pl.ANY)
INVMEM = pl.BlockSpec(memory_space=pltpu.VMEM)
INSMEM = pl.BlockSpec(memory_space=pltpu.SMEM)


def split(x):
    high = x.astype(BF16)
    return high, (x - high.astype(F32)).astype(BF16)


def dot3(a, b, dims):
    one = functools.partial(lax.dot_general, dimension_numbers=(dims, ((), ())), preferred_element_type=F32)
    return one(a[0], b[0]) + (one(a[0], b[1]) + one(a[1], b[0]))


def params():
    return pltpu.CompilerParams(vmem_limit_bytes=VMEM_LIMIT)


def pick(choice, side):
    if isinstance(choice, tuple):
        return pl.multiple_of(jnp.where(side == 0, choice[0], choice[1]), 128)
    return choice


def flatten_kernel(*refs):
    half = len(refs) // 2
    for src, dst in zip(refs[:half], refs[half:]):
        width = src.shape[2]
        for b in range(src.shape[1]):
            dst[:, b * width : (b + 1) * width] = src[:, b, :]


def flatten(arrays, width):
    rows, _, columns = arrays[0].shape
    tile = 64
    deep = pl.BlockSpec((tile, columns // width, width), lambda i: (i, 0, 0))
    flat = pl.BlockSpec((tile, columns), lambda i: (i, 0))
    return pl.pallas_call(
        flatten_kernel,
        grid=(rows // tile,),
        in_specs=[deep] * len(arrays),
        out_specs=[flat] * len(arrays),
        out_shape=[jax.ShapeDtypeStruct((rows, columns), F32)] * len(arrays),
        compiler_params=params(),
        name="flatten",
    )(*[a.reshape(rows, columns // width, width) for a in arrays])


def weight_kernel(nblocks, band_ref, high_ref, low_ref):
    pair = pl.program_id(0)
    width = band_ref.shape[2]
    zero = jnp.zeros((width, width), F32)
    for o in range(2):
        for i in range(4):
            j = i - o
            value = band_ref[o, j] if 0 <= j <= 2 else zero
            if (o, j) == (0, 0):
                value = jnp.where(pair > 0, value, 0.0)
            if (o, j) == (1, 2):
                value = jnp.where(pair < nblocks // 2 - 1, value, 0.0)
            high, low = split(value)
            rows, columns = slice(o * width, (o + 1) * width), slice(i * width, (i + 1) * width)
            high_ref[0, rows, columns] = high
            low_ref[0, rows, columns] = low


def row_weights(band):
    nblocks, _, width, _ = band.shape
    shape = jax.ShapeDtypeStruct((nblocks // 2, 2 * width, 4 * width), BF16)
    out_spec = pl.BlockSpec((1, 2 * width, 4 * width), lambda t: (t, 0, 0))
    return pl.pallas_call(
        functools.partial(weight_kernel, nblocks),
        grid=(nblocks // 2,),
        in_specs=[pl.BlockSpec((2, 3, width, width), lambda t: (t, 0, 0, 0))],
        out_specs=(out_spec, out_spec),
        out_shape=(shape, shape),
        name="row_weights",
    )(band)


def blur_kernel(plan, *refs):
    pieces, narrays, extra, final = plan
    side_ref, refs = refs[0], refs[1:]
    arrays = refs[:narrays]
    band_ref, high_ref, low_ref, extra_ref = refs[narrays : narrays + 4]
    rest = refs[narrays + 4 :]
    if final:
        share_ref, rest = rest[0], rest[1:]
    nouts = GROUPS + 1 if final else 1
    outs = rest[:nouts]
    field, ahigh, alow, yhigh, ylow, whigh, wlow, other = rest[nouts : nouts + 8]
    *results, in_sems, late_sems, out_sems = rest[nouts + 8 :]

    side = side_ref[0]
    nout, _, width, _ = band_ref.shape
    columns = field.shape[1]
    step = columns // GROUPS
    pairs = step // (2 * width)
    inside, late = [], []
    for g in range(GROUPS):
        at = pl.ds(g * step, step)
        inside.append(
            [
                pltpu.make_async_copy(
                    arrays[which].at[pl.ds(pick(row, side), rows), at],
                    field.at[pl.ds(pick(to, side), rows), at],
                    in_sems.at[g, k],
                )
                for k, (which, row, rows, to) in enumerate(pieces)
            ]
        )
        some = pl.ds(g * pairs, pairs)
        late.append(
            [
                pltpu.make_async_copy(high_ref.at[some], whigh.at[some], late_sems.at[g, 0]),
                pltpu.make_async_copy(low_ref.at[some], wlow.at[some], late_sems.at[g, 1]),
                pltpu.make_async_copy(
                    extra_ref.at[pl.ds(pick(extra, side), other.shape[0]), at], other.at[:, at], late_sems.at[g, 2]
                ),
            ]
        )
    for g in range(GROUPS):
        for copy in inside[g]:
            copy.start()
        if g > 0:
            for copy in late[g - 1]:
                copy.start()
    for copy in late[GROUPS - 1]:
        copy.start()

    ahigh[...] = jnp.zeros_like(ahigh)
    alow[...] = jnp.zeros_like(alow)
    for i in range(nout):
        for j in range(3):
            k = i % 2 + j
            place = (slice(i * width, (i + 1) * width), slice(k * width, (k + 1) * width))
            ahigh[place], alow[place] = split(band_ref[i, j])
    blocks = [(i, min(2, nout - i)) for i in range(0, nout, 2)]
    for y in (yhigh, ylow):
        y[:, :width] = jnp.zeros((y.shape[0], width), BF16)
        y[:, columns + width :] = jnp.zeros((y.shape[0], width), BF16)

    def columns_pass(g):
        for copy in inside[g]:
            copy.wait()
        for i in range(g * pairs, (g + 1) * pairs):
            at = slice(i * 2 * width, (i + 1) * 2 * width)
            to = slice((2 * i + 1) * width, (2 * i + 3) * width)
            for first, n in blocks:
                rows = slice(first * width, (first + n) * width)
                a = (ahigh[rows, : (n + 2) * width], alow[rows, : (n + 2) * width])
                y = dot3(a, split(field[first * width : (first + n + 2) * width, at]), ((1,), (0,)))
                yhigh[rows, to], ylow[rows, to] = split(y)

    def rows_pass(g):
        for copy in late[g]:
            copy.wait()
        for t in range(g * pairs, (g + 1) * pairs):
            source = slice(t * 2 * width, (t + 2) * 2 * width)
            at = slice(t * 2 * width, (t + 1) * 2 * width)
            value = dot3((yhigh[:, source], ylow[:, source]), (whigh[t], wlow[t]), ((1,), (1,)))
            if final:
                results[0][:, at] = value
                results[1][:, at] = share_ref[0] * jnp.log(other[:, at] * value)
            else:
                results[0][:, at] = other[:, at] / value
        at = pl.ds(g * step, step)
        targets = [outs[-1].at[:, at]] + ([outs[g]] if final else [])
        copies = [
            pltpu.make_async_copy(src.at[:, at], dst, out_sems.at[g, k])
            for k, (src, dst) in enumerate(zip(results, targets))
        ]
        for copy in copies:
            copy.start()
        return copies

    going = []
    for g in range(GROUPS):
        columns_pass(g)
        if g > 0:
            going += rows_pass(g - 1)
    going += rows_pass(GROUPS - 1)
    for copy in going:
        copy.wait()


def blur(name, side, arrays, pieces, bands, weights, other, extra, share=None):
    nout, _, width, _ = bands.shape
    npairs = weights[0].shape[0]
    columns = npairs * 2 * width
    rows, depth = nout * width, (nout + 2) * width
    final = share is not None
    nouts = 2 if final else 1
    shapes = [jax.ShapeDtypeStruct((rows, columns // GROUPS), F32)] * (GROUPS if final else 0)
    shapes.append(jax.ShapeDtypeStruct((rows, columns), F32))
    plan = (tuple(pieces), len(arrays), extra, final)
    work = 3 * 2 * rows * columns * (depth + 4 * width)
    moved = 4 * (depth + 3 * rows) * columns + npairs * 2 * 2 * 8 * width * width
    result = pl.pallas_call(
        functools.partial(blur_kernel, plan),
        in_specs=[INSMEM] + [ANY] * len(arrays) + [INVMEM, ANY, ANY, ANY] + [INSMEM] * final,
        out_specs=[ANY] * len(shapes),
        out_shape=shapes,
        scratch_shapes=[
            pltpu.VMEM((depth, columns), F32),
            pltpu.VMEM((rows, min(depth, 4 * width)), BF16),
            pltpu.VMEM((rows, min(depth, 4 * width)), BF16),
            pltpu.VMEM((rows, columns + 2 * width), BF16),
            pltpu.VMEM((rows, columns + 2 * width), BF16),
            pltpu.VMEM((npairs, 2 * width, 4 * width), BF16),
            pltpu.VMEM((npairs, 2 * width, 4 * width), BF16),
            pltpu.VMEM((rows, columns), F32),
        ]
        + [pltpu.VMEM((rows, columns), F32)] * nouts
        + [
            pltpu.SemaphoreType.DMA((GROUPS, len(pieces))),
            pltpu.SemaphoreType.DMA((GROUPS, 3)),
            pltpu.SemaphoreType.DMA((GROUPS, nouts)),
        ],
        compiler_params=params(),
        cost_estimate=pl.CostEstimate(flops=work // 64, bytes_accessed=moved // 64, transcendentals=0),
        name=name,
    )(side, *arrays, bands, *weights, other, *([share] if final else []))
    return (result[:-1], result[-1]) if final else result[0]


def raw_kernel(fresh, start_ref, *refs):
    own, peer, m_ref = refs[:GROUPS], refs[GROUPS : 2 * GROUPS], refs[2 * GROUPS]
    raw_ref, quotient_ref, mass_ref = refs[-3:]
    width = quotient_ref.shape[2]
    mass = 0.0
    for g in range(GROUPS):
        raw = jnp.exp(own[g][...] + peer[g][...])
        step = raw.shape[1]
        raw_ref[:, g * step : (g + 1) * step] = raw
        mass += jnp.sum(raw)
        quotient = raw / m_ref[:, g * step : (g + 1) * step]
        for b in range(step // width):
            quotient_ref[:, g * (step // width) + b, :] = quotient[:, b * width : (b + 1) * width]
    before = 0.0 if fresh else refs[2 * GROUPS + 3][0]
    mass_ref[0] = mass + jnp.where(pl.program_id(0) == 0, before, mass_ref[0])


def raw_rows(name, row, t, swap, m, choose, rows_here, width, so_far):
    fresh = so_far is None
    rows, columns = m.shape
    tile = 32
    part = pl.BlockSpec((tile, columns), lambda i, at: (i, 0))
    group = pl.BlockSpec((tile, columns // GROUPS), lambda i, at: (i, 0))
    deep = columns // width
    return pl.pallas_call(
        functools.partial(raw_kernel, fresh),
        grid_spec=pltpu.PrefetchScalarGridSpec(
            num_scalar_prefetch=1,
            grid=(rows // tile,),
            in_specs=[group] * (2 * GROUPS) + [part] + ([] if fresh else [ANY, ANY, INSMEM]),
            out_specs=(
                pl.BlockSpec((tile, columns), lambda i, at: (at[0] + i, 0)),
                pl.BlockSpec((tile, deep, width), lambda i, at: (at[0] + i, 0, 0)),
                INSMEM,
            ),
        ),
        out_shape=(
            jax.ShapeDtypeStruct((rows_here, columns), F32),
            jax.ShapeDtypeStruct((rows_here, deep, width), F32),
            jax.ShapeDtypeStruct((1,), F32),
        ),
        input_output_aliases={} if fresh else {2 * GROUPS + 2: 0, 2 * GROUPS + 3: 1},
        compiler_params=params(),
        cost_estimate=pl.CostEstimate(flops=m.size // 16, bytes_accessed=m.size // 4, transcendentals=0),
        name=name,
    )(choose([r // tile for r in row]).reshape(1), *t, *[swap(part) for part in t], m, *([] if fresh else so_far))


def output_kernel(raw_ref, quotient_ref, scale_ref, barycenter_ref, scaling_ref):
    scale = scale_ref[0]
    barycenter_ref[...] = raw_ref[...] * scale
    scaling_ref[...] = quotient_ref[...] * scale


def outputs(raw, quotient, scale):
    rows, columns = raw.shape
    tile = 64
    flat = pl.BlockSpec((tile, columns), lambda i: (i, 0))
    deep = pl.BlockSpec((tile,) + quotient.shape[1:], lambda i: (i, 0, 0))
    return pl.pallas_call(
        output_kernel,
        grid=(rows // tile,),
        in_specs=[flat, deep, INSMEM],
        out_specs=(flat, deep),
        out_shape=(jax.ShapeDtypeStruct(raw.shape, F32), jax.ShapeDtypeStruct(quotient.shape, F32)),
        compiler_params=params(),
        name="outputs",
    )(raw, quotient, scale)


def local(densities, scaling, weights, band):
    rows_here, maps_here, cols_all = densities.shape
    _, _, width, _ = band.shape
    nlocal = rows_here // width
    inner = max(nlocal - 2, 0)
    place = lax.axis_index("space")
    count = lax.axis_size("space")
    assert maps_here == 1 and lax.axis_size("member") == 2 and count % 2 == 0

    odd = place & 1
    side = odd.reshape(1)
    last = rows_here - width
    cross_row, near_row = (0, last), (last, 0)
    both = lambda pairs: pairs + [(b, a) for a, b in pairs]
    cross = functools.partial(
        lax.ppermute, axis_name="space", perm=both([(i, i + 1) for i in range(1, count - 1, 2)])
    )
    near = functools.partial(lax.ppermute, axis_name="space", perm=both([(i, i + 1) for i in range(0, count, 2)]))
    swap = functools.partial(lax.ppermute, axis_name="member", perm=[(0, 1), (1, 0)])

    def choose(choice):
        return jnp.where(odd == 0, choice[0], choice[1]).astype(jnp.int32)

    def rows_of(choice):
        return lax.dynamic_slice_in_dim(scaling, choose(choice), width, 0).reshape(width, cols_all)

    cross1 = cross(rows_of(cross_row))
    near1 = near(rows_of(near_row))

    shares = weights / jnp.sum(weights)
    share = lax.dynamic_slice_in_dim(shares, lax.axis_index("member"), 1)
    own, dens = flatten([scaling, densities], width)
    wts = row_weights(band)
    mine = place * nlocal
    band_at = lambda row, blocks: lax.dynamic_slice_in_dim(band, mine + row // width, blocks, 0)

    if nlocal > 1:
        two = rows_here - 2 * width
        cross_pieces = [(0, (0, two), 2 * width, (width, 0)), (1, 0, width, (0, 2 * width))]
        near_pieces = [(0, (two, 0), 2 * width, (0, width)), (1, 0, width, (2 * width, 0))]
        edges = [("cross", cross_row, cross_pieces, cross), ("near", near_row, near_pieces, near)]
        halos1 = [[cross1], [near1]]
    else:
        pieces = [(0, 0, width, width), (1, 0, width, (0, 2 * width)), (2, 0, width, (2 * width, 0))]
        edges = [("only", (0, 0), pieces, None)]
        halos1 = [[cross1, near1]]
    edge_bands = [band_at(choose(row), 1) for _, row, _, _ in edges]

    if inner > 0:
        inner_bands = band_at(width, inner)
        ratio_inner = blur(
            "ratio_inner", side, [own], [(0, 0, rows_here, 0)], inner_bands, wts, dens, width
        )
    ratios, halos2 = [], []
    for (name, row, pieces, send), halo, bands in zip(edges, halos1, edge_bands):
        if ratios:
            bands, ratios[-1] = lax.optimization_barrier((bands, ratios[-1]))
        ratio = blur("ratio_" + name, side, [own] + halo, pieces, bands, wts, dens, row)
        ratios.append(ratio)
        halos2.append([cross(ratio), near(ratio)] if send is None else [send(ratio)])

    def finish(name, arrays, pieces, bands, row, share, state):
        t, m = blur("logs_" + name, side, arrays, pieces, bands, wts, own, row, share)
        return raw_rows("raw_" + name, row, t, swap, m, choose, rows_here, width, state)

    if nlocal == 1:
        state = finish("only", ratios + halos2[0], pieces, edge_bands[0], (0, 0), share, None)
    else:
        most, end = rows_here - width, rows_here
        pieces = [(0, 0, width, (width, most)), (1, 0, width, (end, 0)), (2, 0, width, (0, end))]
        if inner > 0:
            pieces.append((3, 0, inner * width, (2 * width, width)))
        arrays = ratios + halos2[0] + ([ratio_inner] if inner > 0 else [])
        row = (0, width)
        state = finish("most", arrays, pieces, band_at(choose(row), nlocal - 1), row, share, None)
        share, state = lax.optimization_barrier((share, state))
        if inner > 0:
            beside = (ratio_inner, ((inner - 1) * width, 0))
        else:
            beside = (ratios[0], 0)
        pieces = [(0, 0, width, width), (1, beside[1], width, (0, 2 * width)), (2, 0, width, (2 * width, 0))]
        state = finish("near", [ratios[1], beside[0]] + halos2[1], pieces, edge_bands[1], near_row, share, state)

    raw, quotient, mass = state
    mass = lax.psum(mass, "space")
    barycenter, new_scaling = outputs(raw, quotient, float(cols_all * cols_all) / mass)
    return barycenter, new_scaling.reshape(rows_here, 1, cols_all)


def solution(mesh):
    return jax.shard_map(
        local,
        mesh=mesh,
        in_specs=(
            P("space", ("parts", "member"), None),
            P("space", ("parts", "member"), None),
            P("parts"),
            P(),
        ),
        out_specs=(P(("parts", "space"), None), P("space", ("parts", "member"), None)),
        check_vma=False,
    )
```

```python
import functools

import jax
import jax.numpy as jnp
from jax import lax
from jax.experimental import pallas as pl
from jax.experimental.pallas import tpu as pltpu
from jax.sharding import PartitionSpec as P

F32 = jnp.float32
BF16 = jnp.bfloat16
GROUPS = 4
ANY = pl.BlockSpec(memory_space=pl.ANY)
INVMEM = pl.BlockSpec(memory_space=pltpu.VMEM)
INSMEM = pl.BlockSpec(memory_space=pltpu.SMEM)


def split(x):
    high = x.astype(BF16)
    return high, (x - high.astype(F32)).astype(BF16)


def dot3(a, b, dims):
    one = functools.partial(lax.dot_general, dimension_numbers=(dims, ((), ())), preferred_element_type=F32)
    return one(a[0], b[0]) + (one(a[0], b[1]) + one(a[1], b[0]))


def params(mebibytes):
    return pltpu.CompilerParams(vmem_limit_bytes=mebibytes * 1024 * 1024)


def hbm(*arrays):
    return [pltpu.with_memory_space_constraint(a, pltpu.HBM) for a in arrays]


def pick(choice, side):
    if isinstance(choice, tuple):
        return pl.multiple_of(jnp.where(side == 0, choice[0], choice[1]), 128)
    return choice


def cut_kernel(first, side_ref, src, dst, sem):
    copy = pltpu.make_async_copy(src.at[pl.ds(pick(first, side_ref[0]), dst.shape[0])], dst, sem)
    copy.start()
    copy.wait()


def cut(name, side, array, first, rows):
    return pl.pallas_call(
        functools.partial(cut_kernel, first),
        in_specs=[INSMEM, ANY],
        out_specs=ANY,
        out_shape=pltpu.HBM((rows,) + array.shape[1:], F32),
        scratch_shapes=[pltpu.SemaphoreType.DMA],
        name=name,
    )(side, *hbm(array))


def area(ref, row, rows, columns):
    return ref.at[pl.ds(row, rows), 0, columns] if len(ref.shape) == 3 else ref.at[pl.ds(row, rows), columns]


def weight_kernel(nblocks, band_ref, high_ref, low_ref):
    pair = pl.program_id(0)
    width = band_ref.shape[2]
    zero = jnp.zeros((width, width), F32)
    for o in range(2):
        for i in range(4):
            j = i - o
            value = band_ref[o, j] if 0 <= j <= 2 else zero
            if (o, j) == (0, 0):
                value = jnp.where(pair > 0, value, 0.0)
            if (o, j) == (1, 2):
                value = jnp.where(pair < nblocks // 2 - 1, value, 0.0)
            high, low = split(value)
            rows, columns = slice(o * width, (o + 1) * width), slice(i * width, (i + 1) * width)
            high_ref[0, rows, columns] = high
            low_ref[0, rows, columns] = low


def row_weights(band):
    nblocks, _, width, _ = band.shape
    shape = pltpu.HBM((nblocks // 2, 2 * width, 4 * width), BF16)
    out_spec = pl.BlockSpec((1, 2 * width, 4 * width), lambda t: (t, 0, 0))
    return pl.pallas_call(
        functools.partial(weight_kernel, nblocks),
        grid=(nblocks // 2,),
        in_specs=[pl.BlockSpec((2, 3, width, width), lambda t: (t, 0, 0, 0))],
        out_specs=(out_spec, out_spec),
        out_shape=(shape, shape),
        name="row_weights",
    )(*hbm(band))


def blur_kernel(plan, *refs):
    pieces, narrays, extra, final = plan
    side_ref, refs = refs[0], refs[1:]
    arrays = refs[:narrays]
    band_ref, high_ref, low_ref, extra_ref = refs[narrays : narrays + 4]
    rest = refs[narrays + 4 :]
    if final:
        share_ref, rest = rest[0], rest[1:]
    nouts = GROUPS + 1 if final else 1
    outs = rest[:nouts]
    field, ahigh, alow, yhigh, ylow, whigh, wlow, other = rest[nouts : nouts + 8]
    *results, in_sems, late_sems, out_sems = rest[nouts + 8 :]

    side = side_ref[0]
    nout, _, width, _ = band_ref.shape
    columns = field.shape[1]
    step = columns // GROUPS
    pairs = step // (2 * width)
    inside, late = [], []
    for g in range(GROUPS):
        at = pl.ds(g * step, step)
        inside.append(
            [
                pltpu.make_async_copy(
                    area(arrays[which], pick(row, side), rows, at),
                    field.at[pl.ds(pick(to, side), rows), at],
                    in_sems.at[g, k],
                )
                for k, (which, row, rows, to) in enumerate(pieces)
            ]
        )
        some = pl.ds(g * pairs, pairs)
        late.append(
            [
                pltpu.make_async_copy(high_ref.at[some], whigh.at[some], late_sems.at[g, 0]),
                pltpu.make_async_copy(low_ref.at[some], wlow.at[some], late_sems.at[g, 1]),
                pltpu.make_async_copy(
                    area(extra_ref, pick(extra, side), other.shape[0], at), other.at[:, at], late_sems.at[g, 2]
                ),
            ]
        )
    for g in range(GROUPS):
        for copy in inside[g]:
            copy.start()
        if g > 0:
            for copy in late[g - 1]:
                copy.start()
    for copy in late[GROUPS - 1]:
        copy.start()

    ahigh[...] = jnp.zeros_like(ahigh)
    alow[...] = jnp.zeros_like(alow)
    for i in range(nout):
        for j in range(3):
            k = i % 2 + j
            place = (slice(i * width, (i + 1) * width), slice(k * width, (k + 1) * width))
            ahigh[place], alow[place] = split(band_ref[i, j])
    blocks = [(i, min(2, nout - i)) for i in range(0, nout, 2)]
    for y in (yhigh, ylow):
        y[:, :width] = jnp.zeros((y.shape[0], width), BF16)
        y[:, columns + width :] = jnp.zeros((y.shape[0], width), BF16)

    def columns_pass(g):
        for copy in inside[g]:
            copy.wait()
        for i in range(g * pairs, (g + 1) * pairs):
            at = slice(i * 2 * width, (i + 1) * 2 * width)
            to = slice((2 * i + 1) * width, (2 * i + 3) * width)
            for first, n in blocks:
                rows = slice(first * width, (first + n) * width)
                a = (ahigh[rows, : (n + 2) * width], alow[rows, : (n + 2) * width])
                y = dot3(a, split(field[first * width : (first + n + 2) * width, at]), ((1,), (0,)))
                yhigh[rows, to], ylow[rows, to] = split(y)

    def rows_pass(g):
        for copy in late[g]:
            copy.wait()
        for t in range(g * pairs, (g + 1) * pairs):
            source = slice(t * 2 * width, (t + 2) * 2 * width)
            at = slice(t * 2 * width, (t + 1) * 2 * width)
            value = dot3((yhigh[:, source], ylow[:, source]), (whigh[t], wlow[t]), ((1,), (1,)))
            if final:
                results[0][:, at] = value
                results[1][:, at] = share_ref[0] * jnp.log(other[:, at] * value)
            else:
                results[0][:, at] = other[:, at] / value
        at = pl.ds(g * step, step)
        targets = [outs[-1].at[:, at]] + ([outs[g]] if final else [])
        copies = [
            pltpu.make_async_copy(src.at[:, at], dst, out_sems.at[g, k])
            for k, (src, dst) in enumerate(zip(results, targets))
        ]
        for copy in copies:
            copy.start()
        return copies

    going = []
    for g in range(GROUPS):
        columns_pass(g)
        if g > 0:
            going += rows_pass(g - 1)
    going += rows_pass(GROUPS - 1)
    for copy in going:
        copy.wait()


def blur(name, side, arrays, pieces, bands, weights, other, extra, share=None, pin=True):
    nout, _, width, _ = bands.shape
    npairs = weights[0].shape[0]
    columns = npairs * 2 * width
    rows, depth = nout * width, (nout + 2) * width
    final = share is not None
    nouts = 2 if final else 1
    kind = pltpu.HBM if pin else jax.ShapeDtypeStruct
    shapes = [kind((rows, columns // GROUPS), F32)] * (GROUPS if final else 0)
    shapes.append(kind((rows, columns), F32))
    plan = (tuple(pieces), len(arrays), extra, final)
    work = 3 * 2 * rows * columns * (depth + 4 * width)
    moved = 4 * (depth + 3 * rows) * columns + npairs * 2 * 2 * 8 * width * width
    size = 4 * columns * (depth + (1 + nouts) * rows) + 4 * rows * columns + npairs * 2 * 2 * 8 * width * width
    result = pl.pallas_call(
        functools.partial(blur_kernel, plan),
        in_specs=[INSMEM] + [ANY] * len(arrays) + [INVMEM, ANY, ANY, ANY] + [INSMEM] * final,
        out_specs=[ANY] * len(shapes),
        out_shape=shapes,
        scratch_shapes=[
            pltpu.VMEM((depth, columns), F32),
            pltpu.VMEM((rows, min(depth, 4 * width)), BF16),
            pltpu.VMEM((rows, min(depth, 4 * width)), BF16),
            pltpu.VMEM((rows, columns + 2 * width), BF16),
            pltpu.VMEM((rows, columns + 2 * width), BF16),
            pltpu.VMEM((npairs, 2 * width, 4 * width), BF16),
            pltpu.VMEM((npairs, 2 * width, 4 * width), BF16),
            pltpu.VMEM((rows, columns), F32),
        ]
        + [pltpu.VMEM((rows, columns), F32)] * nouts
        + [
            pltpu.SemaphoreType.DMA((GROUPS, len(pieces))),
            pltpu.SemaphoreType.DMA((GROUPS, 3)),
            pltpu.SemaphoreType.DMA((GROUPS, nouts)),
        ],
        compiler_params=params(size // 2**20 + 6),
        cost_estimate=pl.CostEstimate(flops=work // 64, bytes_accessed=moved // 64, transcendentals=0),
        name=name,
    )(side, *arrays, bands, *hbm(*weights, other), *([share] if final else []))
    return (result[:-1], result[-1]) if final else result[0]


def raw_kernel(fresh, start_ref, *refs):
    own, peer, m_ref = refs[:GROUPS], refs[GROUPS : 2 * GROUPS], refs[2 * GROUPS]
    raw_ref, quotient_ref, mass_ref, quotient, sems = refs[-5:]
    tile = raw_ref.shape[0]
    at = pl.program_id(0)
    slot = lax.rem(at, 2)

    def copy(step, slot):
        row = pl.multiple_of((start_ref[0] + step) * tile, tile)
        return pltpu.make_async_copy(quotient.at[slot], area(quotient_ref, row, tile, slice(None)), sems.at[slot])

    @pl.when(at >= 2)
    def _():
        copy(at - 2, slot).wait()

    mass = 0.0
    for g in range(GROUPS):
        raw = jnp.exp(own[g][...] + peer[g][...])
        step = raw.shape[1]
        raw_ref[:, g * step : (g + 1) * step] = raw
        mass += jnp.sum(raw)
        quotient[slot, :, g * step : (g + 1) * step] = raw / m_ref[:, g * step : (g + 1) * step]
    before = 0.0 if fresh else refs[2 * GROUPS + 3][0]
    mass_ref[0] = mass + jnp.where(at == 0, before, mass_ref[0])
    copy(at, slot).start()

    @pl.when(at == pl.num_programs(0) - 1)
    def _():
        copy(at - 1, 1 - slot).wait()
        copy(at, slot).wait()


def raw_rows(name, row, t, peers, m, choose, rows_here, so_far):
    fresh = so_far is None
    rows, columns = m.shape
    tile = 32
    part = pl.BlockSpec((tile, columns), lambda i, at: (i, 0))
    group = pl.BlockSpec((tile, columns // GROUPS), lambda i, at: (i, 0))
    return pl.pallas_call(
        functools.partial(raw_kernel, fresh),
        grid_spec=pltpu.PrefetchScalarGridSpec(
            num_scalar_prefetch=1,
            grid=(rows // tile,),
            in_specs=[group] * (2 * GROUPS) + [part] + ([] if fresh else [ANY, ANY, INSMEM]),
            out_specs=(
                pl.BlockSpec((tile, columns), lambda i, at: (at[0] + i, 0)),
                ANY,
                INSMEM,
            ),
            scratch_shapes=[pltpu.VMEM((2, tile, columns), F32), pltpu.SemaphoreType.DMA((2,))],
        ),
        out_shape=(
            pltpu.HBM((rows_here, columns), F32),
            pltpu.HBM((rows_here, 1, columns), F32),
            jax.ShapeDtypeStruct((1,), F32),
        ),
        input_output_aliases={} if fresh else {2 * GROUPS + 2: 0, 2 * GROUPS + 3: 1},
        compiler_params=params(16),
        cost_estimate=pl.CostEstimate(flops=m.size // 16, bytes_accessed=m.size // 4, transcendentals=0),
        name=name,
    )(choose([r // tile for r in row]).reshape(1), *t, *peers, m, *([] if fresh else hbm(*so_far[:2]) + [so_far[2]]))


def output_kernel(raw_ref, quotient_ref, scale_ref, barycenter_ref, scaling_ref):
    scale = scale_ref[0]
    barycenter_ref[...] = raw_ref[...] * scale
    scaling_ref[...] = quotient_ref[...] * scale


def outputs(raw, quotient, scale):
    rows, columns = raw.shape
    tile = 64
    flat = pl.BlockSpec((tile, columns), lambda i: (i, 0))
    deep = pl.BlockSpec((tile,) + quotient.shape[1:], lambda i: (i, 0, 0))
    return pl.pallas_call(
        output_kernel,
        grid=(rows // tile,),
        in_specs=[flat, deep, INSMEM],
        out_specs=(flat, deep),
        out_shape=(jax.ShapeDtypeStruct(raw.shape, F32), jax.ShapeDtypeStruct(quotient.shape, F32)),
        compiler_params=params(16),
        name="outputs",
    )(*hbm(raw, quotient), scale)


def local(densities, scaling, weights, band):
    rows_here, maps_here, cols_all = densities.shape
    _, _, width, _ = band.shape
    nlocal = rows_here // width
    inner = max(nlocal - 2, 0)
    place = lax.axis_index("space")
    count = lax.axis_size("space")
    assert maps_here == 1 and lax.axis_size("member") == 2 and count % 2 == 0

    odd = place & 1
    side = odd.reshape(1)
    last = rows_here - width
    cross_row, near_row = (0, last), (last, 0)
    both = lambda pairs: pairs + [(b, a) for a, b in pairs]
    cross = functools.partial(
        lax.ppermute, axis_name="space", perm=both([(i, i + 1) for i in range(1, count - 1, 2)])
    )
    near = functools.partial(lax.ppermute, axis_name="space", perm=both([(i, i + 1) for i in range(0, count, 2)]))
    swap = functools.partial(lax.ppermute, axis_name="member", perm=[(0, 1), (1, 0)])

    def choose(choice):
        return jnp.where(odd == 0, choice[0], choice[1]).astype(jnp.int32)

    cross1 = cross(cut("cut_cross", side, scaling, cross_row, width))
    near1 = near(cut("cut_near", side, scaling, near_row, width))

    shares = weights / jnp.sum(weights)
    share = lax.dynamic_slice_in_dim(shares, lax.axis_index("member"), 1)
    wts = row_weights(band)
    mine = place * nlocal
    band_at = lambda row, blocks: lax.dynamic_slice_in_dim(band, mine + row // width, blocks, 0)

    if inner > 0:
        inner_bands = band_at(width, inner)
        ratio_inner = blur(
            "ratio_inner", side, hbm(scaling), [(0, 0, rows_here, 0)], inner_bands, wts, densities, width
        )
        cross1, ratio_inner = lax.optimization_barrier((cross1, ratio_inner))
    if nlocal == 1:
        pieces = [(0, 0, width, width), (1, 0, width, (0, 2 * width)), (2, 0, width, (2 * width, 0))]
        bands = band_at(0, 1)
        ratio = blur("ratio_only", side, [scaling, cross1, near1], pieces, bands, wts, densities, 0)
        cross2, near2 = cross(ratio), near(ratio)
    else:
        two = rows_here - 2 * width
        pieces = [(0, (0, two), 2 * width, (width, 0)), (1, 0, width, (0, 2 * width))]
        bands = band_at(choose(cross_row), 1)
        ratio_cross = blur("ratio_cross", side, hbm(scaling) + [cross1], pieces, bands, wts, densities, cross_row)
        ratio_cross, near1 = lax.optimization_barrier((ratio_cross, near1))
        cross2 = cross(ratio_cross)
        pieces = [(0, (two, 0), 2 * width, (0, width)), (1, 0, width, (2 * width, 0))]
        bands = band_at(choose(near_row), 1)
        ratio_near = blur("ratio_near", side, hbm(scaling) + [near1], pieces, bands, wts, densities, near_row)
        near2 = near(ratio_near)

    def finish(name, arrays, pieces, bands, row, share, state, pin=True):
        t, m = blur("logs_" + name, side, arrays, pieces, bands, wts, scaling, row, share, pin)
        keep = hbm if pin else lambda *a: list(a)
        return raw_rows(
            "raw_" + name, row, keep(*t), [swap(part) for part in t], *keep(m), choose, rows_here, state
        )

    if nlocal == 1:
        pieces = [(0, 0, width, width), (1, 0, width, (0, 2 * width)), (2, 0, width, (2 * width, 0))]
        state = finish("only", [ratio, cross2, near2], pieces, bands, (0, 0), share, None)
    else:
        most, end = rows_here - width, rows_here
        pieces = [(0, 0, width, (width, most)), (1, 0, width, (end, 0)), (2, 0, width, (0, end))]
        arrays = [ratio_cross, ratio_near, cross2]
        beside, beside_row = ratio_cross, 0
        if inner > 0:
            pieces.append((3, 0, inner * width, (2 * width, width)))
            arrays.append(ratio_inner)
            beside, beside_row = ratio_inner, ((inner - 1) * width, 0)
        row = (0, width)
        state = finish("most", hbm(*arrays[:2]) + arrays[2:3] + hbm(*arrays[3:]), pieces, band_at(choose(row), nlocal - 1), row, share, None)
        share, state = lax.optimization_barrier((share, state))
        pieces = [(0, 0, width, width), (1, beside_row, width, (0, 2 * width)), (2, 0, width, (2 * width, 0))]
        state = finish("near", hbm(ratio_near, beside) + [near2], pieces, bands, near_row, share, state, False)

    raw, quotient, mass = state
    mass = lax.psum(mass, "space")
    barycenter, new_scaling = outputs(raw, quotient.reshape(rows_here, cols_all // width, width), float(cols_all * cols_all) / mass)
    return barycenter, new_scaling.reshape(rows_here, 1, cols_all)


def solution(mesh):
    return jax.shard_map(
        local,
        mesh=mesh,
        in_specs=(
            P("space", ("parts", "member"), None),
            P("space", ("parts", "member"), None),
            P("parts"),
            P(),
        ),
        out_specs=(P(("parts", "space"), None), P("space", ("parts", "member"), None)),
        check_vma=False,
    )
```

```python
import functools

import jax
import jax.numpy as jnp
from jax import lax
from jax.experimental import pallas as pl
from jax.experimental.pallas import tpu as pltpu
from jax.sharding import PartitionSpec as P

F32 = jnp.float32
BF16 = jnp.bfloat16
GROUPS = 4
ANY = pl.BlockSpec(memory_space=pl.ANY)
INVMEM = pl.BlockSpec(memory_space=pltpu.VMEM)
INSMEM = pl.BlockSpec(memory_space=pltpu.SMEM)


def split(x):
    high = x.astype(BF16)
    return high, (x - high.astype(F32)).astype(BF16)


def dot3(a, b, dims):
    one = functools.partial(lax.dot_general, dimension_numbers=(dims, ((), ())), preferred_element_type=F32)
    return one(a[0], b[0]) + (one(a[0], b[1]) + one(a[1], b[0]))


def params(mebibytes):
    return pltpu.CompilerParams(vmem_limit_bytes=mebibytes * 1024 * 1024)


def hbm(*arrays):
    return [pltpu.with_memory_space_constraint(a, pltpu.HBM) for a in arrays]


def pick(choice, side):
    if isinstance(choice, tuple):
        return pl.multiple_of(jnp.where(side == 0, choice[0], choice[1]), 128)
    return choice


def cut_kernel(first, side_ref, src, dst, stage, sems):
    rows = stage.shape[0] // GROUPS
    start = pick(first, side_ref[0])
    parts = [pl.ds(g * rows, rows) for g in range(GROUPS)]
    inward = [
        pltpu.make_async_copy(src.at[pl.ds(start + g * rows, rows)], stage.at[part], sems.at[0, g])
        for g, part in enumerate(parts)
    ]
    outward = [pltpu.make_async_copy(stage.at[part], dst.at[part], sems.at[1, g]) for g, part in enumerate(parts)]
    for copy in inward:
        copy.start()
    for g in range(GROUPS):
        inward[g].wait()
        outward[g].start()
    for copy in outward:
        copy.wait()


def cut(name, side, array, first, rows):
    shape = (rows,) + array.shape[1:]
    return pl.pallas_call(
        functools.partial(cut_kernel, first),
        in_specs=[INSMEM, ANY],
        out_specs=ANY,
        out_shape=pltpu.HBM(shape, F32),
        scratch_shapes=[pltpu.VMEM(shape, F32), pltpu.SemaphoreType.DMA((2, GROUPS))],
        compiler_params=params(8),
        name=name,
    )(side, *hbm(array))


def area(ref, row, rows, columns):
    return ref.at[pl.ds(row, rows), 0, columns] if len(ref.shape) == 3 else ref.at[pl.ds(row, rows), columns]


def weight_kernel(nblocks, band_ref, high_ref, low_ref):
    pair = pl.program_id(0)
    width = band_ref.shape[2]
    zero = jnp.zeros((width, width), F32)
    for o in range(2):
        for i in range(4):
            j = i - o
            value = band_ref[o, j] if 0 <= j <= 2 else zero
            if (o, j) == (0, 0):
                value = jnp.where(pair > 0, value, 0.0)
            if (o, j) == (1, 2):
                value = jnp.where(pair < nblocks // 2 - 1, value, 0.0)
            high, low = split(value)
            rows, columns = slice(o * width, (o + 1) * width), slice(i * width, (i + 1) * width)
            high_ref[0, rows, columns] = high
            low_ref[0, rows, columns] = low


def row_weights(band):
    nblocks, _, width, _ = band.shape
    shape = pltpu.HBM((nblocks // 2, 2 * width, 4 * width), BF16)
    out_spec = pl.BlockSpec((1, 2 * width, 4 * width), lambda t: (t, 0, 0))
    return pl.pallas_call(
        functools.partial(weight_kernel, nblocks),
        grid=(nblocks // 2,),
        in_specs=[pl.BlockSpec((2, 3, width, width), lambda t: (t, 0, 0, 0))],
        out_specs=(out_spec, out_spec),
        out_shape=(shape, shape),
        name="row_weights",
    )(*hbm(band))


def blur_kernel(plan, *refs):
    pieces, narrays, extra, final = plan
    side_ref, refs = refs[0], refs[1:]
    arrays = refs[:narrays]
    band_ref, high_ref, low_ref, extra_ref = refs[narrays : narrays + 4]
    rest = refs[narrays + 4 :]
    if final:
        share_ref, rest = rest[0], rest[1:]
    nouts = GROUPS + 1 if final else 1
    outs = rest[:nouts]
    field, ahigh, alow, yhigh, ylow, whigh, wlow, other = rest[nouts : nouts + 8]
    *results, in_sems, late_sems, out_sems = rest[nouts + 8 :]

    side = side_ref[0]
    nout, _, width, _ = band_ref.shape
    columns = field.shape[1]
    step = columns // GROUPS
    pairs = step // (2 * width)
    inside, late = [], []
    for g in range(GROUPS):
        at = pl.ds(g * step, step)
        inside.append(
            [
                pltpu.make_async_copy(
                    area(arrays[which], pick(row, side), rows, at),
                    field.at[pl.ds(pick(to, side), rows), at],
                    in_sems.at[g, k],
                )
                for k, (which, row, rows, to) in enumerate(pieces)
            ]
        )
        some = pl.ds(g * pairs, pairs)
        late.append(
            [
                pltpu.make_async_copy(high_ref.at[some], whigh.at[some], late_sems.at[g, 0]),
                pltpu.make_async_copy(low_ref.at[some], wlow.at[some], late_sems.at[g, 1]),
                pltpu.make_async_copy(
                    area(extra_ref, pick(extra, side), other.shape[0], at), other.at[:, at], late_sems.at[g, 2]
                ),
            ]
        )
    for g in range(GROUPS):
        for copy in inside[g]:
            copy.start()
        if g > 0:
            for copy in late[g - 1]:
                copy.start()
    for copy in late[GROUPS - 1]:
        copy.start()

    ahigh[...] = jnp.zeros_like(ahigh)
    alow[...] = jnp.zeros_like(alow)
    for i in range(nout):
        for j in range(3):
            k = i % 2 + j
            place = (slice(i * width, (i + 1) * width), slice(k * width, (k + 1) * width))
            ahigh[place], alow[place] = split(band_ref[i, j])
    blocks = [(i, min(2, nout - i)) for i in range(0, nout, 2)]
    for y in (yhigh, ylow):
        y[:, :width] = jnp.zeros((y.shape[0], width), BF16)
        y[:, columns + width :] = jnp.zeros((y.shape[0], width), BF16)

    def columns_pass(g):
        for copy in inside[g]:
            copy.wait()
        for i in range(g * pairs, (g + 1) * pairs):
            at = slice(i * 2 * width, (i + 1) * 2 * width)
            to = slice((2 * i + 1) * width, (2 * i + 3) * width)
            for first, n in blocks:
                rows = slice(first * width, (first + n) * width)
                a = (ahigh[rows, : (n + 2) * width], alow[rows, : (n + 2) * width])
                y = dot3(a, split(field[first * width : (first + n + 2) * width, at]), ((1,), (0,)))
                yhigh[rows, to], ylow[rows, to] = split(y)

    def rows_pass(g):
        for copy in late[g]:
            copy.wait()
        for t in range(g * pairs, (g + 1) * pairs):
            source = slice(t * 2 * width, (t + 2) * 2 * width)
            at = slice(t * 2 * width, (t + 1) * 2 * width)
            value = dot3((yhigh[:, source], ylow[:, source]), (whigh[t], wlow[t]), ((1,), (1,)))
            if final:
                results[0][:, at] = value
                results[1][:, at] = share_ref[0] * jnp.log(other[:, at] * value)
            else:
                results[0][:, at] = other[:, at] / value
        at = pl.ds(g * step, step)
        targets = [outs[-1].at[:, at]] + ([outs[g]] if final else [])
        copies = [
            pltpu.make_async_copy(src.at[:, at], dst, out_sems.at[g, k])
            for k, (src, dst) in enumerate(zip(results, targets))
        ]
        for copy in copies:
            copy.start()
        return copies

    going = []
    for g in range(GROUPS):
        columns_pass(g)
        if g > 0:
            going += rows_pass(g - 1)
    going += rows_pass(GROUPS - 1)
    for copy in going:
        copy.wait()


def blur(name, side, arrays, pieces, bands, weights, other, extra, share=None, pin=True):
    nout, _, width, _ = bands.shape
    npairs = weights[0].shape[0]
    columns = npairs * 2 * width
    rows, depth = nout * width, (nout + 2) * width
    final = share is not None
    nouts = 2 if final else 1
    kind = pltpu.HBM if pin else jax.ShapeDtypeStruct
    shapes = [kind((rows, columns // GROUPS), F32)] * (GROUPS if final else 0)
    shapes.append(kind((rows, columns), F32))
    plan = (tuple(pieces), len(arrays), extra, final)
    work = 3 * 2 * rows * columns * (depth + 4 * width)
    moved = 4 * (depth + 3 * rows) * columns + npairs * 2 * 2 * 8 * width * width
    size = 4 * columns * (depth + (1 + nouts) * rows) + 4 * rows * columns + npairs * 2 * 2 * 8 * width * width
    result = pl.pallas_call(
        functools.partial(blur_kernel, plan),
        in_specs=[INSMEM] + [ANY] * len(arrays) + [INVMEM, ANY, ANY, ANY] + [INSMEM] * final,
        out_specs=[ANY] * len(shapes),
        out_shape=shapes,
        scratch_shapes=[
            pltpu.VMEM((depth, columns), F32),
            pltpu.VMEM((rows, min(depth, 4 * width)), BF16),
            pltpu.VMEM((rows, min(depth, 4 * width)), BF16),
            pltpu.VMEM((rows, columns + 2 * width), BF16),
            pltpu.VMEM((rows, columns + 2 * width), BF16),
            pltpu.VMEM((npairs, 2 * width, 4 * width), BF16),
            pltpu.VMEM((npairs, 2 * width, 4 * width), BF16),
            pltpu.VMEM((rows, columns), F32),
        ]
        + [pltpu.VMEM((rows, columns), F32)] * nouts
        + [
            pltpu.SemaphoreType.DMA((GROUPS, len(pieces))),
            pltpu.SemaphoreType.DMA((GROUPS, 3)),
            pltpu.SemaphoreType.DMA((GROUPS, nouts)),
        ],
        compiler_params=params(size // 2**20 + 6),
        cost_estimate=pl.CostEstimate(flops=work // 64, bytes_accessed=moved // 64, transcendentals=0),
        name=name,
    )(side, *arrays, bands, *hbm(*weights, other), *([share] if final else []))
    return (result[:-1], result[-1]) if final else result[0]


def raw_kernel(fresh, start_ref, *refs):
    own, peer, m_ref = refs[:GROUPS], refs[GROUPS : 2 * GROUPS], refs[2 * GROUPS]
    raw_ref, quotient_ref, mass_ref, quotient, sems = refs[-5:]
    tile = raw_ref.shape[0]
    at = pl.program_id(0)
    slot = lax.rem(at, 2)

    def copy(step, slot):
        row = pl.multiple_of((start_ref[0] + step) * tile, tile)
        return pltpu.make_async_copy(quotient.at[slot], area(quotient_ref, row, tile, slice(None)), sems.at[slot])

    @pl.when(at >= 2)
    def _():
        copy(at - 2, slot).wait()

    mass = 0.0
    for g in range(GROUPS):
        raw = jnp.exp(own[g][...] + peer[g][...])
        step = raw.shape[1]
        raw_ref[:, g * step : (g + 1) * step] = raw
        mass += jnp.sum(raw)
        quotient[slot, :, g * step : (g + 1) * step] = raw / m_ref[:, g * step : (g + 1) * step]
    before = 0.0 if fresh else refs[2 * GROUPS + 3][0]
    mass_ref[0] = mass + jnp.where(at == 0, before, mass_ref[0])
    copy(at, slot).start()

    @pl.when(at == pl.num_programs(0) - 1)
    def _():
        copy(at - 1, 1 - slot).wait()
        copy(at, slot).wait()


def raw_rows(name, row, t, peers, m, choose, rows_here, so_far):
    fresh = so_far is None
    rows, columns = m.shape
    tile = 32
    part = pl.BlockSpec((tile, columns), lambda i, at: (i, 0))
    group = pl.BlockSpec((tile, columns // GROUPS), lambda i, at: (i, 0))
    return pl.pallas_call(
        functools.partial(raw_kernel, fresh),
        grid_spec=pltpu.PrefetchScalarGridSpec(
            num_scalar_prefetch=1,
            grid=(rows // tile,),
            in_specs=[group] * (2 * GROUPS) + [part] + ([] if fresh else [ANY, ANY, INSMEM]),
            out_specs=(
                pl.BlockSpec((tile, columns), lambda i, at: (at[0] + i, 0)),
                ANY,
                INSMEM,
            ),
            scratch_shapes=[pltpu.VMEM((2, tile, columns), F32), pltpu.SemaphoreType.DMA((2,))],
        ),
        out_shape=(
            pltpu.HBM((rows_here, columns), F32),
            pltpu.HBM((rows_here, 1, columns), F32),
            jax.ShapeDtypeStruct((1,), F32),
        ),
        input_output_aliases={} if fresh else {2 * GROUPS + 2: 0, 2 * GROUPS + 3: 1},
        compiler_params=params(16),
        cost_estimate=pl.CostEstimate(flops=m.size // 16, bytes_accessed=m.size // 4, transcendentals=0),
        name=name,
    )(choose([r // tile for r in row]).reshape(1), *t, *peers, m, *([] if fresh else hbm(*so_far[:2]) + [so_far[2]]))


def output_kernel(raw_ref, quotient_ref, scale_ref, barycenter_ref, scaling_ref):
    scale = scale_ref[0]
    barycenter_ref[...] = raw_ref[...] * scale
    scaling_ref[...] = quotient_ref[...] * scale


def outputs(raw, quotient, scale):
    rows, columns = raw.shape
    tile = 64
    flat = pl.BlockSpec((tile, columns), lambda i: (i, 0))
    deep = pl.BlockSpec((tile,) + quotient.shape[1:], lambda i: (i, 0, 0))
    return pl.pallas_call(
        output_kernel,
        grid=(rows // tile,),
        in_specs=[flat, deep, INSMEM],
        out_specs=(flat, deep),
        out_shape=(jax.ShapeDtypeStruct(raw.shape, F32), jax.ShapeDtypeStruct(quotient.shape, F32)),
        compiler_params=params(16),
        name="outputs",
    )(*hbm(raw, quotient), scale)


def local(densities, scaling, weights, band):
    rows_here, maps_here, cols_all = densities.shape
    _, _, width, _ = band.shape
    nlocal = rows_here // width
    inner = max(nlocal - 2, 0)
    place = lax.axis_index("space")
    count = lax.axis_size("space")
    assert maps_here == 1 and lax.axis_size("member") == 2 and count % 2 == 0

    odd = place & 1
    side = odd.reshape(1)
    last = rows_here - width
    cross_row, near_row = (0, last), (last, 0)
    both = lambda pairs: pairs + [(b, a) for a, b in pairs]
    cross = functools.partial(
        lax.ppermute, axis_name="space", perm=both([(i, i + 1) for i in range(1, count - 1, 2)])
    )
    near = functools.partial(lax.ppermute, axis_name="space", perm=both([(i, i + 1) for i in range(0, count, 2)]))
    swap = functools.partial(lax.ppermute, axis_name="member", perm=[(0, 1), (1, 0)])

    def choose(choice):
        return jnp.where(odd == 0, choice[0], choice[1]).astype(jnp.int32)

    cross1 = cross(cut("cut_cross", side, scaling, cross_row, width))
    near1 = near(cut("cut_near", side, scaling, near_row, width))

    shares = weights / jnp.sum(weights)
    share = lax.dynamic_slice_in_dim(shares, lax.axis_index("member"), 1)
    wts = row_weights(band)
    mine = place * nlocal
    band_at = lambda row, blocks: lax.dynamic_slice_in_dim(band, mine + row // width, blocks, 0)

    if inner > 0:
        inner_bands = band_at(width, inner)
        ratio_inner = blur(
            "ratio_inner", side, hbm(scaling), [(0, 0, rows_here, 0)], inner_bands, wts, densities, width
        )
        cross1, ratio_inner = lax.optimization_barrier((cross1, ratio_inner))
    if nlocal == 1:
        pieces = [(0, 0, width, width), (1, 0, width, (0, 2 * width)), (2, 0, width, (2 * width, 0))]
        bands = band_at(0, 1)
        ratio = blur("ratio_only", side, [scaling, cross1, near1], pieces, bands, wts, densities, 0)
        cross2, near2 = cross(ratio), near(ratio)
    else:
        two = rows_here - 2 * width
        pieces = [(0, (0, two), 2 * width, (width, 0)), (1, 0, width, (0, 2 * width))]
        bands = band_at(choose(cross_row), 1)
        ratio_cross = blur("ratio_cross", side, hbm(scaling) + [cross1], pieces, bands, wts, densities, cross_row)
        ratio_cross, near1 = lax.optimization_barrier((ratio_cross, near1))
        cross2 = cross(ratio_cross)
        pieces = [(0, (two, 0), 2 * width, (0, width)), (1, 0, width, (2 * width, 0))]
        bands = band_at(choose(near_row), 1)
        ratio_near = blur("ratio_near", side, hbm(scaling) + [near1], pieces, bands, wts, densities, near_row)
        near2 = near(ratio_near)

    def finish(name, arrays, pieces, bands, row, share, state, pin=True):
        t, m = blur("logs_" + name, side, arrays, pieces, bands, wts, scaling, row, share, pin)
        keep = hbm if pin else lambda *a: list(a)
        return raw_rows(
            "raw_" + name, row, keep(*t), [swap(part) for part in t], *keep(m), choose, rows_here, state
        )

    if nlocal == 1:
        pieces = [(0, 0, width, width), (1, 0, width, (0, 2 * width)), (2, 0, width, (2 * width, 0))]
        state = finish("only", [ratio, cross2, near2], pieces, bands, (0, 0), share, None)
    else:
        most, end = rows_here - width, rows_here
        pieces = [(0, 0, width, (width, most)), (1, 0, width, (end, 0)), (2, 0, width, (0, end))]
        arrays = [ratio_cross, ratio_near, cross2]
        beside, beside_row = ratio_cross, 0
        if inner > 0:
            pieces.append((3, 0, inner * width, (2 * width, width)))
            arrays.append(ratio_inner)
            beside, beside_row = ratio_inner, ((inner - 1) * width, 0)
        row = (0, width)
        state = finish("most", hbm(*arrays[:2]) + arrays[2:3] + hbm(*arrays[3:]), pieces, band_at(choose(row), nlocal - 1), row, share, None)
        share, state = lax.optimization_barrier((share, state))
        pieces = [(0, 0, width, width), (1, beside_row, width, (0, 2 * width)), (2, 0, width, (2 * width, 0))]
        state = finish("near", hbm(ratio_near, beside) + [near2], pieces, bands, near_row, share, state, False)

    raw, quotient, mass = state
    mass = lax.psum(mass, "space")
    barycenter, new_scaling = outputs(raw, quotient.reshape(rows_here, cols_all // width, width), float(cols_all * cols_all) / mass)
    return barycenter, new_scaling.reshape(rows_here, 1, cols_all)


def solution(mesh):
    return jax.shard_map(
        local,
        mesh=mesh,
        in_specs=(
            P("space", ("parts", "member"), None),
            P("space", ("parts", "member"), None),
            P("parts"),
            P(),
        ),
        out_specs=(P(("parts", "space"), None), P("space", ("parts", "member"), None)),
        check_vma=False,
    )
```

```python
import functools

import jax
import jax.numpy as jnp
from jax import lax
from jax.experimental import pallas as pl
from jax.experimental.pallas import tpu as pltpu
from jax.sharding import PartitionSpec as P

F32 = jnp.float32
BF16 = jnp.bfloat16
GROUPS = 4
ANY = pl.BlockSpec(memory_space=pl.ANY)
INVMEM = pl.BlockSpec(memory_space=pltpu.VMEM)
INSMEM = pl.BlockSpec(memory_space=pltpu.SMEM)


def split(x):
    high = x.astype(BF16)
    return high, (x - high.astype(F32)).astype(BF16)


def dot3(stack, b, dims):
    one = functools.partial(lax.dot_general, dimension_numbers=(dims, ((), ())), preferred_element_type=F32)
    rows = stack.shape[0] // 2
    both = one(stack, b[0])
    return both[:rows] + (one(stack[:rows], b[1]) + both[rows:])


def params(mebibytes):
    return pltpu.CompilerParams(vmem_limit_bytes=mebibytes * 1024 * 1024)


def hbm(*arrays):
    return [pltpu.with_memory_space_constraint(a, pltpu.HBM) for a in arrays]


def vmem(*arrays):
    return [pltpu.with_memory_space_constraint(a, pltpu.VMEM) for a in arrays]


def pick(choice, side):
    if isinstance(choice, tuple):
        return pl.multiple_of(jnp.where(side == 0, choice[0], choice[1]), 128)
    return choice


def cut_kernel(first, side_ref, src, dst, stage, sems):
    rows = stage.shape[0] // GROUPS
    start = pick(first, side_ref[0])
    parts = [pl.ds(g * rows, rows) for g in range(GROUPS)]
    inward = [
        pltpu.make_async_copy(src.at[pl.ds(start + g * rows, rows)], stage.at[part], sems.at[0, g])
        for g, part in enumerate(parts)
    ]
    outward = [pltpu.make_async_copy(stage.at[part], dst.at[part], sems.at[1, g]) for g, part in enumerate(parts)]
    for copy in inward:
        copy.start()
    for g in range(GROUPS):
        inward[g].wait()
        outward[g].start()
    for copy in outward:
        copy.wait()


def cut(name, side, array, first, rows):
    shape = (rows,) + array.shape[1:]
    return pl.pallas_call(
        functools.partial(cut_kernel, first),
        in_specs=[INSMEM, ANY],
        out_specs=ANY,
        out_shape=pltpu.HBM(shape, F32),
        scratch_shapes=[pltpu.VMEM(shape, F32), pltpu.SemaphoreType.DMA((2, GROUPS))],
        compiler_params=params(8),
        name=name,
    )(side, *hbm(array))


def area(ref, row, rows, columns):
    return ref.at[pl.ds(row, rows), 0, columns] if len(ref.shape) == 3 else ref.at[pl.ds(row, rows), columns]


def weight_kernel(nblocks, band_ref, high_ref, low_ref):
    pair = pl.program_id(0)
    width = band_ref.shape[2]
    zero = jnp.zeros((width, width), F32)
    for o in range(2):
        for i in range(4):
            j = i - o
            value = band_ref[o, j] if 0 <= j <= 2 else zero
            if (o, j) == (0, 0):
                value = jnp.where(pair > 0, value, 0.0)
            if (o, j) == (1, 2):
                value = jnp.where(pair < nblocks // 2 - 1, value, 0.0)
            high, low = split(value)
            rows, columns = slice(o * width, (o + 1) * width), slice(i * width, (i + 1) * width)
            high_ref[0, rows, columns] = high
            low_ref[0, rows, columns] = low


def row_weights(band):
    nblocks, _, width, _ = band.shape
    shape = pltpu.HBM((nblocks // 2, 2 * width, 4 * width), BF16)
    out_spec = pl.BlockSpec((1, 2 * width, 4 * width), lambda t: (t, 0, 0))
    return pl.pallas_call(
        functools.partial(weight_kernel, nblocks),
        grid=(nblocks // 2,),
        in_specs=[pl.BlockSpec((2, 3, width, width), lambda t: (t, 0, 0, 0))],
        out_specs=(out_spec, out_spec),
        out_shape=(shape, shape),
        name="row_weights",
    )(*hbm(band))


def blur_kernel(plan, *refs):
    pieces, narrays, extra, final = plan
    side_ref, refs = refs[0], refs[1:]
    arrays = refs[:narrays]
    band_ref, high_ref, low_ref, extra_ref = refs[narrays : narrays + 4]
    rest = refs[narrays + 4 :]
    if final:
        share_ref, rest = rest[0], rest[1:]
    nouts = GROUPS + 1 if final else 1
    outs = rest[:nouts]
    field, a_both, y_both, whigh, wlow, other = rest[nouts : nouts + 6]
    *results, in_sems, late_sems, out_sems = rest[nouts + 6 :]

    side = side_ref[0]
    nout, _, width, _ = band_ref.shape
    columns = field.shape[1]
    step = columns // GROUPS
    pairs = step // (2 * width)
    inside, late = [], []
    for g in range(GROUPS):
        at = pl.ds(g * step, step)
        inside.append(
            [
                pltpu.make_async_copy(
                    area(arrays[which], pick(row, side), rows, at),
                    field.at[pl.ds(pick(to, side), rows), at],
                    in_sems.at[g, k],
                )
                for k, (which, row, rows, to) in enumerate(pieces)
            ]
        )
        some = pl.ds(g * pairs, pairs)
        late.append(
            [
                pltpu.make_async_copy(high_ref.at[some], whigh.at[some], late_sems.at[g, 0]),
                pltpu.make_async_copy(low_ref.at[some], wlow.at[some], late_sems.at[g, 1]),
                pltpu.make_async_copy(
                    area(extra_ref, pick(extra, side), other.shape[0], at), other.at[:, at], late_sems.at[g, 2]
                ),
            ]
        )
    for g in range(GROUPS):
        for copy in inside[g]:
            copy.start()
        if g > 0:
            for copy in late[g - 1]:
                copy.start()
    for copy in late[GROUPS - 1]:
        copy.start()

    blocks = [(i, min(2, nout - i)) for i in range(0, nout, 2)]
    total = nout * width
    a_both[...] = jnp.zeros_like(a_both)
    for first, n in blocks:
        for i in range(n):
            for j in range(3):
                for part, value in enumerate(split(band_ref[first + i, j])):
                    row = (2 * first + part * n + i) * width
                    a_both[row : row + width, (i + j) * width : (i + j + 1) * width] = value
    y_both[:, :width] = jnp.zeros((2 * total, width), BF16)
    y_both[:, columns + width :] = jnp.zeros((2 * total, width), BF16)

    def columns_pass(g):
        for copy in inside[g]:
            copy.wait()
        for i in range(g * pairs, (g + 1) * pairs):
            at = slice(i * 2 * width, (i + 1) * 2 * width)
            to = slice((2 * i + 1) * width, (2 * i + 3) * width)
            for first, n in blocks:
                a = a_both[2 * first * width : 2 * (first + n) * width, : (n + 2) * width]
                y = dot3(a, split(field[first * width : (first + n + 2) * width, at]), ((1,), (0,)))
                for part, value in enumerate(split(y)):
                    row = part * total + first * width
                    y_both[row : row + n * width, to] = value

    def rows_pass(g):
        for copy in late[g]:
            copy.wait()
        for t in range(g * pairs, (g + 1) * pairs):
            source = slice(t * 2 * width, (t + 2) * 2 * width)
            at = slice(t * 2 * width, (t + 1) * 2 * width)
            value = dot3(y_both[:, source], (whigh[t], wlow[t]), ((1,), (1,)))
            if final:
                results[0][:, at] = value
                results[1][:, at] = share_ref[0] * jnp.log(other[:, at] * value)
            else:
                results[0][:, at] = other[:, at] / value
        at = pl.ds(g * step, step)
        targets = [outs[-1].at[:, at]] + ([outs[g]] if final else [])
        copies = [
            pltpu.make_async_copy(src.at[:, at], dst, out_sems.at[g, k])
            for k, (src, dst) in enumerate(zip(results, targets))
        ]
        for copy in copies:
            copy.start()
        return copies

    going = []
    for g in range(GROUPS):
        columns_pass(g)
        if g > 0:
            going += rows_pass(g - 1)
    going += rows_pass(GROUPS - 1)
    for copy in going:
        copy.wait()


def blur(name, side, arrays, pieces, bands, weights, other, extra, share=None, pin=True):
    nout, _, width, _ = bands.shape
    npairs = weights[0].shape[0]
    columns = npairs * 2 * width
    rows, depth = nout * width, (nout + 2) * width
    final = share is not None
    nouts = 2 if final else 1
    kind = pltpu.HBM if pin else jax.ShapeDtypeStruct
    shapes = [kind((rows, columns // GROUPS), F32)] * (GROUPS if final else 0)
    shapes.append(pltpu.HBM((rows, columns), F32))
    plan = (tuple(pieces), len(arrays), extra, final)
    work = 3 * 2 * rows * columns * (depth + 4 * width)
    moved = 4 * (depth + 3 * rows) * columns + npairs * 2 * 2 * 8 * width * width
    size = 4 * columns * (depth + (1 + nouts) * rows) + 4 * rows * columns + npairs * 2 * 2 * 8 * width * width
    result = pl.pallas_call(
        functools.partial(blur_kernel, plan),
        in_specs=[INSMEM] + [ANY] * len(arrays) + [INVMEM, ANY, ANY, ANY] + [INSMEM] * final,
        out_specs=[ANY] * len(shapes),
        out_shape=shapes,
        scratch_shapes=[
            pltpu.VMEM((depth, columns), F32),
            pltpu.VMEM((2 * rows, min(depth, 4 * width)), BF16),
            pltpu.VMEM((2 * rows, columns + 2 * width), BF16),
            pltpu.VMEM((npairs, 2 * width, 4 * width), BF16),
            pltpu.VMEM((npairs, 2 * width, 4 * width), BF16),
            pltpu.VMEM((rows, columns), F32),
        ]
        + [pltpu.VMEM((rows, columns), F32)] * nouts
        + [
            pltpu.SemaphoreType.DMA((GROUPS, len(pieces))),
            pltpu.SemaphoreType.DMA((GROUPS, 3)),
            pltpu.SemaphoreType.DMA((GROUPS, nouts)),
        ],
        compiler_params=params(size // 2**20 + 6),
        cost_estimate=pl.CostEstimate(flops=work // 64, bytes_accessed=moved // 64, transcendentals=0),
        name=name,
    )(side, *arrays, bands, *hbm(*weights, other), *([share] if final else []))
    return (result[:-1], result[-1]) if final else result[0]


def raw_kernel(fresh, start_ref, *refs):
    own, peer, m_ref = refs[:GROUPS], refs[GROUPS : 2 * GROUPS], refs[2 * GROUPS]
    raw_ref, quotient_ref, mass_ref, quotient, sems = refs[-5:]
    tile = raw_ref.shape[0]
    at = pl.program_id(0)
    slot = lax.rem(at, 2)

    def copy(step, slot):
        row = pl.multiple_of((start_ref[0] + step) * tile, tile)
        return pltpu.make_async_copy(quotient.at[slot], area(quotient_ref, row, tile, slice(None)), sems.at[slot])

    @pl.when(at >= 2)
    def _():
        copy(at - 2, slot).wait()

    mass = 0.0
    for g in range(GROUPS):
        raw = jnp.exp(own[g][...] + peer[g][...])
        step = raw.shape[1]
        raw_ref[:, g * step : (g + 1) * step] = raw
        mass += jnp.sum(raw)
        quotient[slot, :, g * step : (g + 1) * step] = raw / m_ref[:, g * step : (g + 1) * step]
    before = 0.0 if fresh else refs[2 * GROUPS + 3][0]
    mass_ref[0] = mass + jnp.where(at == 0, before, mass_ref[0])
    copy(at, slot).start()

    @pl.when(at == pl.num_programs(0) - 1)
    def _():
        copy(at - 1, 1 - slot).wait()
        copy(at, slot).wait()


def raw_rows(name, row, t, peers, m, choose, rows_here, so_far):
    fresh = so_far is None
    rows, columns = m.shape
    tile = 32
    part = pl.BlockSpec((tile, columns), lambda i, at: (i, 0))
    group = pl.BlockSpec((tile, columns // GROUPS), lambda i, at: (i, 0))
    return pl.pallas_call(
        functools.partial(raw_kernel, fresh),
        grid_spec=pltpu.PrefetchScalarGridSpec(
            num_scalar_prefetch=1,
            grid=(rows // tile,),
            in_specs=[group] * (2 * GROUPS) + [part] + ([] if fresh else [ANY, ANY, INSMEM]),
            out_specs=(
                pl.BlockSpec((tile, columns), lambda i, at: (at[0] + i, 0)),
                ANY,
                INSMEM,
            ),
            scratch_shapes=[pltpu.VMEM((2, tile, columns), F32), pltpu.SemaphoreType.DMA((2,))],
        ),
        out_shape=(
            pltpu.VMEM((rows_here, columns), F32),
            pltpu.VMEM((rows_here, 1, columns), F32),
            jax.ShapeDtypeStruct((1,), F32),
        ),
        input_output_aliases={} if fresh else {2 * GROUPS + 2: 0, 2 * GROUPS + 3: 1},
        compiler_params=params(16),
        cost_estimate=pl.CostEstimate(flops=m.size // 16, bytes_accessed=m.size // 4, transcendentals=0),
        name=name,
    )(choose([r // tile for r in row]).reshape(1), *t, *peers, m, *([] if fresh else vmem(*so_far[:2]) + [so_far[2]]))


def output_kernel(raw_ref, quotient_ref, scale_ref, barycenter_ref, scaling_ref):
    scale = scale_ref[0]
    barycenter_ref[...] = raw_ref[...] * scale
    scaling_ref[...] = quotient_ref[...] * scale


def outputs(raw, quotient, scale):
    rows, columns = raw.shape
    tile = 64
    flat = pl.BlockSpec((tile, columns), lambda i: (i, 0))
    deep = pl.BlockSpec((tile,) + quotient.shape[1:], lambda i: (i, 0, 0))
    return pl.pallas_call(
        output_kernel,
        grid=(rows // tile,),
        in_specs=[flat, deep, INSMEM],
        out_specs=(flat, deep),
        out_shape=(jax.ShapeDtypeStruct(raw.shape, F32), jax.ShapeDtypeStruct(quotient.shape, F32)),
        compiler_params=params(16),
        name="outputs",
    )(*vmem(raw, quotient), scale)


def local(densities, scaling, weights, band):
    rows_here, maps_here, cols_all = densities.shape
    _, _, width, _ = band.shape
    nlocal = rows_here // width
    inner = max(nlocal - 2, 0)
    place = lax.axis_index("space")
    count = lax.axis_size("space")
    assert maps_here == 1 and lax.axis_size("member") == 2 and count % 2 == 0

    odd = place & 1
    side = odd.reshape(1)
    last = rows_here - width
    cross_row, near_row = (0, last), (last, 0)
    both = lambda pairs: pairs + [(b, a) for a, b in pairs]
    cross = functools.partial(
        lax.ppermute, axis_name="space", perm=both([(i, i + 1) for i in range(1, count - 1, 2)])
    )
    near = functools.partial(lax.ppermute, axis_name="space", perm=both([(i, i + 1) for i in range(0, count, 2)]))
    swap = functools.partial(lax.ppermute, axis_name="member", perm=[(0, 1), (1, 0)])

    def choose(choice):
        return jnp.where(odd == 0, choice[0], choice[1]).astype(jnp.int32)

    cross1 = cross(cut("cut_cross", side, scaling, cross_row, width))
    near1 = near(cut("cut_near", side, scaling, near_row, width))

    shares = weights / jnp.sum(weights)
    share = lax.dynamic_slice_in_dim(shares, lax.axis_index("member"), 1)
    wts = row_weights(band)
    mine = place * nlocal
    band_at = lambda row, blocks: lax.dynamic_slice_in_dim(band, mine + row // width, blocks, 0)

    if inner > 0:
        inner_bands = band_at(width, inner)
        ratio_inner = blur(
            "ratio_inner", side, hbm(scaling), [(0, 0, rows_here, 0)], inner_bands, wts, densities, width
        )
        cross1, ratio_inner = lax.optimization_barrier((cross1, ratio_inner))
    if nlocal == 1:
        pieces = [(0, 0, width, width), (1, 0, width, (0, 2 * width)), (2, 0, width, (2 * width, 0))]
        bands = band_at(0, 1)
        ratio = blur("ratio_only", side, [scaling, cross1, near1], pieces, bands, wts, densities, 0)
        cross2, near2 = cross(ratio), near(ratio)
    else:
        two = rows_here - 2 * width
        pieces = [(0, (0, two), 2 * width, (width, 0)), (1, 0, width, (0, 2 * width))]
        bands = band_at(choose(cross_row), 1)
        ratio_cross = blur("ratio_cross", side, hbm(scaling) + [cross1], pieces, bands, wts, densities, cross_row)
        ratio_cross, near1 = lax.optimization_barrier((ratio_cross, near1))
        cross2 = cross(ratio_cross)
        pieces = [(0, (two, 0), 2 * width, (0, width)), (1, 0, width, (2 * width, 0))]
        bands = band_at(choose(near_row), 1)
        ratio_near = blur("ratio_near", side, hbm(scaling) + [near1], pieces, bands, wts, densities, near_row)
        near2 = near(ratio_near)

    def finish(name, arrays, pieces, bands, row, share, state, pin=True):
        t, m = blur("logs_" + name, side, arrays, pieces, bands, wts, scaling, row, share, pin)
        keep = hbm if pin else lambda *a: list(a)
        return raw_rows(
            "raw_" + name, row, keep(*t), [swap(part) for part in t], *hbm(m), choose, rows_here, state
        )

    if nlocal == 1:
        pieces = [(0, 0, width, width), (1, 0, width, (0, 2 * width)), (2, 0, width, (2 * width, 0))]
        state = finish("only", [ratio, cross2, near2], pieces, bands, (0, 0), share, None)
    else:
        most, end = rows_here - width, rows_here
        pieces = [(0, 0, width, (width, most)), (1, 0, width, (end, 0)), (2, 0, width, (0, end))]
        arrays = [ratio_cross, ratio_near, cross2]
        beside, beside_row = ratio_cross, 0
        if inner > 0:
            pieces.append((3, 0, inner * width, (2 * width, width)))
            arrays.append(ratio_inner)
            beside, beside_row = ratio_inner, ((inner - 1) * width, 0)
        row = (0, width)
        state = finish("most", hbm(*arrays[:2]) + arrays[2:3] + hbm(*arrays[3:]), pieces, band_at(choose(row), nlocal - 1), row, share, None)
        share, state = lax.optimization_barrier((share, state))
        pieces = [(0, 0, width, width), (1, beside_row, width, (0, 2 * width)), (2, 0, width, (2 * width, 0))]
        state = finish("near", hbm(ratio_near, beside) + [near2], pieces, bands, near_row, share, state, False)

    raw, quotient, mass = state
    mass = lax.psum(mass, "space")
    barycenter, new_scaling = outputs(raw, quotient.reshape(rows_here, cols_all // width, width), float(cols_all * cols_all) / mass)
    return barycenter, new_scaling.reshape(rows_here, 1, cols_all)


def solution(mesh):
    return jax.shard_map(
        local,
        mesh=mesh,
        in_specs=(
            P("space", ("parts", "member"), None),
            P("space", ("parts", "member"), None),
            P("parts"),
            P(),
        ),
        out_specs=(P(("parts", "space"), None), P("space", ("parts", "member"), None)),
        check_vma=False,
    )
```

```python
import functools

import jax
import jax.numpy as jnp
from jax import lax
from jax.experimental import pallas as pl
from jax.experimental.pallas import tpu as pltpu
from jax.sharding import PartitionSpec as P

F32 = jnp.float32
BF16 = jnp.bfloat16
GROUPS = 4
ANY = pl.BlockSpec(memory_space=pl.ANY)
INVMEM = pl.BlockSpec(memory_space=pltpu.VMEM)
INSMEM = pl.BlockSpec(memory_space=pltpu.SMEM)


def split(x):
    high = x.astype(BF16)
    return high, (x - high.astype(F32)).astype(BF16)


def dot3(stack, b, dims):
    one = functools.partial(lax.dot_general, dimension_numbers=(dims, ((), ())), preferred_element_type=F32)
    rows = stack.shape[0] // 2
    both = one(stack, b[0])
    return both[:rows] + (one(stack[:rows], b[1]) + both[rows:])


def params(mebibytes):
    return pltpu.CompilerParams(vmem_limit_bytes=mebibytes * 1024 * 1024)


def hbm(*arrays):
    return [pltpu.with_memory_space_constraint(a, pltpu.HBM) for a in arrays]


def vmem(*arrays):
    return [pltpu.with_memory_space_constraint(a, pltpu.VMEM) for a in arrays]


def pick(choice, side):
    if isinstance(choice, tuple):
        return pl.multiple_of(jnp.where(side == 0, choice[0], choice[1]), 128)
    return choice


def cut_kernel(first, side_ref, src, dst, stage, sems):
    rows = stage.shape[0] // GROUPS
    start = pick(first, side_ref[0])
    parts = [pl.ds(g * rows, rows) for g in range(GROUPS)]
    inward = [
        pltpu.make_async_copy(src.at[pl.ds(start + g * rows, rows)], stage.at[part], sems.at[0, g])
        for g, part in enumerate(parts)
    ]
    outward = [pltpu.make_async_copy(stage.at[part], dst.at[part], sems.at[1, g]) for g, part in enumerate(parts)]
    for copy in inward:
        copy.start()
    for g in range(GROUPS):
        inward[g].wait()
        outward[g].start()
    for copy in outward:
        copy.wait()


def cut(name, side, array, first, rows):
    shape = (rows,) + array.shape[1:]
    return pl.pallas_call(
        functools.partial(cut_kernel, first),
        in_specs=[INSMEM, ANY],
        out_specs=ANY,
        out_shape=pltpu.HBM(shape, F32),
        scratch_shapes=[pltpu.VMEM(shape, F32), pltpu.SemaphoreType.DMA((2, GROUPS))],
        compiler_params=params(8),
        name=name,
    )(side, *hbm(array))


def area(ref, row, rows, columns):
    return ref.at[pl.ds(row, rows), 0, columns] if len(ref.shape) == 3 else ref.at[pl.ds(row, rows), columns]


def weight_kernel(nblocks, band_ref, high_ref, low_ref):
    pair = pl.program_id(0)
    width = band_ref.shape[2]
    zero = jnp.zeros((width, width), F32)
    for o in range(2):
        for i in range(4):
            j = i - o
            value = band_ref[o, j] if 0 <= j <= 2 else zero
            if (o, j) == (0, 0):
                value = jnp.where(pair > 0, value, 0.0)
            if (o, j) == (1, 2):
                value = jnp.where(pair < nblocks // 2 - 1, value, 0.0)
            high, low = split(value)
            rows, columns = slice(o * width, (o + 1) * width), slice(i * width, (i + 1) * width)
            high_ref[0, rows, columns] = high
            low_ref[0, rows, columns] = low


def row_weights(band):
    nblocks, _, width, _ = band.shape
    shape = pltpu.HBM((nblocks // 2, 2 * width, 4 * width), BF16)
    out_spec = pl.BlockSpec((1, 2 * width, 4 * width), lambda t: (t, 0, 0))
    return pl.pallas_call(
        functools.partial(weight_kernel, nblocks),
        grid=(nblocks // 2,),
        in_specs=[pl.BlockSpec((2, 3, width, width), lambda t: (t, 0, 0, 0))],
        out_specs=(out_spec, out_spec),
        out_shape=(shape, shape),
        name="row_weights",
    )(*hbm(band))


def blur_kernel(plan, *refs):
    pieces, narrays, extra, final = plan
    side_ref, refs = refs[0], refs[1:]
    arrays = refs[:narrays]
    band_ref, high_ref, low_ref, extra_ref = refs[narrays : narrays + 4]
    rest = refs[narrays + 4 :]
    if final:
        share_ref, rest = rest[0], rest[1:]
    nouts = GROUPS + 1 if final else 1
    outs = rest[:nouts]
    field, a_both, y_both, whigh, wlow, other = rest[nouts : nouts + 6]
    *results, in_sems, late_sems, out_sems = rest[nouts + 6 :]

    side = side_ref[0]
    nout, _, width, _ = band_ref.shape
    columns = field.shape[1]
    step = columns // GROUPS
    pairs = step // (2 * width)
    inside, late = [], []
    for g in range(GROUPS):
        at = pl.ds(g * step, step)
        inside.append(
            [
                pltpu.make_async_copy(
                    area(arrays[which], pick(row, side), rows, at),
                    field.at[pl.ds(pick(to, side), rows), at],
                    in_sems.at[g, k],
                )
                for k, (which, row, rows, to) in enumerate(pieces)
            ]
        )
        some = pl.ds(g * pairs, pairs)
        late.append(
            [
                pltpu.make_async_copy(high_ref.at[some], whigh.at[some], late_sems.at[g, 0]),
                pltpu.make_async_copy(low_ref.at[some], wlow.at[some], late_sems.at[g, 1]),
                pltpu.make_async_copy(
                    area(extra_ref, pick(extra, side), other.shape[0], at), other.at[:, at], late_sems.at[g, 2]
                ),
            ]
        )
    for g in range(GROUPS):
        for copy in inside[g]:
            copy.start()
        if g > 0:
            for copy in late[g - 1]:
                copy.start()
    for copy in late[GROUPS - 1]:
        copy.start()

    blocks = [(i, min(2, nout - i)) for i in range(0, nout, 2)]
    total = nout * width
    a_both[...] = jnp.zeros_like(a_both)
    for first, n in blocks:
        for i in range(n):
            for j in range(3):
                for part, value in enumerate(split(band_ref[first + i, j])):
                    row = (2 * first + part * n + i) * width
                    a_both[row : row + width, (i + j) * width : (i + j + 1) * width] = value
    y_both[:, :width] = jnp.zeros((2 * total, width), BF16)
    y_both[:, columns + width :] = jnp.zeros((2 * total, width), BF16)

    def columns_pass(g):
        for copy in inside[g]:
            copy.wait()
        for i in range(g * pairs, (g + 1) * pairs):
            at = slice(i * 2 * width, (i + 1) * 2 * width)
            to = slice((2 * i + 1) * width, (2 * i + 3) * width)
            for first, n in blocks:
                a = a_both[2 * first * width : 2 * (first + n) * width, : (n + 2) * width]
                y = dot3(a, split(field[first * width : (first + n + 2) * width, at]), ((1,), (0,)))
                for part, value in enumerate(split(y)):
                    row = part * total + first * width
                    y_both[row : row + n * width, to] = value

    def rows_pass(g):
        for copy in late[g]:
            copy.wait()
        for t in range(g * pairs, (g + 1) * pairs):
            source = slice(t * 2 * width, (t + 2) * 2 * width)
            at = slice(t * 2 * width, (t + 1) * 2 * width)
            value = dot3(y_both[:, source], (whigh[t], wlow[t]), ((1,), (1,)))
            if final:
                results[0][:, at] = value
                results[1][:, at] = share_ref[0] * jnp.log(other[:, at] * value)
            else:
                results[0][:, at] = other[:, at] / value
        at = pl.ds(g * step, step)
        targets = [outs[-1].at[:, at]] + ([outs[g]] if final else [])
        copies = [
            pltpu.make_async_copy(src.at[:, at], dst, out_sems.at[g, k])
            for k, (src, dst) in enumerate(zip(results, targets))
        ]
        for copy in copies:
            copy.start()
        return copies

    going = []
    for g in range(GROUPS):
        columns_pass(g)
        if g > 0:
            going += rows_pass(g - 1)
    going += rows_pass(GROUPS - 1)
    for copy in going:
        copy.wait()


def blur(name, side, arrays, pieces, bands, weights, other, extra, share=None, pin=True):
    nout, _, width, _ = bands.shape
    npairs = weights[0].shape[0]
    columns = npairs * 2 * width
    rows, depth = nout * width, (nout + 2) * width
    final = share is not None
    nouts = 2 if final else 1
    kind = pltpu.HBM if pin else jax.ShapeDtypeStruct
    shapes = [kind((rows, columns // GROUPS), F32)] * (GROUPS if final else 0)
    shapes.append(pltpu.HBM((rows, columns), F32))
    plan = (tuple(pieces), len(arrays), extra, final)
    work = 3 * 2 * rows * columns * (depth + 4 * width)
    moved = 4 * (depth + 3 * rows) * columns + npairs * 2 * 2 * 8 * width * width
    size = 4 * columns * (depth + (1 + nouts) * rows) + 4 * rows * columns + npairs * 2 * 2 * 8 * width * width
    result = pl.pallas_call(
        functools.partial(blur_kernel, plan),
        in_specs=[INSMEM] + [ANY] * len(arrays) + [INVMEM, ANY, ANY, ANY] + [INSMEM] * final,
        out_specs=[ANY] * len(shapes),
        out_shape=shapes,
        scratch_shapes=[
            pltpu.VMEM((depth, columns), F32),
            pltpu.VMEM((2 * rows, min(depth, 4 * width)), BF16),
            pltpu.VMEM((2 * rows, columns + 2 * width), BF16),
            pltpu.VMEM((npairs, 2 * width, 4 * width), BF16),
            pltpu.VMEM((npairs, 2 * width, 4 * width), BF16),
            pltpu.VMEM((rows, columns), F32),
        ]
        + [pltpu.VMEM((rows, columns), F32)] * nouts
        + [
            pltpu.SemaphoreType.DMA((GROUPS, len(pieces))),
            pltpu.SemaphoreType.DMA((GROUPS, 3)),
            pltpu.SemaphoreType.DMA((GROUPS, nouts)),
        ],
        compiler_params=params(size // 2**20 + 6),
        cost_estimate=pl.CostEstimate(flops=work // 64, bytes_accessed=moved // 64, transcendentals=0),
        name=name,
    )(side, *arrays, bands, *hbm(*weights, other), *([share] if final else []))
    return (result[:-1], result[-1]) if final else result[0]


def raw_kernel(fresh, first, side_ref, *refs):
    own, peer, m_ref = refs[:GROUPS], refs[GROUPS : 2 * GROUPS], refs[2 * GROUPS]
    raw_ref, quotient_ref, mass_ref, quotient, sems = refs[-5:]
    tile = raw_ref.shape[0]
    at = pl.program_id(0)
    slot = lax.rem(at, 2)

    def copy(step, slot):
        row = pl.multiple_of(pick(first, side_ref[0]) + step * tile, tile)
        return pltpu.make_async_copy(quotient.at[slot], area(quotient_ref, row, tile, slice(None)), sems.at[slot])

    @pl.when(at >= 2)
    def _():
        copy(at - 2, slot).wait()

    mass = 0.0
    for g in range(GROUPS):
        raw = jnp.exp(own[g][...] + peer[g][...])
        step = raw.shape[1]
        raw_ref[:, g * step : (g + 1) * step] = raw
        mass += jnp.sum(raw)
        quotient[slot, :, g * step : (g + 1) * step] = raw / m_ref[:, g * step : (g + 1) * step]
    before = 0.0 if fresh else refs[2 * GROUPS + 3][0]
    mass_ref[0] = mass + jnp.where(at == 0, before, mass_ref[0])
    copy(at, slot).start()

    @pl.when(at == pl.num_programs(0) - 1)
    def _():
        copy(at - 1, 1 - slot).wait()
        copy(at, slot).wait()


def raw_rows(name, side, row, t, peers, m, rows_here, so_far):
    fresh = so_far is None
    rows, columns = m.shape
    tile = 32
    starts = [r // tile for r in row]
    part = pl.BlockSpec((tile, columns), lambda i, at: (i, 0))
    group = pl.BlockSpec((tile, columns // GROUPS), lambda i, at: (i, 0))
    return pl.pallas_call(
        functools.partial(raw_kernel, fresh, row),
        grid_spec=pltpu.PrefetchScalarGridSpec(
            num_scalar_prefetch=1,
            grid=(rows // tile,),
            in_specs=[group] * (2 * GROUPS) + [part] + ([] if fresh else [ANY, ANY, INSMEM]),
            out_specs=(
                pl.BlockSpec((tile, columns), lambda i, at: (jnp.where(at[0] == 0, *starts) + i, 0)),
                ANY,
                INSMEM,
            ),
            scratch_shapes=[pltpu.VMEM((2, tile, columns), F32), pltpu.SemaphoreType.DMA((2,))],
        ),
        out_shape=(
            pltpu.VMEM((rows_here, columns), F32),
            pltpu.VMEM((rows_here, 1, columns), F32),
            jax.ShapeDtypeStruct((1,), F32),
        ),
        input_output_aliases={} if fresh else {2 * GROUPS + 2: 0, 2 * GROUPS + 3: 1},
        compiler_params=params(16),
        cost_estimate=pl.CostEstimate(flops=m.size // 16, bytes_accessed=m.size // 4, transcendentals=0),
        name=name,
    )(side, *t, *peers, m, *([] if fresh else vmem(*so_far[:2]) + [so_far[2]]))


def sum_kernel(a_ref, b_ref, out_ref):
    out_ref[0] = a_ref[0] + b_ref[0]


def mass_parts(mass):
    count = lax.axis_size("space")
    if count & (count - 1):
        return [lax.psum(mass, "space")]
    parts = [mass]
    for bit in range(count.bit_length() - 1):
        if len(parts) == 2:
            parts = [
                pl.pallas_call(
                    sum_kernel,
                    in_specs=[INSMEM, INSMEM],
                    out_specs=INSMEM,
                    out_shape=jax.ShapeDtypeStruct((1,), F32),
                    compiler_params=params(1),
                    name="mass",
                )(*parts)
            ]
        parts.append(lax.ppermute(parts[0], "space", [(i, i ^ (1 << bit)) for i in range(count)]))
    return parts


def output_kernel(total, raw_ref, quotient_ref, *refs):
    *masses, barycenter_ref, scaling_ref = refs
    mass = masses[0][0]
    for part in masses[1:]:
        mass += part[0]
    scale = jnp.full((1, raw_ref.shape[1]), total, F32) / jnp.full((1, raw_ref.shape[1]), mass, F32)
    barycenter_ref[...] = raw_ref[...] * scale
    scaling_ref[...] = quotient_ref[...] * scale[:, : quotient_ref.shape[2]].reshape(1, 1, quotient_ref.shape[2])


def outputs(raw, quotient, masses):
    rows, columns = raw.shape
    tile = 64
    flat = pl.BlockSpec((tile, columns), lambda i: (i, 0))
    deep = pl.BlockSpec((tile,) + quotient.shape[1:], lambda i: (i, 0, 0))
    return pl.pallas_call(
        functools.partial(output_kernel, float(columns * columns)),
        grid=(rows // tile,),
        in_specs=[flat, deep] + [INSMEM] * len(masses),
        out_specs=(flat, deep),
        out_shape=(jax.ShapeDtypeStruct(raw.shape, F32), jax.ShapeDtypeStruct(quotient.shape, F32)),
        compiler_params=params(16),
        name="outputs",
    )(*vmem(raw, quotient), *masses)


def local(densities, scaling, weights, band):
    rows_here, maps_here, cols_all = densities.shape
    _, _, width, _ = band.shape
    nlocal = rows_here // width
    inner = max(nlocal - 2, 0)
    place = lax.axis_index("space")
    count = lax.axis_size("space")
    assert maps_here == 1 and lax.axis_size("member") == 2 and count % 2 == 0

    odd = place & 1
    side = odd.reshape(1)
    last = rows_here - width
    cross_row, near_row = (0, last), (last, 0)
    both = lambda pairs: pairs + [(b, a) for a, b in pairs]
    cross = functools.partial(
        lax.ppermute, axis_name="space", perm=both([(i, i + 1) for i in range(1, count - 1, 2)])
    )
    near = functools.partial(lax.ppermute, axis_name="space", perm=both([(i, i + 1) for i in range(0, count, 2)]))
    swap = functools.partial(lax.ppermute, axis_name="member", perm=[(0, 1), (1, 0)])

    def choose(choice):
        return jnp.where(odd == 0, *[c // width for c in choice]).astype(jnp.int32)

    cross1 = cross(cut("cut_cross", side, scaling, cross_row, width))
    near1 = near(cut("cut_near", side, scaling, near_row, width))

    shares = weights / jnp.sum(weights)
    share = lax.dynamic_slice_in_dim(shares, lax.axis_index("member"), 1)
    wts = row_weights(band)
    mine = place * nlocal
    band_at = lambda block, blocks: lax.dynamic_slice_in_dim(band, mine + block, blocks, 0)

    if inner > 0:
        inner_bands = band_at(1, inner)
        ratio_inner = blur(
            "ratio_inner", side, hbm(scaling), [(0, 0, rows_here, 0)], inner_bands, wts, densities, width
        )
        cross1, ratio_inner = lax.optimization_barrier((cross1, ratio_inner))
    if nlocal == 1:
        pieces = [(0, 0, width, width), (1, 0, width, (0, 2 * width)), (2, 0, width, (2 * width, 0))]
        bands = band_at(0, 1)
        ratio = blur("ratio_only", side, [scaling, cross1, near1], pieces, bands, wts, densities, 0)
        cross2, near2 = cross(ratio), near(ratio)
    else:
        two = rows_here - 2 * width
        pieces = [(0, (0, two), 2 * width, (width, 0)), (1, 0, width, (0, 2 * width))]
        bands = band_at(choose(cross_row), 1)
        ratio_cross = blur("ratio_cross", side, hbm(scaling) + [cross1], pieces, bands, wts, densities, cross_row)
        ratio_cross, near1 = lax.optimization_barrier((ratio_cross, near1))
        cross2 = cross(ratio_cross)
        pieces = [(0, (two, 0), 2 * width, (0, width)), (1, 0, width, (2 * width, 0))]
        bands = band_at(choose(near_row), 1)
        ratio_near = blur("ratio_near", side, hbm(scaling) + [near1], pieces, bands, wts, densities, near_row)
        near2 = near(ratio_near)

    def finish(name, arrays, pieces, bands, row, share, state, pin=True):
        t, m = blur("logs_" + name, side, arrays, pieces, bands, wts, scaling, row, share, pin)
        keep = hbm if pin else lambda *a: list(a)
        return raw_rows(
            "raw_" + name, side, row, keep(*t), [swap(part) for part in t], *hbm(m), rows_here, state
        )

    if nlocal == 1:
        pieces = [(0, 0, width, width), (1, 0, width, (0, 2 * width)), (2, 0, width, (2 * width, 0))]
        state = finish("only", [ratio, cross2, near2], pieces, bands, (0, 0), share, None)
    else:
        most, end = rows_here - width, rows_here
        pieces = [(0, 0, width, (width, most)), (1, 0, width, (end, 0)), (2, 0, width, (0, end))]
        arrays = [ratio_cross, ratio_near, cross2]
        beside, beside_row = ratio_cross, 0
        if inner > 0:
            pieces.append((3, 0, inner * width, (2 * width, width)))
            arrays.append(ratio_inner)
            beside, beside_row = ratio_inner, ((inner - 1) * width, 0)
        row = (0, width)
        state = finish("most", hbm(*arrays[:2]) + arrays[2:3] + hbm(*arrays[3:]), pieces, band_at(choose(row), nlocal - 1), row, share, None)
        share, state = lax.optimization_barrier((share, state))
        pieces = [(0, 0, width, width), (1, beside_row, width, (0, 2 * width)), (2, 0, width, (2 * width, 0))]
        state = finish("near", hbm(ratio_near, beside) + [near2], pieces, bands, near_row, share, state, False)

    raw, quotient, mass = state
    barycenter, new_scaling = outputs(raw, quotient.reshape(rows_here, cols_all // width, width), mass_parts(mass))
    return barycenter, new_scaling.reshape(rows_here, 1, cols_all)


def solution(mesh):
    return jax.shard_map(
        local,
        mesh=mesh,
        in_specs=(
            P("space", ("parts", "member"), None),
            P("space", ("parts", "member"), None),
            P("parts"),
            P(),
        ),
        out_specs=(P(("parts", "space"), None), P("space", ("parts", "member"), None)),
        check_vma=False,
    )
```

```python
import functools

import jax
import jax.numpy as jnp
from jax import lax
from jax.experimental import pallas as pl
from jax.experimental.pallas import tpu as pltpu
from jax.sharding import PartitionSpec as P

F32 = jnp.float32
BF16 = jnp.bfloat16
GROUPS = 4
SPREAD_BOTH = False
ANY = pl.BlockSpec(memory_space=pl.ANY)
INVMEM = pl.BlockSpec(memory_space=pltpu.VMEM)
INSMEM = pl.BlockSpec(memory_space=pltpu.SMEM)


def split(x):
    high = x.astype(BF16)
    return high, (x - high.astype(F32)).astype(BF16)


def dot3(stack, b, dims):
    one = functools.partial(lax.dot_general, dimension_numbers=(dims, ((), ())), preferred_element_type=F32)
    rows = stack.shape[0] // 2
    both = one(stack, b[0])
    return both[:rows] + (one(stack[:rows], b[1]) + both[rows:])


def params(mebibytes):
    return pltpu.CompilerParams(vmem_limit_bytes=mebibytes * 1024 * 1024)


def hbm(*arrays):
    return [pltpu.with_memory_space_constraint(a, pltpu.HBM) for a in arrays]


def vmem(*arrays):
    return [pltpu.with_memory_space_constraint(a, pltpu.VMEM) for a in arrays]


def pick(choice, side):
    if isinstance(choice, tuple):
        return pl.multiple_of(jnp.where(side == 0, choice[0], choice[1]), 128)
    return choice


def cut_kernel(first, columns, side_ref, src, *refs):
    *outs, stage, sems = refs
    rows = stage.shape[0] // GROUPS
    start = pick(first, side_ref[0])
    outward = []
    inward = [
        pltpu.make_async_copy(src.at[pl.ds(start + g * rows, rows)], stage.at[pl.ds(g * rows, rows)], sems.at[0, g])
        for g in range(GROUPS)
    ]
    for copy in inward:
        copy.start()
    for g in range(GROUPS):
        inward[g].wait()
        part = pl.ds(g * rows, rows)
        for k, (out, column) in enumerate(zip(outs, columns)):
            at = pl.ds(column_of(column, side_ref), out.shape[2])
            outward.append(pltpu.make_async_copy(stage.at[part, :, at], out.at[part], sems.at[1 + k, g]))
            outward[-1].start()
    for copy in outward:
        copy.wait()


def cut(name, side, array, first, rows, parts):
    columns = array.shape[2]
    return pl.pallas_call(
        functools.partial(cut_kernel, first, [column for column, _ in parts]),
        in_specs=[INSMEM, ANY],
        out_specs=[ANY] * len(parts),
        out_shape=[pltpu.HBM((rows, 1, n), F32) for _, n in parts],
        scratch_shapes=[
            pltpu.VMEM((rows, 1, columns), F32),
            pltpu.SemaphoreType.DMA((1 + len(parts), GROUPS)),
        ],
        compiler_params=params(8),
        name=name,
    )(side, *hbm(array))


def column_of(column, side_ref):
    if isinstance(column, tuple):
        return pl.multiple_of(jnp.where(side_ref[1] == 1, column[0], column[1]), 128)
    return column


def cross_parts(columns):
    half, quarter = columns // 2, columns // 4
    return [(0, half), (half, quarter), ((half, 0), half), (3 * quarter, quarter)]


def cross_send(parts, behind=()):
    def send(part, numbers, ends):
        pairs = []
        for k in range(3):
            for direction, number in ((0, k), (1, 2 - k)):
                if number in numbers:
                    pairs.append(ends(k)[direction])
        return lax.ppermute(part, "space", pairs)

    to_partner = lambda k: ((2 * k + 1, 2 * k), (2 * k + 2, 2 * k + 3))
    onward = lambda k: ((2 * k, 2 * k + 2), (2 * k + 3, 2 * k + 1))
    direct = lambda k: ((2 * k + 1, 2 * k + 2), (2 * k + 2, 2 * k + 1))
    relayed = [send(part, numbers, to_partner) for part, numbers in zip(parts[:2], ((0, 1), (0, 2)))]
    straight = [send(part, numbers, direct) for part, numbers in zip(parts[2:], ((1, 2), (0, 2)))]
    a, b, c, d, *behind = lax.optimization_barrier((*relayed, *straight, *behind))
    relayed, straight = [a, b], [c, d]
    passed = [send(part, numbers, onward) for part, numbers in zip(relayed, ((0, 1), (0, 2)))]
    return passed + straight, behind


def cross_received(base, columns):
    a, b, c, d = range(base, base + 4)
    q = columns // 4
    return ((2, (c, 0), (a, 0)), (2, (c, q), (a, q)), (1, (c, 0), (b, 0)), (1, (c, q), (d, 0)))


def cross_own(base, columns):
    return ((base, 0), (base, columns // 4), (base + 1, 0), (base + 3, 0))


def area(ref, row, rows, columns):
    return ref.at[pl.ds(row, rows), 0, columns] if len(ref.shape) == 3 else ref.at[pl.ds(row, rows), columns]


def weight_kernel(nblocks, band_ref, high_ref, low_ref):
    pair = pl.program_id(0)
    width = band_ref.shape[2]
    zero = jnp.zeros((width, width), F32)
    for o in range(2):
        for i in range(4):
            j = i - o
            value = band_ref[o, j] if 0 <= j <= 2 else zero
            if (o, j) == (0, 0):
                value = jnp.where(pair > 0, value, 0.0)
            if (o, j) == (1, 2):
                value = jnp.where(pair < nblocks // 2 - 1, value, 0.0)
            high, low = split(value)
            rows, columns = slice(o * width, (o + 1) * width), slice(i * width, (i + 1) * width)
            high_ref[0, rows, columns] = high
            low_ref[0, rows, columns] = low


def row_weights(band):
    nblocks, _, width, _ = band.shape
    shape = pltpu.HBM((nblocks // 2, 2 * width, 4 * width), BF16)
    out_spec = pl.BlockSpec((1, 2 * width, 4 * width), lambda t: (t, 0, 0))
    return pl.pallas_call(
        functools.partial(weight_kernel, nblocks),
        grid=(nblocks // 2,),
        in_specs=[pl.BlockSpec((2, 3, width, width), lambda t: (t, 0, 0, 0))],
        out_specs=(out_spec, out_spec),
        out_shape=(shape, shape),
        name="row_weights",
    )(*hbm(band))


def blur_kernel(plan, *refs):
    pieces, narrays, extra, final, split_out = plan
    side_ref, refs = refs[0], refs[1:]
    arrays = refs[:narrays]
    band_ref, high_ref, low_ref, extra_ref = refs[narrays : narrays + 4]
    rest = refs[narrays + 4 :]
    if final:
        share_ref, rest = rest[0], rest[1:]
    nouts = GROUPS + 1 if final else 4 if split_out else 1
    outs = rest[:nouts]
    field, a_both, y_both, whigh, wlow, other = rest[nouts : nouts + 6]
    *results, in_sems, late_sems, out_sems = rest[nouts + 6 :]

    side = side_ref[0]
    nout, _, width, _ = band_ref.shape
    columns = field.shape[1]
    step = columns // GROUPS
    pairs = step // (2 * width)
    inside, late = [], []

    def copy_in(g, k, place):
        _, row, rows, to = pieces[k]
        which, column = place
        return pltpu.make_async_copy(
            area(arrays[which], pick(row, side), rows, pl.ds(column, step)),
            field.at[pl.ds(pick(to, side), rows), pl.ds(g * step, step)],
            in_sems.at[g, k],
        )

    def start_in(g, k):
        source = pieces[k][0]
        if isinstance(source, int):
            copy = copy_in(g, k, (source, g * step))
        elif len(source[g]) == 2:
            copy = copy_in(g, k, source[g])
        else:
            number, this, other_one = source[g]
            pl.when(side_ref[2] == number)(copy_in(g, k, this).start)
            pl.when(side_ref[2] != number)(copy_in(g, k, other_one).start)
            return copy_in(g, k, other_one)
        copy.start()
        return copy

    for g in range(GROUPS):
        at = pl.ds(g * step, step)
        some = pl.ds(g * pairs, pairs)
        late.append(
            [
                pltpu.make_async_copy(high_ref.at[some], whigh.at[some], late_sems.at[g, 0]),
                pltpu.make_async_copy(low_ref.at[some], wlow.at[some], late_sems.at[g, 1]),
                pltpu.make_async_copy(
                    area(extra_ref, pick(extra, side), other.shape[0], at), other.at[:, at], late_sems.at[g, 2]
                ),
            ]
        )
    for g in range(GROUPS):
        inside.append([start_in(g, k) for k in range(len(pieces))])
        if g > 0:
            for copy in late[g - 1]:
                copy.start()
    for copy in late[GROUPS - 1]:
        copy.start()

    blocks = [(i, min(2, nout - i)) for i in range(0, nout, 2)]
    total = nout * width
    a_both[...] = jnp.zeros_like(a_both)
    for first, n in blocks:
        for i in range(n):
            for j in range(3):
                for part, value in enumerate(split(band_ref[first + i, j])):
                    row = (2 * first + part * n + i) * width
                    a_both[row : row + width, (i + j) * width : (i + j + 1) * width] = value
    y_both[:, :width] = jnp.zeros((2 * total, width), BF16)
    y_both[:, columns + width :] = jnp.zeros((2 * total, width), BF16)

    def columns_pass(g):
        for copy in inside[g]:
            copy.wait()
        for i in range(g * pairs, (g + 1) * pairs):
            at = slice(i * 2 * width, (i + 1) * 2 * width)
            to = slice((2 * i + 1) * width, (2 * i + 3) * width)
            for first, n in blocks:
                a = a_both[2 * first * width : 2 * (first + n) * width, : (n + 2) * width]
                y = dot3(a, split(field[first * width : (first + n + 2) * width, at]), ((1,), (0,)))
                for part, value in enumerate(split(y)):
                    row = part * total + first * width
                    y_both[row : row + n * width, to] = value

    def rows_pass(g):
        for copy in late[g]:
            copy.wait()
        for t in range(g * pairs, (g + 1) * pairs):
            source = slice(t * 2 * width, (t + 2) * 2 * width)
            at = slice(t * 2 * width, (t + 1) * 2 * width)
            value = dot3(y_both[:, source], (whigh[t], wlow[t]), ((1,), (1,)))
            if final:
                results[0][:, at] = value
                results[1][:, at] = share_ref[0] * jnp.log(other[:, at] * value)
            else:
                results[0][:, at] = other[:, at] / value
        at = pl.ds(g * step, step)
        if split_out:
            which, column = cross_own(0, columns)[g]
            targets = [outs[which].at[:, pl.ds(column, step)]]
        else:
            targets = [outs[-1].at[:, at]] + ([outs[g]] if final else [])
        copies = [
            pltpu.make_async_copy(src.at[:, at], dst, out_sems.at[g, k])
            for k, (src, dst) in enumerate(zip(results, targets))
        ]
        for copy in copies:
            copy.start()
        return copies

    going = []
    for g in range(GROUPS):
        columns_pass(g)
        if g > 0:
            going += rows_pass(g - 1)
    going += rows_pass(GROUPS - 1)
    if split_out:
        column, n = cross_parts(columns)[2]
        at = pl.ds(column_of(column, side_ref), n)
        going.append(pltpu.make_async_copy(results[0].at[:, at], outs[2], out_sems.at[GROUPS, 0]))
        going[-1].start()
    for copy in going:
        copy.wait()


def blur(name, side, arrays, pieces, bands, weights, other, extra, share=None, pin=True, split_out=False):
    nout, _, width, _ = bands.shape
    npairs = weights[0].shape[0]
    columns = npairs * 2 * width
    rows, depth = nout * width, (nout + 2) * width
    final = share is not None
    nouts = 2 if final else 1
    kind = pltpu.HBM if pin else jax.ShapeDtypeStruct
    shapes = [kind((rows, columns // GROUPS), F32)] * (GROUPS if final else 0)
    if split_out:
        shapes = [pltpu.HBM((rows, n), F32) for _, n in cross_parts(columns)]
    else:
        shapes.append(pltpu.HBM((rows, columns), F32))
    plan = (tuple(pieces), len(arrays), extra, final, split_out)
    work = 3 * 2 * rows * columns * (depth + 4 * width)
    moved = 4 * (depth + 3 * rows) * columns + npairs * 2 * 2 * 8 * width * width
    size = 4 * columns * (depth + (1 + nouts) * rows) + 4 * rows * columns + npairs * 2 * 2 * 8 * width * width
    result = pl.pallas_call(
        functools.partial(blur_kernel, plan),
        in_specs=[INSMEM] + [ANY] * len(arrays) + [INVMEM, ANY, ANY, ANY] + [INSMEM] * final,
        out_specs=[ANY] * len(shapes),
        out_shape=shapes,
        scratch_shapes=[
            pltpu.VMEM((depth, columns), F32),
            pltpu.VMEM((2 * rows, min(depth, 4 * width)), BF16),
            pltpu.VMEM((2 * rows, columns + 2 * width), BF16),
            pltpu.VMEM((npairs, 2 * width, 4 * width), BF16),
            pltpu.VMEM((npairs, 2 * width, 4 * width), BF16),
            pltpu.VMEM((rows, columns), F32),
        ]
        + [pltpu.VMEM((rows, columns), F32)] * nouts
        + [
            pltpu.SemaphoreType.DMA((GROUPS, len(pieces))),
            pltpu.SemaphoreType.DMA((GROUPS, 3)),
            pltpu.SemaphoreType.DMA((GROUPS + 1, nouts)),
        ],
        compiler_params=params(size // 2**20 + 6),
        cost_estimate=pl.CostEstimate(flops=work // 64, bytes_accessed=moved // 64, transcendentals=0),
        name=name,
    )(side, *arrays, bands, *hbm(*weights, other), *([share] if final else []))
    return (result[:-1], result[-1]) if final else list(result) if split_out else result[0]


def raw_kernel(fresh, first, side_ref, *refs):
    own, peer, m_ref = refs[:GROUPS], refs[GROUPS : 2 * GROUPS], refs[2 * GROUPS]
    raw_ref, quotient_ref, mass_ref, quotient, sems = refs[-5:]
    tile = raw_ref.shape[0]
    at = pl.program_id(0)
    slot = lax.rem(at, 2)

    def copy(step, slot):
        row = pl.multiple_of(pick(first, side_ref[0]) + step * tile, tile)
        return pltpu.make_async_copy(quotient.at[slot], area(quotient_ref, row, tile, slice(None)), sems.at[slot])

    @pl.when(at >= 2)
    def _():
        copy(at - 2, slot).wait()

    mass = 0.0
    for g in range(GROUPS):
        raw = jnp.exp(own[g][...] + peer[g][...])
        step = raw.shape[1]
        raw_ref[:, g * step : (g + 1) * step] = raw
        mass += jnp.sum(raw)
        quotient[slot, :, g * step : (g + 1) * step] = raw / m_ref[:, g * step : (g + 1) * step]
    before = 0.0 if fresh else refs[2 * GROUPS + 3][0]
    mass_ref[0] = mass + jnp.where(at == 0, before, mass_ref[0])
    copy(at, slot).start()

    @pl.when(at == pl.num_programs(0) - 1)
    def _():
        copy(at - 1, 1 - slot).wait()
        copy(at, slot).wait()


def raw_rows(name, side, row, t, peers, m, rows_here, so_far):
    fresh = so_far is None
    rows, columns = m.shape
    tile = 32
    starts = [r // tile for r in row]
    part = pl.BlockSpec((tile, columns), lambda i, at: (i, 0))
    group = pl.BlockSpec((tile, columns // GROUPS), lambda i, at: (i, 0))
    return pl.pallas_call(
        functools.partial(raw_kernel, fresh, row),
        grid_spec=pltpu.PrefetchScalarGridSpec(
            num_scalar_prefetch=1,
            grid=(rows // tile,),
            in_specs=[group] * (2 * GROUPS) + [part] + ([] if fresh else [ANY, ANY, INSMEM]),
            out_specs=(
                pl.BlockSpec((tile, columns), lambda i, at: (jnp.where(at[0] == 0, *starts) + i, 0)),
                ANY,
                INSMEM,
            ),
            scratch_shapes=[pltpu.VMEM((2, tile, columns), F32), pltpu.SemaphoreType.DMA((2,))],
        ),
        out_shape=(
            pltpu.VMEM((rows_here, columns), F32),
            pltpu.VMEM((rows_here, 1, columns), F32),
            jax.ShapeDtypeStruct((1,), F32),
        ),
        input_output_aliases={} if fresh else {2 * GROUPS + 2: 0, 2 * GROUPS + 3: 1},
        compiler_params=params(16),
        cost_estimate=pl.CostEstimate(flops=m.size // 16, bytes_accessed=m.size // 4, transcendentals=0),
        name=name,
    )(side, *t, *peers, m, *([] if fresh else vmem(*so_far[:2]) + [so_far[2]]))


def sum_kernel(a_ref, b_ref, out_ref):
    out_ref[0] = a_ref[0] + b_ref[0]


def mass_parts(mass):
    count = lax.axis_size("space")
    if count & (count - 1):
        return [lax.psum(mass, "space")]
    parts = [mass]
    for bit in range(count.bit_length() - 1):
        if len(parts) == 2:
            parts = [
                pl.pallas_call(
                    sum_kernel,
                    in_specs=[INSMEM, INSMEM],
                    out_specs=INSMEM,
                    out_shape=jax.ShapeDtypeStruct((1,), F32),
                    compiler_params=params(1),
                    name="mass",
                )(*parts)
            ]
        parts.append(lax.ppermute(parts[0], "space", [(i, i ^ (1 << bit)) for i in range(count)]))
    return parts


def output_kernel(total, raw_ref, quotient_ref, *refs):
    *masses, barycenter_ref, scaling_ref = refs
    mass = masses[0][0]
    for part in masses[1:]:
        mass += part[0]
    scale = jnp.full((1, raw_ref.shape[1]), total, F32) / jnp.full((1, raw_ref.shape[1]), mass, F32)
    barycenter_ref[...] = raw_ref[...] * scale
    scaling_ref[...] = quotient_ref[...] * scale[:, : quotient_ref.shape[2]].reshape(1, 1, quotient_ref.shape[2])


def outputs(raw, quotient, masses):
    rows, columns = raw.shape
    tile = 64
    flat = pl.BlockSpec((tile, columns), lambda i: (i, 0))
    deep = pl.BlockSpec((tile,) + quotient.shape[1:], lambda i: (i, 0, 0))
    return pl.pallas_call(
        functools.partial(output_kernel, float(columns * columns)),
        grid=(rows // tile,),
        in_specs=[flat, deep] + [INSMEM] * len(masses),
        out_specs=(flat, deep),
        out_shape=(jax.ShapeDtypeStruct(raw.shape, F32), jax.ShapeDtypeStruct(quotient.shape, F32)),
        compiler_params=params(16),
        name="outputs",
    )(*vmem(raw, quotient), *masses)


def local(densities, scaling, weights, band):
    rows_here, maps_here, cols_all = densities.shape
    _, _, width, _ = band.shape
    nlocal = rows_here // width
    inner = max(nlocal - 2, 0)
    place = lax.axis_index("space")
    count = lax.axis_size("space")
    assert maps_here == 1 and lax.axis_size("member") == 2 and count % 2 == 0

    odd = place & 1
    middle = place >> 1
    side = jnp.stack([odd, jnp.where(odd == 1, middle, 3 - middle), jnp.where(odd == 1, 2 - middle, middle - 1)])
    spread = count == 8 and nlocal > 1
    last = rows_here - width
    cross_row, near_row = (0, last), (last, 0)
    both = lambda pairs: pairs + [(b, a) for a, b in pairs]
    cross = functools.partial(
        lax.ppermute, axis_name="space", perm=both([(i, i + 1) for i in range(1, count - 1, 2)])
    )
    near = functools.partial(lax.ppermute, axis_name="space", perm=both([(i, i + 1) for i in range(0, count, 2)]))
    swap = functools.partial(lax.ppermute, axis_name="member", perm=[(0, 1), (1, 0)])

    def choose(choice):
        return jnp.where(odd == 0, *[c // width for c in choice]).astype(jnp.int32)

    whole_rows = [(0, cols_all)]
    near_edge = cut("cut_near", side, scaling, near_row, width, whole_rows)
    if spread:
        edge = cut("cut_cross", side, scaling, cross_row, width, cross_parts(cols_all))
        cross1, near_edge = cross_send(edge, near_edge)
    else:
        cross1 = [cross(cut("cut_cross", side, scaling, cross_row, width, whole_rows)[0])]
    near1 = near(near_edge[0])

    shares = weights / jnp.sum(weights)
    share = lax.dynamic_slice_in_dim(shares, lax.axis_index("member"), 1)
    wts = row_weights(band)
    mine = place * nlocal
    band_at = lambda block, blocks: lax.dynamic_slice_in_dim(band, mine + block, blocks, 0)

    if inner > 0:
        inner_bands = band_at(1, inner)
        ratio_inner = blur(
            "ratio_inner", side, hbm(scaling), [(0, 0, rows_here, 0)], inner_bands, wts, densities, width
        )
        *cross1, ratio_inner = lax.optimization_barrier((*cross1, ratio_inner))
    if nlocal == 1:
        pieces = [(0, 0, width, width), (1, 0, width, (0, 2 * width)), (2, 0, width, (2 * width, 0))]
        bands = band_at(0, 1)
        ratio = blur("ratio_only", side, [scaling, *cross1, near1], pieces, bands, wts, densities, 0)
        cross2, near2 = cross(ratio), near(ratio)
    else:
        two = rows_here - 2 * width
        halo = cross_received(1, cols_all) if spread else 1
        pieces = [(0, (0, two), 2 * width, (width, 0)), (halo, 0, width, (0, 2 * width))]
        bands = band_at(choose(cross_row), 1)
        ratio_cross = blur(
            "ratio_cross", side, hbm(scaling) + cross1, pieces, bands, wts, densities, cross_row,
            split_out=spread and SPREAD_BOTH,
        )
        ratio_cross, near1 = lax.optimization_barrier((ratio_cross, near1))
        if spread and SPREAD_BOTH:
            cross2, _ = cross_send(ratio_cross)
        else:
            cross2, ratio_cross = [cross(ratio_cross)], [ratio_cross]
        pieces = [(0, (two, 0), 2 * width, (0, width)), (1, 0, width, (2 * width, 0))]
        near_bands = band_at(choose(near_row), 1)
        ratio_near = blur("ratio_near", side, hbm(scaling) + [near1], pieces, near_bands, wts, densities, near_row)
        near2 = near(ratio_near)

    def finish(name, arrays, pieces, bands, row, share, state, pin=True):
        t, m = blur("logs_" + name, side, arrays, pieces, bands, wts, scaling, row, share, pin)
        keep = hbm if pin else lambda *a: list(a)
        return raw_rows(
            "raw_" + name, side, row, keep(*t), [swap(part) for part in t], *hbm(m), rows_here, state
        )

    if nlocal == 1:
        pieces = [(0, 0, width, width), (1, 0, width, (0, 2 * width)), (2, 0, width, (2 * width, 0))]
        state = finish("only", [ratio, cross2, near2], pieces, bands, (0, 0), share, None)
    else:
        most, end = rows_here - width, rows_here
        n = len(ratio_cross)
        own = cross_own(1, cols_all) if n == 4 else 1
        halo = cross_received(1 + n, cols_all) if n == 4 else 1 + n
        arrays = hbm(ratio_near, *ratio_cross) + cross2
        pieces = [(own, 0, width, (width, most)), (0, 0, width, (end, 0)), (halo, 0, width, (0, end))]
        beside, beside_row = ratio_cross[0], 0
        if inner > 0:
            pieces.append((len(arrays), 0, inner * width, (2 * width, width)))
            arrays += hbm(ratio_inner)
            beside, beside_row = ratio_inner, ((inner - 1) * width, 0)
        row = (0, width)
        bands = band_at(choose(row), nlocal - 1)
        state = finish("most", arrays, pieces, bands, row, share, None)
        share, state = lax.optimization_barrier((share, state))
        pieces = [(0, 0, width, width), (1, beside_row, width, (0, 2 * width)), (2, 0, width, (2 * width, 0))]
        state = finish("near", hbm(ratio_near, beside) + [near2], pieces, near_bands, near_row, share, state, False)

    raw, quotient, mass = state
    barycenter, new_scaling = outputs(raw, quotient.reshape(rows_here, cols_all // width, width), mass_parts(mass))
    return barycenter, new_scaling.reshape(rows_here, 1, cols_all)


def solution(mesh):
    return jax.shard_map(
        local,
        mesh=mesh,
        in_specs=(
            P("space", ("parts", "member"), None),
            P("space", ("parts", "member"), None),
            P("parts"),
            P(),
        ),
        out_specs=(P(("parts", "space"), None), P("space", ("parts", "member"), None)),
        check_vma=False,
    )
```

```python
import functools

import jax
import jax.numpy as jnp
from jax import lax
from jax.experimental import pallas as pl
from jax.experimental.pallas import tpu as pltpu
from jax.sharding import PartitionSpec as P

F32 = jnp.float32
BF16 = jnp.bfloat16
GROUPS = 4
SPREAD_BOTH = False
ANY = pl.BlockSpec(memory_space=pl.ANY)
INVMEM = pl.BlockSpec(memory_space=pltpu.VMEM)
INSMEM = pl.BlockSpec(memory_space=pltpu.SMEM)


def split(x):
    high = x.astype(BF16)
    return high, (x - high.astype(F32)).astype(BF16)


def dot3(stack, b, dims):
    one = functools.partial(lax.dot_general, dimension_numbers=(dims, ((), ())), preferred_element_type=F32)
    rows = stack.shape[0] // 2
    both = one(stack, b[0])
    return both[:rows] + (one(stack[:rows], b[1]) + both[rows:])


def params(mebibytes):
    return pltpu.CompilerParams(vmem_limit_bytes=mebibytes * 1024 * 1024)


def hbm(*arrays):
    return [pltpu.with_memory_space_constraint(a, pltpu.HBM) for a in arrays]


def vmem(*arrays):
    return [pltpu.with_memory_space_constraint(a, pltpu.VMEM) for a in arrays]


def pick(choice, side):
    if isinstance(choice, tuple):
        return pl.multiple_of(jnp.where(side == 0, choice[0], choice[1]), 128)
    return choice


def cut_kernel(first, columns, side_ref, src, *refs):
    *outs, stage, sems = refs
    rows = stage.shape[0] // GROUPS
    start = pick(first, side_ref[0])
    outward = []
    inward = [
        pltpu.make_async_copy(src.at[pl.ds(start + g * rows, rows)], stage.at[pl.ds(g * rows, rows)], sems.at[0, g])
        for g in range(GROUPS)
    ]
    for copy in inward:
        copy.start()
    for g in range(GROUPS):
        inward[g].wait()
        part = pl.ds(g * rows, rows)
        for k, (out, column) in enumerate(zip(outs, columns)):
            at = pl.ds(column_of(column, side_ref), out.shape[2])
            outward.append(pltpu.make_async_copy(stage.at[part, :, at], out.at[part], sems.at[1 + k, g]))
            outward[-1].start()
    for copy in outward:
        copy.wait()


def cut(name, side, array, first, rows, parts):
    columns = array.shape[2]
    return pl.pallas_call(
        functools.partial(cut_kernel, first, [column for column, _ in parts]),
        in_specs=[INSMEM, ANY],
        out_specs=[ANY] * len(parts),
        out_shape=[pltpu.HBM((rows, 1, n), F32) for _, n in parts],
        scratch_shapes=[
            pltpu.VMEM((rows, 1, columns), F32),
            pltpu.SemaphoreType.DMA((1 + len(parts), GROUPS)),
        ],
        compiler_params=params(8),
        name=name,
    )(side, *hbm(array))


def column_of(column, side_ref):
    if isinstance(column, tuple):
        return pl.multiple_of(jnp.where(side_ref[1] == 1, column[0], column[1]), 128)
    return column


def cross_parts(columns):
    half, quarter = columns // 2, columns // 4
    return [(0, half), (half, quarter), ((half, 0), half), (3 * quarter, quarter)]


def cross_send(parts, behind=()):
    def send(part, numbers, ends):
        pairs = []
        for k in range(3):
            for direction, number in ((0, k), (1, 2 - k)):
                if number in numbers:
                    pairs.append(ends(k)[direction])
        return lax.ppermute(part, "space", pairs)

    to_partner = lambda k: ((2 * k + 1, 2 * k), (2 * k + 2, 2 * k + 3))
    onward = lambda k: ((2 * k, 2 * k + 2), (2 * k + 3, 2 * k + 1))
    direct = lambda k: ((2 * k + 1, 2 * k + 2), (2 * k + 2, 2 * k + 1))
    relayed = [send(part, numbers, to_partner) for part, numbers in zip(parts[:2], ((0, 1), (0, 2)))]
    straight = [send(part, numbers, direct) for part, numbers in zip(parts[2:], ((1, 2), (0, 2)))]
    a, b, c, d, *behind = lax.optimization_barrier((*relayed, *straight, *behind))
    relayed, straight = [a, b], [c, d]
    passed = [send(part, numbers, onward) for part, numbers in zip(relayed, ((0, 1), (0, 2)))]
    return passed + straight, behind


def cross_received(base, columns):
    a, b, c, d = range(base, base + 4)
    q = columns // 4
    return ((2, (c, 0), (a, 0)), (2, (c, q), (a, q)), (1, (c, 0), (b, 0)), (1, (c, q), (d, 0)))


def cross_own(base, columns):
    return ((base, 0), (base, columns // 4), (base + 1, 0), (base + 3, 0))


def area(ref, row, rows, columns):
    return ref.at[pl.ds(row, rows), 0, columns] if len(ref.shape) == 3 else ref.at[pl.ds(row, rows), columns]


def weight_kernel(nblocks, band_ref, high_ref, low_ref):
    pair = pl.program_id(0)
    width = band_ref.shape[2]
    zero = jnp.zeros((width, width), F32)
    for o in range(2):
        for i in range(4):
            j = i - o
            value = band_ref[o, j] if 0 <= j <= 2 else zero
            if (o, j) == (0, 0):
                value = jnp.where(pair > 0, value, 0.0)
            if (o, j) == (1, 2):
                value = jnp.where(pair < nblocks // 2 - 1, value, 0.0)
            high, low = split(value)
            rows, columns = slice(o * width, (o + 1) * width), slice(i * width, (i + 1) * width)
            high_ref[0, rows, columns] = high
            low_ref[0, rows, columns] = low


def row_weights(band):
    nblocks, _, width, _ = band.shape
    shape = pltpu.HBM((nblocks // 2, 2 * width, 4 * width), BF16)
    out_spec = pl.BlockSpec((1, 2 * width, 4 * width), lambda t: (t, 0, 0))
    return pl.pallas_call(
        functools.partial(weight_kernel, nblocks),
        grid=(nblocks // 2,),
        in_specs=[pl.BlockSpec((2, 3, width, width), lambda t: (t, 0, 0, 0))],
        out_specs=(out_spec, out_spec),
        out_shape=(shape, shape),
        name="row_weights",
    )(*hbm(band))


def blur_kernel(plan, *refs):
    pieces, narrays, extra, final, split_out = plan
    side_ref, refs = refs[0], refs[1:]
    arrays = refs[:narrays]
    band_ref, high_ref, low_ref, extra_ref = refs[narrays : narrays + 4]
    rest = refs[narrays + 4 :]
    if final:
        share_ref, rest = rest[0], rest[1:]
    nouts = GROUPS + 1 if final else 4 if split_out else 1
    outs = rest[:nouts]
    field, a_both, y_both, whigh, wlow, other = rest[nouts : nouts + 6]
    *results, in_sems, late_sems, out_sems = rest[nouts + 6 :]

    side = side_ref[0]
    nout, _, width, _ = band_ref.shape
    columns = field.shape[1]
    step = columns // GROUPS
    pairs = step // (2 * width)
    inside, late = [], []

    def copy_in(g, k, place):
        _, row, rows, to = pieces[k]
        which, column = place
        return pltpu.make_async_copy(
            area(arrays[which], pick(row, side), rows, pl.ds(column, step)),
            field.at[pl.ds(pick(to, side), rows), pl.ds(g * step, step)],
            in_sems.at[g, k],
        )

    def start_in(g, k):
        source = pieces[k][0]
        if isinstance(source, int):
            copy = copy_in(g, k, (source, g * step))
        elif len(source[g]) == 2:
            copy = copy_in(g, k, source[g])
        else:
            number, this, other_one = source[g]
            pl.when(side_ref[2] == number)(copy_in(g, k, this).start)
            pl.when(side_ref[2] != number)(copy_in(g, k, other_one).start)
            return copy_in(g, k, other_one)
        copy.start()
        return copy

    for g in range(GROUPS):
        at = pl.ds(g * step, step)
        some = pl.ds(g * pairs, pairs)
        late.append(
            [
                pltpu.make_async_copy(high_ref.at[some], whigh.at[some], late_sems.at[g, 0]),
                pltpu.make_async_copy(low_ref.at[some], wlow.at[some], late_sems.at[g, 1]),
                pltpu.make_async_copy(
                    area(extra_ref, pick(extra, side), other.shape[0], at), other.at[:, at], late_sems.at[g, 2]
                ),
            ]
        )
    for g in range(GROUPS):
        inside.append([start_in(g, k) for k in range(len(pieces))])
        if g > 0:
            for copy in late[g - 1]:
                copy.start()
    for copy in late[GROUPS - 1]:
        copy.start()

    blocks = [(i, min(2, nout - i)) for i in range(0, nout, 2)]
    total = nout * width
    a_both[...] = jnp.zeros_like(a_both)
    for first, n in blocks:
        for i in range(n):
            for j in range(3):
                for part, value in enumerate(split(band_ref[first + i, j])):
                    row = (2 * first + part * n + i) * width
                    a_both[row : row + width, (i + j) * width : (i + j + 1) * width] = value
    y_both[:, :width] = jnp.zeros((2 * total, width), BF16)
    y_both[:, columns + width :] = jnp.zeros((2 * total, width), BF16)

    def columns_pass(g):
        for copy in inside[g]:
            copy.wait()
        for i in range(g * pairs, (g + 1) * pairs):
            at = slice(i * 2 * width, (i + 1) * 2 * width)
            to = slice((2 * i + 1) * width, (2 * i + 3) * width)
            for first, n in blocks:
                a = a_both[2 * first * width : 2 * (first + n) * width, : (n + 2) * width]
                y = dot3(a, split(field[first * width : (first + n + 2) * width, at]), ((1,), (0,)))
                for part, value in enumerate(split(y)):
                    row = part * total + first * width
                    y_both[row : row + n * width, to] = value

    def rows_pass(g):
        for copy in late[g]:
            copy.wait()
        for t in range(g * pairs, (g + 1) * pairs):
            source = slice(t * 2 * width, (t + 2) * 2 * width)
            at = slice(t * 2 * width, (t + 1) * 2 * width)
            value = dot3(y_both[:, source], (whigh[t], wlow[t]), ((1,), (1,)))
            if final:
                results[0][:, at] = value
                results[1][:, at] = share_ref[0] * jnp.log(other[:, at] * value)
            else:
                results[0][:, at] = other[:, at] / value
        at = pl.ds(g * step, step)
        if split_out:
            which, column = cross_own(0, columns)[g]
            targets = [outs[which].at[:, pl.ds(column, step)]]
        else:
            targets = [outs[-1].at[:, at]] + ([outs[g]] if final else [])
        copies = [
            pltpu.make_async_copy(src.at[:, at], dst, out_sems.at[g, k])
            for k, (src, dst) in enumerate(zip(results, targets))
        ]
        for copy in copies:
            copy.start()
        return copies

    going = []
    for g in range(GROUPS):
        columns_pass(g)
        if g > 0:
            going += rows_pass(g - 1)
    going += rows_pass(GROUPS - 1)
    if split_out:
        column, n = cross_parts(columns)[2]
        at = pl.ds(column_of(column, side_ref), n)
        going.append(pltpu.make_async_copy(results[0].at[:, at], outs[2], out_sems.at[GROUPS, 0]))
        going[-1].start()
    for copy in going:
        copy.wait()


def blur(name, side, arrays, pieces, bands, weights, other, extra, share=None, pin=True, split_out=False):
    nout, _, width, _ = bands.shape
    npairs = weights[0].shape[0]
    columns = npairs * 2 * width
    rows, depth = nout * width, (nout + 2) * width
    final = share is not None
    nouts = 2 if final else 1
    kind = pltpu.HBM if pin else jax.ShapeDtypeStruct
    shapes = [kind((rows, columns // GROUPS), F32)] * (GROUPS if final else 0)
    if split_out:
        shapes = [pltpu.HBM((rows, n), F32) for _, n in cross_parts(columns)]
    else:
        shapes.append(pltpu.HBM((rows, columns), F32))
    plan = (tuple(pieces), len(arrays), extra, final, split_out)
    work = 3 * 2 * rows * columns * (depth + 4 * width)
    moved = 4 * (depth + 3 * rows) * columns + npairs * 2 * 2 * 8 * width * width
    size = 4 * columns * (depth + (1 + nouts) * rows) + 4 * rows * columns + npairs * 2 * 2 * 8 * width * width
    result = pl.pallas_call(
        functools.partial(blur_kernel, plan),
        in_specs=[INSMEM] + [ANY] * len(arrays) + [INVMEM, ANY, ANY, ANY] + [INSMEM] * final,
        out_specs=[ANY] * len(shapes),
        out_shape=shapes,
        scratch_shapes=[
            pltpu.VMEM((depth, columns), F32),
            pltpu.VMEM((2 * rows, min(depth, 4 * width)), BF16),
            pltpu.VMEM((2 * rows, columns + 2 * width), BF16),
            pltpu.VMEM((npairs, 2 * width, 4 * width), BF16),
            pltpu.VMEM((npairs, 2 * width, 4 * width), BF16),
            pltpu.VMEM((rows, columns), F32),
        ]
        + [pltpu.VMEM((rows, columns), F32)] * nouts
        + [
            pltpu.SemaphoreType.DMA((GROUPS, len(pieces))),
            pltpu.SemaphoreType.DMA((GROUPS, 3)),
            pltpu.SemaphoreType.DMA((GROUPS + 1, nouts)),
        ],
        compiler_params=params(size // 2**20 + 6),
        cost_estimate=pl.CostEstimate(flops=work // 64, bytes_accessed=moved // 64, transcendentals=0),
        name=name,
    )(side, *arrays, bands, *hbm(*weights, other), *([share] if final else []))
    return (result[:-1], result[-1]) if final else list(result) if split_out else result[0]


def raw_kernel(fresh, first, side_ref, *refs):
    own, peer, m_ref = refs[:GROUPS], refs[GROUPS : 2 * GROUPS], refs[2 * GROUPS]
    raw_ref, quotient_ref, mass_ref, quotient, sems = refs[-5:]
    tile = raw_ref.shape[0]
    at = pl.program_id(0)
    slot = lax.rem(at, 2)

    def copy(step, slot):
        row = pl.multiple_of(pick(first, side_ref[0]) + step * tile, tile)
        return pltpu.make_async_copy(quotient.at[slot], area(quotient_ref, row, tile, slice(None)), sems.at[slot])

    @pl.when(at >= 2)
    def _():
        copy(at - 2, slot).wait()

    mass = 0.0
    for g in range(GROUPS):
        raw = jnp.exp(own[g][...] + peer[g][...])
        step = raw.shape[1]
        raw_ref[:, g * step : (g + 1) * step] = raw
        mass += jnp.sum(raw)
        quotient[slot, :, g * step : (g + 1) * step] = raw / m_ref[:, g * step : (g + 1) * step]
    before = 0.0 if fresh else refs[2 * GROUPS + 3][0]
    mass_ref[0] = mass + jnp.where(at == 0, before, mass_ref[0])
    copy(at, slot).start()

    @pl.when(at == pl.num_programs(0) - 1)
    def _():
        copy(at - 1, 1 - slot).wait()
        copy(at, slot).wait()


def raw_rows(name, side, row, t, peers, m, rows_here, so_far):
    fresh = so_far is None
    rows, columns = m.shape
    tile = 32
    starts = [r // tile for r in row]
    part = pl.BlockSpec((tile, columns), lambda i, at: (i, 0))
    group = pl.BlockSpec((tile, columns // GROUPS), lambda i, at: (i, 0))
    return pl.pallas_call(
        functools.partial(raw_kernel, fresh, row),
        grid_spec=pltpu.PrefetchScalarGridSpec(
            num_scalar_prefetch=1,
            grid=(rows // tile,),
            in_specs=[group] * (2 * GROUPS) + [part] + ([] if fresh else [ANY, ANY, INSMEM]),
            out_specs=(
                pl.BlockSpec((tile, columns), lambda i, at: (jnp.where(at[0] == 0, *starts) + i, 0)),
                ANY,
                INSMEM,
            ),
            scratch_shapes=[pltpu.VMEM((2, tile, columns), F32), pltpu.SemaphoreType.DMA((2,))],
        ),
        out_shape=(
            pltpu.VMEM((rows_here, columns), F32),
            pltpu.VMEM((rows_here, 1, columns), F32),
            jax.ShapeDtypeStruct((1,), F32),
        ),
        input_output_aliases={} if fresh else {2 * GROUPS + 2: 0, 2 * GROUPS + 3: 1},
        compiler_params=params(16),
        cost_estimate=pl.CostEstimate(flops=m.size // 16, bytes_accessed=m.size // 4, transcendentals=0),
        name=name,
    )(side, *t, *peers, m, *([] if fresh else vmem(*so_far[:2]) + [so_far[2]]))


def raw_only_kernel(side_ref, *refs):
    own, peer, before_ref, raw_ref, mass_ref = refs[:GROUPS], refs[GROUPS : 2 * GROUPS], *refs[-3:]
    mass = 0.0
    for g in range(GROUPS):
        raw = jnp.exp(own[g][...] + peer[g][...])
        step = raw.shape[1]
        raw_ref[:, g * step : (g + 1) * step] = raw
        mass += jnp.sum(raw)
    mass_ref[0] = mass + jnp.where(pl.program_id(0) == 0, before_ref[0], mass_ref[0])


def raw_only(name, side, row, t, peers, raw_all, mass):
    rows, columns = t[0].shape[0], raw_all.shape[1]
    tile = 64
    starts = [r // tile for r in row]
    group = pl.BlockSpec((tile, columns // GROUPS), lambda i, at: (i, 0))
    return pl.pallas_call(
        raw_only_kernel,
        grid_spec=pltpu.PrefetchScalarGridSpec(
            num_scalar_prefetch=1,
            grid=(rows // tile,),
            in_specs=[group] * (2 * GROUPS) + [ANY, INSMEM],
            out_specs=(pl.BlockSpec((tile, columns), lambda i, at: (jnp.where(at[0] == 0, *starts) + i, 0)), INSMEM),
        ),
        out_shape=(pltpu.VMEM(raw_all.shape, F32), jax.ShapeDtypeStruct((1,), F32)),
        input_output_aliases={2 * GROUPS + 1: 0},
        compiler_params=params(16),
        cost_estimate=pl.CostEstimate(flops=rows * columns // 16, bytes_accessed=rows * columns // 4, transcendentals=0),
        name=name,
    )(side, *t, *peers, *vmem(raw_all), mass)


def quotient_kernel(first, side_ref, raw_ref, m_ref, _, quotient_ref, quotient, sems):
    tile = raw_ref.shape[0]
    at = pl.program_id(0)
    row = pl.multiple_of(pick(first, side_ref[0]) + at * tile, tile)
    quotient[at] = raw_ref[...] / m_ref[...]
    copies = [
        pltpu.make_async_copy(quotient.at[k], area(quotient_ref, row + (k - at) * tile, tile, slice(None)), sems.at[k])
        for k in range(quotient.shape[0])
    ]
    for k, copy in enumerate(copies):
        pl.when(at == k)(copy.start)

    @pl.when(at == len(copies) - 1)
    def _():
        for copy in copies:
            copy.wait()


def quotient_rows(name, side, row, raw_all, m, quotient_all):
    rows, columns = m.shape
    tile = 64
    starts = [r // tile for r in row]
    return pl.pallas_call(
        functools.partial(quotient_kernel, row),
        grid_spec=pltpu.PrefetchScalarGridSpec(
            num_scalar_prefetch=1,
            grid=(rows // tile,),
            in_specs=[
                pl.BlockSpec((tile, columns), lambda i, at: (jnp.where(at[0] == 0, *starts) + i, 0)),
                pl.BlockSpec((tile, columns), lambda i, at: (i, 0)),
                ANY,
            ],
            out_specs=ANY,
            scratch_shapes=[
                pltpu.VMEM((rows // tile, tile, columns), F32),
                pltpu.SemaphoreType.DMA((rows // tile,)),
            ],
        ),
        out_shape=pltpu.VMEM(quotient_all.shape, F32),
        input_output_aliases={3: 0},
        compiler_params=params(16),
        cost_estimate=pl.CostEstimate(flops=rows * columns // 16, bytes_accessed=rows * columns // 4, transcendentals=0),
        name=name,
    )(side, *vmem(raw_all), *hbm(m), *vmem(quotient_all))


def sum_kernel(a_ref, b_ref, out_ref):
    out_ref[0] = a_ref[0] + b_ref[0]


def mass_parts(mass):
    count = lax.axis_size("space")
    if count & (count - 1):
        return [lax.psum(mass, "space")]
    across = lambda part, distance: lax.ppermute(part, "space", [(i, i ^ distance) for i in range(count)])
    far = count
    while far > 8:
        far //= 2
        mass = pl.pallas_call(
            sum_kernel,
            in_specs=[INSMEM, INSMEM],
            out_specs=INSMEM,
            out_shape=jax.ShapeDtypeStruct((1,), F32),
            compiler_params=params(1),
            name="mass",
        )(mass, across(mass, far))
    return [mass] + [across(mass, distance) for distance in range(1, far)]


def output_kernel(total, raw_ref, quotient_ref, *refs):
    *masses, barycenter_ref, scaling_ref = refs
    mass = masses[0][0]
    for part in masses[1:]:
        mass += part[0]
    scale = jnp.full((1, raw_ref.shape[1]), total, F32) / jnp.full((1, raw_ref.shape[1]), mass, F32)
    barycenter_ref[...] = raw_ref[...] * scale
    scaling_ref[...] = quotient_ref[...] * scale[:, : quotient_ref.shape[2]].reshape(1, 1, quotient_ref.shape[2])


def outputs(raw, quotient, masses):
    rows, columns = raw.shape
    tile = 64
    flat = pl.BlockSpec((tile, columns), lambda i: (i, 0))
    deep = pl.BlockSpec((tile,) + quotient.shape[1:], lambda i: (i, 0, 0))
    return pl.pallas_call(
        functools.partial(output_kernel, float(columns * columns)),
        grid=(rows // tile,),
        in_specs=[flat, deep] + [INSMEM] * len(masses),
        out_specs=(flat, deep),
        out_shape=(jax.ShapeDtypeStruct(raw.shape, F32), jax.ShapeDtypeStruct(quotient.shape, F32)),
        compiler_params=params(16),
        name="outputs",
    )(*vmem(raw, quotient), *masses)


def local(densities, scaling, weights, band):
    rows_here, maps_here, cols_all = densities.shape
    _, _, width, _ = band.shape
    nlocal = rows_here // width
    inner = max(nlocal - 2, 0)
    place = lax.axis_index("space")
    count = lax.axis_size("space")
    assert maps_here == 1 and lax.axis_size("member") == 2 and count % 2 == 0

    odd = place & 1
    middle = place >> 1
    side = jnp.stack([odd, jnp.where(odd == 1, middle, 3 - middle), jnp.where(odd == 1, 2 - middle, middle - 1)])
    spread = count == 8 and nlocal > 1
    last = rows_here - width
    cross_row, near_row = (0, last), (last, 0)
    both = lambda pairs: pairs + [(b, a) for a, b in pairs]
    cross = functools.partial(
        lax.ppermute, axis_name="space", perm=both([(i, i + 1) for i in range(1, count - 1, 2)])
    )
    near = functools.partial(lax.ppermute, axis_name="space", perm=both([(i, i + 1) for i in range(0, count, 2)]))
    swap = functools.partial(lax.ppermute, axis_name="member", perm=[(0, 1), (1, 0)])

    def choose(choice):
        return jnp.where(odd == 0, *[c // width for c in choice]).astype(jnp.int32)

    whole_rows = [(0, cols_all)]
    near_edge = cut("cut_near", side, scaling, near_row, width, whole_rows)
    if spread:
        edge = cut("cut_cross", side, scaling, cross_row, width, cross_parts(cols_all))
        cross1, near_edge = cross_send(edge, near_edge)
    else:
        cross1 = [cross(cut("cut_cross", side, scaling, cross_row, width, whole_rows)[0])]
    near1 = near(near_edge[0])

    shares = weights / jnp.sum(weights)
    share = lax.dynamic_slice_in_dim(shares, lax.axis_index("member"), 1)
    wts = row_weights(band)
    mine = place * nlocal
    band_at = lambda block, blocks: lax.dynamic_slice_in_dim(band, mine + block, blocks, 0)

    if inner > 0:
        inner_bands = band_at(1, inner)
        ratio_inner = blur(
            "ratio_inner", side, hbm(scaling), [(0, 0, rows_here, 0)], inner_bands, wts, densities, width
        )
        *cross1, ratio_inner = lax.optimization_barrier((*cross1, ratio_inner))
    if nlocal == 1:
        pieces = [(0, 0, width, width), (1, 0, width, (0, 2 * width)), (2, 0, width, (2 * width, 0))]
        bands = band_at(0, 1)
        ratio = blur("ratio_only", side, [scaling, *cross1, near1], pieces, bands, wts, densities, 0)
        cross2, near2 = cross(ratio), near(ratio)
    else:
        two = rows_here - 2 * width
        halo = cross_received(1, cols_all) if spread else 1
        pieces = [(0, (0, two), 2 * width, (width, 0)), (halo, 0, width, (0, 2 * width))]
        bands = band_at(choose(cross_row), 1)
        ratio_cross = blur(
            "ratio_cross", side, hbm(scaling) + cross1, pieces, bands, wts, densities, cross_row,
            split_out=spread and SPREAD_BOTH,
        )
        ratio_cross, near1 = lax.optimization_barrier((ratio_cross, near1))
        if spread and SPREAD_BOTH:
            cross2, _ = cross_send(ratio_cross)
        else:
            cross2, ratio_cross = [cross(ratio_cross)], [ratio_cross]
        pieces = [(0, (two, 0), 2 * width, (0, width)), (1, 0, width, (2 * width, 0))]
        near_bands = band_at(choose(near_row), 1)
        ratio_near = blur("ratio_near", side, hbm(scaling) + [near1], pieces, near_bands, wts, densities, near_row)
        near2 = near(ratio_near)

    def finish(name, arrays, pieces, bands, row, share, state, pin=True):
        t, m = blur("logs_" + name, side, arrays, pieces, bands, wts, scaling, row, share, pin)
        keep = hbm if pin else lambda *a: list(a)
        if state is not None:
            raw, quotient, mass = state
            raw, mass = raw_only("raw_" + name, side, row, t, [swap(part) for part in t], raw, mass)
            return raw, quotient_rows("quotient_" + name, side, row, raw, m, quotient), mass
        return raw_rows(
            "raw_" + name, side, row, keep(*t), [swap(part) for part in t], *hbm(m), rows_here, state
        )

    if nlocal == 1:
        pieces = [(0, 0, width, width), (1, 0, width, (0, 2 * width)), (2, 0, width, (2 * width, 0))]
        state = finish("only", [ratio, cross2, near2], pieces, bands, (0, 0), share, None)
    else:
        most, end = rows_here - width, rows_here
        n = len(ratio_cross)
        own = cross_own(1, cols_all) if n == 4 else 1
        halo = cross_received(1 + n, cols_all) if n == 4 else 1 + n
        arrays = hbm(ratio_near, *ratio_cross) + cross2
        pieces = [(own, 0, width, (width, most)), (0, 0, width, (end, 0)), (halo, 0, width, (0, end))]
        beside, beside_row = ratio_cross[0], 0
        if inner > 0:
            pieces.append((len(arrays), 0, inner * width, (2 * width, width)))
            arrays += hbm(ratio_inner)
            beside, beside_row = ratio_inner, ((inner - 1) * width, 0)
        row = (0, width)
        bands = band_at(choose(row), nlocal - 1)
        state = finish("most", arrays, pieces, bands, row, share, None)
        share, state = lax.optimization_barrier((share, state))
        pieces = [(0, 0, width, width), (1, beside_row, width, (0, 2 * width)), (2, 0, width, (2 * width, 0))]
        state = finish("near", hbm(ratio_near, beside) + [near2], pieces, near_bands, near_row, share, state, False)

    raw, quotient, mass = state
    barycenter, new_scaling = outputs(raw, quotient.reshape(rows_here, cols_all // width, width), mass_parts(mass))
    return barycenter, new_scaling.reshape(rows_here, 1, cols_all)


def solution(mesh):
    return jax.shard_map(
        local,
        mesh=mesh,
        in_specs=(
            P("space", ("parts", "member"), None),
            P("space", ("parts", "member"), None),
            P("parts"),
            P(),
        ),
        out_specs=(P(("parts", "space"), None), P("space", ("parts", "member"), None)),
        check_vma=False,
    )
```

```python
import functools

import jax
import jax.numpy as jnp
from jax import lax
from jax.experimental import pallas as pl
from jax.experimental.pallas import tpu as pltpu
from jax.sharding import PartitionSpec as P

F32 = jnp.float32
BF16 = jnp.bfloat16
GROUPS = 4
ANY = pl.BlockSpec(memory_space=pl.ANY)
INVMEM = pl.BlockSpec(memory_space=pltpu.VMEM)
INSMEM = pl.BlockSpec(memory_space=pltpu.SMEM)


def split(x):
    high = x.astype(BF16)
    return high, (x - high.astype(F32)).astype(BF16)


def dot3(stack, b, dims):
    one = functools.partial(lax.dot_general, dimension_numbers=(dims, ((), ())), preferred_element_type=F32)
    rows = stack.shape[0] // 2
    both = one(stack, b[0])
    return both[:rows] + (one(stack[:rows], b[1]) + both[rows:])


def params(mebibytes):
    return pltpu.CompilerParams(vmem_limit_bytes=mebibytes * 1024 * 1024)


def hbm(*arrays):
    return [pltpu.with_memory_space_constraint(a, pltpu.HBM) for a in arrays]


def vmem(*arrays):
    return [pltpu.with_memory_space_constraint(a, pltpu.VMEM) for a in arrays]


def pick(choice, side):
    if isinstance(choice, tuple):
        return pl.multiple_of(jnp.where(side == 0, choice[0], choice[1]), 128)
    return choice


def cut_kernel(first, columns, side_ref, src, *refs):
    *outs, stage, sems = refs
    rows = stage.shape[0] // GROUPS
    start = pick(first, side_ref[0])
    outward = []
    inward = [
        pltpu.make_async_copy(src.at[pl.ds(start + g * rows, rows)], stage.at[pl.ds(g * rows, rows)], sems.at[0, g])
        for g in range(GROUPS)
    ]
    for copy in inward:
        copy.start()
    for g in range(GROUPS):
        inward[g].wait()
        part = pl.ds(g * rows, rows)
        for k, (out, column) in enumerate(zip(outs, columns)):
            at = pl.ds(column_of(column, side_ref), out.shape[2])
            outward.append(pltpu.make_async_copy(stage.at[part, :, at], out.at[part], sems.at[1 + k, g]))
            outward[-1].start()
    for copy in outward:
        copy.wait()


def cut(name, side, array, first, rows, parts):
    columns = array.shape[2]
    return pl.pallas_call(
        functools.partial(cut_kernel, first, [column for column, _ in parts]),
        in_specs=[INSMEM, ANY],
        out_specs=[ANY] * len(parts),
        out_shape=[pltpu.HBM((rows, 1, n), F32) for _, n in parts],
        scratch_shapes=[
            pltpu.VMEM((rows, 1, columns), F32),
            pltpu.SemaphoreType.DMA((1 + len(parts), GROUPS)),
        ],
        compiler_params=params(8),
        name=name,
    )(side, *hbm(array))


def column_of(column, side_ref):
    if isinstance(column, tuple):
        return pl.multiple_of(jnp.where(side_ref[1] == 1, column[0], column[1]), 128)
    return column


def cross_parts(columns):
    half, quarter = columns // 2, columns // 4
    return [(0, half), (half, quarter), ((half, 0), half), (3 * quarter, quarter)]


def cross_send(parts, behind=()):
    def send(part, numbers, ends):
        pairs = []
        for k in range(3):
            for direction, number in ((0, k), (1, 2 - k)):
                if number in numbers:
                    pairs.append(ends(k)[direction])
        return lax.ppermute(part, "space", pairs)

    to_partner = lambda k: ((2 * k + 1, 2 * k), (2 * k + 2, 2 * k + 3))
    onward = lambda k: ((2 * k, 2 * k + 2), (2 * k + 3, 2 * k + 1))
    direct = lambda k: ((2 * k + 1, 2 * k + 2), (2 * k + 2, 2 * k + 1))
    relayed = [send(part, numbers, to_partner) for part, numbers in zip(parts[:2], ((0, 1), (0, 2)))]
    straight = [send(part, numbers, direct) for part, numbers in zip(parts[2:], ((1, 2), (0, 2)))]
    a, b, c, d, *behind = lax.optimization_barrier((*relayed, *straight, *behind))
    relayed, straight = [a, b], [c, d]
    passed = [send(part, numbers, onward) for part, numbers in zip(relayed, ((0, 1), (0, 2)))]
    return passed + straight, behind


def cross_received(base, columns):
    a, b, c, d = range(base, base + 4)
    q = columns // 4
    return ((2, (c, 0), (a, 0)), (2, (c, q), (a, q)), (1, (c, 0), (b, 0)), (1, (c, q), (d, 0)))


def area(ref, row, rows, columns):
    return ref.at[pl.ds(row, rows), 0, columns] if len(ref.shape) == 3 else ref.at[pl.ds(row, rows), columns]


def weight_kernel(nblocks, band_ref, high_ref, low_ref):
    pair = pl.program_id(0)
    width = band_ref.shape[2]
    zero = jnp.zeros((width, width), F32)
    for o in range(2):
        for i in range(4):
            j = i - o
            value = band_ref[o, j] if 0 <= j <= 2 else zero
            if (o, j) == (0, 0):
                value = jnp.where(pair > 0, value, 0.0)
            if (o, j) == (1, 2):
                value = jnp.where(pair < nblocks // 2 - 1, value, 0.0)
            high, low = split(value)
            rows, columns = slice(o * width, (o + 1) * width), slice(i * width, (i + 1) * width)
            high_ref[0, rows, columns] = high
            low_ref[0, rows, columns] = low


def row_weights(band):
    nblocks, _, width, _ = band.shape
    shape = pltpu.HBM((nblocks // 2, 2 * width, 4 * width), BF16)
    out_spec = pl.BlockSpec((1, 2 * width, 4 * width), lambda t: (t, 0, 0))
    return pl.pallas_call(
        functools.partial(weight_kernel, nblocks),
        grid=(nblocks // 2,),
        in_specs=[pl.BlockSpec((2, 3, width, width), lambda t: (t, 0, 0, 0))],
        out_specs=(out_spec, out_spec),
        out_shape=(shape, shape),
        name="row_weights",
    )(*hbm(band))


def blur_kernel(plan, *refs):
    pieces, narrays, extra, final, split_out, units, groups = plan
    side_ref, refs = refs[0], refs[1:]
    arrays = refs[:narrays]
    band_ref, high_ref, low_ref, extra_ref = refs[narrays : narrays + 4]
    rest = refs[narrays + 4 :]
    if final:
        share_ref, rest = rest[0], rest[1:]
    nouts = len(groups) + 1 if final else 1 + len(split_out)
    outs = rest[:nouts]
    field, a_both, y_both, whigh, wlow, other = rest[nouts : nouts + 6]
    *results, in_sems, late_sems, out_sems = rest[nouts + 6 :]

    side = side_ref[0]
    nout, _, width, _ = band_ref.shape
    columns = field.shape[1]
    step = columns // GROUPS
    pairs = step // (2 * width)
    inside, late = [], {}

    def copy_in(u, k, place):
        _, row, rows, to = pieces[k]
        which, column = place
        start, stop = units[u]
        return pltpu.make_async_copy(
            area(arrays[which], pick(row, side), rows, pl.ds(column, stop - start)),
            field.at[pl.ds(pick(to, side), rows), pl.ds(start, stop - start)],
            in_sems.at[u, k],
        )

    def start_in(u, k):
        source = pieces[k][0]
        if isinstance(source, int):
            copy = copy_in(u, k, (source, units[u][0]))
        elif len(source[u]) == 2:
            copy = copy_in(u, k, source[u])
        else:
            number, this, other_one = source[u]
            pl.when(side_ref[2] == number)(copy_in(u, k, this).start)
            pl.when(side_ref[2] != number)(copy_in(u, k, other_one).start)
            return copy_in(u, k, other_one)
        copy.start()
        return copy

    for g in groups:
        at = pl.ds(g * step, step)
        some = pl.ds(g * pairs, pairs)
        late[g] = [
            pltpu.make_async_copy(high_ref.at[some], whigh.at[some], late_sems.at[g, 0]),
            pltpu.make_async_copy(low_ref.at[some], wlow.at[some], late_sems.at[g, 1]),
            pltpu.make_async_copy(
                area(extra_ref, pick(extra, side), other.shape[0], at), other.at[:, at], late_sems.at[g, 2]
            ),
        ]
    waiting = list(groups)
    for u in range(len(units)):
        inside.append([start_in(u, k) for k in range(len(pieces))])
        if u > 0 and waiting:
            for copy in late[waiting.pop(0)]:
                copy.start()
    for g in waiting:
        for copy in late[g]:
            copy.start()

    blocks = [(i, min(2, nout - i)) for i in range(0, nout, 2)]
    total = nout * width
    a_both[...] = jnp.zeros_like(a_both)
    for first, n in blocks:
        for i in range(n):
            for j in range(3):
                for part, value in enumerate(split(band_ref[first + i, j])):
                    row = (2 * first + part * n + i) * width
                    a_both[row : row + width, (i + j) * width : (i + j + 1) * width] = value
    y_both[:, :width] = jnp.zeros((2 * total, width), BF16)
    y_both[:, columns + width :] = jnp.zeros((2 * total, width), BF16)

    def columns_pass(u):
        for copy in inside[u]:
            copy.wait()
        for i in range(units[u][0] // (2 * width), units[u][1] // (2 * width)):
            at = slice(i * 2 * width, (i + 1) * 2 * width)
            to = slice((2 * i + 1) * width, (2 * i + 3) * width)
            for first, n in blocks:
                a = a_both[2 * first * width : 2 * (first + n) * width, : (n + 2) * width]
                y = dot3(a, split(field[first * width : (first + n + 2) * width, at]), ((1,), (0,)))
                for part, value in enumerate(split(y)):
                    row = part * total + first * width
                    y_both[row : row + n * width, to] = value

    def rows_pass(g):
        for copy in late[g]:
            copy.wait()
        for t in range(g * pairs, (g + 1) * pairs):
            source = slice(t * 2 * width, (t + 2) * 2 * width)
            at = slice(t * 2 * width, (t + 1) * 2 * width)
            value = dot3(y_both[:, source], (whigh[t], wlow[t]), ((1,), (1,)))
            if final:
                results[0][:, at] = value
                results[1][:, at] = share_ref[0] * jnp.log(other[:, at] * value)
            else:
                results[0][:, at] = other[:, at] / value
        at = pl.ds(g * step, step)
        targets = [outs[-1].at[:, pl.ds((g - groups[0]) * step, step)]] + ([outs[groups.index(g)]] if final else [])
        copies = [
            pltpu.make_async_copy(src.at[:, at], dst, out_sems.at[g, k])
            for k, (src, dst) in enumerate(zip(results, targets))
        ]
        for k, (start, stop) in enumerate(split_out):
            if g * step < stop <= (g + 1) * step:
                part = results[0].at[:, pl.ds(start, stop - start)]
                copies.append(pltpu.make_async_copy(part, outs[k], out_sems.at[GROUPS, k]))
        for copy in copies:
            copy.start()
        return copies

    going = []
    waiting = list(groups)
    for u, (_, stop) in enumerate(units):
        columns_pass(u)
        while waiting and u > 0 and (stop == columns or (waiting[0] + 1) * step + width <= stop):
            going += rows_pass(waiting.pop(0))
    for copy in going:
        copy.wait()


def blur(
    name, side, arrays, pieces, bands, weights, other, extra,
    share=None, pin=True, split_out=(), units=None, groups=tuple(range(GROUPS)),
):
    nout, _, width, _ = bands.shape
    npairs = weights[0].shape[0]
    columns = npairs * 2 * width
    rows, depth = nout * width, (nout + 2) * width
    final = share is not None
    nouts = 2 if final else 1
    kind = pltpu.HBM if pin else jax.ShapeDtypeStruct
    step = columns // GROUPS
    units = tuple((g * step, (g + 1) * step) for g in range(GROUPS)) if units is None else units
    shapes = [kind((rows, step), F32)] * (len(groups) if final else 0)
    shapes += [pltpu.HBM((rows, stop - start), F32) for start, stop in split_out]
    shapes.append(pltpu.HBM((rows, len(groups) * step), F32))
    plan = (tuple(pieces), len(arrays), extra, final, split_out, units, groups)
    work = 3 * 2 * rows * columns * (depth + 4 * width)
    moved = 4 * (depth + 3 * rows) * columns + npairs * 2 * 2 * 8 * width * width
    size = 4 * columns * (depth + (1 + nouts) * rows) + 4 * rows * columns + npairs * 2 * 2 * 8 * width * width
    result = pl.pallas_call(
        functools.partial(blur_kernel, plan),
        in_specs=[INSMEM] + [ANY] * len(arrays) + [INVMEM, ANY, ANY, ANY] + [INSMEM] * final,
        out_specs=[ANY] * len(shapes),
        out_shape=shapes,
        scratch_shapes=[
            pltpu.VMEM((depth, columns), F32),
            pltpu.VMEM((2 * rows, min(depth, 4 * width)), BF16),
            pltpu.VMEM((2 * rows, columns + 2 * width), BF16),
            pltpu.VMEM((npairs, 2 * width, 4 * width), BF16),
            pltpu.VMEM((npairs, 2 * width, 4 * width), BF16),
            pltpu.VMEM((rows, columns), F32),
        ]
        + [pltpu.VMEM((rows, columns), F32)] * nouts
        + [
            pltpu.SemaphoreType.DMA((len(units), len(pieces))),
            pltpu.SemaphoreType.DMA((GROUPS, 3)),
            pltpu.SemaphoreType.DMA((GROUPS + 1, 2)),
        ],
        compiler_params=params(size // 2**20 + 6),
        cost_estimate=pl.CostEstimate(flops=work // 64, bytes_accessed=moved // 64, transcendentals=0),
        name=name,
    )(side, *arrays, bands, *hbm(*weights, other), *([share] if final else []))
    return (result[:-1], result[-1]) if final else result if split_out else result[0]


def raw_kernel(fresh, first, side_ref, *refs):
    own, peer, m_ref = refs[:GROUPS], refs[GROUPS : 2 * GROUPS], refs[2 * GROUPS]
    raw_ref, quotient_ref, mass_ref, quotient, sems = refs[-5:]
    tile = raw_ref.shape[0]
    at = pl.program_id(0)
    slot = lax.rem(at, 2)

    def copy(step, slot):
        row = pl.multiple_of(pick(first, side_ref[0]) + step * tile, tile)
        return pltpu.make_async_copy(quotient.at[slot], area(quotient_ref, row, tile, slice(None)), sems.at[slot])

    @pl.when(at >= 2)
    def _():
        copy(at - 2, slot).wait()

    mass = 0.0
    for g in range(GROUPS):
        raw = jnp.exp(own[g][...] + peer[g][...])
        step = raw.shape[1]
        raw_ref[:, g * step : (g + 1) * step] = raw
        mass += jnp.sum(raw)
        quotient[slot, :, g * step : (g + 1) * step] = raw / m_ref[:, g * step : (g + 1) * step]
    before = 0.0 if fresh else refs[2 * GROUPS + 3][...]
    mass_ref[...] = mass + jnp.where(at == 0, before, mass_ref[...])
    copy(at, slot).start()

    @pl.when(at == pl.num_programs(0) - 1)
    def _():
        copy(at - 1, 1 - slot).wait()
        copy(at, slot).wait()


def raw_rows(name, side, row, t, peers, m, rows_here, so_far):
    fresh = so_far is None
    rows, columns = m.shape
    tile = 32
    starts = [r // tile for r in row]
    part = pl.BlockSpec((tile, columns), lambda i, at: (i, 0))
    group = pl.BlockSpec((tile, columns // GROUPS), lambda i, at: (i, 0))
    return pl.pallas_call(
        functools.partial(raw_kernel, fresh, row),
        grid_spec=pltpu.PrefetchScalarGridSpec(
            num_scalar_prefetch=1,
            grid=(rows // tile,),
            in_specs=[group] * (2 * GROUPS) + [part] + ([] if fresh else [ANY, ANY, INVMEM]),
            out_specs=(
                pl.BlockSpec((tile, columns), lambda i, at: (jnp.where(at[0] == 0, *starts) + i, 0)),
                ANY,
                INVMEM,
            ),
            scratch_shapes=[pltpu.VMEM((2, tile, columns), F32), pltpu.SemaphoreType.DMA((2,))],
        ),
        out_shape=(
            pltpu.VMEM((rows_here, columns), F32),
            pltpu.VMEM((rows_here, 1, columns), F32),
            jax.ShapeDtypeStruct((1, 128), F32),
        ),
        input_output_aliases={} if fresh else {2 * GROUPS + 2: 0, 2 * GROUPS + 3: 1},
        compiler_params=params(16),
        cost_estimate=pl.CostEstimate(flops=m.size // 16, bytes_accessed=m.size // 4, transcendentals=0),
        name=name,
    )(side, *t, *peers, m, *([] if fresh else vmem(*so_far[:2]) + [so_far[2]]))


def raw_only_kernel(side_ref, *refs):
    *logs, _, before_ref, raw_ref, mass_ref = refs
    parts = len(logs) // 2
    mass = 0.0
    for g in range(parts):
        raw = jnp.exp(logs[g][...] + logs[parts + g][...])
        step = raw.shape[1]
        raw_ref[:, g * step : (g + 1) * step] = raw
        mass += jnp.sum(raw)
    mass_ref[...] = mass + jnp.where(pl.program_id(0) == 0, before_ref[...], mass_ref[...])


def piece_spec(tile, columns, row, column):
    starts = [r // tile for r in row]
    return pl.BlockSpec((tile, columns), lambda i, at: (jnp.where(at[0] == 0, *starts) + i, column // columns))


def raw_only(name, side, row, column, t, peers, raw_all, mass):
    rows, step = t[0].shape
    columns = len(t) * step
    tile = 64
    group = pl.BlockSpec((tile, step), lambda i, at: (i, 0))
    return pl.pallas_call(
        raw_only_kernel,
        grid_spec=pltpu.PrefetchScalarGridSpec(
            num_scalar_prefetch=1,
            grid=(rows // tile,),
            in_specs=[group] * (2 * len(t)) + [ANY, INVMEM],
            out_specs=(piece_spec(tile, columns, row, column), INVMEM),
        ),
        out_shape=(pltpu.VMEM(raw_all.shape, F32), jax.ShapeDtypeStruct(mass.shape, F32)),
        input_output_aliases={2 * len(t) + 1: 0},
        compiler_params=params(16),
        cost_estimate=pl.CostEstimate(flops=rows * columns // 16, bytes_accessed=rows * columns // 4, transcendentals=0),
        name=name,
    )(side, *t, *peers, *vmem(raw_all), mass)


def quotient_kernel(first, column, side_ref, raw_ref, m_ref, _, quotient_ref, quotient, sems):
    tile, columns = raw_ref.shape
    at = pl.program_id(0)
    row = pick(first, side_ref[0])
    quotient[at] = raw_ref[...] / m_ref[...]
    copies = [
        pltpu.make_async_copy(
            quotient.at[k], area(quotient_ref, row + k * tile, tile, pl.ds(column, columns)), sems.at[k]
        )
        for k in range(quotient.shape[0])
    ]
    for k, copy in enumerate(copies):
        pl.when(at == k)(copy.start)

    @pl.when(at == len(copies) - 1)
    def _():
        for copy in copies:
            copy.wait()


def quotient_part(name, side, row, column, raw_all, m, quotient_all):
    rows, columns = m.shape
    tile = 64
    return pl.pallas_call(
        functools.partial(quotient_kernel, row, column),
        grid_spec=pltpu.PrefetchScalarGridSpec(
            num_scalar_prefetch=1,
            grid=(rows // tile,),
            in_specs=[
                piece_spec(tile, columns, row, column),
                pl.BlockSpec((tile, columns), lambda i, at: (i, 0)),
                ANY,
            ],
            out_specs=ANY,
            scratch_shapes=[
                pltpu.VMEM((rows // tile, tile, columns), F32),
                pltpu.SemaphoreType.DMA((rows // tile,)),
            ],
        ),
        out_shape=pltpu.VMEM(quotient_all.shape, F32),
        input_output_aliases={3: 0},
        compiler_params=params(16),
        cost_estimate=pl.CostEstimate(flops=rows * columns // 16, bytes_accessed=rows * columns // 4, transcendentals=0),
        name=name,
    )(side, *vmem(raw_all), *hbm(m), *vmem(quotient_all))


def sum_kernel(a_ref, b_ref, out_ref):
    out_ref[...] = a_ref[...] + b_ref[...]


def mass_parts(mass):
    count = lax.axis_size("space")
    if count & (count - 1):
        return [lax.psum(mass, "space")]
    parts = [mass]
    for bit in range(count.bit_length() - 1):
        if len(parts) == 2:
            parts = [
                pl.pallas_call(
                    sum_kernel,
                    in_specs=[INVMEM, INVMEM],
                    out_specs=INVMEM,
                    out_shape=jax.ShapeDtypeStruct(mass.shape, F32),
                    compiler_params=params(1),
                    name="mass",
                )(*parts)
            ]
        parts.append(lax.ppermute(parts[0], "space", [(i, i ^ (1 << bit)) for i in range(count)]))
    return parts


def output_kernel(total, raw_ref, quotient_ref, *refs):
    *masses, barycenter_ref, scaling_ref = refs
    mass = masses[0][...]
    for part in masses[1:]:
        mass += part[...]
    scale = total / mass
    width = scale.shape[1]
    for b in range(raw_ref.shape[1] // width):
        at = slice(b * width, (b + 1) * width)
        barycenter_ref[:, at] = raw_ref[:, at] * scale
    scaling_ref[...] = quotient_ref[...] * scale.reshape(1, 1, width)


def outputs(raw, quotient, masses):
    rows, columns = raw.shape
    tile = 64
    flat = pl.BlockSpec((tile, columns), lambda i: (i, 0))
    deep = pl.BlockSpec((tile,) + quotient.shape[1:], lambda i: (i, 0, 0))
    return pl.pallas_call(
        functools.partial(output_kernel, float(columns * columns)),
        grid=(rows // tile,),
        in_specs=[flat, deep] + [INVMEM] * len(masses),
        out_specs=(flat, deep),
        out_shape=(jax.ShapeDtypeStruct(raw.shape, F32), jax.ShapeDtypeStruct(quotient.shape, F32)),
        compiler_params=params(16),
        name="outputs",
    )(*vmem(raw, quotient), *masses)


def local(densities, scaling, weights, band):
    rows_here, maps_here, cols_all = densities.shape
    _, _, width, _ = band.shape
    nlocal = rows_here // width
    inner = max(nlocal - 2, 0)
    place = lax.axis_index("space")
    count = lax.axis_size("space")
    assert maps_here == 1 and lax.axis_size("member") == 2 and count % 2 == 0

    odd = place & 1
    middle = place >> 1
    side = jnp.stack([odd, jnp.where(odd == 1, middle, 3 - middle), jnp.where(odd == 1, 2 - middle, middle - 1)])
    spread = count == 8 and nlocal > 1
    last = rows_here - width
    cross_row, near_row = (0, last), (last, 0)
    both = lambda pairs: pairs + [(b, a) for a, b in pairs]
    cross = functools.partial(
        lax.ppermute, axis_name="space", perm=both([(i, i + 1) for i in range(1, count - 1, 2)])
    )
    near = functools.partial(lax.ppermute, axis_name="space", perm=both([(i, i + 1) for i in range(0, count, 2)]))
    swap = functools.partial(lax.ppermute, axis_name="member", perm=[(0, 1), (1, 0)])

    def choose(choice):
        return jnp.where(odd == 0, *[c // width for c in choice]).astype(jnp.int32)

    whole_rows = [(0, cols_all)]
    near_edge = cut("cut_near", side, scaling, near_row, width, whole_rows)
    if spread:
        edge = cut("cut_cross", side, scaling, cross_row, width, cross_parts(cols_all))
        cross1, near_edge = cross_send(edge, near_edge)
    else:
        cross1 = [cross(cut("cut_cross", side, scaling, cross_row, width, whole_rows)[0])]
    near1 = near(near_edge[0])

    shares = weights / jnp.sum(weights)
    share = lax.dynamic_slice_in_dim(shares, lax.axis_index("member"), 1)
    wts = row_weights(band)
    mine = place * nlocal
    band_at = lambda block, blocks: lax.dynamic_slice_in_dim(band, mine + block, blocks, 0)

    if inner > 0:
        inner_bands = band_at(1, inner)
        ratio_inner = blur(
            "ratio_inner", side, hbm(scaling), [(0, 0, rows_here, 0)], inner_bands, wts, densities, width
        )
        *cross1, ratio_inner = lax.optimization_barrier((*cross1, ratio_inner))
    if nlocal == 1:
        pieces = [(0, 0, width, width), (1, 0, width, (0, 2 * width)), (2, 0, width, (2 * width, 0))]
        bands = band_at(0, 1)
        ratio = blur("ratio_only", side, [scaling, *cross1, near1], pieces, bands, wts, densities, 0)
        cross2, near2 = cross(ratio), near(ratio)
    else:
        two = rows_here - 2 * width
        halo = cross_received(1, cols_all) if spread else 1
        pieces = [(0, (0, two), 2 * width, (width, 0)), (halo, 0, width, (0, 2 * width))]
        cross_bands = band_at(choose(cross_row), 1)
        ratio_cross = blur(
            "ratio_cross", side, hbm(scaling) + cross1, pieces, cross_bands, wts, densities, cross_row
        )
        ratio_cross, near1 = lax.optimization_barrier((ratio_cross, near1))
        cross2 = cross(ratio_cross)
        half, more = cols_all // 2, 2 * width
        pieces = [(0, (two, 0), 2 * width, (0, width)), (1, 0, width, (2 * width, 0))]
        near_bands = band_at(choose(near_row), 1)
        *parts, ratio_near = blur(
            "ratio_near", side, hbm(scaling) + [near1], pieces, near_bands, wts, densities, near_row,
            split_out=((0, half + more), (half + more, cols_all)),
        )
        near2 = [near(part) for part in parts]

    def finish(name, arrays, pieces, bands, row, share, state):
        t, m = blur("logs_" + name, side, arrays, pieces, bands, wts, scaling, row, share)
        return raw_rows(
            "raw_" + name, side, row, hbm(*t), [swap(part) for part in t], *hbm(m), rows_here, state
        )

    if nlocal == 1:
        pieces = [(0, 0, width, width), (1, 0, width, (0, 2 * width)), (2, 0, width, (2 * width, 0))]
        state = finish("only", [ratio, cross2, near2], pieces, bands, (0, 0), share, None)
    else:
        state = None
        beside, beside_row = ratio_near, (0, 0)
        if inner > 0:
            arrays = hbm(ratio_inner, ratio_cross, ratio_near)
            pieces = [(0, 0, inner * width, width), (1, 0, width, cross_row), (2, 0, width, near_row)]
            state = finish("inner", arrays, pieces, inner_bands, (width, width), share, None)
            share, state = lax.optimization_barrier((share, state))
            beside, beside_row = ratio_inner, (0, (inner - 1) * width)
        arrays = hbm(ratio_cross, beside) + [cross2]
        pieces = [(0, 0, width, width), (1, beside_row, width, (2 * width, 0)), (2, 0, width, (0, 2 * width))]
        state = finish("cross", arrays, pieces, cross_bands, cross_row, share, state)
        share, state = lax.optimization_barrier((share, state))
        if inner == 0:
            beside = ratio_cross
        raw, quotient, mass = state
        step = cols_all // GROUPS
        first_units = tuple((g * step, (g + 1) * step) for g in range(GROUPS // 2)) + ((half, half + more),)
        later_units = ((half - more, half + more), (half + more, half + step)) + tuple(
            (g * step, (g + 1) * step) for g in range(GROUPS // 2 + 1, GROUPS)
        )
        plans = [
            ("near_first", first_units, 0, [(2, start) for start, _ in first_units]),
            ("near_later", later_units, half, [(2, half - more)] + [(3, a - half - more) for a, _ in later_units[1:]]),
        ]
        for part, (name, units, column, halo) in enumerate(plans):
            arrays = hbm(ratio_near, beside) + near2[: part + 1]
            pieces = [
                (0, 0, width, width),
                (1, beside_row[::-1], width, (0, 2 * width)),
                (tuple(halo), 0, width, (2 * width, 0)),
            ]
            groups = tuple(g for g in range(GROUPS) if column <= g * step < column + half)
            t, m = blur(
                "logs_" + name, side, arrays, pieces, near_bands, wts, scaling, near_row, share,
                pin=False, units=units, groups=groups,
            )
            raw, mass = raw_only("raw_" + name, side, near_row, column, t, [swap(part) for part in t], raw, mass)
            quotient = quotient_part("quotient_" + name, side, near_row, column, raw, m, quotient)
            if part == 0:
                share, raw, mass, quotient = lax.optimization_barrier((share, raw, mass, quotient))
        state = raw, quotient, mass

    raw, quotient, mass = state
    barycenter, new_scaling = outputs(raw, quotient.reshape(rows_here, cols_all // width, width), mass_parts(mass))
    return barycenter, new_scaling.reshape(rows_here, 1, cols_all)


def solution(mesh):
    return jax.shard_map(
        local,
        mesh=mesh,
        in_specs=(
            P("space", ("parts", "member"), None),
            P("space", ("parts", "member"), None),
            P("parts"),
            P(),
        ),
        out_specs=(P(("parts", "space"), None), P("space", ("parts", "member"), None)),
        check_vma=False,
    )
```

```python
import functools

import jax
import jax.numpy as jnp
from jax import lax
from jax.experimental import pallas as pl
from jax.experimental.pallas import tpu as pltpu
from jax.sharding import PartitionSpec as P

F32 = jnp.float32
BF16 = jnp.bfloat16
GROUPS = 4
ANY = pl.BlockSpec(memory_space=pl.ANY)
INVMEM = pl.BlockSpec(memory_space=pltpu.VMEM)
INSMEM = pl.BlockSpec(memory_space=pltpu.SMEM)


def split(x):
    high = x.astype(BF16)
    return high, (x - high.astype(F32)).astype(BF16)


def dot3(stack, b, dims):
    one = functools.partial(lax.dot_general, dimension_numbers=(dims, ((), ())), preferred_element_type=F32)
    rows = stack.shape[0] // 2
    both = one(stack, b[0])
    return both[:rows] + (one(stack[:rows], b[1]) + both[rows:])


def params(mebibytes):
    return pltpu.CompilerParams(vmem_limit_bytes=mebibytes * 1024 * 1024)


def hbm(*arrays):
    return [pltpu.with_memory_space_constraint(a, pltpu.HBM) for a in arrays]


def vmem(*arrays):
    return [pltpu.with_memory_space_constraint(a, pltpu.VMEM) for a in arrays]


def pick(choice, side):
    if isinstance(choice, tuple):
        return pl.multiple_of(jnp.where(side == 0, choice[0], choice[1]), 128)
    return choice


def cut_kernel(first, columns, side_ref, src, *refs):
    *outs, stage, sems = refs
    rows = stage.shape[0] // GROUPS
    start = pick(first, side_ref[0])
    outward = []
    inward = [
        pltpu.make_async_copy(src.at[pl.ds(start + g * rows, rows)], stage.at[pl.ds(g * rows, rows)], sems.at[0, g])
        for g in range(GROUPS)
    ]
    for copy in inward:
        copy.start()
    for g in range(GROUPS):
        inward[g].wait()
        part = pl.ds(g * rows, rows)
        for k, (out, column) in enumerate(zip(outs, columns)):
            at = pl.ds(column_of(column, side_ref), out.shape[2])
            outward.append(pltpu.make_async_copy(stage.at[part, :, at], out.at[part], sems.at[1 + k, g]))
            outward[-1].start()
    for copy in outward:
        copy.wait()


def cut(name, side, array, first, rows, parts):
    columns = array.shape[2]
    return pl.pallas_call(
        functools.partial(cut_kernel, first, [column for column, _ in parts]),
        in_specs=[INSMEM, ANY],
        out_specs=[ANY] * len(parts),
        out_shape=[pltpu.HBM((rows, 1, n), F32) for _, n in parts],
        scratch_shapes=[
            pltpu.VMEM((rows, 1, columns), F32),
            pltpu.SemaphoreType.DMA((1 + len(parts), GROUPS)),
        ],
        compiler_params=params(8),
        name=name,
    )(side, *hbm(array))


def column_of(column, side_ref):
    if isinstance(column, tuple):
        return pl.multiple_of(jnp.where(side_ref[1] == 1, column[0], column[1]), 128)
    return column


def cross_parts(columns):
    half, quarter = columns // 2, columns // 4
    return [(0, half), (half, quarter), ((half, 0), half), (3 * quarter, quarter)]


def cross_send(parts, behind=()):
    def send(part, numbers, ends):
        pairs = []
        for k in range(3):
            for direction, number in ((0, k), (1, 2 - k)):
                if number in numbers:
                    pairs.append(ends(k)[direction])
        return lax.ppermute(part, "space", pairs)

    to_partner = lambda k: ((2 * k + 1, 2 * k), (2 * k + 2, 2 * k + 3))
    onward = lambda k: ((2 * k, 2 * k + 2), (2 * k + 3, 2 * k + 1))
    direct = lambda k: ((2 * k + 1, 2 * k + 2), (2 * k + 2, 2 * k + 1))
    relayed = [send(part, numbers, to_partner) for part, numbers in zip(parts[:2], ((0, 1), (0, 2)))]
    straight = [send(part, numbers, direct) for part, numbers in zip(parts[2:], ((1, 2), (0, 2)))]
    a, b, c, d, *behind = lax.optimization_barrier((*relayed, *straight, *behind))
    relayed, straight = [a, b], [c, d]
    passed = [send(part, numbers, onward) for part, numbers in zip(relayed, ((0, 1), (0, 2)))]
    return passed + straight, behind


def cross_received(base, columns):
    a, b, c, d = range(base, base + 4)
    q = columns // 4
    return ((2, (c, 0), (a, 0)), (2, (c, q), (a, q)), (1, (c, 0), (b, 0)), (1, (c, q), (d, 0)))


def area(ref, row, rows, columns):
    return ref.at[pl.ds(row, rows), 0, columns] if len(ref.shape) == 3 else ref.at[pl.ds(row, rows), columns]


def weight_kernel(nblocks, band_ref, high_ref, low_ref):
    pair = pl.program_id(0)
    width = band_ref.shape[2]
    zero = jnp.zeros((width, width), F32)
    for o in range(2):
        for i in range(4):
            j = i - o
            value = band_ref[o, j] if 0 <= j <= 2 else zero
            if (o, j) == (0, 0):
                value = jnp.where(pair > 0, value, 0.0)
            if (o, j) == (1, 2):
                value = jnp.where(pair < nblocks // 2 - 1, value, 0.0)
            high, low = split(value)
            rows, columns = slice(o * width, (o + 1) * width), slice(i * width, (i + 1) * width)
            high_ref[0, rows, columns] = high
            low_ref[0, rows, columns] = low


def row_weights(band):
    nblocks, _, width, _ = band.shape
    shape = pltpu.HBM((nblocks // 2, 2 * width, 4 * width), BF16)
    out_spec = pl.BlockSpec((1, 2 * width, 4 * width), lambda t: (t, 0, 0))
    return pl.pallas_call(
        functools.partial(weight_kernel, nblocks),
        grid=(nblocks // 2,),
        in_specs=[pl.BlockSpec((2, 3, width, width), lambda t: (t, 0, 0, 0))],
        out_specs=(out_spec, out_spec),
        out_shape=(shape, shape),
        name="row_weights",
    )(*hbm(band))


def blur_kernel(plan, *refs):
    pieces, narrays, extra, final, split_out, units, groups = plan
    side_ref, refs = refs[0], refs[1:]
    arrays = refs[:narrays]
    band_ref, high_ref, low_ref, extra_ref = refs[narrays : narrays + 4]
    rest = refs[narrays + 4 :]
    if final:
        weights_ref, rest = rest[0], rest[1:]
        all_weights = weights_ref[0]
        for k in range(1, weights_ref.shape[0]):
            all_weights += weights_ref[k]
        row_shape = (1, 2 * band_ref.shape[2])
        share = jnp.full(row_shape, weights_ref[side_ref[3]]) / jnp.full(row_shape, all_weights)
    nouts = len(groups) + 1 if final else 1 + len(split_out)
    outs = rest[:nouts]
    field, a_both, y_both, whigh, wlow, other = rest[nouts : nouts + 6]
    *results, in_sems, late_sems, out_sems = rest[nouts + 6 :]

    side = side_ref[0]
    nout, _, width, _ = band_ref.shape
    columns = field.shape[1]
    step = columns // GROUPS
    pairs = step // (2 * width)
    inside, late = [], {}

    def copy_in(u, k, place):
        _, row, rows, to = pieces[k]
        which, column = place
        start, stop = units[u]
        return pltpu.make_async_copy(
            area(arrays[which], pick(row, side), rows, pl.ds(column, stop - start)),
            field.at[pl.ds(pick(to, side), rows), pl.ds(start, stop - start)],
            in_sems.at[u, k],
        )

    def start_in(u, k):
        source = pieces[k][0]
        if isinstance(source, int):
            copy = copy_in(u, k, (source, units[u][0]))
        elif len(source[u]) == 2:
            copy = copy_in(u, k, source[u])
        else:
            number, this, other_one = source[u]
            pl.when(side_ref[2] == number)(copy_in(u, k, this).start)
            pl.when(side_ref[2] != number)(copy_in(u, k, other_one).start)
            return copy_in(u, k, other_one)
        copy.start()
        return copy

    for g in groups:
        at = pl.ds(g * step, step)
        some = pl.ds(g * pairs, pairs)
        late[g] = [
            pltpu.make_async_copy(high_ref.at[some], whigh.at[some], late_sems.at[g, 0]),
            pltpu.make_async_copy(low_ref.at[some], wlow.at[some], late_sems.at[g, 1]),
            pltpu.make_async_copy(
                area(extra_ref, pick(extra, side), other.shape[0], at), other.at[:, at], late_sems.at[g, 2]
            ),
        ]
    waiting = list(groups)
    for u in range(len(units)):
        inside.append([start_in(u, k) for k in range(len(pieces))])
        if u > 0 and waiting:
            for copy in late[waiting.pop(0)]:
                copy.start()
    for g in waiting:
        for copy in late[g]:
            copy.start()

    blocks = [(i, min(2, nout - i)) for i in range(0, nout, 2)]
    total = nout * width
    a_both[...] = jnp.zeros_like(a_both)
    for first, n in blocks:
        for i in range(n):
            for j in range(3):
                for part, value in enumerate(split(band_ref[first + i, j])):
                    row = (2 * first + part * n + i) * width
                    a_both[row : row + width, (i + j) * width : (i + j + 1) * width] = value
    y_both[:, :width] = jnp.zeros((2 * total, width), BF16)
    y_both[:, columns + width :] = jnp.zeros((2 * total, width), BF16)

    def columns_pass(u):
        for copy in inside[u]:
            copy.wait()
        for i in range(units[u][0] // (2 * width), units[u][1] // (2 * width)):
            at = slice(i * 2 * width, (i + 1) * 2 * width)
            to = slice((2 * i + 1) * width, (2 * i + 3) * width)
            for first, n in blocks:
                a = a_both[2 * first * width : 2 * (first + n) * width, : (n + 2) * width]
                y = dot3(a, split(field[first * width : (first + n + 2) * width, at]), ((1,), (0,)))
                for part, value in enumerate(split(y)):
                    row = part * total + first * width
                    y_both[row : row + n * width, to] = value

    def rows_pass(g):
        for copy in late[g]:
            copy.wait()
        for t in range(g * pairs, (g + 1) * pairs):
            source = slice(t * 2 * width, (t + 2) * 2 * width)
            at = slice(t * 2 * width, (t + 1) * 2 * width)
            value = dot3(y_both[:, source], (whigh[t], wlow[t]), ((1,), (1,)))
            if final:
                results[0][:, at] = value
                results[1][:, at] = share * jnp.log(other[:, at] * value)
            else:
                results[0][:, at] = other[:, at] / value
        at = pl.ds(g * step, step)
        targets = [outs[-1].at[:, pl.ds((g - groups[0]) * step, step)]] + ([outs[groups.index(g)]] if final else [])
        copies = [
            pltpu.make_async_copy(src.at[:, at], dst, out_sems.at[g, k])
            for k, (src, dst) in enumerate(zip(results, targets))
        ]
        for k, (start, stop) in enumerate(split_out):
            if g * step < stop <= (g + 1) * step:
                part = results[0].at[:, pl.ds(start, stop - start)]
                copies.append(pltpu.make_async_copy(part, outs[k], out_sems.at[GROUPS, k]))
        for copy in copies:
            copy.start()
        return copies

    going = []
    waiting = list(groups)
    for u, (_, stop) in enumerate(units):
        columns_pass(u)
        while waiting and u > 0 and (stop == columns or (waiting[0] + 1) * step + width <= stop):
            going += rows_pass(waiting.pop(0))
    for copy in going:
        copy.wait()


def blur(
    name, side, arrays, pieces, bands, weights, other, extra,
    map_weights=None, pin=True, split_out=(), units=None, groups=tuple(range(GROUPS)),
):
    nout, _, width, _ = bands.shape
    npairs = weights[0].shape[0]
    columns = npairs * 2 * width
    rows, depth = nout * width, (nout + 2) * width
    final = map_weights is not None
    nouts = 2 if final else 1
    kind = pltpu.HBM if pin else jax.ShapeDtypeStruct
    step = columns // GROUPS
    units = tuple((g * step, (g + 1) * step) for g in range(GROUPS)) if units is None else units
    shapes = [kind((rows, step), F32)] * (len(groups) if final else 0)
    shapes += [pltpu.HBM((rows, stop - start), F32) for start, stop in split_out]
    shapes.append(pltpu.HBM((rows, len(groups) * step), F32))
    plan = (tuple(pieces), len(arrays), extra, final, split_out, units, groups)
    work = 3 * 2 * rows * columns * (depth + 4 * width)
    moved = 4 * (depth + 3 * rows) * columns + npairs * 2 * 2 * 8 * width * width
    size = 4 * columns * (depth + (1 + nouts) * rows) + 4 * rows * columns + npairs * 2 * 2 * 8 * width * width
    result = pl.pallas_call(
        functools.partial(blur_kernel, plan),
        in_specs=[INSMEM] + [ANY] * len(arrays) + [INVMEM, ANY, ANY, ANY] + [INSMEM] * final,
        out_specs=[ANY] * len(shapes),
        out_shape=shapes,
        scratch_shapes=[
            pltpu.VMEM((depth, columns), F32),
            pltpu.VMEM((2 * rows, min(depth, 4 * width)), BF16),
            pltpu.VMEM((2 * rows, columns + 2 * width), BF16),
            pltpu.VMEM((npairs, 2 * width, 4 * width), BF16),
            pltpu.VMEM((npairs, 2 * width, 4 * width), BF16),
            pltpu.VMEM((rows, columns), F32),
        ]
        + [pltpu.VMEM((rows, columns), F32)] * nouts
        + [
            pltpu.SemaphoreType.DMA((len(units), len(pieces))),
            pltpu.SemaphoreType.DMA((GROUPS, 3)),
            pltpu.SemaphoreType.DMA((GROUPS + 1, 2)),
        ],
        compiler_params=params(size // 2**20 + 6),
        cost_estimate=pl.CostEstimate(flops=work // 64, bytes_accessed=moved // 64, transcendentals=0),
        name=name,
    )(side, *arrays, bands, *hbm(*weights, other), *(hbm(map_weights) if final else []))
    return (result[:-1], result[-1]) if final else result if split_out else result[0]


def raw_kernel(fresh, first, side_ref, *refs):
    own, peer, m_ref = refs[:GROUPS], refs[GROUPS : 2 * GROUPS], refs[2 * GROUPS]
    raw_ref, quotient_ref, mass_ref, quotient, sems = refs[-5:]
    tile = raw_ref.shape[0]
    at = pl.program_id(0)
    slot = lax.rem(at, 2)

    def copy(step, slot):
        row = pl.multiple_of(pick(first, side_ref[0]) + step * tile, tile)
        return pltpu.make_async_copy(quotient.at[slot], area(quotient_ref, row, tile, slice(None)), sems.at[slot])

    @pl.when(at >= 2)
    def _():
        copy(at - 2, slot).wait()

    mass = 0.0
    for g in range(GROUPS):
        raw = jnp.exp(own[g][...] + peer[g][...])
        step = raw.shape[1]
        raw_ref[:, g * step : (g + 1) * step] = raw
        mass += jnp.sum(raw)
        quotient[slot, :, g * step : (g + 1) * step] = raw / m_ref[:, g * step : (g + 1) * step]
    before = 0.0 if fresh else refs[2 * GROUPS + 3][...]
    mass_ref[...] = mass + jnp.where(at == 0, before, mass_ref[...])
    copy(at, slot).start()

    @pl.when(at == pl.num_programs(0) - 1)
    def _():
        copy(at - 1, 1 - slot).wait()
        copy(at, slot).wait()


def raw_rows(name, side, row, t, peers, m, rows_here, so_far):
    fresh = so_far is None
    rows, columns = m.shape
    tile = 32
    starts = [r // tile for r in row]
    part = pl.BlockSpec((tile, columns), lambda i, at: (i, 0))
    group = pl.BlockSpec((tile, columns // GROUPS), lambda i, at: (i, 0))
    return pl.pallas_call(
        functools.partial(raw_kernel, fresh, row),
        grid_spec=pltpu.PrefetchScalarGridSpec(
            num_scalar_prefetch=1,
            grid=(rows // tile,),
            in_specs=[group] * (2 * GROUPS) + [part] + ([] if fresh else [ANY, ANY, INVMEM]),
            out_specs=(
                pl.BlockSpec((tile, columns), lambda i, at: (jnp.where(at[0] == 0, *starts) + i, 0)),
                ANY,
                INVMEM,
            ),
            scratch_shapes=[pltpu.VMEM((2, tile, columns), F32), pltpu.SemaphoreType.DMA((2,))],
        ),
        out_shape=(
            pltpu.VMEM((rows_here, columns), F32),
            pltpu.VMEM((rows_here, 1, columns), F32),
            jax.ShapeDtypeStruct((1, 128), F32),
        ),
        input_output_aliases={} if fresh else {2 * GROUPS + 2: 0, 2 * GROUPS + 3: 1},
        compiler_params=params(16),
        cost_estimate=pl.CostEstimate(flops=m.size // 16, bytes_accessed=m.size // 4, transcendentals=0),
        name=name,
    )(side, *t, *peers, m, *([] if fresh else vmem(*so_far[:2]) + [so_far[2]]))


def raw_only_kernel(side_ref, *refs):
    *logs, _, before_ref, raw_ref, mass_ref = refs
    parts = len(logs) // 2
    mass = 0.0
    for g in range(parts):
        raw = jnp.exp(logs[g][...] + logs[parts + g][...])
        step = raw.shape[1]
        raw_ref[:, g * step : (g + 1) * step] = raw
        mass += jnp.sum(raw)
    mass_ref[...] = mass + jnp.where(pl.program_id(0) == 0, before_ref[...], mass_ref[...])


def piece_spec(tile, columns, row, column):
    starts = [r // tile for r in row]
    return pl.BlockSpec((tile, columns), lambda i, at: (jnp.where(at[0] == 0, *starts) + i, column // columns))


def raw_only(name, side, row, column, t, peers, raw_all, mass):
    rows, step = t[0].shape
    columns = len(t) * step
    tile = 64
    group = pl.BlockSpec((tile, step), lambda i, at: (i, 0))
    return pl.pallas_call(
        raw_only_kernel,
        grid_spec=pltpu.PrefetchScalarGridSpec(
            num_scalar_prefetch=1,
            grid=(rows // tile,),
            in_specs=[group] * (2 * len(t)) + [ANY, INVMEM],
            out_specs=(piece_spec(tile, columns, row, column), INVMEM),
        ),
        out_shape=(pltpu.VMEM(raw_all.shape, F32), jax.ShapeDtypeStruct(mass.shape, F32)),
        input_output_aliases={2 * len(t) + 1: 0},
        compiler_params=params(16),
        cost_estimate=pl.CostEstimate(flops=rows * columns // 16, bytes_accessed=rows * columns // 4, transcendentals=0),
        name=name,
    )(side, *t, *peers, *vmem(raw_all), mass)


def quotient_kernel(first, column, side_ref, raw_ref, m_ref, _, quotient_ref, quotient, sems):
    tile, columns = raw_ref.shape
    at = pl.program_id(0)
    row = pick(first, side_ref[0])
    quotient[at] = raw_ref[...] / m_ref[...]
    copies = [
        pltpu.make_async_copy(
            quotient.at[k], area(quotient_ref, row + k * tile, tile, pl.ds(column, columns)), sems.at[k]
        )
        for k in range(quotient.shape[0])
    ]
    for k, copy in enumerate(copies):
        pl.when(at == k)(copy.start)

    @pl.when(at == len(copies) - 1)
    def _():
        for copy in copies:
            copy.wait()


def quotient_part(name, side, row, column, raw_all, m, quotient_all):
    rows, columns = m.shape
    tile = 64
    return pl.pallas_call(
        functools.partial(quotient_kernel, row, column),
        grid_spec=pltpu.PrefetchScalarGridSpec(
            num_scalar_prefetch=1,
            grid=(rows // tile,),
            in_specs=[
                piece_spec(tile, columns, row, column),
                pl.BlockSpec((tile, columns), lambda i, at: (i, 0)),
                ANY,
            ],
            out_specs=ANY,
            scratch_shapes=[
                pltpu.VMEM((rows // tile, tile, columns), F32),
                pltpu.SemaphoreType.DMA((rows // tile,)),
            ],
        ),
        out_shape=pltpu.VMEM(quotient_all.shape, F32),
        input_output_aliases={3: 0},
        compiler_params=params(16),
        cost_estimate=pl.CostEstimate(flops=rows * columns // 16, bytes_accessed=rows * columns // 4, transcendentals=0),
        name=name,
    )(side, *vmem(raw_all), *hbm(m), *vmem(quotient_all))


def sum_kernel(a_ref, b_ref, out_ref):
    out_ref[...] = a_ref[...] + b_ref[...]


def mass_parts(mass, quotient):
    count = lax.axis_size("space")
    if count & (count - 1):
        return [lax.psum(mass, "space")], quotient
    parts = [mass]
    for bit in range(count.bit_length() - 1):
        if len(parts) == 2:
            if bit == 1:
                parts[1], quotient = lax.optimization_barrier((parts[1], quotient))
            parts = [
                pl.pallas_call(
                    sum_kernel,
                    in_specs=[INVMEM, INVMEM],
                    out_specs=INVMEM,
                    out_shape=jax.ShapeDtypeStruct(mass.shape, F32),
                    compiler_params=params(1),
                    name="mass",
                )(*parts)
            ]
        parts.append(lax.ppermute(parts[0], "space", [(i, i ^ (1 << bit)) for i in range(count)]))
    return parts, quotient


def output_kernel(total, raw_ref, quotient_ref, *refs):
    *masses, barycenter_ref, scaling_ref = refs
    mass = masses[0][...]
    for part in masses[1:]:
        mass += part[...]
    scale = total / mass
    width = scale.shape[1]
    for b in range(raw_ref.shape[1] // width):
        at = slice(b * width, (b + 1) * width)
        barycenter_ref[:, at] = raw_ref[:, at] * scale
    scaling_ref[...] = quotient_ref[...] * scale.reshape(1, 1, width)


def outputs(raw, quotient, masses):
    rows, columns = raw.shape
    tile = 64
    flat = pl.BlockSpec((tile, columns), lambda i: (i, 0))
    deep = pl.BlockSpec((tile,) + quotient.shape[1:], lambda i: (i, 0, 0))
    return pl.pallas_call(
        functools.partial(output_kernel, float(columns * columns)),
        grid=(rows // tile,),
        in_specs=[flat, deep] + [INVMEM] * len(masses),
        out_specs=(flat, deep),
        out_shape=(jax.ShapeDtypeStruct(raw.shape, F32), jax.ShapeDtypeStruct(quotient.shape, F32)),
        compiler_params=params(16),
        name="outputs",
    )(*vmem(raw, quotient), *masses)


def local(densities, scaling, weights, band):
    rows_here, maps_here, cols_all = densities.shape
    _, _, width, _ = band.shape
    nlocal = rows_here // width
    inner = max(nlocal - 2, 0)
    place = lax.axis_index("space")
    count = lax.axis_size("space")
    assert maps_here == 1 and lax.axis_size("member") == 2 and count % 2 == 0

    odd = place & 1
    middle = place >> 1
    numbers = [jnp.where(odd == 1, middle, 3 - middle), jnp.where(odd == 1, 2 - middle, middle - 1)]
    side = jnp.stack([odd, *numbers, lax.axis_index("member")])
    spread = count == 8 and nlocal > 1
    last = rows_here - width
    cross_row, near_row = (0, last), (last, 0)
    both = lambda pairs: pairs + [(b, a) for a, b in pairs]
    cross = functools.partial(
        lax.ppermute, axis_name="space", perm=both([(i, i + 1) for i in range(1, count - 1, 2)])
    )
    near = functools.partial(lax.ppermute, axis_name="space", perm=both([(i, i + 1) for i in range(0, count, 2)]))
    swap = functools.partial(lax.ppermute, axis_name="member", perm=[(0, 1), (1, 0)])

    def choose(choice):
        return jnp.where(odd == 0, *[c // width for c in choice]).astype(jnp.int32)

    whole_rows = [(0, cols_all)]
    near_edge = cut("cut_near", side, scaling, near_row, width, whole_rows)
    if spread:
        edge = cut("cut_cross", side, scaling, cross_row, width, cross_parts(cols_all))
        cross1, near_edge = cross_send(edge, near_edge)
    else:
        cross1 = [cross(cut("cut_cross", side, scaling, cross_row, width, whole_rows)[0])]
    near1 = near(near_edge[0])

    wts = row_weights(band)
    mine = place * nlocal
    band_at = lambda block, blocks: lax.dynamic_slice_in_dim(band, mine + block, blocks, 0)

    if inner > 0:
        inner_bands = band_at(1, inner)
        ratio_inner = blur(
            "ratio_inner", side, hbm(scaling), [(0, 0, rows_here, 0)], inner_bands, wts, densities, width
        )
        *cross1, ratio_inner = lax.optimization_barrier((*cross1, ratio_inner))
    if nlocal == 1:
        pieces = [(0, 0, width, width), (1, 0, width, (0, 2 * width)), (2, 0, width, (2 * width, 0))]
        bands = band_at(0, 1)
        ratio = blur("ratio_only", side, [scaling, *cross1, near1], pieces, bands, wts, densities, 0)
        cross2, near2 = cross(ratio), near(ratio)
    else:
        two = rows_here - 2 * width
        halo = cross_received(1, cols_all) if spread else 1
        pieces = [(0, (0, two), 2 * width, (width, 0)), (halo, 0, width, (0, 2 * width))]
        cross_bands = band_at(choose(cross_row), 1)
        ratio_cross = blur(
            "ratio_cross", side, hbm(scaling) + cross1, pieces, cross_bands, wts, densities, cross_row
        )
        ratio_cross, near1 = lax.optimization_barrier((ratio_cross, near1))
        cross2 = cross(ratio_cross)
        half, more = cols_all // 2, 2 * width
        pieces = [(0, (two, 0), 2 * width, (0, width)), (1, 0, width, (2 * width, 0))]
        near_bands = band_at(choose(near_row), 1)
        *parts, ratio_near = blur(
            "ratio_near", side, hbm(scaling) + [near1], pieces, near_bands, wts, densities, near_row,
            split_out=((0, half + more), (half + more, cols_all)),
        )
        near2 = [near(part) for part in parts]

    def finish(name, arrays, pieces, bands, row, weights, state):
        t, m = blur("logs_" + name, side, arrays, pieces, bands, wts, scaling, row, weights)
        return raw_rows(
            "raw_" + name, side, row, hbm(*t), [swap(part) for part in t], *hbm(m), rows_here, state
        )

    if nlocal == 1:
        pieces = [(0, 0, width, width), (1, 0, width, (0, 2 * width)), (2, 0, width, (2 * width, 0))]
        state = finish("only", [ratio, cross2, near2], pieces, bands, (0, 0), weights, None)
    else:
        state = None
        beside, beside_row = ratio_near, (0, 0)
        if inner > 0:
            arrays = hbm(ratio_inner, ratio_cross, ratio_near)
            pieces = [(0, 0, inner * width, width), (1, 0, width, cross_row), (2, 0, width, near_row)]
            state = finish("inner", arrays, pieces, inner_bands, (width, width), weights, None)
            weights, state = lax.optimization_barrier((weights, state))
            beside, beside_row = ratio_inner, (0, (inner - 1) * width)
        arrays = hbm(ratio_cross, beside) + [cross2]
        pieces = [(0, 0, width, width), (1, beside_row, width, (2 * width, 0)), (2, 0, width, (0, 2 * width))]
        state = finish("cross", arrays, pieces, cross_bands, cross_row, weights, state)
        weights, state = lax.optimization_barrier((weights, state))
        if inner == 0:
            beside = ratio_cross
        raw, quotient, mass = state
        step = cols_all // GROUPS
        first_units = tuple((g * step, (g + 1) * step) for g in range(GROUPS // 2)) + ((half, half + more),)
        later_units = ((half - more, half + more), (half + more, half + step)) + tuple(
            (g * step, (g + 1) * step) for g in range(GROUPS // 2 + 1, GROUPS)
        )
        plans = [
            ("near_first", first_units, 0, [(2, start) for start, _ in first_units]),
            ("near_later", later_units, half, [(2, half - more)] + [(3, a - half - more) for a, _ in later_units[1:]]),
        ]
        for part, (name, units, column, halo) in enumerate(plans):
            arrays = hbm(ratio_near, beside) + near2[: part + 1]
            pieces = [
                (0, 0, width, width),
                (1, beside_row[::-1], width, (0, 2 * width)),
                (tuple(halo), 0, width, (2 * width, 0)),
            ]
            groups = tuple(g for g in range(GROUPS) if column <= g * step < column + half)
            t, m = blur(
                "logs_" + name, side, arrays, pieces, near_bands, wts, scaling, near_row, weights,
                pin=False, units=units, groups=groups,
            )
            raw, mass = raw_only("raw_" + name, side, near_row, column, t, [swap(part) for part in t], raw, mass)
            quotient = quotient_part("quotient_" + name, side, near_row, column, raw, m, quotient)
            if part == 0:
                weights, raw, mass, quotient = lax.optimization_barrier((weights, raw, mass, quotient))
        state = raw, quotient, mass

    raw, quotient, mass = state
    masses, quotient = mass_parts(mass, quotient)
    barycenter, new_scaling = outputs(raw, quotient.reshape(rows_here, cols_all // width, width), masses)
    return barycenter, new_scaling.reshape(rows_here, 1, cols_all)


def solution(mesh):
    return jax.shard_map(
        local,
        mesh=mesh,
        in_specs=(
            P("space", ("parts", "member"), None),
            P("space", ("parts", "member"), None),
            P("parts"),
            P(),
        ),
        out_specs=(P(("parts", "space"), None), P("space", ("parts", "member"), None)),
        check_vma=False,
    )
```

```python
import functools

import jax
import jax.numpy as jnp
from jax import lax
from jax.experimental import pallas as pl
from jax.experimental.pallas import tpu as pltpu
from jax.sharding import PartitionSpec as P

F32 = jnp.float32
BF16 = jnp.bfloat16
GROUPS = 4
ANY = pl.BlockSpec(memory_space=pl.ANY)
INVMEM = pl.BlockSpec(memory_space=pltpu.VMEM)
INSMEM = pl.BlockSpec(memory_space=pltpu.SMEM)


def split(x):
    high = x.astype(BF16)
    return high, (x - high.astype(F32)).astype(BF16)


def dot3(stack, b, dims):
    one = functools.partial(lax.dot_general, dimension_numbers=(dims, ((), ())), preferred_element_type=F32)
    rows = stack.shape[0] // 2
    both = one(stack, b[0])
    return both[:rows] + (one(stack[:rows], b[1]) + both[rows:])


def params(mebibytes):
    return pltpu.CompilerParams(vmem_limit_bytes=mebibytes * 1024 * 1024)


def hbm(*arrays):
    return [pltpu.with_memory_space_constraint(a, pltpu.HBM) for a in arrays]


def vmem(*arrays):
    return [pltpu.with_memory_space_constraint(a, pltpu.VMEM) for a in arrays]


def pick(choice, side):
    if isinstance(choice, tuple):
        return pl.multiple_of(jnp.where(side == 0, choice[0], choice[1]), 128)
    return choice


def cut_kernel(first, columns, side_ref, src, *refs):
    *outs, stage, sems = refs
    rows = stage.shape[0] // GROUPS
    start = pick(first, side_ref[0])
    outward = []
    inward = [
        pltpu.make_async_copy(src.at[pl.ds(start + g * rows, rows)], stage.at[pl.ds(g * rows, rows)], sems.at[0, g])
        for g in range(GROUPS)
    ]
    for copy in inward:
        copy.start()
    for g in range(GROUPS):
        inward[g].wait()
        part = pl.ds(g * rows, rows)
        for k, (out, column) in enumerate(zip(outs, columns)):
            at = pl.ds(column_of(column, side_ref), out.shape[2])
            outward.append(pltpu.make_async_copy(stage.at[part, :, at], out.at[part], sems.at[1 + k, g]))
            outward[-1].start()
    for copy in outward:
        copy.wait()


def cut(name, side, array, first, rows, parts):
    columns = array.shape[2]
    return pl.pallas_call(
        functools.partial(cut_kernel, first, [column for column, _ in parts]),
        in_specs=[INSMEM, ANY],
        out_specs=[ANY] * len(parts),
        out_shape=[pltpu.HBM((rows, 1, n), F32) for _, n in parts],
        scratch_shapes=[
            pltpu.VMEM((rows, 1, columns), F32),
            pltpu.SemaphoreType.DMA((1 + len(parts), GROUPS)),
        ],
        compiler_params=params(8),
        name=name,
    )(side, *hbm(array))


def column_of(column, side_ref):
    if isinstance(column, tuple):
        return pl.multiple_of(jnp.where(side_ref[1] == 1, column[0], column[1]), 128)
    return column


def cross_parts(columns):
    half, quarter = columns // 2, columns // 4
    return [(0, half), (half, quarter), ((half, 0), half), (3 * quarter, quarter)]


def cross_send(parts, behind=()):
    def send(part, numbers, ends):
        pairs = []
        for k in range(3):
            for direction, number in ((0, k), (1, 2 - k)):
                if number in numbers:
                    pairs.append(ends(k)[direction])
        return lax.ppermute(part, "space", pairs)

    to_partner = lambda k: ((2 * k + 1, 2 * k), (2 * k + 2, 2 * k + 3))
    onward = lambda k: ((2 * k, 2 * k + 2), (2 * k + 3, 2 * k + 1))
    direct = lambda k: ((2 * k + 1, 2 * k + 2), (2 * k + 2, 2 * k + 1))
    relayed = [send(part, numbers, to_partner) for part, numbers in zip(parts[:2], ((0, 1), (0, 2)))]
    straight = [send(part, numbers, direct) for part, numbers in zip(parts[2:], ((1, 2), (0, 2)))]
    a, b, c, d, *behind = lax.optimization_barrier((*relayed, *straight, *behind))
    relayed, straight = [a, b], [c, d]
    passed = [send(part, numbers, onward) for part, numbers in zip(relayed, ((0, 1), (0, 2)))]
    return passed + straight, behind


def cross_received(base, columns):
    a, b, c, d = range(base, base + 4)
    q = columns // 4
    return ((2, (c, 0), (a, 0)), (2, (c, q), (a, q)), (1, (c, 0), (b, 0)), (1, (c, q), (d, 0)))


def area(ref, row, rows, columns):
    return ref.at[pl.ds(row, rows), 0, columns] if len(ref.shape) == 3 else ref.at[pl.ds(row, rows), columns]


def weight_kernel(nblocks, band_ref, high_ref, low_ref):
    pair = pl.program_id(0)
    width = band_ref.shape[2]
    zero = jnp.zeros((width, width), F32)
    for o in range(2):
        for i in range(4):
            j = i - o
            value = band_ref[o, j] if 0 <= j <= 2 else zero
            if (o, j) == (0, 0):
                value = jnp.where(pair > 0, value, 0.0)
            if (o, j) == (1, 2):
                value = jnp.where(pair < nblocks // 2 - 1, value, 0.0)
            high, low = split(value)
            rows, columns = slice(o * width, (o + 1) * width), slice(i * width, (i + 1) * width)
            high_ref[0, rows, columns] = high
            low_ref[0, rows, columns] = low


def row_weights(band):
    nblocks, _, width, _ = band.shape
    shape = pltpu.HBM((nblocks // 2, 2 * width, 4 * width), BF16)
    out_spec = pl.BlockSpec((1, 2 * width, 4 * width), lambda t: (t, 0, 0))
    return pl.pallas_call(
        functools.partial(weight_kernel, nblocks),
        grid=(nblocks // 2,),
        in_specs=[pl.BlockSpec((2, 3, width, width), lambda t: (t, 0, 0, 0))],
        out_specs=(out_spec, out_spec),
        out_shape=(shape, shape),
        name="row_weights",
    )(*hbm(band))


def blur_kernel(plan, *refs):
    pieces, narrays, extra, final, split_out, units, groups = plan
    side_ref, refs = refs[0], refs[1:]
    arrays = refs[:narrays]
    band_ref, high_ref, low_ref, extra_ref = refs[narrays : narrays + 4]
    rest = refs[narrays + 4 :]
    if final:
        weights_ref, rest = rest[0], rest[1:]
        all_weights = weights_ref[0]
        for k in range(1, weights_ref.shape[0]):
            all_weights += weights_ref[k]
        row_shape = (1, 2 * band_ref.shape[2])
        share = jnp.full(row_shape, weights_ref[side_ref[3]]) / jnp.full(row_shape, all_weights)
    nouts = len(groups) + 1 if final else 1 + len(split_out)
    outs = rest[:nouts]
    field, a_both, y_both, whigh, wlow, other = rest[nouts : nouts + 6]
    *results, in_sems, late_sems, out_sems = rest[nouts + 6 :]

    side = side_ref[0]
    nout, _, width, _ = band_ref.shape
    columns = field.shape[1]
    step = columns // GROUPS
    pairs = step // (2 * width)
    inside, late = [], {}

    def copy_in(u, k, place):
        _, row, rows, to = pieces[k]
        which, column = place
        start, stop = units[u]
        return pltpu.make_async_copy(
            area(arrays[which], pick(row, side), rows, pl.ds(column, stop - start)),
            field.at[pl.ds(pick(to, side), rows), pl.ds(start, stop - start)],
            in_sems.at[u, k],
        )

    def start_in(u, k):
        source = pieces[k][0]
        if isinstance(source, int):
            copy = copy_in(u, k, (source, units[u][0]))
        elif len(source[u]) == 2:
            copy = copy_in(u, k, source[u])
        else:
            number, this, other_one = source[u]
            pl.when(side_ref[2] == number)(copy_in(u, k, this).start)
            pl.when(side_ref[2] != number)(copy_in(u, k, other_one).start)
            return copy_in(u, k, other_one)
        copy.start()
        return copy

    for g in groups:
        at = pl.ds(g * step, step)
        some = pl.ds(g * pairs, pairs)
        late[g] = [
            pltpu.make_async_copy(high_ref.at[some], whigh.at[some], late_sems.at[g, 0]),
            pltpu.make_async_copy(low_ref.at[some], wlow.at[some], late_sems.at[g, 1]),
            pltpu.make_async_copy(
                area(extra_ref, pick(extra, side), other.shape[0], at), other.at[:, at], late_sems.at[g, 2]
            ),
        ]
    waiting = list(groups)
    for u in range(len(units)):
        inside.append([start_in(u, k) for k in range(len(pieces))])
        if u > 0 and waiting:
            for copy in late[waiting.pop(0)]:
                copy.start()
    for g in waiting:
        for copy in late[g]:
            copy.start()

    blocks = [(i, min(2, nout - i)) for i in range(0, nout, 2)]
    total = nout * width
    a_both[...] = jnp.zeros_like(a_both)
    for first, n in blocks:
        for i in range(n):
            for j in range(3):
                for part, value in enumerate(split(band_ref[first + i, j])):
                    row = (2 * first + part * n + i) * width
                    a_both[row : row + width, (i + j) * width : (i + j + 1) * width] = value
    y_both[:, :width] = jnp.zeros((2 * total, width), BF16)
    y_both[:, columns + width :] = jnp.zeros((2 * total, width), BF16)

    def columns_pass(u):
        for copy in inside[u]:
            copy.wait()
        for i in range(units[u][0] // (2 * width), units[u][1] // (2 * width)):
            at = slice(i * 2 * width, (i + 1) * 2 * width)
            to = slice((2 * i + 1) * width, (2 * i + 3) * width)
            for first, n in blocks:
                a = a_both[2 * first * width : 2 * (first + n) * width, : (n + 2) * width]
                y = dot3(a, split(field[first * width : (first + n + 2) * width, at]), ((1,), (0,)))
                for part, value in enumerate(split(y)):
                    row = part * total + first * width
                    y_both[row : row + n * width, to] = value

    def rows_pass(g):
        for copy in late[g]:
            copy.wait()
        for t in range(g * pairs, (g + 1) * pairs):
            source = slice(t * 2 * width, (t + 2) * 2 * width)
            at = slice(t * 2 * width, (t + 1) * 2 * width)
            value = dot3(y_both[:, source], (whigh[t], wlow[t]), ((1,), (1,)))
            if final:
                results[0][:, at] = value
                results[1][:, at] = share * jnp.log(other[:, at] * value)
            else:
                results[0][:, at] = other[:, at] / value
        at = pl.ds(g * step, step)
        targets = [outs[-1].at[:, pl.ds((g - groups[0]) * step, step)]] + ([outs[groups.index(g)]] if final else [])
        copies = [
            pltpu.make_async_copy(src.at[:, at], dst, out_sems.at[g, k])
            for k, (src, dst) in enumerate(zip(results, targets))
        ]
        for k, (start, stop) in enumerate(split_out):
            if g * step < stop <= (g + 1) * step:
                part = results[0].at[:, pl.ds(start, stop - start)]
                copies.append(pltpu.make_async_copy(part, outs[k], out_sems.at[GROUPS, k]))
        for copy in copies:
            copy.start()
        return copies

    going = []
    waiting = list(groups)
    for u, (_, stop) in enumerate(units):
        columns_pass(u)
        while waiting and u > 0 and (stop == columns or (waiting[0] + 1) * step + width <= stop):
            going += rows_pass(waiting.pop(0))
    for copy in going:
        copy.wait()


def blur(
    name, side, arrays, pieces, bands, weights, other, extra,
    map_weights=None, pin=True, split_out=(), units=None, groups=tuple(range(GROUPS)),
):
    nout, _, width, _ = bands.shape
    npairs = weights[0].shape[0]
    columns = npairs * 2 * width
    rows, depth = nout * width, (nout + 2) * width
    final = map_weights is not None
    nouts = 2 if final else 1
    kind = pltpu.HBM if pin else jax.ShapeDtypeStruct
    step = columns // GROUPS
    units = tuple((g * step, (g + 1) * step) for g in range(GROUPS)) if units is None else units
    shapes = [kind((rows, step), F32)] * (len(groups) if final else 0)
    shapes += [pltpu.HBM((rows, stop - start), F32) for start, stop in split_out]
    shapes.append(pltpu.HBM((rows, len(groups) * step), F32))
    plan = (tuple(pieces), len(arrays), extra, final, split_out, units, groups)
    work = 3 * 2 * rows * columns * (depth + 4 * width)
    moved = 4 * (depth + 3 * rows) * columns + npairs * 2 * 2 * 8 * width * width
    size = 4 * columns * (depth + (1 + nouts) * rows) + 4 * rows * columns + npairs * 2 * 2 * 8 * width * width
    result = pl.pallas_call(
        functools.partial(blur_kernel, plan),
        in_specs=[INSMEM] + [ANY] * len(arrays) + [INVMEM, ANY, ANY, ANY] + [INSMEM] * final,
        out_specs=[ANY] * len(shapes),
        out_shape=shapes,
        scratch_shapes=[
            pltpu.VMEM((depth, columns), F32),
            pltpu.VMEM((2 * rows, min(depth, 4 * width)), BF16),
            pltpu.VMEM((2 * rows, columns + 2 * width), BF16),
            pltpu.VMEM((npairs, 2 * width, 4 * width), BF16),
            pltpu.VMEM((npairs, 2 * width, 4 * width), BF16),
            pltpu.VMEM((rows, columns), F32),
        ]
        + [pltpu.VMEM((rows, columns), F32)] * nouts
        + [
            pltpu.SemaphoreType.DMA((len(units), len(pieces))),
            pltpu.SemaphoreType.DMA((GROUPS, 3)),
            pltpu.SemaphoreType.DMA((GROUPS + 1, 2)),
        ],
        compiler_params=params(size // 2**20 + 6),
        cost_estimate=pl.CostEstimate(flops=work // 64, bytes_accessed=moved // 64, transcendentals=0),
        name=name,
    )(side, *arrays, bands, *hbm(*weights, other), *(hbm(map_weights) if final else []))
    return (result[:-1], result[-1]) if final else result if split_out else result[0]


def raw_kernel(fresh, first, side_ref, *refs):
    own, peer, m_ref = refs[:GROUPS], refs[GROUPS : 2 * GROUPS], refs[2 * GROUPS]
    raw_ref, quotient_ref, mass_ref, quotient, sems = refs[-5:]
    tile = raw_ref.shape[0]
    at = pl.program_id(0)
    slot = lax.rem(at, 2)

    def copy(step, slot):
        row = pl.multiple_of(pick(first, side_ref[0]) + step * tile, tile)
        return pltpu.make_async_copy(quotient.at[slot], area(quotient_ref, row, tile, slice(None)), sems.at[slot])

    @pl.when(at >= 2)
    def _():
        copy(at - 2, slot).wait()

    mass = 0.0
    for g in range(GROUPS):
        raw = jnp.exp(own[g][...] + peer[g][...])
        step = raw.shape[1]
        raw_ref[:, g * step : (g + 1) * step] = raw
        mass += jnp.sum(raw)
        quotient[slot, :, g * step : (g + 1) * step] = raw / m_ref[:, g * step : (g + 1) * step]
    before = 0.0 if fresh else refs[2 * GROUPS + 3][...]
    mass_ref[...] = mass + jnp.where(at == 0, before, mass_ref[...])
    copy(at, slot).start()

    @pl.when(at == pl.num_programs(0) - 1)
    def _():
        copy(at - 1, 1 - slot).wait()
        copy(at, slot).wait()


def raw_rows(name, side, row, t, peers, m, rows_here, so_far):
    fresh = so_far is None
    rows, columns = m.shape
    tile = 32
    starts = [r // tile for r in row]
    part = pl.BlockSpec((tile, columns), lambda i, at: (i, 0))
    group = pl.BlockSpec((tile, columns // GROUPS), lambda i, at: (i, 0))
    return pl.pallas_call(
        functools.partial(raw_kernel, fresh, row),
        grid_spec=pltpu.PrefetchScalarGridSpec(
            num_scalar_prefetch=1,
            grid=(rows // tile,),
            in_specs=[group] * (2 * GROUPS) + [part] + ([] if fresh else [ANY, ANY, INVMEM]),
            out_specs=(
                pl.BlockSpec((tile, columns), lambda i, at: (jnp.where(at[0] == 0, *starts) + i, 0)),
                ANY,
                INVMEM,
            ),
            scratch_shapes=[pltpu.VMEM((2, tile, columns), F32), pltpu.SemaphoreType.DMA((2,))],
        ),
        out_shape=(
            pltpu.VMEM((rows_here, columns), F32),
            pltpu.VMEM((rows_here, 1, columns), F32),
            jax.ShapeDtypeStruct((1, 128), F32),
        ),
        input_output_aliases={} if fresh else {2 * GROUPS + 2: 0, 2 * GROUPS + 3: 1},
        compiler_params=params(16),
        cost_estimate=pl.CostEstimate(flops=m.size // 16, bytes_accessed=m.size // 4, transcendentals=0),
        name=name,
    )(side, *t, *peers, m, *([] if fresh else vmem(*so_far[:2]) + [so_far[2]]))


def raw_only_kernel(side_ref, *refs):
    *logs, _, before_ref, raw_ref, mass_ref = refs
    parts = len(logs) // 2
    mass = 0.0
    for g in range(parts):
        raw = jnp.exp(logs[g][...] + logs[parts + g][...])
        step = raw.shape[1]
        raw_ref[:, g * step : (g + 1) * step] = raw
        mass += jnp.sum(raw)
    mass_ref[...] = mass + jnp.where(pl.program_id(0) == 0, before_ref[...], mass_ref[...])


def piece_spec(tile, columns, row, column):
    starts = [r // tile for r in row]
    return pl.BlockSpec((tile, columns), lambda i, at: (jnp.where(at[0] == 0, *starts) + i, column // columns))


def raw_only(name, side, row, column, t, peers, raw_all, mass):
    rows, step = t[0].shape
    columns = len(t) * step
    tile = 64
    group = pl.BlockSpec((tile, step), lambda i, at: (i, 0))
    return pl.pallas_call(
        raw_only_kernel,
        grid_spec=pltpu.PrefetchScalarGridSpec(
            num_scalar_prefetch=1,
            grid=(rows // tile,),
            in_specs=[group] * (2 * len(t)) + [ANY, INVMEM],
            out_specs=(piece_spec(tile, columns, row, column), INVMEM),
        ),
        out_shape=(pltpu.VMEM(raw_all.shape, F32), jax.ShapeDtypeStruct(mass.shape, F32)),
        input_output_aliases={2 * len(t) + 1: 0},
        compiler_params=params(16),
        cost_estimate=pl.CostEstimate(flops=rows * columns // 16, bytes_accessed=rows * columns // 4, transcendentals=0),
        name=name,
    )(side, *t, *peers, *vmem(raw_all), mass)


def quotient_kernel(first, column, side_ref, raw_ref, m_ref, _, quotient_ref, quotient, sems):
    tile, columns = raw_ref.shape
    at = pl.program_id(0)
    row = pick(first, side_ref[0])
    quotient[at] = raw_ref[...] / m_ref[...]
    copies = [
        pltpu.make_async_copy(
            quotient.at[k], area(quotient_ref, row + k * tile, tile, pl.ds(column, columns)), sems.at[k]
        )
        for k in range(quotient.shape[0])
    ]
    for k, copy in enumerate(copies):
        pl.when(at == k)(copy.start)

    @pl.when(at == len(copies) - 1)
    def _():
        for copy in copies:
            copy.wait()


def quotient_part(name, side, row, column, raw_all, m, quotient_all):
    rows, columns = m.shape
    tile = 64
    return pl.pallas_call(
        functools.partial(quotient_kernel, row, column),
        grid_spec=pltpu.PrefetchScalarGridSpec(
            num_scalar_prefetch=1,
            grid=(rows // tile,),
            in_specs=[
                piece_spec(tile, columns, row, column),
                pl.BlockSpec((tile, columns), lambda i, at: (i, 0)),
                ANY,
            ],
            out_specs=ANY,
            scratch_shapes=[
                pltpu.VMEM((rows // tile, tile, columns), F32),
                pltpu.SemaphoreType.DMA((rows // tile,)),
            ],
        ),
        out_shape=pltpu.VMEM(quotient_all.shape, F32),
        input_output_aliases={3: 0},
        compiler_params=params(16),
        cost_estimate=pl.CostEstimate(flops=rows * columns // 16, bytes_accessed=rows * columns // 4, transcendentals=0),
        name=name,
    )(side, *vmem(raw_all), *hbm(m), *vmem(quotient_all))


def sum_kernel(a_ref, b_ref, out_ref):
    out_ref[...] = a_ref[...] + b_ref[...]


def mass_parts(mass, quotient):
    count = lax.axis_size("space")
    if count & (count - 1):
        return [lax.psum(mass, "space")], quotient
    parts = [mass]
    for bit in range(count.bit_length() - 1):
        if len(parts) == 2:
            if bit == 1:
                parts[1], quotient = lax.optimization_barrier((parts[1], quotient))
            parts = [
                pl.pallas_call(
                    sum_kernel,
                    in_specs=[INVMEM, INVMEM],
                    out_specs=INVMEM,
                    out_shape=jax.ShapeDtypeStruct(mass.shape, F32),
                    compiler_params=params(1),
                    name="mass",
                )(*parts)
            ]
        parts.append(lax.ppermute(parts[0], "space", [(i, i ^ (1 << bit)) for i in range(count)]))
    return parts, quotient


def output_kernel(total, raw_ref, quotient_ref, *refs):
    *masses, barycenter_ref, scaling_ref = refs
    mass = masses[0][...]
    for part in masses[1:]:
        mass += part[...]
    scale = total / mass
    width = scale.shape[1]
    for b in range(raw_ref.shape[1] // width):
        at = slice(b * width, (b + 1) * width)
        barycenter_ref[:, at] = raw_ref[:, at] * scale
    scaling_ref[...] = quotient_ref[...] * scale.reshape(1, 1, width)


def outputs(raw, quotient, masses):
    rows, columns = raw.shape
    tile = 64
    flat = pl.BlockSpec((tile, columns), lambda i: (i, 0))
    deep = pl.BlockSpec((tile,) + quotient.shape[1:], lambda i: (i, 0, 0))
    return pl.pallas_call(
        functools.partial(output_kernel, float(columns * columns)),
        grid=(rows // tile,),
        in_specs=[flat, deep] + [INVMEM] * len(masses),
        out_specs=(flat, deep),
        out_shape=(jax.ShapeDtypeStruct(raw.shape, F32), jax.ShapeDtypeStruct(quotient.shape, F32)),
        compiler_params=params(16),
        name="outputs",
    )(*vmem(raw, quotient), *masses)


def local(densities, scaling, weights, band):
    rows_here, maps_here, cols_all = densities.shape
    _, _, width, _ = band.shape
    nlocal = rows_here // width
    inner = max(nlocal - 2, 0)
    place = lax.axis_index("space")
    count = lax.axis_size("space")
    assert maps_here == 1 and lax.axis_size("member") == 2 and count % 2 == 0

    odd = place & 1
    middle = place >> 1
    numbers = [jnp.where(odd == 1, middle, 3 - middle), jnp.where(odd == 1, 2 - middle, middle - 1)]
    side = jnp.stack([odd, *numbers, lax.axis_index("member")])
    spread = count == 8 and nlocal > 1
    last = rows_here - width
    cross_row, near_row = (0, last), (last, 0)
    both = lambda pairs: pairs + [(b, a) for a, b in pairs]
    cross = functools.partial(
        lax.ppermute, axis_name="space", perm=both([(i, i + 1) for i in range(1, count - 1, 2)])
    )
    near = functools.partial(lax.ppermute, axis_name="space", perm=both([(i, i + 1) for i in range(0, count, 2)]))
    swap = functools.partial(lax.ppermute, axis_name="member", perm=[(0, 1), (1, 0)])

    def choose(choice):
        return jnp.where(odd == 0, *[c // width for c in choice]).astype(jnp.int32)

    whole_rows = [(0, cols_all)]
    near_edge = cut("cut_near", side, scaling, near_row, width, whole_rows)
    if spread:
        edge = cut("cut_cross", side, scaling, cross_row, width, cross_parts(cols_all))
        cross1, near_edge = cross_send(edge, near_edge)
    else:
        cross1 = [cross(cut("cut_cross", side, scaling, cross_row, width, whole_rows)[0])]
    near1 = near(near_edge[0])

    wts = row_weights(band)
    mine = place * nlocal
    band_at = lambda block, blocks: lax.dynamic_slice_in_dim(band, mine + block, blocks, 0)

    if inner > 0:
        inner_bands = band_at(1, inner)
        ratio_inner = blur(
            "ratio_inner", side, hbm(scaling), [(0, 0, rows_here, 0)], inner_bands, wts, densities, width
        )
        *cross1, ratio_inner = lax.optimization_barrier((*cross1, ratio_inner))
    if nlocal == 1:
        pieces = [(0, 0, width, width), (1, 0, width, (0, 2 * width)), (2, 0, width, (2 * width, 0))]
        bands = band_at(0, 1)
        ratio = blur("ratio_only", side, [scaling, *cross1, near1], pieces, bands, wts, densities, 0)
        cross2, near2 = cross(ratio), near(ratio)
    else:
        two = rows_here - 2 * width
        halo = cross_received(1, cols_all) if spread else 1
        pieces = [(0, (0, two), 2 * width, (width, 0)), (halo, 0, width, (0, 2 * width))]
        cross_bands = band_at(choose(cross_row), 1)
        ratio_cross = blur(
            "ratio_cross", side, hbm(scaling, *cross1), pieces, cross_bands, wts, densities, cross_row
        )
        ratio_cross, near1 = lax.optimization_barrier((ratio_cross, near1))
        cross2 = cross(ratio_cross)
        half, more = cols_all // 2, 2 * width
        pieces = [(0, (two, 0), 2 * width, (0, width)), (1, 0, width, (2 * width, 0))]
        near_bands = band_at(choose(near_row), 1)
        *parts, ratio_near = blur(
            "ratio_near", side, hbm(scaling) + [near1], pieces, near_bands, wts, densities, near_row,
            split_out=((0, half + more), (half + more, cols_all)),
        )
        near2 = [near(part) for part in parts]

    def finish(name, arrays, pieces, bands, row, weights, state):
        t, m = blur("logs_" + name, side, arrays, pieces, bands, wts, scaling, row, weights)
        return raw_rows(
            "raw_" + name, side, row, hbm(*t), [swap(part) for part in t], *hbm(m), rows_here, state
        )

    if nlocal == 1:
        pieces = [(0, 0, width, width), (1, 0, width, (0, 2 * width)), (2, 0, width, (2 * width, 0))]
        state = finish("only", [ratio, cross2, near2], pieces, bands, (0, 0), weights, None)
    else:
        state = None
        beside, beside_row = ratio_near, (0, 0)
        if inner > 0:
            arrays = hbm(ratio_inner, ratio_cross, ratio_near)
            pieces = [(0, 0, inner * width, width), (1, 0, width, cross_row), (2, 0, width, near_row)]
            state = finish("inner", arrays, pieces, inner_bands, (width, width), weights, None)
            weights, state = lax.optimization_barrier((weights, state))
            beside, beside_row = ratio_inner, (0, (inner - 1) * width)
        arrays = hbm(ratio_cross, beside) + [cross2]
        pieces = [(0, 0, width, width), (1, beside_row, width, (2 * width, 0)), (2, 0, width, (0, 2 * width))]
        state = finish("cross", arrays, pieces, cross_bands, cross_row, weights, state)
        weights, state = lax.optimization_barrier((weights, state))
        if inner == 0:
            beside = ratio_cross
        raw, quotient, mass = state
        step = cols_all // GROUPS
        first_units = tuple((g * step, (g + 1) * step) for g in range(GROUPS // 2)) + ((half, half + more),)
        later_units = ((half - more, half + more), (half + more, half + step)) + tuple(
            (g * step, (g + 1) * step) for g in range(GROUPS // 2 + 1, GROUPS)
        )
        plans = [
            ("near_first", first_units, 0, [(2, start) for start, _ in first_units]),
            ("near_later", later_units, half, [(2, half - more)] + [(3, a - half - more) for a, _ in later_units[1:]]),
        ]
        for part, (name, units, column, halo) in enumerate(plans):
            arrays = hbm(ratio_near, beside) + near2[: part + 1]
            pieces = [
                (0, 0, width, width),
                (1, beside_row[::-1], width, (0, 2 * width)),
                (tuple(halo), 0, width, (2 * width, 0)),
            ]
            groups = tuple(g for g in range(GROUPS) if column <= g * step < column + half)
            t, m = blur(
                "logs_" + name, side, arrays, pieces, near_bands, wts, scaling, near_row, weights,
                pin=False, units=units, groups=groups,
            )
            raw, mass = raw_only("raw_" + name, side, near_row, column, t, [swap(part) for part in t], raw, mass)
            quotient = quotient_part("quotient_" + name, side, near_row, column, raw, m, quotient)
            if part == 0:
                weights, raw, mass, quotient = lax.optimization_barrier((weights, raw, mass, quotient))
        state = raw, quotient, mass

    raw, quotient, mass = state
    masses, quotient = mass_parts(mass, quotient)
    barycenter, new_scaling = outputs(raw, quotient.reshape(rows_here, cols_all // width, width), masses)
    return barycenter, new_scaling.reshape(rows_here, 1, cols_all)


def solution(mesh):
    return jax.shard_map(
        local,
        mesh=mesh,
        in_specs=(
            P("space", ("parts", "member"), None),
            P("space", ("parts", "member"), None),
            P("parts"),
            P(),
        ),
        out_specs=(P(("parts", "space"), None), P("space", ("parts", "member"), None)),
        check_vma=False,
    )
```

```python
import functools

import jax
import jax.numpy as jnp
from jax import lax
from jax.experimental import pallas as pl
from jax.experimental.pallas import tpu as pltpu
from jax.sharding import PartitionSpec as P

F32 = jnp.float32
BF16 = jnp.bfloat16
GROUPS = 4
ANY = pl.BlockSpec(memory_space=pl.ANY)
INVMEM = pl.BlockSpec(memory_space=pltpu.VMEM)
INSMEM = pl.BlockSpec(memory_space=pltpu.SMEM)


def split(x):
    high = x.astype(BF16)
    return high, (x - high.astype(F32)).astype(BF16)


def dot3(stack, b, dims):
    one = functools.partial(lax.dot_general, dimension_numbers=(dims, ((), ())), preferred_element_type=F32)
    rows = stack.shape[0] // 2
    both = one(stack, b[0])
    return both[:rows] + (one(stack[:rows], b[1]) + both[rows:])


def params(mebibytes):
    return pltpu.CompilerParams(vmem_limit_bytes=mebibytes * 1024 * 1024)


def hbm(*arrays):
    return [pltpu.with_memory_space_constraint(a, pltpu.HBM) for a in arrays]


def vmem(*arrays):
    return [pltpu.with_memory_space_constraint(a, pltpu.VMEM) for a in arrays]


def pick(choice, side):
    if isinstance(choice, tuple):
        return pl.multiple_of(jnp.where(side == 0, choice[0], choice[1]), 128)
    return choice


def cut_kernel(first, columns, side_ref, src, *refs):
    *outs, stage, sems = refs
    rows = stage.shape[0] // GROUPS
    start = pick(first, side_ref[0])
    outward = []
    inward = [
        pltpu.make_async_copy(src.at[pl.ds(start + g * rows, rows)], stage.at[pl.ds(g * rows, rows)], sems.at[0, g])
        for g in range(GROUPS)
    ]
    for copy in inward:
        copy.start()
    for g in range(GROUPS):
        inward[g].wait()
        part = pl.ds(g * rows, rows)
        for k, (out, column) in enumerate(zip(outs, columns)):
            at = pl.ds(column_of(column, side_ref), out.shape[2])
            outward.append(pltpu.make_async_copy(stage.at[part, :, at], out.at[part], sems.at[1 + k, g]))
            outward[-1].start()
    for copy in outward:
        copy.wait()


def cut(name, side, array, first, rows, parts):
    columns = array.shape[2]
    return pl.pallas_call(
        functools.partial(cut_kernel, first, [column for column, _ in parts]),
        in_specs=[INSMEM, ANY],
        out_specs=[ANY] * len(parts),
        out_shape=[pltpu.HBM((rows, 1, n), F32) for _, n in parts],
        scratch_shapes=[
            pltpu.VMEM((rows, 1, columns), F32),
            pltpu.SemaphoreType.DMA((1 + len(parts), GROUPS)),
        ],
        compiler_params=params(8),
        name=name,
    )(side, *hbm(array))


def column_of(column, side_ref):
    if isinstance(column, tuple):
        return pl.multiple_of(jnp.where(side_ref[1] == 1, column[0], column[1]), 128)
    return column


def cross_parts(columns):
    half, quarter = columns // 2, columns // 4
    return [(0, half), (half, quarter), ((half, 0), half), (3 * quarter, quarter)]


def cross_send(parts):
    def send(part, numbers, ends):
        pairs = []
        for k in range(3):
            for direction, number in ((0, k), (1, 2 - k)):
                if number in numbers:
                    pairs.append(ends(k)[direction])
        return lax.ppermute(part, "space", pairs)

    to_partner = lambda k: ((2 * k + 1, 2 * k), (2 * k + 2, 2 * k + 3))
    onward = lambda k: ((2 * k, 2 * k + 2), (2 * k + 3, 2 * k + 1))
    direct = lambda k: ((2 * k + 1, 2 * k + 2), (2 * k + 2, 2 * k + 1))
    relayed = [send(part, numbers, to_partner) for part, numbers in zip(parts[:2], ((0, 1), (0, 2)))]
    straight = [send(part, numbers, direct) for part, numbers in zip(parts[2:], ((1, 2), (0, 2)))]
    a, b, c, d = lax.optimization_barrier((*relayed, *straight))
    relayed, straight = [a, b], [c, d]
    passed = [send(part, numbers, onward) for part, numbers in zip(relayed, ((0, 1), (0, 2)))]
    return passed + straight


def cross_received(base, columns):
    a, b, c, d = range(base, base + 4)
    q = columns // 4
    return ((2, (c, 0), (a, 0)), (2, (c, q), (a, q)), (1, (c, 0), (b, 0)), (1, (c, q), (d, 0)))


def area(ref, row, rows, columns):
    return ref.at[pl.ds(row, rows), 0, columns] if len(ref.shape) == 3 else ref.at[pl.ds(row, rows), columns]


def weight_kernel(nblocks, band_ref, high_ref, low_ref):
    pair = pl.program_id(0)
    width = band_ref.shape[2]
    zero = jnp.zeros((width, width), F32)
    for o in range(2):
        for i in range(4):
            j = i - o
            value = band_ref[o, j] if 0 <= j <= 2 else zero
            if (o, j) == (0, 0):
                value = jnp.where(pair > 0, value, 0.0)
            if (o, j) == (1, 2):
                value = jnp.where(pair < nblocks // 2 - 1, value, 0.0)
            high, low = split(value)
            rows, columns = slice(o * width, (o + 1) * width), slice(i * width, (i + 1) * width)
            high_ref[0, rows, columns] = high
            low_ref[0, rows, columns] = low


def row_weights(band):
    nblocks, _, width, _ = band.shape
    shape = pltpu.HBM((nblocks // 2, 2 * width, 4 * width), BF16)
    out_spec = pl.BlockSpec((1, 2 * width, 4 * width), lambda t: (t, 0, 0))
    return pl.pallas_call(
        functools.partial(weight_kernel, nblocks),
        grid=(nblocks // 2,),
        in_specs=[pl.BlockSpec((2, 3, width, width), lambda t: (t, 0, 0, 0))],
        out_specs=(out_spec, out_spec),
        out_shape=(shape, shape),
        name="row_weights",
    )(*hbm(band))


def blur_kernel(plan, *refs):
    pieces, narrays, extra, final, split_out, units, groups = plan
    side_ref, refs = refs[0], refs[1:]
    arrays = refs[:narrays]
    band_ref, high_ref, low_ref, extra_ref = refs[narrays : narrays + 4]
    rest = refs[narrays + 4 :]
    if final:
        weights_ref, rest = rest[0], rest[1:]
        all_weights = weights_ref[0]
        for k in range(1, weights_ref.shape[0]):
            all_weights += weights_ref[k]
        row_shape = (1, 2 * band_ref.shape[2])
        share = jnp.full(row_shape, weights_ref[side_ref[3]]) / jnp.full(row_shape, all_weights)
    nouts = len(groups) + 1 if final else 1 + len(split_out)
    outs = rest[:nouts]
    field, a_both, y_both, whigh, wlow, other = rest[nouts : nouts + 6]
    *results, in_sems, late_sems, out_sems = rest[nouts + 6 :]

    side = side_ref[0]
    nout, _, width, _ = band_ref.shape
    columns = field.shape[1]
    step = columns // GROUPS
    pairs = step // (2 * width)
    inside, late = [], {}

    def copy_in(u, k, place):
        _, row, rows, to = pieces[k]
        which, column = place
        start, stop = units[u]
        return pltpu.make_async_copy(
            area(arrays[which], pick(row, side), rows, pl.ds(column, stop - start)),
            field.at[pl.ds(pick(to, side), rows), pl.ds(start, stop - start)],
            in_sems.at[u, k],
        )

    def start_in(u, k):
        source = pieces[k][0]
        if isinstance(source, int):
            copy = copy_in(u, k, (source, units[u][0]))
        elif len(source[u]) == 2:
            copy = copy_in(u, k, source[u])
        else:
            number, this, other_one = source[u]
            pl.when(side_ref[2] == number)(copy_in(u, k, this).start)
            pl.when(side_ref[2] != number)(copy_in(u, k, other_one).start)
            return copy_in(u, k, other_one)
        copy.start()
        return copy

    for g in groups:
        at = pl.ds(g * step, step)
        some = pl.ds(g * pairs, pairs)
        late[g] = [
            pltpu.make_async_copy(high_ref.at[some], whigh.at[some], late_sems.at[g, 0]),
            pltpu.make_async_copy(low_ref.at[some], wlow.at[some], late_sems.at[g, 1]),
            pltpu.make_async_copy(
                area(extra_ref, pick(extra, side), other.shape[0], at), other.at[:, at], late_sems.at[g, 2]
            ),
        ]
    waiting = list(groups)
    for u in range(len(units)):
        inside.append([start_in(u, k) for k in range(len(pieces))])
        if u > 0 and waiting:
            for copy in late[waiting.pop(0)]:
                copy.start()
    for g in waiting:
        for copy in late[g]:
            copy.start()

    blocks = [(i, min(2, nout - i)) for i in range(0, nout, 2)]
    total = nout * width
    a_both[...] = jnp.zeros_like(a_both)
    for first, n in blocks:
        for i in range(n):
            for j in range(3):
                for part, value in enumerate(split(band_ref[first + i, j])):
                    row = (2 * first + part * n + i) * width
                    a_both[row : row + width, (i + j) * width : (i + j + 1) * width] = value
    y_both[:, :width] = jnp.zeros((2 * total, width), BF16)
    y_both[:, columns + width :] = jnp.zeros((2 * total, width), BF16)

    def columns_pass(u):
        for copy in inside[u]:
            copy.wait()
        for i in range(units[u][0] // (2 * width), units[u][1] // (2 * width)):
            at = slice(i * 2 * width, (i + 1) * 2 * width)
            to = slice((2 * i + 1) * width, (2 * i + 3) * width)
            for first, n in blocks:
                a = a_both[2 * first * width : 2 * (first + n) * width, : (n + 2) * width]
                y = dot3(a, split(field[first * width : (first + n + 2) * width, at]), ((1,), (0,)))
                for part, value in enumerate(split(y)):
                    row = part * total + first * width
                    y_both[row : row + n * width, to] = value

    def rows_pass(g):
        for copy in late[g]:
            copy.wait()
        for t in range(g * pairs, (g + 1) * pairs):
            source = slice(t * 2 * width, (t + 2) * 2 * width)
            at = slice(t * 2 * width, (t + 1) * 2 * width)
            value = dot3(y_both[:, source], (whigh[t], wlow[t]), ((1,), (1,)))
            if final:
                results[0][:, at] = value
                results[1][:, at] = share * jnp.log(other[:, at] * value)
            else:
                results[0][:, at] = other[:, at] / value
        at = pl.ds(g * step, step)
        targets = [outs[-1].at[:, pl.ds((g - groups[0]) * step, step)]] + ([outs[groups.index(g)]] if final else [])
        copies = [
            pltpu.make_async_copy(src.at[:, at], dst, out_sems.at[g, k])
            for k, (src, dst) in enumerate(zip(results, targets))
        ]
        for k, (start, stop) in enumerate(split_out):
            if g * step < stop <= (g + 1) * step:
                part = results[0].at[:, pl.ds(start, stop - start)]
                copies.append(pltpu.make_async_copy(part, outs[k], out_sems.at[GROUPS, k]))
        for copy in copies:
            copy.start()
        return copies

    going = []
    waiting = list(groups)
    for u, (_, stop) in enumerate(units):
        columns_pass(u)
        while waiting and u > 0 and (stop == columns or (waiting[0] + 1) * step + width <= stop):
            going += rows_pass(waiting.pop(0))
    for copy in going:
        copy.wait()


def blur(
    name, side, arrays, pieces, bands, weights, other, extra,
    map_weights=None, pin=True, split_out=(), units=None, groups=tuple(range(GROUPS)),
):
    nout, _, width, _ = bands.shape
    npairs = weights[0].shape[0]
    columns = npairs * 2 * width
    rows, depth = nout * width, (nout + 2) * width
    final = map_weights is not None
    nouts = 2 if final else 1
    kind = pltpu.HBM if pin else jax.ShapeDtypeStruct
    step = columns // GROUPS
    units = tuple((g * step, (g + 1) * step) for g in range(GROUPS)) if units is None else units
    shapes = [kind((rows, step), F32)] * (len(groups) if final else 0)
    shapes += [pltpu.HBM((rows, stop - start), F32) for start, stop in split_out]
    shapes.append(pltpu.HBM((rows, len(groups) * step), F32))
    plan = (tuple(pieces), len(arrays), extra, final, split_out, units, groups)
    work = 3 * 2 * rows * columns * (depth + 4 * width)
    moved = 4 * (depth + 3 * rows) * columns + npairs * 2 * 2 * 8 * width * width
    size = 4 * columns * (depth + (1 + nouts) * rows) + 4 * rows * columns + npairs * 2 * 2 * 8 * width * width
    result = pl.pallas_call(
        functools.partial(blur_kernel, plan),
        in_specs=[INSMEM] + [ANY] * len(arrays) + [INVMEM, ANY, ANY, ANY] + [INSMEM] * final,
        out_specs=[ANY] * len(shapes),
        out_shape=shapes,
        scratch_shapes=[
            pltpu.VMEM((depth, columns), F32),
            pltpu.VMEM((2 * rows, min(depth, 4 * width)), BF16),
            pltpu.VMEM((2 * rows, columns + 2 * width), BF16),
            pltpu.VMEM((npairs, 2 * width, 4 * width), BF16),
            pltpu.VMEM((npairs, 2 * width, 4 * width), BF16),
            pltpu.VMEM((rows, columns), F32),
        ]
        + [pltpu.VMEM((rows, columns), F32)] * nouts
        + [
            pltpu.SemaphoreType.DMA((len(units), len(pieces))),
            pltpu.SemaphoreType.DMA((GROUPS, 3)),
            pltpu.SemaphoreType.DMA((GROUPS + 1, 2)),
        ],
        compiler_params=params(size // 2**20 + 6),
        cost_estimate=pl.CostEstimate(flops=work // 64, bytes_accessed=moved // 64, transcendentals=0),
        name=name,
    )(side, *arrays, bands, *hbm(*weights, other), *(hbm(map_weights) if final else []))
    return (result[:-1], result[-1]) if final else result if split_out else result[0]


def raw_kernel(fresh, first, side_ref, *refs):
    own, peer, m_ref = refs[:GROUPS], refs[GROUPS : 2 * GROUPS], refs[2 * GROUPS]
    raw_ref, quotient_ref, mass_ref, quotient, sems = refs[-5:]
    tile = raw_ref.shape[0]
    at = pl.program_id(0)
    slot = lax.rem(at, 2)

    def copy(step, slot):
        row = pl.multiple_of(pick(first, side_ref[0]) + step * tile, tile)
        return pltpu.make_async_copy(quotient.at[slot], area(quotient_ref, row, tile, slice(None)), sems.at[slot])

    @pl.when(at >= 2)
    def _():
        copy(at - 2, slot).wait()

    mass = 0.0
    for g in range(GROUPS):
        raw = jnp.exp(own[g][...] + peer[g][...])
        step = raw.shape[1]
        raw_ref[:, g * step : (g + 1) * step] = raw
        mass += jnp.sum(raw)
        quotient[slot, :, g * step : (g + 1) * step] = raw / m_ref[:, g * step : (g + 1) * step]
    before = 0.0 if fresh else refs[2 * GROUPS + 3][...]
    mass_ref[...] = mass + jnp.where(at == 0, before, mass_ref[...])
    copy(at, slot).start()

    @pl.when(at == pl.num_programs(0) - 1)
    def _():
        copy(at - 1, 1 - slot).wait()
        copy(at, slot).wait()


def raw_rows(name, side, row, t, peers, m, rows_here, so_far):
    fresh = so_far is None
    rows, columns = m.shape
    tile = 32
    starts = [r // tile for r in row]
    part = pl.BlockSpec((tile, columns), lambda i, at: (i, 0))
    group = pl.BlockSpec((tile, columns // GROUPS), lambda i, at: (i, 0))
    return pl.pallas_call(
        functools.partial(raw_kernel, fresh, row),
        grid_spec=pltpu.PrefetchScalarGridSpec(
            num_scalar_prefetch=1,
            grid=(rows // tile,),
            in_specs=[group] * (2 * GROUPS) + [part] + ([] if fresh else [ANY, ANY, INVMEM]),
            out_specs=(
                pl.BlockSpec((tile, columns), lambda i, at: (jnp.where(at[0] == 0, *starts) + i, 0)),
                ANY,
                INVMEM,
            ),
            scratch_shapes=[pltpu.VMEM((2, tile, columns), F32), pltpu.SemaphoreType.DMA((2,))],
        ),
        out_shape=(
            pltpu.VMEM((rows_here, columns), F32),
            pltpu.VMEM((rows_here, 1, columns), F32),
            jax.ShapeDtypeStruct((1, 128), F32),
        ),
        input_output_aliases={} if fresh else {2 * GROUPS + 2: 0, 2 * GROUPS + 3: 1},
        compiler_params=params(16),
        cost_estimate=pl.CostEstimate(flops=m.size // 16, bytes_accessed=m.size // 4, transcendentals=0),
        name=name,
    )(side, *t, *peers, m, *([] if fresh else vmem(*so_far[:2]) + [so_far[2]]))


def raw_only_kernel(side_ref, *refs):
    *logs, _, before_ref, raw_ref, mass_ref = refs
    parts = len(logs) // 2
    mass = 0.0
    for g in range(parts):
        raw = jnp.exp(logs[g][...] + logs[parts + g][...])
        step = raw.shape[1]
        raw_ref[:, g * step : (g + 1) * step] = raw
        mass += jnp.sum(raw)
    mass_ref[...] = mass + jnp.where(pl.program_id(0) == 0, before_ref[...], mass_ref[...])


def piece_spec(tile, columns, row, column):
    starts = [r // tile for r in row]
    return pl.BlockSpec((tile, columns), lambda i, at: (jnp.where(at[0] == 0, *starts) + i, column // columns))


def raw_only(name, side, row, column, t, peers, raw_all, mass):
    rows, step = t[0].shape
    columns = len(t) * step
    tile = 64
    group = pl.BlockSpec((tile, step), lambda i, at: (i, 0))
    return pl.pallas_call(
        raw_only_kernel,
        grid_spec=pltpu.PrefetchScalarGridSpec(
            num_scalar_prefetch=1,
            grid=(rows // tile,),
            in_specs=[group] * (2 * len(t)) + [ANY, INVMEM],
            out_specs=(piece_spec(tile, columns, row, column), INVMEM),
        ),
        out_shape=(pltpu.VMEM(raw_all.shape, F32), jax.ShapeDtypeStruct(mass.shape, F32)),
        input_output_aliases={2 * len(t) + 1: 0},
        compiler_params=params(16),
        cost_estimate=pl.CostEstimate(flops=rows * columns // 16, bytes_accessed=rows * columns // 4, transcendentals=0),
        name=name,
    )(side, *t, *peers, *vmem(raw_all), mass)


def quotient_kernel(first, column, side_ref, raw_ref, m_ref, _, quotient_ref, quotient, sems):
    tile, columns = raw_ref.shape
    at = pl.program_id(0)
    row = pick(first, side_ref[0])
    quotient[at] = raw_ref[...] / m_ref[...]
    copies = [
        pltpu.make_async_copy(
            quotient.at[k], area(quotient_ref, row + k * tile, tile, pl.ds(column, columns)), sems.at[k]
        )
        for k in range(quotient.shape[0])
    ]
    for k, copy in enumerate(copies):
        pl.when(at == k)(copy.start)

    @pl.when(at == len(copies) - 1)
    def _():
        for copy in copies:
            copy.wait()


def quotient_part(name, side, row, column, raw_all, m, quotient_all):
    rows, columns = m.shape
    tile = 64
    return pl.pallas_call(
        functools.partial(quotient_kernel, row, column),
        grid_spec=pltpu.PrefetchScalarGridSpec(
            num_scalar_prefetch=1,
            grid=(rows // tile,),
            in_specs=[
                piece_spec(tile, columns, row, column),
                pl.BlockSpec((tile, columns), lambda i, at: (i, 0)),
                ANY,
            ],
            out_specs=ANY,
            scratch_shapes=[
                pltpu.VMEM((rows // tile, tile, columns), F32),
                pltpu.SemaphoreType.DMA((rows // tile,)),
            ],
        ),
        out_shape=pltpu.VMEM(quotient_all.shape, F32),
        input_output_aliases={3: 0},
        compiler_params=params(16),
        cost_estimate=pl.CostEstimate(flops=rows * columns // 16, bytes_accessed=rows * columns // 4, transcendentals=0),
        name=name,
    )(side, *vmem(raw_all), *hbm(m), *vmem(quotient_all))


def sum_kernel(a_ref, b_ref, out_ref):
    out_ref[...] = a_ref[...] + b_ref[...]


def mass_parts(mass, quotient):
    count = lax.axis_size("space")
    if count & (count - 1):
        return [lax.psum(mass, "space")], quotient
    parts = [mass]
    for bit in range(count.bit_length() - 1):
        if len(parts) == 2:
            if bit == 1:
                parts[1], quotient = lax.optimization_barrier((parts[1], quotient))
            parts = [
                pl.pallas_call(
                    sum_kernel,
                    in_specs=[INVMEM, INVMEM],
                    out_specs=INVMEM,
                    out_shape=jax.ShapeDtypeStruct(mass.shape, F32),
                    compiler_params=params(1),
                    name="mass",
                )(*parts)
            ]
        parts.append(lax.ppermute(parts[0], "space", [(i, i ^ (1 << bit)) for i in range(count)]))
    return parts, quotient


def output_kernel(total, raw_ref, quotient_ref, *refs):
    *masses, barycenter_ref, scaling_ref = refs
    mass = masses[0][...]
    for part in masses[1:]:
        mass += part[...]
    scale = total / mass
    width = scale.shape[1]
    for b in range(raw_ref.shape[1] // width):
        at = slice(b * width, (b + 1) * width)
        barycenter_ref[:, at] = raw_ref[:, at] * scale
    scaling_ref[...] = quotient_ref[...] * scale.reshape(1, 1, width)


def outputs(raw, quotient, masses):
    rows, columns = raw.shape
    tile = 64
    flat = pl.BlockSpec((tile, columns), lambda i: (i, 0))
    deep = pl.BlockSpec((tile,) + quotient.shape[1:], lambda i: (i, 0, 0))
    return pl.pallas_call(
        functools.partial(output_kernel, float(columns * columns)),
        grid=(rows // tile,),
        in_specs=[flat, deep] + [INVMEM] * len(masses),
        out_specs=(flat, deep),
        out_shape=(jax.ShapeDtypeStruct(raw.shape, F32), jax.ShapeDtypeStruct(quotient.shape, F32)),
        compiler_params=params(16),
        name="outputs",
    )(*vmem(raw, quotient), *masses)


def local(densities, scaling, weights, band):
    rows_here, maps_here, cols_all = densities.shape
    _, _, width, _ = band.shape
    nlocal = rows_here // width
    inner = max(nlocal - 2, 0)
    place = lax.axis_index("space")
    count = lax.axis_size("space")
    assert maps_here == 1 and lax.axis_size("member") == 2 and count % 2 == 0

    odd = place & 1
    middle = place >> 1
    numbers = [jnp.where(odd == 1, middle, 3 - middle), jnp.where(odd == 1, 2 - middle, middle - 1)]
    side = jnp.stack([odd, *numbers, lax.axis_index("member")])
    spread = count == 8 and nlocal > 1
    last = rows_here - width
    cross_row, near_row = (0, last), (last, 0)
    both = lambda pairs: pairs + [(b, a) for a, b in pairs]
    cross = functools.partial(
        lax.ppermute, axis_name="space", perm=both([(i, i + 1) for i in range(1, count - 1, 2)])
    )
    near = functools.partial(lax.ppermute, axis_name="space", perm=both([(i, i + 1) for i in range(0, count, 2)]))
    swap = functools.partial(lax.ppermute, axis_name="member", perm=[(0, 1), (1, 0)])

    def choose(choice):
        return jnp.where(odd == 0, *[c // width for c in choice]).astype(jnp.int32)

    near_columns = [(0, cols_all * 3 // 4), (cols_all * 3 // 4, cols_all // 4)]
    if spread:
        cross1 = cross_send(cut("cut_cross", side, scaling, cross_row, width, cross_parts(cols_all)))
    else:
        cross1 = [cross(cut("cut_cross", side, scaling, cross_row, width, [(0, cols_all)])[0])]
    near1 = [near(part) for part in cut("cut_near", side, scaling, near_row, width, near_columns)]

    def near1_at(base):
        quarter = cols_all // GROUPS
        return tuple((base, g * quarter) if g < GROUPS - 1 else (base + 1, 0) for g in range(GROUPS))

    wts = row_weights(band)
    mine = place * nlocal
    band_at = lambda block, blocks: lax.dynamic_slice_in_dim(band, mine + block, blocks, 0)

    if inner > 0:
        inner_bands = band_at(1, inner)
        ratio_inner = blur(
            "ratio_inner", side, hbm(scaling), [(0, 0, rows_here, 0)], inner_bands, wts, densities, width
        )
        *cross1, ratio_inner = lax.optimization_barrier((*cross1, ratio_inner))
    if nlocal == 1:
        pieces = [(0, 0, width, width), (1, 0, width, (0, 2 * width)), (near1_at(2), 0, width, (2 * width, 0))]
        bands = band_at(0, 1)
        ratio = blur("ratio_only", side, [scaling, *cross1, *near1], pieces, bands, wts, densities, 0)
        cross2, near2 = cross(ratio), near(ratio)
    else:
        two = rows_here - 2 * width
        halo = cross_received(1, cols_all) if spread else 1
        pieces = [(0, (0, two), 2 * width, (width, 0)), (halo, 0, width, (0, 2 * width))]
        cross_bands = band_at(choose(cross_row), 1)
        ratio_cross = blur(
            "ratio_cross", side, hbm(scaling, *cross1), pieces, cross_bands, wts, densities, cross_row
        )
        ratio_cross, *near1 = lax.optimization_barrier((ratio_cross, *near1))
        cross2 = cross(ratio_cross)
        half, more = cols_all // 2, 2 * width
        pieces = [(0, (two, 0), 2 * width, (0, width)), (near1_at(1), 0, width, (2 * width, 0))]
        near_bands = band_at(choose(near_row), 1)
        *parts, ratio_near = blur(
            "ratio_near", side, hbm(scaling, *near1), pieces, near_bands, wts, densities, near_row,
            split_out=((0, half + more), (half + more, cols_all)),
        )
        near2 = [near(part) for part in parts]

    def finish(name, arrays, pieces, bands, row, weights, state):
        t, m = blur("logs_" + name, side, arrays, pieces, bands, wts, scaling, row, weights)
        return raw_rows(
            "raw_" + name, side, row, hbm(*t), [swap(part) for part in t], *hbm(m), rows_here, state
        )

    if nlocal == 1:
        pieces = [(0, 0, width, width), (1, 0, width, (0, 2 * width)), (2, 0, width, (2 * width, 0))]
        state = finish("only", [ratio, cross2, near2], pieces, bands, (0, 0), weights, None)
    else:
        state = None
        beside, beside_row = ratio_near, (0, 0)
        if inner > 0:
            arrays = hbm(ratio_inner, ratio_cross, ratio_near)
            pieces = [(0, 0, inner * width, width), (1, 0, width, cross_row), (2, 0, width, near_row)]
            state = finish("inner", arrays, pieces, inner_bands, (width, width), weights, None)
            weights, state = lax.optimization_barrier((weights, state))
            beside, beside_row = ratio_inner, (0, (inner - 1) * width)
        arrays = hbm(ratio_cross, beside) + [cross2]
        pieces = [(0, 0, width, width), (1, beside_row, width, (2 * width, 0)), (2, 0, width, (0, 2 * width))]
        state = finish("cross", arrays, pieces, cross_bands, cross_row, weights, state)
        weights, state = lax.optimization_barrier((weights, state))
        if inner == 0:
            beside = ratio_cross
        raw, quotient, mass = state
        step = cols_all // GROUPS
        first_units = tuple((g * step, (g + 1) * step) for g in range(GROUPS // 2)) + ((half, half + more),)
        later_units = ((half - more, half + more), (half + more, half + step)) + tuple(
            (g * step, (g + 1) * step) for g in range(GROUPS // 2 + 1, GROUPS)
        )
        plans = [
            ("near_first", first_units, 0, [(2, start) for start, _ in first_units]),
            ("near_later", later_units, half, [(2, half - more)] + [(3, a - half - more) for a, _ in later_units[1:]]),
        ]
        for part, (name, units, column, halo) in enumerate(plans):
            arrays = hbm(ratio_near, beside) + near2[: part + 1]
            pieces = [
                (0, 0, width, width),
                (1, beside_row[::-1], width, (0, 2 * width)),
                (tuple(halo), 0, width, (2 * width, 0)),
            ]
            groups = tuple(g for g in range(GROUPS) if column <= g * step < column + half)
            t, m = blur(
                "logs_" + name, side, arrays, pieces, near_bands, wts, scaling, near_row, weights,
                pin=False, units=units, groups=groups,
            )
            raw, mass = raw_only("raw_" + name, side, near_row, column, t, [swap(part) for part in t], raw, mass)
            quotient = quotient_part("quotient_" + name, side, near_row, column, raw, m, quotient)
            if part == 0:
                weights, raw, mass, quotient = lax.optimization_barrier((weights, raw, mass, quotient))
        state = raw, quotient, mass

    raw, quotient, mass = state
    masses, quotient = mass_parts(mass, quotient)
    barycenter, new_scaling = outputs(raw, quotient.reshape(rows_here, cols_all // width, width), masses)
    return barycenter, new_scaling.reshape(rows_here, 1, cols_all)


def solution(mesh):
    return jax.shard_map(
        local,
        mesh=mesh,
        in_specs=(
            P("space", ("parts", "member"), None),
            P("space", ("parts", "member"), None),
            P("parts"),
            P(),
        ),
        out_specs=(P(("parts", "space"), None), P("space", ("parts", "member"), None)),
        check_vma=False,
    )
```

```python
import functools

import jax
import jax.numpy as jnp
from jax import lax
from jax.experimental import pallas as pl
from jax.experimental.pallas import tpu as pltpu
from jax.sharding import PartitionSpec as P

F32 = jnp.float32
BF16 = jnp.bfloat16
GROUPS = 4
ANY = pl.BlockSpec(memory_space=pl.ANY)
INVMEM = pl.BlockSpec(memory_space=pltpu.VMEM)
INSMEM = pl.BlockSpec(memory_space=pltpu.SMEM)


def split(x):
    high = x.astype(BF16)
    return high, (x - high.astype(F32)).astype(BF16)


def dot3(stack, b, dims):
    one = functools.partial(lax.dot_general, dimension_numbers=(dims, ((), ())), preferred_element_type=F32)
    rows = stack.shape[0] // 2
    both = one(stack, b[0])
    return both[:rows] + (one(stack[:rows], b[1]) + both[rows:])


def params(mebibytes):
    return pltpu.CompilerParams(vmem_limit_bytes=mebibytes * 1024 * 1024)


def hbm(*arrays):
    return [pltpu.with_memory_space_constraint(a, pltpu.HBM) for a in arrays]


def vmem(*arrays):
    return [pltpu.with_memory_space_constraint(a, pltpu.VMEM) for a in arrays]


def pick(choice, side):
    if isinstance(choice, tuple):
        return pl.multiple_of(jnp.where(side == 0, choice[0], choice[1]), 128)
    return choice


def cut_kernel(first, columns, side_ref, src, *refs):
    *outs, stage, sems = refs
    rows = stage.shape[0] // GROUPS
    start = pick(first, side_ref[0])
    outward = []
    inward = [
        pltpu.make_async_copy(src.at[pl.ds(start + g * rows, rows)], stage.at[pl.ds(g * rows, rows)], sems.at[0, g])
        for g in range(GROUPS)
    ]
    for copy in inward:
        copy.start()
    for g in range(GROUPS):
        inward[g].wait()
        part = pl.ds(g * rows, rows)
        for k, (out, column) in enumerate(zip(outs, columns)):
            at = pl.ds(column_of(column, side_ref), out.shape[2])
            outward.append(pltpu.make_async_copy(stage.at[part, :, at], out.at[part], sems.at[1 + k, g]))
            outward[-1].start()
    for copy in outward:
        copy.wait()


def cut(name, side, array, first, rows, parts):
    columns = array.shape[2]
    return pl.pallas_call(
        functools.partial(cut_kernel, first, [column for column, _ in parts]),
        in_specs=[INSMEM, ANY],
        out_specs=[ANY] * len(parts),
        out_shape=[pltpu.HBM((rows, 1, n), F32) for _, n in parts],
        scratch_shapes=[
            pltpu.VMEM((rows, 1, columns), F32),
            pltpu.SemaphoreType.DMA((1 + len(parts), GROUPS)),
        ],
        compiler_params=params(8),
        name=name,
    )(side, *hbm(array))


def column_of(column, side_ref):
    if isinstance(column, tuple):
        return pl.multiple_of(jnp.where(side_ref[1] == 1, column[0], column[1]), 128)
    return column


def cross_parts(columns):
    half, quarter = columns // 2, columns // 4
    return [(0, half), (half, quarter), ((half, 0), half), (3 * quarter, quarter)]


def cross_send(parts):
    def send(part, numbers, ends):
        pairs = []
        for k in range(3):
            for direction, number in ((0, k), (1, 2 - k)):
                if number in numbers:
                    pairs.append(ends(k)[direction])
        return lax.ppermute(part, "space", pairs)

    to_partner = lambda k: ((2 * k + 1, 2 * k), (2 * k + 2, 2 * k + 3))
    onward = lambda k: ((2 * k, 2 * k + 2), (2 * k + 3, 2 * k + 1))
    direct = lambda k: ((2 * k + 1, 2 * k + 2), (2 * k + 2, 2 * k + 1))
    relayed = [send(part, numbers, to_partner) for part, numbers in zip(parts[:2], ((0, 1), (0, 2)))]
    straight = [send(part, numbers, direct) for part, numbers in zip(parts[2:], ((1, 2), (0, 2)))]
    a, b, c, d = lax.optimization_barrier((*relayed, *straight))
    relayed, straight = [a, b], [c, d]
    passed = [send(part, numbers, onward) for part, numbers in zip(relayed, ((0, 1), (0, 2)))]
    return passed + straight


def cross_received(base, columns):
    a, b, c, d = range(base, base + 4)
    q = columns // 4
    return ((2, (c, 0), (a, 0)), (2, (c, q), (a, q)), (1, (c, 0), (b, 0)), (1, (c, q), (d, 0)))


def area(ref, row, rows, columns):
    return ref.at[pl.ds(row, rows), 0, columns] if len(ref.shape) == 3 else ref.at[pl.ds(row, rows), columns]


def weight_kernel(nblocks, band_ref, high_ref, low_ref):
    pair = pl.program_id(0)
    width = band_ref.shape[2]
    zero = jnp.zeros((width, width), F32)
    for o in range(2):
        for i in range(4):
            j = i - o
            value = band_ref[o, j] if 0 <= j <= 2 else zero
            if (o, j) == (0, 0):
                value = jnp.where(pair > 0, value, 0.0)
            if (o, j) == (1, 2):
                value = jnp.where(pair < nblocks // 2 - 1, value, 0.0)
            high, low = split(value)
            rows, columns = slice(o * width, (o + 1) * width), slice(i * width, (i + 1) * width)
            high_ref[0, rows, columns] = high
            low_ref[0, rows, columns] = low


def row_weights(band):
    nblocks, _, width, _ = band.shape
    shape = pltpu.HBM((nblocks // 2, 2 * width, 4 * width), BF16)
    out_spec = pl.BlockSpec((1, 2 * width, 4 * width), lambda t: (t, 0, 0))
    return pl.pallas_call(
        functools.partial(weight_kernel, nblocks),
        grid=(nblocks // 2,),
        in_specs=[pl.BlockSpec((2, 3, width, width), lambda t: (t, 0, 0, 0))],
        out_specs=(out_spec, out_spec),
        out_shape=(shape, shape),
        name="row_weights",
    )(*hbm(band))


def blur_kernel(plan, *refs):
    pieces, narrays, extra, final, split_out, units, groups, begun_at = plan
    side_ref, refs = refs[0], refs[1:]
    arrays = refs[:narrays]
    band_ref, high_ref, low_ref, extra_ref = refs[narrays : narrays + 4]
    rest = refs[narrays + 4 :]
    if begun_at is not None:
        begun_ref, rest = rest[0], rest[1:]
    if final:
        weights_ref, rest = rest[0], rest[1:]
        all_weights = weights_ref[0]
        for k in range(1, weights_ref.shape[0]):
            all_weights += weights_ref[k]
        row_shape = (1, 2 * band_ref.shape[2])
        share = jnp.full(row_shape, weights_ref[side_ref[3]]) / jnp.full(row_shape, all_weights)
    nouts = len(groups) + 1 if final else 1 + len(split_out)
    outs = rest[:nouts]
    field, a_both, y_both, whigh, wlow, other = rest[nouts : nouts + 6]
    *results, in_sems, late_sems, out_sems = rest[nouts + 6 :]
    if begun_at is not None:
        *results, begun = results

    side = side_ref[0]
    nout, _, width, _ = band_ref.shape
    columns = field.shape[1]
    step = columns // GROUPS
    pairs = step // (2 * width)
    inside, late = [], {}

    def copy_in(u, k, place):
        _, row, rows, to = pieces[k]
        which, column = place
        start, stop = units[u]
        return pltpu.make_async_copy(
            area(arrays[which], pick(row, side), rows, pl.ds(column, stop - start)),
            field.at[pl.ds(pick(to, side), rows), pl.ds(start, stop - start)],
            in_sems.at[u, k],
        )

    def start_in(u, k):
        source = pieces[k][0]
        if isinstance(source, int):
            copy = copy_in(u, k, (source, units[u][0]))
        elif len(source[u]) == 2:
            copy = copy_in(u, k, source[u])
        else:
            number, this, other_one = source[u]
            pl.when(side_ref[2] == number)(copy_in(u, k, this).start)
            pl.when(side_ref[2] != number)(copy_in(u, k, other_one).start)
            return copy_in(u, k, other_one)
        copy.start()
        return copy

    for g in groups:
        at = pl.ds(g * step, step)
        some = pl.ds(g * pairs, pairs)
        late[g] = [
            pltpu.make_async_copy(high_ref.at[some], whigh.at[some], late_sems.at[g, 0]),
            pltpu.make_async_copy(low_ref.at[some], wlow.at[some], late_sems.at[g, 1]),
            pltpu.make_async_copy(
                area(extra_ref, pick(extra, side), other.shape[0], at), other.at[:, at], late_sems.at[g, 2]
            ),
        ]
    waiting = list(groups)
    for u in range(len(units)):
        inside.append([start_in(u, k) for k in range(len(pieces))])
        if begun_at is not None:
            start, stop = units[u]
            inside[u].append(
                pltpu.make_async_copy(
                    begun_ref.at[:, pl.ds(start - begun_at, stop - start)],
                    begun.at[:, pl.ds(start, stop - start)],
                    in_sems.at[u, len(pieces)],
                )
            )
            inside[u][-1].start()
        if u > 0 and waiting:
            for copy in late[waiting.pop(0)]:
                copy.start()
    for g in waiting:
        for copy in late[g]:
            copy.start()

    blocks = [(i, min(2, nout - i)) for i in range(0, nout, 2)]
    total = nout * width
    if begun_at is None:
        a_both[...] = jnp.zeros_like(a_both)
    else:
        for part, value in enumerate(split(jnp.where(side == 0, band_ref[0, 2], band_ref[0, 0]))):
            a_both[part * width : (part + 1) * width, :] = value
    for first, n in blocks if begun_at is None else ():
        for i in range(n):
            for j in range(3):
                for part, value in enumerate(split(band_ref[first + i, j])):
                    row = (2 * first + part * n + i) * width
                    a_both[row : row + width, (i + j) * width : (i + j + 1) * width] = value
    y_both[:, :width] = jnp.zeros((2 * total, width), BF16)
    y_both[:, columns + width :] = jnp.zeros((2 * total, width), BF16)

    def columns_pass(u):
        for copy in inside[u]:
            copy.wait()
        for i in range(units[u][0] // (2 * width), units[u][1] // (2 * width)):
            at = slice(i * 2 * width, (i + 1) * 2 * width)
            to = slice((2 * i + 1) * width, (2 * i + 3) * width)
            for first, n in blocks:
                k = width if begun_at is not None else (n + 2) * width
                a = a_both[2 * first * width : 2 * (first + n) * width, :k]
                y = dot3(a, split(field[first * width : first * width + k, at]), ((1,), (0,)))
                if begun_at is not None:
                    y += begun[:, at]
                for part, value in enumerate(split(y)):
                    row = part * total + first * width
                    y_both[row : row + n * width, to] = value

    def rows_pass(g):
        for copy in late[g]:
            copy.wait()
        for t in range(g * pairs, (g + 1) * pairs):
            source = slice(t * 2 * width, (t + 2) * 2 * width)
            at = slice(t * 2 * width, (t + 1) * 2 * width)
            value = dot3(y_both[:, source], (whigh[t], wlow[t]), ((1,), (1,)))
            if final:
                results[0][:, at] = value
                results[1][:, at] = share * jnp.log(other[:, at] * value)
            else:
                results[0][:, at] = other[:, at] / value
        at = pl.ds(g * step, step)
        targets = [outs[-1].at[:, pl.ds((g - groups[0]) * step, step)]] + ([outs[groups.index(g)]] if final else [])
        copies = [
            pltpu.make_async_copy(src.at[:, at], dst, out_sems.at[g, k])
            for k, (src, dst) in enumerate(zip(results, targets))
        ]
        for k, (start, stop) in enumerate(split_out):
            if g * step < stop <= (g + 1) * step:
                part = results[0].at[:, pl.ds(start, stop - start)]
                copies.append(pltpu.make_async_copy(part, outs[k], out_sems.at[GROUPS, k]))
        for copy in copies:
            copy.start()
        return copies

    going = []
    waiting = list(groups)
    for u, (_, stop) in enumerate(units):
        columns_pass(u)
        while waiting and u > 0 and (stop == columns or (waiting[0] + 1) * step + width <= stop):
            going += rows_pass(waiting.pop(0))
    for copy in going:
        copy.wait()


def blur(
    name, side, arrays, pieces, bands, weights, other, extra,
    map_weights=None, pin=True, split_out=(), units=None, groups=tuple(range(GROUPS)), begun=None,
):
    nout, _, width, _ = bands.shape
    npairs = weights[0].shape[0]
    columns = npairs * 2 * width
    rows, depth = nout * width, (nout + 2) * width if begun is None else width
    final = map_weights is not None
    nouts = 2 if final else 1
    kind = pltpu.HBM if pin else jax.ShapeDtypeStruct
    step = columns // GROUPS
    units = tuple((g * step, (g + 1) * step) for g in range(GROUPS)) if units is None else units
    shapes = [kind((rows, step), F32)] * (len(groups) if final else 0)
    shapes += [pltpu.HBM((rows, stop - start), F32) for start, stop in split_out]
    shapes.append(pltpu.HBM((rows, len(groups) * step), F32))
    plan = (tuple(pieces), len(arrays), extra, final, split_out, units, groups, None if begun is None else begun[0])
    work = 3 * 2 * rows * columns * (depth + 4 * width)
    moved = 4 * (depth + 3 * rows) * columns + npairs * 2 * 2 * 8 * width * width
    size = 4 * columns * (depth + (1 + nouts) * rows) + 4 * rows * columns + npairs * 2 * 2 * 8 * width * width
    result = pl.pallas_call(
        functools.partial(blur_kernel, plan),
        in_specs=[INSMEM] + [ANY] * len(arrays) + [INVMEM, ANY, ANY, ANY] + [ANY] * (begun is not None) + [INSMEM] * final,
        out_specs=[ANY] * len(shapes),
        out_shape=shapes,
        scratch_shapes=[
            pltpu.VMEM((depth, columns), F32),
            pltpu.VMEM((2 * rows, min(depth, 4 * width)), BF16),
            pltpu.VMEM((2 * rows, columns + 2 * width), BF16),
            pltpu.VMEM((npairs, 2 * width, 4 * width), BF16),
            pltpu.VMEM((npairs, 2 * width, 4 * width), BF16),
            pltpu.VMEM((rows, columns), F32),
        ]
        + [pltpu.VMEM((rows, columns), F32)] * (nouts + (begun is not None))
        + [
            pltpu.SemaphoreType.DMA((len(units), len(pieces) + (begun is not None))),
            pltpu.SemaphoreType.DMA((GROUPS, 3)),
            pltpu.SemaphoreType.DMA((GROUPS + 1, 2)),
        ],
        compiler_params=params(size // 2**20 + 6),
        cost_estimate=pl.CostEstimate(flops=work // 64, bytes_accessed=moved // 64, transcendentals=0),
        name=name,
    )(side, *arrays, bands, *hbm(*weights, other), *(hbm(begun[1]) if begun else []), *(hbm(map_weights) if final else []))
    return (result[:-1], result[-1]) if final else result if split_out else result[0]


def begin_kernel(beside_row, start, side_ref, own_ref, beside_ref, band_ref, out_ref, field, a_both, result, sems):
    width, columns = result.shape
    side = side_ref[0]
    at = pl.ds(start, columns)
    copies = [
        pltpu.make_async_copy(area(own_ref, 0, width, at), field.at[pl.ds(pick((width, 0), side), width)], sems.at[0]),
        pltpu.make_async_copy(
            area(beside_ref, pick(beside_row, side), width, at),
            field.at[pl.ds(pick((0, width), side), width)],
            sems.at[1],
        ),
    ]
    for copy in copies:
        copy.start()
    for j in range(2):
        for part, value in enumerate(split(jnp.where(side == 0, band_ref[0, j], band_ref[0, j + 1]))):
            a_both[part * width : (part + 1) * width, j * width : (j + 1) * width] = value
    for copy in copies:
        copy.wait()
    for i in range(columns // (2 * width)):
        tile = slice(i * 2 * width, (i + 1) * 2 * width)
        result[:, tile] = dot3(a_both[...], split(field[:, tile]), ((1,), (0,)))
    copy = pltpu.make_async_copy(result, out_ref, sems.at[2])
    copy.start()
    copy.wait()


def begin(name, side, own, beside, beside_row, bands, start):
    width, columns = own.shape[0], own.shape[1] - start
    return pl.pallas_call(
        functools.partial(begin_kernel, beside_row, start),
        in_specs=[INSMEM, ANY, ANY, INVMEM],
        out_specs=ANY,
        out_shape=pltpu.HBM((width, columns), F32),
        scratch_shapes=[
            pltpu.VMEM((2 * width, columns), F32),
            pltpu.VMEM((2 * width, 2 * width), BF16),
            pltpu.VMEM((width, columns), F32),
            pltpu.SemaphoreType.DMA((3,)),
        ],
        compiler_params=params(12),
        cost_estimate=pl.CostEstimate(flops=width * columns, bytes_accessed=width * columns, transcendentals=0),
        name=name,
    )(side, *hbm(own, beside), bands)


def raw_kernel(fresh, first, side_ref, *refs):
    own, peer, m_ref = refs[:GROUPS], refs[GROUPS : 2 * GROUPS], refs[2 * GROUPS]
    raw_ref, quotient_ref, mass_ref, quotient, sems = refs[-5:]
    tile = raw_ref.shape[0]
    at = pl.program_id(0)
    slot = lax.rem(at, 2)

    def copy(step, slot):
        row = pl.multiple_of(pick(first, side_ref[0]) + step * tile, tile)
        return pltpu.make_async_copy(quotient.at[slot], area(quotient_ref, row, tile, slice(None)), sems.at[slot])

    @pl.when(at >= 2)
    def _():
        copy(at - 2, slot).wait()

    mass = 0.0
    for g in range(GROUPS):
        raw = jnp.exp(own[g][...] + peer[g][...])
        step = raw.shape[1]
        raw_ref[:, g * step : (g + 1) * step] = raw
        mass += jnp.sum(raw)
        quotient[slot, :, g * step : (g + 1) * step] = raw / m_ref[:, g * step : (g + 1) * step]
    before = 0.0 if fresh else refs[2 * GROUPS + 3][...]
    mass_ref[...] = mass + jnp.where(at == 0, before, mass_ref[...])
    copy(at, slot).start()

    @pl.when(at == pl.num_programs(0) - 1)
    def _():
        copy(at - 1, 1 - slot).wait()
        copy(at, slot).wait()


def raw_rows(name, side, row, t, peers, m, rows_here, so_far):
    fresh = so_far is None
    rows, columns = m.shape
    tile = 32
    starts = [r // tile for r in row]
    part = pl.BlockSpec((tile, columns), lambda i, at: (i, 0))
    group = pl.BlockSpec((tile, columns // GROUPS), lambda i, at: (i, 0))
    return pl.pallas_call(
        functools.partial(raw_kernel, fresh, row),
        grid_spec=pltpu.PrefetchScalarGridSpec(
            num_scalar_prefetch=1,
            grid=(rows // tile,),
            in_specs=[group] * (2 * GROUPS) + [part] + ([] if fresh else [ANY, ANY, INVMEM]),
            out_specs=(
                pl.BlockSpec((tile, columns), lambda i, at: (jnp.where(at[0] == 0, *starts) + i, 0)),
                ANY,
                INVMEM,
            ),
            scratch_shapes=[pltpu.VMEM((2, tile, columns), F32), pltpu.SemaphoreType.DMA((2,))],
        ),
        out_shape=(
            pltpu.VMEM((rows_here, columns), F32),
            pltpu.VMEM((rows_here, 1, columns), F32),
            jax.ShapeDtypeStruct((1, 128), F32),
        ),
        input_output_aliases={} if fresh else {2 * GROUPS + 2: 0, 2 * GROUPS + 3: 1},
        compiler_params=params(16),
        cost_estimate=pl.CostEstimate(flops=m.size // 16, bytes_accessed=m.size // 4, transcendentals=0),
        name=name,
    )(side, *t, *peers, m, *([] if fresh else vmem(*so_far[:2]) + [so_far[2]]))


def raw_only_kernel(side_ref, *refs):
    *logs, _, before_ref, raw_ref, mass_ref = refs
    parts = len(logs) // 2
    mass = 0.0
    for g in range(parts):
        raw = jnp.exp(logs[g][...] + logs[parts + g][...])
        step = raw.shape[1]
        raw_ref[:, g * step : (g + 1) * step] = raw
        mass += jnp.sum(raw)
    mass_ref[...] = mass + jnp.where(pl.program_id(0) == 0, before_ref[...], mass_ref[...])


def piece_spec(tile, columns, row, column):
    starts = [r // tile for r in row]
    return pl.BlockSpec((tile, columns), lambda i, at: (jnp.where(at[0] == 0, *starts) + i, column // columns))


def raw_only(name, side, row, column, t, peers, raw_all, mass):
    rows, step = t[0].shape
    columns = len(t) * step
    tile = 64
    group = pl.BlockSpec((tile, step), lambda i, at: (i, 0))
    return pl.pallas_call(
        raw_only_kernel,
        grid_spec=pltpu.PrefetchScalarGridSpec(
            num_scalar_prefetch=1,
            grid=(rows // tile,),
            in_specs=[group] * (2 * len(t)) + [ANY, INVMEM],
            out_specs=(piece_spec(tile, columns, row, column), INVMEM),
        ),
        out_shape=(pltpu.VMEM(raw_all.shape, F32), jax.ShapeDtypeStruct(mass.shape, F32)),
        input_output_aliases={2 * len(t) + 1: 0},
        compiler_params=params(16),
        cost_estimate=pl.CostEstimate(flops=rows * columns // 16, bytes_accessed=rows * columns // 4, transcendentals=0),
        name=name,
    )(side, *t, *peers, *vmem(raw_all), mass)


def quotient_kernel(first, column, side_ref, raw_ref, m_ref, _, quotient_ref, quotient, sems):
    tile, columns = raw_ref.shape
    at = pl.program_id(0)
    row = pick(first, side_ref[0])
    quotient[at] = raw_ref[...] / m_ref[...]
    copies = [
        pltpu.make_async_copy(
            quotient.at[k], area(quotient_ref, row + k * tile, tile, pl.ds(column, columns)), sems.at[k]
        )
        for k in range(quotient.shape[0])
    ]
    for k, copy in enumerate(copies):
        pl.when(at == k)(copy.start)

    @pl.when(at == len(copies) - 1)
    def _():
        for copy in copies:
            copy.wait()


def quotient_part(name, side, row, column, raw_all, m, quotient_all):
    rows, columns = m.shape
    tile = 64
    return pl.pallas_call(
        functools.partial(quotient_kernel, row, column),
        grid_spec=pltpu.PrefetchScalarGridSpec(
            num_scalar_prefetch=1,
            grid=(rows // tile,),
            in_specs=[
                piece_spec(tile, columns, row, column),
                pl.BlockSpec((tile, columns), lambda i, at: (i, 0)),
                ANY,
            ],
            out_specs=ANY,
            scratch_shapes=[
                pltpu.VMEM((rows // tile, tile, columns), F32),
                pltpu.SemaphoreType.DMA((rows // tile,)),
            ],
        ),
        out_shape=pltpu.VMEM(quotient_all.shape, F32),
        input_output_aliases={3: 0},
        compiler_params=params(16),
        cost_estimate=pl.CostEstimate(flops=rows * columns // 16, bytes_accessed=rows * columns // 4, transcendentals=0),
        name=name,
    )(side, *vmem(raw_all), *hbm(m), *vmem(quotient_all))


def sum_kernel(a_ref, b_ref, out_ref):
    out_ref[...] = a_ref[...] + b_ref[...]


def mass_parts(mass, quotient):
    count = lax.axis_size("space")
    if count & (count - 1):
        return [lax.psum(mass, "space")], quotient
    parts = [mass]
    for bit in range(count.bit_length() - 1):
        if len(parts) == 2:
            if bit == 1:
                parts[1], quotient = lax.optimization_barrier((parts[1], quotient))
            parts = [
                pl.pallas_call(
                    sum_kernel,
                    in_specs=[INVMEM, INVMEM],
                    out_specs=INVMEM,
                    out_shape=jax.ShapeDtypeStruct(mass.shape, F32),
                    compiler_params=params(1),
                    name="mass",
                )(*parts)
            ]
        parts.append(lax.ppermute(parts[0], "space", [(i, i ^ (1 << bit)) for i in range(count)]))
    return parts, quotient


def output_kernel(total, raw_ref, quotient_ref, *refs):
    *masses, barycenter_ref, scaling_ref = refs
    mass = masses[0][...]
    for part in masses[1:]:
        mass += part[...]
    scale = total / mass
    width = scale.shape[1]
    for b in range(raw_ref.shape[1] // width):
        at = slice(b * width, (b + 1) * width)
        barycenter_ref[:, at] = raw_ref[:, at] * scale
    scaling_ref[...] = quotient_ref[...] * scale.reshape(1, 1, width)


def outputs(raw, quotient, masses):
    rows, columns = raw.shape
    tile = 64
    flat = pl.BlockSpec((tile, columns), lambda i: (i, 0))
    deep = pl.BlockSpec((tile,) + quotient.shape[1:], lambda i: (i, 0, 0))
    return pl.pallas_call(
        functools.partial(output_kernel, float(columns * columns)),
        grid=(rows // tile,),
        in_specs=[flat, deep] + [INVMEM] * len(masses),
        out_specs=(flat, deep),
        out_shape=(jax.ShapeDtypeStruct(raw.shape, F32), jax.ShapeDtypeStruct(quotient.shape, F32)),
        compiler_params=params(16),
        name="outputs",
    )(*vmem(raw, quotient), *masses)


def local(densities, scaling, weights, band):
    rows_here, maps_here, cols_all = densities.shape
    _, _, width, _ = band.shape
    nlocal = rows_here // width
    inner = max(nlocal - 2, 0)
    place = lax.axis_index("space")
    count = lax.axis_size("space")
    assert maps_here == 1 and lax.axis_size("member") == 2 and count % 2 == 0

    odd = place & 1
    middle = place >> 1
    numbers = [jnp.where(odd == 1, middle, 3 - middle), jnp.where(odd == 1, 2 - middle, middle - 1)]
    side = jnp.stack([odd, *numbers, lax.axis_index("member")])
    spread = count == 8 and nlocal > 1
    last = rows_here - width
    cross_row, near_row = (0, last), (last, 0)
    both = lambda pairs: pairs + [(b, a) for a, b in pairs]
    cross = functools.partial(
        lax.ppermute, axis_name="space", perm=both([(i, i + 1) for i in range(1, count - 1, 2)])
    )
    near = functools.partial(lax.ppermute, axis_name="space", perm=both([(i, i + 1) for i in range(0, count, 2)]))
    swap = functools.partial(lax.ppermute, axis_name="member", perm=[(0, 1), (1, 0)])

    def choose(choice):
        return jnp.where(odd == 0, *[c // width for c in choice]).astype(jnp.int32)

    near_columns = [(0, cols_all * 3 // 4), (cols_all * 3 // 4, cols_all // 4)]
    if spread:
        cross1 = cross_send(cut("cut_cross", side, scaling, cross_row, width, cross_parts(cols_all)))
    else:
        cross1 = [cross(cut("cut_cross", side, scaling, cross_row, width, [(0, cols_all)])[0])]
    near1 = [near(part) for part in cut("cut_near", side, scaling, near_row, width, near_columns)]

    def near1_at(base):
        quarter = cols_all // GROUPS
        return tuple((base, g * quarter) if g < GROUPS - 1 else (base + 1, 0) for g in range(GROUPS))

    wts = row_weights(band)
    mine = place * nlocal
    band_at = lambda block, blocks: lax.dynamic_slice_in_dim(band, mine + block, blocks, 0)

    if inner > 0:
        inner_bands = band_at(1, inner)
        ratio_inner = blur(
            "ratio_inner", side, hbm(scaling), [(0, 0, rows_here, 0)], inner_bands, wts, densities, width
        )
        *cross1, ratio_inner = lax.optimization_barrier((*cross1, ratio_inner))
    if nlocal == 1:
        pieces = [(0, 0, width, width), (1, 0, width, (0, 2 * width)), (near1_at(2), 0, width, (2 * width, 0))]
        bands = band_at(0, 1)
        ratio = blur("ratio_only", side, [scaling, *cross1, *near1], pieces, bands, wts, densities, 0)
        cross2, near2 = cross(ratio), near(ratio)
    else:
        two = rows_here - 2 * width
        halo = cross_received(1, cols_all) if spread else 1
        pieces = [(0, (0, two), 2 * width, (width, 0)), (halo, 0, width, (0, 2 * width))]
        cross_bands = band_at(choose(cross_row), 1)
        ratio_cross = blur(
            "ratio_cross", side, hbm(scaling, *cross1), pieces, cross_bands, wts, densities, cross_row
        )
        ratio_cross, *near1 = lax.optimization_barrier((ratio_cross, *near1))
        cross2 = cross(ratio_cross)
        half, more = cols_all // 2, 2 * width
        pieces = [(0, (two, 0), 2 * width, (0, width)), (near1_at(1), 0, width, (2 * width, 0))]
        near_bands = band_at(choose(near_row), 1)
        *parts, ratio_near = blur(
            "ratio_near", side, hbm(scaling, *near1), pieces, near_bands, wts, densities, near_row,
            split_out=((0, half + more), (half + more, cols_all)),
        )
        near2 = [near(part) for part in parts]

    def finish(name, arrays, pieces, bands, row, weights, state):
        t, m = blur("logs_" + name, side, arrays, pieces, bands, wts, scaling, row, weights)
        return raw_rows(
            "raw_" + name, side, row, hbm(*t), [swap(part) for part in t], *hbm(m), rows_here, state
        )

    if nlocal == 1:
        pieces = [(0, 0, width, width), (1, 0, width, (0, 2 * width)), (2, 0, width, (2 * width, 0))]
        state = finish("only", [ratio, cross2, near2], pieces, bands, (0, 0), weights, None)
    else:
        state = None
        beside, beside_row = ratio_near, (0, 0)
        if inner > 0:
            arrays = hbm(ratio_inner, ratio_cross, ratio_near)
            pieces = [(0, 0, inner * width, width), (1, 0, width, cross_row), (2, 0, width, near_row)]
            state = finish("inner", arrays, pieces, inner_bands, (width, width), weights, None)
            weights, state = lax.optimization_barrier((weights, state))
            beside, beside_row = ratio_inner, (0, (inner - 1) * width)
        arrays = hbm(ratio_cross, beside) + [cross2]
        pieces = [(0, 0, width, width), (1, beside_row, width, (2 * width, 0)), (2, 0, width, (0, 2 * width))]
        state = finish("cross", arrays, pieces, cross_bands, cross_row, weights, state)
        weights, state = lax.optimization_barrier((weights, state))
        if inner == 0:
            beside = ratio_cross
        raw, quotient, mass = state
        step = cols_all // GROUPS
        first_units = tuple((g * step, (g + 1) * step) for g in range(GROUPS // 2)) + ((half, half + more),)
        later_units = ((half - more, half + more), (half + more, half + step + more), (half + step + more, cols_all))
        begun = begin("begin_near", side, ratio_near, beside, beside_row[::-1], near_bands, half - more)
        plans = [
            ("near_first", first_units, 0, [(2, start) for start, _ in first_units]),
            ("near_later", later_units, half, [(2, half - more)] + [(3, a - half - more) for a, _ in later_units[1:]]),
        ]
        for part, (name, units, column, halo) in enumerate(plans):
            arrays = hbm(ratio_near, beside) + near2[: part + 1]
            pieces = [
                (0, 0, width, width),
                (1, beside_row[::-1], width, (0, 2 * width)),
                (tuple(halo), 0, width, (2 * width, 0)),
            ]
            if part == 1:
                pieces = [(tuple(halo), 0, width, 0)]
            groups = tuple(g for g in range(GROUPS) if column <= g * step < column + half)
            t, m = blur(
                "logs_" + name, side, arrays, pieces, near_bands, wts, scaling, near_row, weights,
                pin=False, units=units, groups=groups, begun=(half - more, begun) if part == 1 else None,
            )
            raw, mass = raw_only("raw_" + name, side, near_row, column, t, [swap(part) for part in t], raw, mass)
            quotient = quotient_part("quotient_" + name, side, near_row, column, raw, m, quotient)
            if part == 0:
                weights, raw, mass, quotient = lax.optimization_barrier((weights, raw, mass, quotient))
        state = raw, quotient, mass

    raw, quotient, mass = state
    masses, quotient = mass_parts(mass, quotient)
    barycenter, new_scaling = outputs(raw, quotient.reshape(rows_here, cols_all // width, width), masses)
    return barycenter, new_scaling.reshape(rows_here, 1, cols_all)


def solution(mesh):
    return jax.shard_map(
        local,
        mesh=mesh,
        in_specs=(
            P("space", ("parts", "member"), None),
            P("space", ("parts", "member"), None),
            P("parts"),
            P(),
        ),
        out_specs=(P(("parts", "space"), None), P("space", ("parts", "member"), None)),
        check_vma=False,
    )
```

```python
import functools

import jax
import jax.numpy as jnp
from jax import lax
from jax.experimental import pallas as pl
from jax.experimental.pallas import tpu as pltpu
from jax.sharding import PartitionSpec as P

F32 = jnp.float32
BF16 = jnp.bfloat16
GROUPS = 4
ANY = pl.BlockSpec(memory_space=pl.ANY)
INVMEM = pl.BlockSpec(memory_space=pltpu.VMEM)
INSMEM = pl.BlockSpec(memory_space=pltpu.SMEM)


def split(x):
    high = x.astype(BF16)
    return high, (x - high.astype(F32)).astype(BF16)


def dot3(stack, b, dims):
    one = functools.partial(lax.dot_general, dimension_numbers=(dims, ((), ())), preferred_element_type=F32)
    rows = stack.shape[0] // 2
    both = one(stack, b[0])
    return both[:rows] + (one(stack[:rows], b[1]) + both[rows:])


def params(mebibytes):
    return pltpu.CompilerParams(vmem_limit_bytes=mebibytes * 1024 * 1024)


def hbm(*arrays):
    return [pltpu.with_memory_space_constraint(a, pltpu.HBM) for a in arrays]


def vmem(*arrays):
    return [pltpu.with_memory_space_constraint(a, pltpu.VMEM) for a in arrays]


def pick(choice, side):
    if isinstance(choice, tuple):
        return pl.multiple_of(jnp.where(side == 0, choice[0], choice[1]), 128)
    return choice


def cut_kernel(first, columns, side_ref, src, *refs):
    *outs, stage, sems = refs
    rows = stage.shape[0] // GROUPS
    start = pick(first, side_ref[0])
    outward = []
    inward = [
        pltpu.make_async_copy(src.at[pl.ds(start + g * rows, rows)], stage.at[pl.ds(g * rows, rows)], sems.at[0, g])
        for g in range(GROUPS)
    ]
    for copy in inward:
        copy.start()
    for g in range(GROUPS):
        inward[g].wait()
        part = pl.ds(g * rows, rows)
        for k, (out, column) in enumerate(zip(outs, columns)):
            at = pl.ds(column_of(column, side_ref), out.shape[2])
            outward.append(pltpu.make_async_copy(stage.at[part, :, at], out.at[part], sems.at[1 + k, g]))
            outward[-1].start()
    for copy in outward:
        copy.wait()


def cut(name, side, array, first, rows, parts):
    columns = array.shape[2]
    return pl.pallas_call(
        functools.partial(cut_kernel, first, [column for column, _ in parts]),
        in_specs=[INSMEM, ANY],
        out_specs=[ANY] * len(parts),
        out_shape=[pltpu.HBM((rows, 1, n), F32) for _, n in parts],
        scratch_shapes=[
            pltpu.VMEM((rows, 1, columns), F32),
            pltpu.SemaphoreType.DMA((1 + len(parts), GROUPS)),
        ],
        compiler_params=params(8),
        name=name,
    )(side, *hbm(array))


def column_of(column, side_ref):
    if isinstance(column, tuple):
        return pl.multiple_of(jnp.where(side_ref[1] == 1, column[0], column[1]), 128)
    return column


def cross_parts(columns):
    half, quarter = columns // 2, columns // 4
    return [(0, half), (half, quarter), ((half, 0), half), (3 * quarter, quarter)]


def cross_send(parts):
    def send(part, numbers, ends):
        pairs = []
        for k in range(3):
            for direction, number in ((0, k), (1, 2 - k)):
                if number in numbers:
                    pairs.append(ends(k)[direction])
        return lax.ppermute(part, "space", pairs)

    to_partner = lambda k: ((2 * k + 1, 2 * k), (2 * k + 2, 2 * k + 3))
    onward = lambda k: ((2 * k, 2 * k + 2), (2 * k + 3, 2 * k + 1))
    direct = lambda k: ((2 * k + 1, 2 * k + 2), (2 * k + 2, 2 * k + 1))
    relayed = [send(part, numbers, to_partner) for part, numbers in zip(parts[:2], ((0, 1), (0, 2)))]
    straight = [send(part, numbers, direct) for part, numbers in zip(parts[2:], ((1, 2), (0, 2)))]
    a, b, c, d = lax.optimization_barrier((*relayed, *straight))
    relayed, straight = [a, b], [c, d]
    passed = [send(part, numbers, onward) for part, numbers in zip(relayed, ((0, 1), (0, 2)))]
    return passed + straight


def cross_received(base, columns):
    a, b, c, d = range(base, base + 4)
    q = columns // 4
    return ((2, (c, 0), (a, 0)), (2, (c, q), (a, q)), (1, (c, 0), (b, 0)), (1, (c, q), (d, 0)))


def area(ref, row, rows, columns):
    return ref.at[pl.ds(row, rows), 0, columns] if len(ref.shape) == 3 else ref.at[pl.ds(row, rows), columns]


def weight_kernel(nblocks, band_ref, high_ref, low_ref):
    pair = pl.program_id(0)
    width = band_ref.shape[2]
    zero = jnp.zeros((width, width), F32)
    for o in range(2):
        for i in range(4):
            j = i - o
            value = band_ref[o, j] if 0 <= j <= 2 else zero
            if (o, j) == (0, 0):
                value = jnp.where(pair > 0, value, 0.0)
            if (o, j) == (1, 2):
                value = jnp.where(pair < nblocks // 2 - 1, value, 0.0)
            high, low = split(value)
            rows, columns = slice(o * width, (o + 1) * width), slice(i * width, (i + 1) * width)
            high_ref[0, rows, columns] = high
            low_ref[0, rows, columns] = low


def row_weights(band):
    nblocks, _, width, _ = band.shape
    shape = pltpu.HBM((nblocks // 2, 2 * width, 4 * width), BF16)
    out_spec = pl.BlockSpec((1, 2 * width, 4 * width), lambda t: (t, 0, 0))
    return pl.pallas_call(
        functools.partial(weight_kernel, nblocks),
        grid=(nblocks // 2,),
        in_specs=[pl.BlockSpec((2, 3, width, width), lambda t: (t, 0, 0, 0))],
        out_specs=(out_spec, out_spec),
        out_shape=(shape, shape),
        name="row_weights",
    )(*hbm(band))


def blur_kernel(plan, *refs):
    pieces, narrays, extra, final, split_out, units, groups, begun_at, joined = plan
    side_ref, refs = refs[0], refs[1:]
    arrays = refs[:narrays]
    band_ref, high_ref, low_ref, extra_ref = refs[narrays : narrays + 4]
    rest = refs[narrays + 4 :]
    if begun_at is not None:
        begun_ref, rest = rest[0], rest[1:]
    if final:
        weights_ref, rest = rest[0], rest[1:]
        all_weights = weights_ref[0]
        for k in range(1, weights_ref.shape[0]):
            all_weights += weights_ref[k]
        row_shape = (1, 2 * band_ref.shape[2])
        share = jnp.full(row_shape, weights_ref[side_ref[3]]) / jnp.full(row_shape, all_weights)
    nouts = (1 if joined else len(groups)) + 1 if final else 1 + len(split_out)
    outs = rest[:nouts]
    field, a_both, y_both, whigh, wlow, other = rest[nouts : nouts + 6]
    *results, in_sems, late_sems, out_sems = rest[nouts + 6 :]
    if begun_at is not None:
        *results, begun = results

    side = side_ref[0]
    nout, _, width, _ = band_ref.shape
    columns = field.shape[1]
    step = columns // GROUPS
    pairs = step // (2 * width)
    inside, late = [], {}

    def copy_in(u, k, place):
        _, row, rows, to = pieces[k]
        which, column = place
        start, stop = units[u]
        return pltpu.make_async_copy(
            area(arrays[which], pick(row, side), rows, pl.ds(column, stop - start)),
            field.at[pl.ds(pick(to, side), rows), pl.ds(start, stop - start)],
            in_sems.at[u, k],
        )

    def start_in(u, k):
        source = pieces[k][0]
        if isinstance(source, int):
            copy = copy_in(u, k, (source, units[u][0]))
        elif len(source[u]) == 2:
            copy = copy_in(u, k, source[u])
        else:
            number, this, other_one = source[u]
            pl.when(side_ref[2] == number)(copy_in(u, k, this).start)
            pl.when(side_ref[2] != number)(copy_in(u, k, other_one).start)
            return copy_in(u, k, other_one)
        copy.start()
        return copy

    for g in groups:
        at = pl.ds(g * step, step)
        some = pl.ds(g * pairs, pairs)
        late[g] = [
            pltpu.make_async_copy(high_ref.at[some], whigh.at[some], late_sems.at[g, 0]),
            pltpu.make_async_copy(low_ref.at[some], wlow.at[some], late_sems.at[g, 1]),
            pltpu.make_async_copy(
                area(extra_ref, pick(extra, side), other.shape[0], at), other.at[:, at], late_sems.at[g, 2]
            ),
        ]
    waiting = list(groups)
    for u in range(len(units)):
        inside.append([start_in(u, k) for k in range(len(pieces))])
        if begun_at is not None:
            start, stop = units[u]
            inside[u].append(
                pltpu.make_async_copy(
                    begun_ref.at[:, pl.ds(start - begun_at, stop - start)],
                    begun.at[:, pl.ds(start, stop - start)],
                    in_sems.at[u, len(pieces)],
                )
            )
            inside[u][-1].start()
        if u > 0 and waiting:
            for copy in late[waiting.pop(0)]:
                copy.start()
    for g in waiting:
        for copy in late[g]:
            copy.start()

    blocks = [(i, min(2, nout - i)) for i in range(0, nout, 2)]
    total = nout * width
    if begun_at is None:
        a_both[...] = jnp.zeros_like(a_both)
    else:
        for part, value in enumerate(split(jnp.where(side == 0, band_ref[0, 2], band_ref[0, 0]))):
            a_both[part * width : (part + 1) * width, :] = value
    for first, n in blocks if begun_at is None else ():
        for i in range(n):
            for j in range(3):
                for part, value in enumerate(split(band_ref[first + i, j])):
                    row = (2 * first + part * n + i) * width
                    a_both[row : row + width, (i + j) * width : (i + j + 1) * width] = value
    y_both[:, :width] = jnp.zeros((2 * total, width), BF16)
    y_both[:, columns + width :] = jnp.zeros((2 * total, width), BF16)

    def columns_pass(u):
        for copy in inside[u]:
            copy.wait()
        for i in range(units[u][0] // (2 * width), units[u][1] // (2 * width)):
            at = slice(i * 2 * width, (i + 1) * 2 * width)
            to = slice((2 * i + 1) * width, (2 * i + 3) * width)
            for first, n in blocks:
                k = width if begun_at is not None else (n + 2) * width
                a = a_both[2 * first * width : 2 * (first + n) * width, :k]
                y = dot3(a, split(field[first * width : first * width + k, at]), ((1,), (0,)))
                if begun_at is not None:
                    y += begun[:, at]
                for part, value in enumerate(split(y)):
                    row = part * total + first * width
                    y_both[row : row + n * width, to] = value

    def rows_pass(g):
        for copy in late[g]:
            copy.wait()
        for t in range(g * pairs, (g + 1) * pairs):
            source = slice(t * 2 * width, (t + 2) * 2 * width)
            at = slice(t * 2 * width, (t + 1) * 2 * width)
            value = dot3(y_both[:, source], (whigh[t], wlow[t]), ((1,), (1,)))
            if final:
                results[0][:, at] = value
                results[1][:, at] = share * jnp.log(other[:, at] * value)
            else:
                results[0][:, at] = other[:, at] / value
        at = pl.ds(g * step, step)
        place = pl.ds((g - groups[0]) * step, step)
        targets = [outs[-1].at[:, place]]
        if final:
            targets.append(outs[0].at[:, place] if joined else outs[groups.index(g)])
        copies = [
            pltpu.make_async_copy(src.at[:, at], dst, out_sems.at[g, k])
            for k, (src, dst) in enumerate(zip(results, targets))
        ]
        for k, (start, stop) in enumerate(split_out):
            if g * step < stop <= (g + 1) * step:
                part = results[0].at[:, pl.ds(start, stop - start)]
                copies.append(pltpu.make_async_copy(part, outs[k], out_sems.at[GROUPS, k]))
        for copy in copies:
            copy.start()
        return copies

    going = []
    waiting = list(groups)
    for u, (_, stop) in enumerate(units):
        columns_pass(u)
        while waiting and u > 0 and (stop == columns or (waiting[0] + 1) * step + width <= stop):
            going += rows_pass(waiting.pop(0))
    for copy in going:
        copy.wait()


def blur(
    name, side, arrays, pieces, bands, weights, other, extra,
    map_weights=None, pin=True, split_out=(), units=None, groups=tuple(range(GROUPS)), begun=None, joined=False,
):
    nout, _, width, _ = bands.shape
    npairs = weights[0].shape[0]
    columns = npairs * 2 * width
    rows, depth = nout * width, (nout + 2) * width if begun is None else width
    final = map_weights is not None
    nouts = 2 if final else 1
    kind = pltpu.HBM if pin else jax.ShapeDtypeStruct
    step = columns // GROUPS
    units = tuple((g * step, (g + 1) * step) for g in range(GROUPS)) if units is None else units
    parts = 1 if joined else len(groups)
    shapes = [kind((rows, len(groups) // parts * step), F32)] * (parts if final else 0)
    shapes += [pltpu.HBM((rows, stop - start), F32) for start, stop in split_out]
    shapes.append(pltpu.HBM((rows, len(groups) * step), F32))
    plan = (tuple(pieces), len(arrays), extra, final, split_out, units, groups, None if begun is None else begun[0], joined)
    work = 3 * 2 * rows * columns * (depth + 4 * width)
    moved = 4 * (depth + 3 * rows) * columns + npairs * 2 * 2 * 8 * width * width
    size = 4 * columns * (depth + (1 + nouts) * rows) + 4 * rows * columns + npairs * 2 * 2 * 8 * width * width
    result = pl.pallas_call(
        functools.partial(blur_kernel, plan),
        in_specs=[INSMEM] + [ANY] * len(arrays) + [INVMEM, ANY, ANY, ANY] + [ANY] * (begun is not None) + [INSMEM] * final,
        out_specs=[ANY] * len(shapes),
        out_shape=shapes,
        scratch_shapes=[
            pltpu.VMEM((depth, columns), F32),
            pltpu.VMEM((2 * rows, min(depth, 4 * width)), BF16),
            pltpu.VMEM((2 * rows, columns + 2 * width), BF16),
            pltpu.VMEM((npairs, 2 * width, 4 * width), BF16),
            pltpu.VMEM((npairs, 2 * width, 4 * width), BF16),
            pltpu.VMEM((rows, columns), F32),
        ]
        + [pltpu.VMEM((rows, columns), F32)] * (nouts + (begun is not None))
        + [
            pltpu.SemaphoreType.DMA((len(units), len(pieces) + (begun is not None))),
            pltpu.SemaphoreType.DMA((GROUPS, 3)),
            pltpu.SemaphoreType.DMA((GROUPS + 1, 2)),
        ],
        compiler_params=params(size // 2**20 + 6),
        cost_estimate=pl.CostEstimate(flops=work // 64, bytes_accessed=moved // 64, transcendentals=0),
        name=name,
    )(side, *arrays, bands, *hbm(*weights, other), *(hbm(begun[1]) if begun else []), *(hbm(map_weights) if final else []))
    return (result[:-1], result[-1]) if final else result if split_out else result[0]


def begin_kernel(beside_row, start, side_ref, own_ref, beside_ref, band_ref, out_ref, field, a_both, result, sems):
    width, columns = result.shape
    side = side_ref[0]
    at = pl.ds(start, columns)
    copies = [
        pltpu.make_async_copy(area(own_ref, 0, width, at), field.at[pl.ds(pick((width, 0), side), width)], sems.at[0]),
        pltpu.make_async_copy(
            area(beside_ref, pick(beside_row, side), width, at),
            field.at[pl.ds(pick((0, width), side), width)],
            sems.at[1],
        ),
    ]
    for copy in copies:
        copy.start()
    for j in range(2):
        for part, value in enumerate(split(jnp.where(side == 0, band_ref[0, j], band_ref[0, j + 1]))):
            a_both[part * width : (part + 1) * width, j * width : (j + 1) * width] = value
    for copy in copies:
        copy.wait()
    for i in range(columns // (2 * width)):
        tile = slice(i * 2 * width, (i + 1) * 2 * width)
        result[:, tile] = dot3(a_both[...], split(field[:, tile]), ((1,), (0,)))
    copy = pltpu.make_async_copy(result, out_ref, sems.at[2])
    copy.start()
    copy.wait()


def begin(name, side, own, beside, beside_row, bands, start):
    width, columns = own.shape[0], own.shape[1] - start
    return pl.pallas_call(
        functools.partial(begin_kernel, beside_row, start),
        in_specs=[INSMEM, ANY, ANY, INVMEM],
        out_specs=ANY,
        out_shape=pltpu.HBM((width, columns), F32),
        scratch_shapes=[
            pltpu.VMEM((2 * width, columns), F32),
            pltpu.VMEM((2 * width, 2 * width), BF16),
            pltpu.VMEM((width, columns), F32),
            pltpu.SemaphoreType.DMA((3,)),
        ],
        compiler_params=params(12),
        cost_estimate=pl.CostEstimate(flops=width * columns, bytes_accessed=width * columns, transcendentals=0),
        name=name,
    )(side, *hbm(own, beside), bands)


def raw_kernel(fresh, first, side_ref, *refs):
    own, peer, m_ref = refs[:GROUPS], refs[GROUPS : 2 * GROUPS], refs[2 * GROUPS]
    raw_ref, quotient_ref, mass_ref, quotient, sems = refs[-5:]
    tile = raw_ref.shape[0]
    at = pl.program_id(0)
    slot = lax.rem(at, 2)

    def copy(step, slot):
        row = pl.multiple_of(pick(first, side_ref[0]) + step * tile, tile)
        return pltpu.make_async_copy(quotient.at[slot], area(quotient_ref, row, tile, slice(None)), sems.at[slot])

    @pl.when(at >= 2)
    def _():
        copy(at - 2, slot).wait()

    mass = 0.0
    for g in range(GROUPS):
        raw = jnp.exp(own[g][...] + peer[g][...])
        step = raw.shape[1]
        raw_ref[:, g * step : (g + 1) * step] = raw
        mass += jnp.sum(raw)
        quotient[slot, :, g * step : (g + 1) * step] = raw / m_ref[:, g * step : (g + 1) * step]
    before = 0.0 if fresh else refs[2 * GROUPS + 3][...]
    mass_ref[...] = mass + jnp.where(at == 0, before, mass_ref[...])
    copy(at, slot).start()

    @pl.when(at == pl.num_programs(0) - 1)
    def _():
        copy(at - 1, 1 - slot).wait()
        copy(at, slot).wait()


def raw_rows(name, side, row, t, peers, m, rows_here, so_far):
    fresh = so_far is None
    rows, columns = m.shape
    tile = 32
    starts = [r // tile for r in row]
    part = pl.BlockSpec((tile, columns), lambda i, at: (i, 0))
    group = pl.BlockSpec((tile, columns // GROUPS), lambda i, at: (i, 0))
    return pl.pallas_call(
        functools.partial(raw_kernel, fresh, row),
        grid_spec=pltpu.PrefetchScalarGridSpec(
            num_scalar_prefetch=1,
            grid=(rows // tile,),
            in_specs=[group] * (2 * GROUPS) + [part] + ([] if fresh else [ANY, ANY, INVMEM]),
            out_specs=(
                pl.BlockSpec((tile, columns), lambda i, at: (jnp.where(at[0] == 0, *starts) + i, 0)),
                ANY,
                INVMEM,
            ),
            scratch_shapes=[pltpu.VMEM((2, tile, columns), F32), pltpu.SemaphoreType.DMA((2,))],
        ),
        out_shape=(
            pltpu.VMEM((rows_here, columns), F32),
            pltpu.VMEM((rows_here, 1, columns), F32),
            jax.ShapeDtypeStruct((1, 128), F32),
        ),
        input_output_aliases={} if fresh else {2 * GROUPS + 2: 0, 2 * GROUPS + 3: 1},
        compiler_params=params(16),
        cost_estimate=pl.CostEstimate(flops=m.size // 16, bytes_accessed=m.size // 4, transcendentals=0),
        name=name,
    )(side, *t, *peers, m, *([] if fresh else vmem(*so_far[:2]) + [so_far[2]]))


def raw_only_kernel(side_ref, *refs):
    *logs, _, before_ref, raw_ref, mass_ref = refs
    parts = len(logs) // 2
    mass = 0.0
    for g in range(parts):
        raw = jnp.exp(logs[g][...] + logs[parts + g][...])
        step = raw.shape[1]
        raw_ref[:, g * step : (g + 1) * step] = raw
        mass += jnp.sum(raw)
    mass_ref[...] = mass + jnp.where(pl.program_id(0) == 0, before_ref[...], mass_ref[...])


def piece_spec(tile, columns, row, column):
    starts = [r // tile for r in row]
    return pl.BlockSpec((tile, columns), lambda i, at: (jnp.where(at[0] == 0, *starts) + i, column // columns))


def raw_only(name, side, row, column, t, peers, raw_all, mass):
    rows, step = t[0].shape
    columns = len(t) * step
    tile = 64
    group = pl.BlockSpec((tile, step), lambda i, at: (i, 0))
    return pl.pallas_call(
        raw_only_kernel,
        grid_spec=pltpu.PrefetchScalarGridSpec(
            num_scalar_prefetch=1,
            grid=(rows // tile,),
            in_specs=[group] * (2 * len(t)) + [ANY, INVMEM],
            out_specs=(piece_spec(tile, columns, row, column), INVMEM),
        ),
        out_shape=(pltpu.VMEM(raw_all.shape, F32), jax.ShapeDtypeStruct(mass.shape, F32)),
        input_output_aliases={2 * len(t) + 1: 0},
        compiler_params=params(16),
        cost_estimate=pl.CostEstimate(flops=rows * columns // 16, bytes_accessed=rows * columns // 4, transcendentals=0),
        name=name,
    )(side, *t, *peers, *vmem(raw_all), mass)


def quotient_kernel(first, column, side_ref, raw_ref, m_ref, _, quotient_ref, quotient, sems):
    tile, columns = raw_ref.shape
    at = pl.program_id(0)
    row = pick(first, side_ref[0])
    quotient[at] = raw_ref[...] / m_ref[...]
    copies = [
        pltpu.make_async_copy(
            quotient.at[k], area(quotient_ref, row + k * tile, tile, pl.ds(column, columns)), sems.at[k]
        )
        for k in range(quotient.shape[0])
    ]
    for k, copy in enumerate(copies):
        pl.when(at == k)(copy.start)

    @pl.when(at == len(copies) - 1)
    def _():
        for copy in copies:
            copy.wait()


def quotient_part(name, side, row, column, raw_all, m, quotient_all):
    rows, columns = m.shape
    tile = 64
    return pl.pallas_call(
        functools.partial(quotient_kernel, row, column),
        grid_spec=pltpu.PrefetchScalarGridSpec(
            num_scalar_prefetch=1,
            grid=(rows // tile,),
            in_specs=[
                piece_spec(tile, columns, row, column),
                pl.BlockSpec((tile, columns), lambda i, at: (i, 0)),
                ANY,
            ],
            out_specs=ANY,
            scratch_shapes=[
                pltpu.VMEM((rows // tile, tile, columns), F32),
                pltpu.SemaphoreType.DMA((rows // tile,)),
            ],
        ),
        out_shape=pltpu.VMEM(quotient_all.shape, F32),
        input_output_aliases={3: 0},
        compiler_params=params(16),
        cost_estimate=pl.CostEstimate(flops=rows * columns // 16, bytes_accessed=rows * columns // 4, transcendentals=0),
        name=name,
    )(side, *vmem(raw_all), *hbm(m), *vmem(quotient_all))


def sum_kernel(a_ref, b_ref, out_ref):
    out_ref[...] = a_ref[...] + b_ref[...]


def mass_parts(mass, quotient):
    count = lax.axis_size("space")
    if count & (count - 1):
        return [lax.psum(mass, "space")], quotient
    parts = [mass]
    for bit in range(count.bit_length() - 1):
        if len(parts) == 2:
            if bit == 1:
                parts[1], quotient = lax.optimization_barrier((parts[1], quotient))
            parts = [
                pl.pallas_call(
                    sum_kernel,
                    in_specs=[INVMEM, INVMEM],
                    out_specs=INVMEM,
                    out_shape=jax.ShapeDtypeStruct(mass.shape, F32),
                    compiler_params=params(1),
                    name="mass",
                )(*parts)
            ]
        parts.append(lax.ppermute(parts[0], "space", [(i, i ^ (1 << bit)) for i in range(count)]))
    return parts, quotient


def output_kernel(total, raw_ref, quotient_ref, *refs):
    *masses, barycenter_ref, scaling_ref = refs
    mass = masses[0][...]
    for part in masses[1:]:
        mass += part[...]
    scale = total / mass
    width = scale.shape[1]
    for b in range(raw_ref.shape[1] // width):
        at = slice(b * width, (b + 1) * width)
        barycenter_ref[:, at] = raw_ref[:, at] * scale
    scaling_ref[...] = quotient_ref[...] * scale.reshape(1, 1, width)


def outputs(raw, quotient, masses):
    rows, columns = raw.shape
    tile = 64
    flat = pl.BlockSpec((tile, columns), lambda i: (i, 0))
    deep = pl.BlockSpec((tile,) + quotient.shape[1:], lambda i: (i, 0, 0))
    return pl.pallas_call(
        functools.partial(output_kernel, float(columns * columns)),
        grid=(rows // tile,),
        in_specs=[flat, deep] + [INVMEM] * len(masses),
        out_specs=(flat, deep),
        out_shape=(jax.ShapeDtypeStruct(raw.shape, F32), jax.ShapeDtypeStruct(quotient.shape, F32)),
        compiler_params=params(16),
        name="outputs",
    )(*vmem(raw, quotient), *masses)


def local(densities, scaling, weights, band):
    rows_here, maps_here, cols_all = densities.shape
    _, _, width, _ = band.shape
    nlocal = rows_here // width
    inner = max(nlocal - 2, 0)
    place = lax.axis_index("space")
    count = lax.axis_size("space")
    assert maps_here == 1 and lax.axis_size("member") == 2 and count % 2 == 0

    odd = place & 1
    middle = place >> 1
    numbers = [jnp.where(odd == 1, middle, 3 - middle), jnp.where(odd == 1, 2 - middle, middle - 1)]
    side = jnp.stack([odd, *numbers, lax.axis_index("member")])
    spread = count == 8 and nlocal > 1
    last = rows_here - width
    cross_row, near_row = (0, last), (last, 0)
    both = lambda pairs: pairs + [(b, a) for a, b in pairs]
    cross = functools.partial(
        lax.ppermute, axis_name="space", perm=both([(i, i + 1) for i in range(1, count - 1, 2)])
    )
    near = functools.partial(lax.ppermute, axis_name="space", perm=both([(i, i + 1) for i in range(0, count, 2)]))
    swap = functools.partial(lax.ppermute, axis_name="member", perm=[(0, 1), (1, 0)])

    def choose(choice):
        return jnp.where(odd == 0, *[c // width for c in choice]).astype(jnp.int32)

    near_columns = [(0, cols_all * 3 // 4), (cols_all * 3 // 4, cols_all // 4)]
    if spread:
        parts = cross_parts(cols_all)
        halves = cut("cut_cross_halves", side, scaling, cross_row, width, parts[0::2])
        quarters = cut("cut_cross_quarters", side, scaling, cross_row, width, parts[1::2])
        cross1 = cross_send([halves[0], quarters[0], halves[1], quarters[1]])
    else:
        cross1 = [cross(cut("cut_cross", side, scaling, cross_row, width, [(0, cols_all)])[0])]
    near1 = [near(part) for part in cut("cut_near", side, scaling, near_row, width, near_columns)]

    def near1_at(base):
        quarter = cols_all // GROUPS
        return tuple((base, g * quarter) if g < GROUPS - 1 else (base + 1, 0) for g in range(GROUPS))

    wts = row_weights(band)
    mine = place * nlocal
    band_at = lambda block, blocks: lax.dynamic_slice_in_dim(band, mine + block, blocks, 0)

    if inner > 0:
        inner_bands = band_at(1, inner)
        ratio_inner = blur(
            "ratio_inner", side, hbm(scaling), [(0, 0, rows_here, 0)], inner_bands, wts, densities, width
        )
        *cross1, ratio_inner = lax.optimization_barrier((*cross1, ratio_inner))
    if nlocal == 1:
        pieces = [(0, 0, width, width), (1, 0, width, (0, 2 * width)), (near1_at(2), 0, width, (2 * width, 0))]
        bands = band_at(0, 1)
        ratio = blur("ratio_only", side, [scaling, *cross1, *near1], pieces, bands, wts, densities, 0)
        cross2, near2 = cross(ratio), near(ratio)
    else:
        two = rows_here - 2 * width
        halo = cross_received(1, cols_all) if spread else 1
        pieces = [(0, (0, two), 2 * width, (width, 0)), (halo, 0, width, (0, 2 * width))]
        cross_bands = band_at(choose(cross_row), 1)
        ratio_cross = blur(
            "ratio_cross", side, hbm(scaling, *cross1), pieces, cross_bands, wts, densities, cross_row
        )
        ratio_cross, *near1 = lax.optimization_barrier((ratio_cross, *near1))
        cross2 = cross(ratio_cross)
        half, more = cols_all // 2, 2 * width
        pieces = [(0, (two, 0), 2 * width, (0, width)), (near1_at(1), 0, width, (2 * width, 0))]
        near_bands = band_at(choose(near_row), 1)
        *parts, ratio_near = blur(
            "ratio_near", side, hbm(scaling, *near1), pieces, near_bands, wts, densities, near_row,
            split_out=((0, half + more), (half + more, cols_all)),
        )
        near2 = [near(part) for part in parts]

    def finish(name, arrays, pieces, bands, row, weights, state):
        t, m = blur("logs_" + name, side, arrays, pieces, bands, wts, scaling, row, weights)
        return raw_rows(
            "raw_" + name, side, row, hbm(*t), [swap(part) for part in t], *hbm(m), rows_here, state
        )

    if nlocal == 1:
        pieces = [(0, 0, width, width), (1, 0, width, (0, 2 * width)), (2, 0, width, (2 * width, 0))]
        state = finish("only", [ratio, cross2, near2], pieces, bands, (0, 0), weights, None)
    else:
        state = None
        beside, beside_row = ratio_near, (0, 0)
        if inner > 0:
            arrays = hbm(ratio_inner, ratio_cross, ratio_near)
            pieces = [(0, 0, inner * width, width), (1, 0, width, cross_row), (2, 0, width, near_row)]
            state = finish("inner", arrays, pieces, inner_bands, (width, width), weights, None)
            weights, state = lax.optimization_barrier((weights, state))
            beside, beside_row = ratio_inner, (0, (inner - 1) * width)
        arrays = hbm(ratio_cross, beside) + [cross2]
        pieces = [(0, 0, width, width), (1, beside_row, width, (2 * width, 0)), (2, 0, width, (0, 2 * width))]
        state = finish("cross", arrays, pieces, cross_bands, cross_row, weights, state)
        weights, state = lax.optimization_barrier((weights, state))
        if inner == 0:
            beside = ratio_cross
        raw, quotient, mass = state
        step = cols_all // GROUPS
        first_units = tuple((g * step, (g + 1) * step) for g in range(GROUPS // 2)) + ((half, half + more),)
        later_units = ((half - more, half + more), (half + more, half + step + more), (half + step + more, cols_all))
        begun = begin("begin_near", side, ratio_near, beside, beside_row[::-1], near_bands, half - more)
        plans = [
            ("near_first", first_units, 0, [(2, start) for start, _ in first_units]),
            ("near_later", later_units, half, [(2, half - more)] + [(3, a - half - more) for a, _ in later_units[1:]]),
        ]
        for part, (name, units, column, halo) in enumerate(plans):
            arrays = hbm(ratio_near, beside) + near2[: part + 1]
            pieces = [
                (0, 0, width, width),
                (1, beside_row[::-1], width, (0, 2 * width)),
                (tuple(halo), 0, width, (2 * width, 0)),
            ]
            if part == 1:
                pieces = [(tuple(halo), 0, width, 0)]
            groups = tuple(g for g in range(GROUPS) if column <= g * step < column + half)
            t, m = blur(
                "logs_" + name, side, arrays, pieces, near_bands, wts, scaling, near_row, weights,
                pin=False, units=units, groups=groups, begun=(half - more, begun) if part == 1 else None, joined=part == 1,
            )
            raw, mass = raw_only("raw_" + name, side, near_row, column, t, [swap(part) for part in t], raw, mass)
            quotient = quotient_part("quotient_" + name, side, near_row, column, raw, m, quotient)
            if part == 0:
                weights, raw, mass, quotient = lax.optimization_barrier((weights, raw, mass, quotient))
        state = raw, quotient, mass

    raw, quotient, mass = state
    masses, quotient = mass_parts(mass, quotient)
    barycenter, new_scaling = outputs(raw, quotient.reshape(rows_here, cols_all // width, width), masses)
    return barycenter, new_scaling.reshape(rows_here, 1, cols_all)


def solution(mesh):
    return jax.shard_map(
        local,
        mesh=mesh,
        in_specs=(
            P("space", ("parts", "member"), None),
            P("space", ("parts", "member"), None),
            P("parts"),
            P(),
        ),
        out_specs=(P(("parts", "space"), None), P("space", ("parts", "member"), None)),
        check_vma=False,
    )
```

```python
import functools

import jax
import jax.numpy as jnp
from jax import lax
from jax.experimental import pallas as pl
from jax.experimental.pallas import tpu as pltpu
from jax.sharding import PartitionSpec as P

F32 = jnp.float32
BF16 = jnp.bfloat16
GROUPS = 4
ANY = pl.BlockSpec(memory_space=pl.ANY)
INVMEM = pl.BlockSpec(memory_space=pltpu.VMEM)
INSMEM = pl.BlockSpec(memory_space=pltpu.SMEM)


def split(x):
    high = x.astype(BF16)
    return high, (x - high.astype(F32)).astype(BF16)


def dot3(stack, b, dims):
    one = functools.partial(lax.dot_general, dimension_numbers=(dims, ((), ())), preferred_element_type=F32)
    rows = stack.shape[0] // 2
    both = one(stack, b[0])
    return both[:rows] + (one(stack[:rows], b[1]) + both[rows:])


def params(mebibytes):
    return pltpu.CompilerParams(vmem_limit_bytes=mebibytes * 1024 * 1024)


def hbm(*arrays):
    return [pltpu.with_memory_space_constraint(a, pltpu.HBM) for a in arrays]


def vmem(*arrays):
    return [pltpu.with_memory_space_constraint(a, pltpu.VMEM) for a in arrays]


def pick(choice, side):
    if isinstance(choice, tuple):
        return pl.multiple_of(jnp.where(side == 0, choice[0], choice[1]), 128)
    return choice


def cut_kernel(first, columns, side_ref, src, *refs):
    *outs, stage, sems = refs
    rows = stage.shape[0] // GROUPS
    start = pick(first, side_ref[0])
    outward = []
    inward = [
        pltpu.make_async_copy(src.at[pl.ds(start + g * rows, rows)], stage.at[pl.ds(g * rows, rows)], sems.at[0, g])
        for g in range(GROUPS)
    ]
    for copy in inward:
        copy.start()
    for g in range(GROUPS):
        inward[g].wait()
        part = pl.ds(g * rows, rows)
        for k, (out, column) in enumerate(zip(outs, columns)):
            at = pl.ds(column_of(column, side_ref), out.shape[2])
            outward.append(pltpu.make_async_copy(stage.at[part, :, at], out.at[part], sems.at[1 + k, g]))
            outward[-1].start()
    for copy in outward:
        copy.wait()


def cut(name, side, array, first, rows, parts):
    columns = array.shape[2]
    return pl.pallas_call(
        functools.partial(cut_kernel, first, [column for column, _ in parts]),
        in_specs=[INSMEM, ANY],
        out_specs=[ANY] * len(parts),
        out_shape=[pltpu.HBM((rows, 1, n), F32) for _, n in parts],
        scratch_shapes=[
            pltpu.VMEM((rows, 1, columns), F32),
            pltpu.SemaphoreType.DMA((1 + len(parts), GROUPS)),
        ],
        compiler_params=params(8),
        name=name,
    )(side, *hbm(array))


def column_of(column, side_ref):
    if isinstance(column, tuple):
        return pl.multiple_of(jnp.where(side_ref[1] == 1, column[0], column[1]), 128)
    return column


def cross_parts(columns):
    half, quarter = columns // 2, columns // 4
    return [(0, half), (half, quarter), ((half, 0), half), (3 * quarter, quarter)]


def cross_send(parts):
    def send(part, numbers, ends):
        pairs = []
        for k in range(3):
            for direction, number in ((0, k), (1, 2 - k)):
                if number in numbers:
                    pairs.append(ends(k)[direction])
        return lax.ppermute(part, "space", pairs)

    to_partner = lambda k: ((2 * k + 1, 2 * k), (2 * k + 2, 2 * k + 3))
    onward = lambda k: ((2 * k, 2 * k + 2), (2 * k + 3, 2 * k + 1))
    direct = lambda k: ((2 * k + 1, 2 * k + 2), (2 * k + 2, 2 * k + 1))
    straight = [send(part, numbers, direct) for part, numbers in zip(parts[2:], ((1, 2), (0, 2)))]
    relayed = [send(part, numbers, to_partner) for part, numbers in zip(parts[:2], ((0, 1), (0, 2)))]
    c, d, a, b = lax.optimization_barrier((*straight, *relayed))
    relayed, straight = [a, b], [c, d]
    passed = [send(part, numbers, onward) for part, numbers in zip(relayed, ((0, 1), (0, 2)))]
    return passed + straight


def cross_received(base, columns):
    a, b, c, d = range(base, base + 4)
    q = columns // 4
    return ((2, (c, 0), (a, 0)), (2, (c, q), (a, q)), (1, (c, 0), (b, 0)), (1, (c, q), (d, 0)))


def area(ref, row, rows, columns):
    return ref.at[pl.ds(row, rows), 0, columns] if len(ref.shape) == 3 else ref.at[pl.ds(row, rows), columns]


def weight_kernel(nblocks, band_ref, high_ref, low_ref):
    pair = pl.program_id(0)
    width = band_ref.shape[2]
    zero = jnp.zeros((width, width), F32)
    for o in range(2):
        for i in range(4):
            j = i - o
            value = band_ref[o, j] if 0 <= j <= 2 else zero
            if (o, j) == (0, 0):
                value = jnp.where(pair > 0, value, 0.0)
            if (o, j) == (1, 2):
                value = jnp.where(pair < nblocks // 2 - 1, value, 0.0)
            high, low = split(value)
            rows, columns = slice(o * width, (o + 1) * width), slice(i * width, (i + 1) * width)
            high_ref[0, rows, columns] = high
            low_ref[0, rows, columns] = low


def row_weights(band):
    nblocks, _, width, _ = band.shape
    shape = pltpu.HBM((nblocks // 2, 2 * width, 4 * width), BF16)
    out_spec = pl.BlockSpec((1, 2 * width, 4 * width), lambda t: (t, 0, 0))
    return pl.pallas_call(
        functools.partial(weight_kernel, nblocks),
        grid=(nblocks // 2,),
        in_specs=[pl.BlockSpec((2, 3, width, width), lambda t: (t, 0, 0, 0))],
        out_specs=(out_spec, out_spec),
        out_shape=(shape, shape),
        name="row_weights",
    )(*hbm(band))


def blur_kernel(plan, *refs):
    pieces, narrays, extra, final, split_out, units, groups, begun_at, joined = plan
    side_ref, refs = refs[0], refs[1:]
    arrays = refs[:narrays]
    band_ref, high_ref, low_ref, extra_ref = refs[narrays : narrays + 4]
    rest = refs[narrays + 4 :]
    if begun_at is not None:
        begun_ref, rest = rest[0], rest[1:]
    if final:
        weights_ref, rest = rest[0], rest[1:]
        all_weights = weights_ref[0]
        for k in range(1, weights_ref.shape[0]):
            all_weights += weights_ref[k]
        row_shape = (1, 2 * band_ref.shape[2])
        share = jnp.full(row_shape, weights_ref[side_ref[3]]) / jnp.full(row_shape, all_weights)
    nouts = (1 if joined else len(groups)) + 1 if final else 1 + len(split_out)
    outs = rest[:nouts]
    field, a_both, y_both, whigh, wlow, other = rest[nouts : nouts + 6]
    *results, in_sems, late_sems, out_sems = rest[nouts + 6 :]
    if begun_at is not None:
        *results, begun = results

    side = side_ref[0]
    nout, _, width, _ = band_ref.shape
    columns = field.shape[1]
    step = columns // GROUPS
    pairs = step // (2 * width)
    inside, late = [], {}

    def copy_in(u, k, place):
        _, row, rows, to = pieces[k]
        which, column = place
        start, stop = units[u]
        return pltpu.make_async_copy(
            area(arrays[which], pick(row, side), rows, pl.ds(column, stop - start)),
            field.at[pl.ds(pick(to, side), rows), pl.ds(start, stop - start)],
            in_sems.at[u, k],
        )

    def start_in(u, k):
        source = pieces[k][0]
        if isinstance(source, int):
            copy = copy_in(u, k, (source, units[u][0]))
        elif len(source[u]) == 2:
            copy = copy_in(u, k, source[u])
        else:
            number, this, other_one = source[u]
            pl.when(side_ref[2] == number)(copy_in(u, k, this).start)
            pl.when(side_ref[2] != number)(copy_in(u, k, other_one).start)
            return copy_in(u, k, other_one)
        copy.start()
        return copy

    for g in groups:
        at = pl.ds(g * step, step)
        some = pl.ds(g * pairs, pairs)
        late[g] = [
            pltpu.make_async_copy(high_ref.at[some], whigh.at[some], late_sems.at[g, 0]),
            pltpu.make_async_copy(low_ref.at[some], wlow.at[some], late_sems.at[g, 1]),
            pltpu.make_async_copy(
                area(extra_ref, pick(extra, side), other.shape[0], at), other.at[:, at], late_sems.at[g, 2]
            ),
        ]
    waiting = list(groups)
    for u in range(len(units)):
        inside.append([start_in(u, k) for k in range(len(pieces))])
        if begun_at is not None:
            start, stop = units[u]
            inside[u].append(
                pltpu.make_async_copy(
                    begun_ref.at[:, pl.ds(start - begun_at, stop - start)],
                    begun.at[:, pl.ds(start, stop - start)],
                    in_sems.at[u, len(pieces)],
                )
            )
            inside[u][-1].start()
        if u > 0 and waiting:
            for copy in late[waiting.pop(0)]:
                copy.start()
    for g in waiting:
        for copy in late[g]:
            copy.start()

    blocks = [(i, min(2, nout - i)) for i in range(0, nout, 2)]
    total = nout * width
    if begun_at is None:
        a_both[...] = jnp.zeros_like(a_both)
    else:
        for part, value in enumerate(split(jnp.where(side == 0, band_ref[0, 2], band_ref[0, 0]))):
            a_both[part * width : (part + 1) * width, :] = value
    for first, n in blocks if begun_at is None else ():
        for i in range(n):
            for j in range(3):
                for part, value in enumerate(split(band_ref[first + i, j])):
                    row = (2 * first + part * n + i) * width
                    a_both[row : row + width, (i + j) * width : (i + j + 1) * width] = value
    y_both[:, :width] = jnp.zeros((2 * total, width), BF16)
    y_both[:, columns + width :] = jnp.zeros((2 * total, width), BF16)

    def columns_pass(u):
        for copy in inside[u]:
            copy.wait()
        for i in range(units[u][0] // (2 * width), units[u][1] // (2 * width)):
            at = slice(i * 2 * width, (i + 1) * 2 * width)
            to = slice((2 * i + 1) * width, (2 * i + 3) * width)
            for first, n in blocks:
                k = width if begun_at is not None else (n + 2) * width
                a = a_both[2 * first * width : 2 * (first + n) * width, :k]
                y = dot3(a, split(field[first * width : first * width + k, at]), ((1,), (0,)))
                if begun_at is not None:
                    y += begun[:, at]
                for part, value in enumerate(split(y)):
                    row = part * total + first * width
                    y_both[row : row + n * width, to] = value

    def rows_pass(g):
        for copy in late[g]:
            copy.wait()
        for t in range(g * pairs, (g + 1) * pairs):
            source = slice(t * 2 * width, (t + 2) * 2 * width)
            at = slice(t * 2 * width, (t + 1) * 2 * width)
            value = dot3(y_both[:, source], (whigh[t], wlow[t]), ((1,), (1,)))
            if final:
                results[0][:, at] = value
                results[1][:, at] = share * jnp.log(other[:, at] * value)
            else:
                results[0][:, at] = other[:, at] / value
        at = pl.ds(g * step, step)
        place = pl.ds((g - groups[0]) * step, step)
        targets = [outs[-1].at[:, place]]
        if final:
            targets.append(outs[0].at[:, place] if joined else outs[groups.index(g)])
        copies = [
            pltpu.make_async_copy(src.at[:, at], dst, out_sems.at[g, k])
            for k, (src, dst) in enumerate(zip(results, targets))
        ]
        for k, (start, stop) in enumerate(split_out):
            if g * step < stop <= (g + 1) * step:
                part = results[0].at[:, pl.ds(start, stop - start)]
                copies.append(pltpu.make_async_copy(part, outs[k], out_sems.at[GROUPS, k]))
        for copy in copies:
            copy.start()
        return copies

    going = []
    waiting = list(groups)
    for u, (_, stop) in enumerate(units):
        columns_pass(u)
        while waiting and u > 0 and (stop == columns or (waiting[0] + 1) * step + width <= stop):
            going += rows_pass(waiting.pop(0))
    for copy in going:
        copy.wait()


def blur(
    name, side, arrays, pieces, bands, weights, other, extra,
    map_weights=None, pin=True, split_out=(), units=None, groups=tuple(range(GROUPS)), begun=None, joined=False,
):
    nout, _, width, _ = bands.shape
    npairs = weights[0].shape[0]
    columns = npairs * 2 * width
    rows, depth = nout * width, (nout + 2) * width if begun is None else width
    final = map_weights is not None
    nouts = 2 if final else 1
    kind = pltpu.HBM if pin else jax.ShapeDtypeStruct
    step = columns // GROUPS
    units = tuple((g * step, (g + 1) * step) for g in range(GROUPS)) if units is None else units
    parts = 1 if joined else len(groups)
    shapes = [kind((rows, len(groups) // parts * step), F32)] * (parts if final else 0)
    shapes += [pltpu.HBM((rows, stop - start), F32) for start, stop in split_out]
    shapes.append(pltpu.HBM((rows, len(groups) * step), F32))
    plan = (tuple(pieces), len(arrays), extra, final, split_out, units, groups, None if begun is None else begun[0], joined)
    work = 3 * 2 * rows * columns * (depth + 4 * width)
    moved = 4 * (depth + 3 * rows) * columns + npairs * 2 * 2 * 8 * width * width
    size = 4 * columns * (depth + (1 + nouts) * rows) + 4 * rows * columns + npairs * 2 * 2 * 8 * width * width
    result = pl.pallas_call(
        functools.partial(blur_kernel, plan),
        in_specs=[INSMEM] + [ANY] * len(arrays) + [INVMEM, ANY, ANY, ANY] + [ANY] * (begun is not None) + [INSMEM] * final,
        out_specs=[ANY] * len(shapes),
        out_shape=shapes,
        scratch_shapes=[
            pltpu.VMEM((depth, columns), F32),
            pltpu.VMEM((2 * rows, min(depth, 4 * width)), BF16),
            pltpu.VMEM((2 * rows, columns + 2 * width), BF16),
            pltpu.VMEM((npairs, 2 * width, 4 * width), BF16),
            pltpu.VMEM((npairs, 2 * width, 4 * width), BF16),
            pltpu.VMEM((rows, columns), F32),
        ]
        + [pltpu.VMEM((rows, columns), F32)] * (nouts + (begun is not None))
        + [
            pltpu.SemaphoreType.DMA((len(units), len(pieces) + (begun is not None))),
            pltpu.SemaphoreType.DMA((GROUPS, 3)),
            pltpu.SemaphoreType.DMA((GROUPS + 1, 2)),
        ],
        compiler_params=params(size // 2**20 + 6),
        cost_estimate=pl.CostEstimate(flops=work // 64, bytes_accessed=moved // 64, transcendentals=0),
        name=name,
    )(side, *arrays, bands, *hbm(*weights, other), *(hbm(begun[1]) if begun else []), *(hbm(map_weights) if final else []))
    return (result[:-1], result[-1]) if final else result if split_out else result[0]


def begin_kernel(beside_row, start, side_ref, own_ref, beside_ref, band_ref, out_ref, field, a_both, result, sems):
    width, columns = result.shape
    side = side_ref[0]
    at = pl.ds(start, columns)
    copies = [
        pltpu.make_async_copy(area(own_ref, 0, width, at), field.at[pl.ds(pick((width, 0), side), width)], sems.at[0]),
        pltpu.make_async_copy(
            area(beside_ref, pick(beside_row, side), width, at),
            field.at[pl.ds(pick((0, width), side), width)],
            sems.at[1],
        ),
    ]
    for copy in copies:
        copy.start()
    for j in range(2):
        for part, value in enumerate(split(jnp.where(side == 0, band_ref[0, j], band_ref[0, j + 1]))):
            a_both[part * width : (part + 1) * width, j * width : (j + 1) * width] = value
    for copy in copies:
        copy.wait()
    for i in range(columns // (2 * width)):
        tile = slice(i * 2 * width, (i + 1) * 2 * width)
        result[:, tile] = dot3(a_both[...], split(field[:, tile]), ((1,), (0,)))
    copy = pltpu.make_async_copy(result, out_ref, sems.at[2])
    copy.start()
    copy.wait()


def begin(name, side, own, beside, beside_row, bands, start):
    width, columns = own.shape[0], own.shape[1] - start
    return pl.pallas_call(
        functools.partial(begin_kernel, beside_row, start),
        in_specs=[INSMEM, ANY, ANY, INVMEM],
        out_specs=ANY,
        out_shape=pltpu.HBM((width, columns), F32),
        scratch_shapes=[
            pltpu.VMEM((2 * width, columns), F32),
            pltpu.VMEM((2 * width, 2 * width), BF16),
            pltpu.VMEM((width, columns), F32),
            pltpu.SemaphoreType.DMA((3,)),
        ],
        compiler_params=params(12),
        cost_estimate=pl.CostEstimate(flops=width * columns, bytes_accessed=width * columns, transcendentals=0),
        name=name,
    )(side, *hbm(own, beside), bands)


def raw_kernel(fresh, first, side_ref, *refs):
    own, peer, m_ref = refs[:GROUPS], refs[GROUPS : 2 * GROUPS], refs[2 * GROUPS]
    raw_ref, quotient_ref, mass_ref, quotient, sems = refs[-5:]
    tile = raw_ref.shape[0]
    at = pl.program_id(0)
    slot = lax.rem(at, 2)

    def copy(step, slot):
        row = pl.multiple_of(pick(first, side_ref[0]) + step * tile, tile)
        return pltpu.make_async_copy(quotient.at[slot], area(quotient_ref, row, tile, slice(None)), sems.at[slot])

    @pl.when(at >= 2)
    def _():
        copy(at - 2, slot).wait()

    mass = 0.0
    for g in range(GROUPS):
        raw = jnp.exp(own[g][...] + peer[g][...])
        step = raw.shape[1]
        raw_ref[:, g * step : (g + 1) * step] = raw
        mass += jnp.sum(raw)
        quotient[slot, :, g * step : (g + 1) * step] = raw / m_ref[:, g * step : (g + 1) * step]
    before = 0.0 if fresh else refs[2 * GROUPS + 3][...]
    mass_ref[...] = mass + jnp.where(at == 0, before, mass_ref[...])
    copy(at, slot).start()

    @pl.when(at == pl.num_programs(0) - 1)
    def _():
        copy(at - 1, 1 - slot).wait()
        copy(at, slot).wait()


def raw_rows(name, side, row, t, peers, m, rows_here, so_far):
    fresh = so_far is None
    rows, columns = m.shape
    tile = 32
    starts = [r // tile for r in row]
    part = pl.BlockSpec((tile, columns), lambda i, at: (i, 0))
    group = pl.BlockSpec((tile, columns // GROUPS), lambda i, at: (i, 0))
    return pl.pallas_call(
        functools.partial(raw_kernel, fresh, row),
        grid_spec=pltpu.PrefetchScalarGridSpec(
            num_scalar_prefetch=1,
            grid=(rows // tile,),
            in_specs=[group] * (2 * GROUPS) + [part] + ([] if fresh else [ANY, ANY, INVMEM]),
            out_specs=(
                pl.BlockSpec((tile, columns), lambda i, at: (jnp.where(at[0] == 0, *starts) + i, 0)),
                ANY,
                INVMEM,
            ),
            scratch_shapes=[pltpu.VMEM((2, tile, columns), F32), pltpu.SemaphoreType.DMA((2,))],
        ),
        out_shape=(
            pltpu.VMEM((rows_here, columns), F32),
            pltpu.VMEM((rows_here, 1, columns), F32),
            jax.ShapeDtypeStruct((1, 128), F32),
        ),
        input_output_aliases={} if fresh else {2 * GROUPS + 2: 0, 2 * GROUPS + 3: 1},
        compiler_params=params(16),
        cost_estimate=pl.CostEstimate(flops=m.size // 16, bytes_accessed=m.size // 4, transcendentals=0),
        name=name,
    )(side, *t, *peers, m, *([] if fresh else vmem(*so_far[:2]) + [so_far[2]]))


def raw_only_kernel(side_ref, *refs):
    *logs, _, before_ref, raw_ref, mass_ref = refs
    parts = len(logs) // 2
    mass = 0.0
    for g in range(parts):
        raw = jnp.exp(logs[g][...] + logs[parts + g][...])
        step = raw.shape[1]
        raw_ref[:, g * step : (g + 1) * step] = raw
        mass += jnp.sum(raw)
    mass_ref[...] = mass + jnp.where(pl.program_id(0) == 0, before_ref[...], mass_ref[...])


def piece_spec(tile, columns, row, column):
    starts = [r // tile for r in row]
    return pl.BlockSpec((tile, columns), lambda i, at: (jnp.where(at[0] == 0, *starts) + i, column // columns))


def raw_only(name, side, row, column, t, peers, raw_all, mass):
    rows, step = t[0].shape
    columns = len(t) * step
    tile = 64
    group = pl.BlockSpec((tile, step), lambda i, at: (i, 0))
    return pl.pallas_call(
        raw_only_kernel,
        grid_spec=pltpu.PrefetchScalarGridSpec(
            num_scalar_prefetch=1,
            grid=(rows // tile,),
            in_specs=[group] * (2 * len(t)) + [ANY, INVMEM],
            out_specs=(piece_spec(tile, columns, row, column), INVMEM),
        ),
        out_shape=(pltpu.VMEM(raw_all.shape, F32), jax.ShapeDtypeStruct(mass.shape, F32)),
        input_output_aliases={2 * len(t) + 1: 0},
        compiler_params=params(16),
        cost_estimate=pl.CostEstimate(flops=rows * columns // 16, bytes_accessed=rows * columns // 4, transcendentals=0),
        name=name,
    )(side, *t, *peers, *vmem(raw_all), mass)


def quotient_kernel(first, column, side_ref, raw_ref, m_ref, _, quotient_ref, quotient, sems):
    tile, columns = raw_ref.shape
    at = pl.program_id(0)
    row = pick(first, side_ref[0])
    quotient[at] = raw_ref[...] / m_ref[...]
    copies = [
        pltpu.make_async_copy(
            quotient.at[k], area(quotient_ref, row + k * tile, tile, pl.ds(column, columns)), sems.at[k]
        )
        for k in range(quotient.shape[0])
    ]
    for k, copy in enumerate(copies):
        pl.when(at == k)(copy.start)

    @pl.when(at == len(copies) - 1)
    def _():
        for copy in copies:
            copy.wait()


def quotient_part(name, side, row, column, raw_all, m, quotient_all):
    rows, columns = m.shape
    tile = 64
    return pl.pallas_call(
        functools.partial(quotient_kernel, row, column),
        grid_spec=pltpu.PrefetchScalarGridSpec(
            num_scalar_prefetch=1,
            grid=(rows // tile,),
            in_specs=[
                piece_spec(tile, columns, row, column),
                pl.BlockSpec((tile, columns), lambda i, at: (i, 0)),
                ANY,
            ],
            out_specs=ANY,
            scratch_shapes=[
                pltpu.VMEM((rows // tile, tile, columns), F32),
                pltpu.SemaphoreType.DMA((rows // tile,)),
            ],
        ),
        out_shape=pltpu.VMEM(quotient_all.shape, F32),
        input_output_aliases={3: 0},
        compiler_params=params(16),
        cost_estimate=pl.CostEstimate(flops=rows * columns // 16, bytes_accessed=rows * columns // 4, transcendentals=0),
        name=name,
    )(side, *vmem(raw_all), *hbm(m), *vmem(quotient_all))


def sum_kernel(a_ref, b_ref, out_ref):
    out_ref[...] = a_ref[...] + b_ref[...]


def mass_parts(mass, quotient):
    count = lax.axis_size("space")
    if count & (count - 1):
        return [lax.psum(mass, "space")], quotient
    parts = [mass]
    for bit in range(count.bit_length() - 1):
        if len(parts) == 2:
            if bit == 1:
                parts[1], quotient = lax.optimization_barrier((parts[1], quotient))
            parts = [
                pl.pallas_call(
                    sum_kernel,
                    in_specs=[INVMEM, INVMEM],
                    out_specs=INVMEM,
                    out_shape=jax.ShapeDtypeStruct(mass.shape, F32),
                    compiler_params=params(1),
                    name="mass",
                )(*parts)
            ]
        parts.append(lax.ppermute(parts[0], "space", [(i, i ^ (1 << bit)) for i in range(count)]))
    return parts, quotient


def output_kernel(total, raw_ref, quotient_ref, *refs):
    *masses, barycenter_ref, scaling_ref = refs
    mass = masses[0][...]
    for part in masses[1:]:
        mass += part[...]
    scale = total / mass
    width = scale.shape[1]
    for b in range(raw_ref.shape[1] // width):
        at = slice(b * width, (b + 1) * width)
        barycenter_ref[:, at] = raw_ref[:, at] * scale
    scaling_ref[...] = quotient_ref[...] * scale.reshape(1, 1, width)


def outputs(raw, quotient, masses):
    rows, columns = raw.shape
    tile = 64
    flat = pl.BlockSpec((tile, columns), lambda i: (i, 0))
    deep = pl.BlockSpec((tile,) + quotient.shape[1:], lambda i: (i, 0, 0))
    return pl.pallas_call(
        functools.partial(output_kernel, float(columns * columns)),
        grid=(rows // tile,),
        in_specs=[flat, deep] + [INVMEM] * len(masses),
        out_specs=(flat, deep),
        out_shape=(jax.ShapeDtypeStruct(raw.shape, F32), jax.ShapeDtypeStruct(quotient.shape, F32)),
        compiler_params=params(16),
        name="outputs",
    )(*vmem(raw, quotient), *masses)


def local(densities, scaling, weights, band):
    rows_here, maps_here, cols_all = densities.shape
    _, _, width, _ = band.shape
    nlocal = rows_here // width
    inner = max(nlocal - 2, 0)
    place = lax.axis_index("space")
    count = lax.axis_size("space")
    assert maps_here == 1 and lax.axis_size("member") == 2 and count % 2 == 0

    odd = place & 1
    middle = place >> 1
    numbers = [jnp.where(odd == 1, middle, 3 - middle), jnp.where(odd == 1, 2 - middle, middle - 1)]
    side = jnp.stack([odd, *numbers, lax.axis_index("member")])
    spread = count == 8 and nlocal > 1
    last = rows_here - width
    cross_row, near_row = (0, last), (last, 0)
    both = lambda pairs: pairs + [(b, a) for a, b in pairs]
    cross = functools.partial(
        lax.ppermute, axis_name="space", perm=both([(i, i + 1) for i in range(1, count - 1, 2)])
    )
    near = functools.partial(lax.ppermute, axis_name="space", perm=both([(i, i + 1) for i in range(0, count, 2)]))
    swap = functools.partial(lax.ppermute, axis_name="member", perm=[(0, 1), (1, 0)])

    def choose(choice):
        return jnp.where(odd == 0, *[c // width for c in choice]).astype(jnp.int32)

    near_columns = [(0, cols_all * 3 // 4), (cols_all * 3 // 4, cols_all // 4)]
    if spread:
        parts = cross_parts(cols_all)
        halves = cut("cut_cross_halves", side, scaling, cross_row, width, parts[0::2])
        quarters = cut("cut_cross_quarters", side, scaling, cross_row, width, parts[1::2])
        cross1 = cross_send([halves[0], quarters[0], halves[1], quarters[1]])
    else:
        cross1 = [cross(cut("cut_cross", side, scaling, cross_row, width, [(0, cols_all)])[0])]
    near1 = [near(part) for part in cut("cut_near", side, scaling, near_row, width, near_columns)]

    def near1_at(base):
        quarter = cols_all // GROUPS
        return tuple((base, g * quarter) if g < GROUPS - 1 else (base + 1, 0) for g in range(GROUPS))

    wts = row_weights(band)
    mine = place * nlocal
    band_at = lambda block, blocks: lax.dynamic_slice_in_dim(band, mine + block, blocks, 0)

    if inner > 0:
        inner_bands = band_at(1, inner)
        ratio_inner = blur(
            "ratio_inner", side, hbm(scaling), [(0, 0, rows_here, 0)], inner_bands, wts, densities, width
        )
        *cross1, ratio_inner = lax.optimization_barrier((*cross1, ratio_inner))
    if nlocal == 1:
        pieces = [(0, 0, width, width), (1, 0, width, (0, 2 * width)), (near1_at(2), 0, width, (2 * width, 0))]
        bands = band_at(0, 1)
        ratio = blur("ratio_only", side, [scaling, *cross1, *near1], pieces, bands, wts, densities, 0)
        cross2, near2 = cross(ratio), near(ratio)
    else:
        two = rows_here - 2 * width
        halo = cross_received(1, cols_all) if spread else 1
        pieces = [(0, (0, two), 2 * width, (width, 0)), (halo, 0, width, (0, 2 * width))]
        cross_bands = band_at(choose(cross_row), 1)
        ratio_cross = blur(
            "ratio_cross", side, hbm(scaling, *cross1), pieces, cross_bands, wts, densities, cross_row
        )
        ratio_cross, *near1 = lax.optimization_barrier((ratio_cross, *near1))
        cross2 = cross(ratio_cross)
        half, more = cols_all // 2, 2 * width
        pieces = [(0, (two, 0), 2 * width, (0, width)), (near1_at(1), 0, width, (2 * width, 0))]
        near_bands = band_at(choose(near_row), 1)
        *parts, ratio_near = blur(
            "ratio_near", side, hbm(scaling, *near1), pieces, near_bands, wts, densities, near_row,
            split_out=((0, half + more), (half + more, cols_all)),
        )
        near2 = [near(part) for part in parts]

    def finish(name, arrays, pieces, bands, row, weights, state):
        t, m = blur("logs_" + name, side, arrays, pieces, bands, wts, scaling, row, weights)
        return raw_rows(
            "raw_" + name, side, row, hbm(*t), [swap(part) for part in t], *hbm(m), rows_here, state
        )

    if nlocal == 1:
        pieces = [(0, 0, width, width), (1, 0, width, (0, 2 * width)), (2, 0, width, (2 * width, 0))]
        state = finish("only", [ratio, cross2, near2], pieces, bands, (0, 0), weights, None)
    else:
        state = None
        beside, beside_row = ratio_near, (0, 0)
        if inner > 0:
            arrays = hbm(ratio_inner, ratio_cross, ratio_near)
            pieces = [(0, 0, inner * width, width), (1, 0, width, cross_row), (2, 0, width, near_row)]
            state = finish("inner", arrays, pieces, inner_bands, (width, width), weights, None)
            weights, state = lax.optimization_barrier((weights, state))
            beside, beside_row = ratio_inner, (0, (inner - 1) * width)
        arrays = hbm(ratio_cross, beside) + [cross2]
        pieces = [(0, 0, width, width), (1, beside_row, width, (2 * width, 0)), (2, 0, width, (0, 2 * width))]
        state = finish("cross", arrays, pieces, cross_bands, cross_row, weights, state)
        weights, state = lax.optimization_barrier((weights, state))
        if inner == 0:
            beside = ratio_cross
        raw, quotient, mass = state
        step = cols_all // GROUPS
        first_units = tuple((g * step, (g + 1) * step) for g in range(GROUPS // 2)) + ((half, half + more),)
        later_units = ((half - more, half + more), (half + more, half + step + more), (half + step + more, cols_all))
        begun = begin("begin_near", side, ratio_near, beside, beside_row[::-1], near_bands, half - more)
        plans = [
            ("near_first", first_units, 0, [(2, start) for start, _ in first_units]),
            ("near_later", later_units, half, [(2, half - more)] + [(3, a - half - more) for a, _ in later_units[1:]]),
        ]
        for part, (name, units, column, halo) in enumerate(plans):
            arrays = hbm(ratio_near, beside) + near2[: part + 1]
            pieces = [
                (0, 0, width, width),
                (1, beside_row[::-1], width, (0, 2 * width)),
                (tuple(halo), 0, width, (2 * width, 0)),
            ]
            if part == 1:
                pieces = [(tuple(halo), 0, width, 0)]
            groups = tuple(g for g in range(GROUPS) if column <= g * step < column + half)
            t, m = blur(
                "logs_" + name, side, arrays, pieces, near_bands, wts, scaling, near_row, weights,
                pin=False, units=units, groups=groups, begun=(half - more, begun) if part == 1 else None, joined=part == 1,
            )
            raw, mass = raw_only("raw_" + name, side, near_row, column, t, [swap(part) for part in t], raw, mass)
            quotient = quotient_part("quotient_" + name, side, near_row, column, raw, m, quotient)
            if part == 0:
                weights, raw, mass, quotient = lax.optimization_barrier((weights, raw, mass, quotient))
        state = raw, quotient, mass

    raw, quotient, mass = state
    masses, quotient = mass_parts(mass, quotient)
    barycenter, new_scaling = outputs(raw, quotient.reshape(rows_here, cols_all // width, width), masses)
    return barycenter, new_scaling.reshape(rows_here, 1, cols_all)


def solution(mesh):
    return jax.shard_map(
        local,
        mesh=mesh,
        in_specs=(
            P("space", ("parts", "member"), None),
            P("space", ("parts", "member"), None),
            P("parts"),
            P(),
        ),
        out_specs=(P(("parts", "space"), None), P("space", ("parts", "member"), None)),
        check_vma=False,
    )
```

```python
import functools

import jax
import jax.numpy as jnp
from jax import lax
from jax.experimental import pallas as pl
from jax.experimental.pallas import tpu as pltpu
from jax.sharding import PartitionSpec as P

F32 = jnp.float32
BF16 = jnp.bfloat16
GROUPS = 4
ANY = pl.BlockSpec(memory_space=pl.ANY)
INVMEM = pl.BlockSpec(memory_space=pltpu.VMEM)
INSMEM = pl.BlockSpec(memory_space=pltpu.SMEM)


def split(x):
    high = x.astype(BF16)
    return high, (x - high.astype(F32)).astype(BF16)


def dot3(stack, b, dims):
    one = functools.partial(lax.dot_general, dimension_numbers=(dims, ((), ())), preferred_element_type=F32)
    rows = stack.shape[0] // 2
    both = one(stack, b[0])
    return both[:rows] + (one(stack[:rows], b[1]) + both[rows:])


def params(mebibytes):
    return pltpu.CompilerParams(vmem_limit_bytes=mebibytes * 1024 * 1024)


def hbm(*arrays):
    return [pltpu.with_memory_space_constraint(a, pltpu.HBM) for a in arrays]


def vmem(*arrays):
    return [pltpu.with_memory_space_constraint(a, pltpu.VMEM) for a in arrays]


def pick(choice, side):
    if isinstance(choice, tuple):
        return pl.multiple_of(jnp.where(side == 0, choice[0], choice[1]), 128)
    return choice


def cut_kernel(first, columns, side_ref, src, *refs):
    *outs, stage, sems = refs
    rows = stage.shape[0] // GROUPS
    start = pick(first, side_ref[0])
    outward = []
    inward = [
        pltpu.make_async_copy(src.at[pl.ds(start + g * rows, rows)], stage.at[pl.ds(g * rows, rows)], sems.at[0, g])
        for g in range(GROUPS)
    ]
    for copy in inward:
        copy.start()
    for g in range(GROUPS):
        inward[g].wait()
        part = pl.ds(g * rows, rows)
        for k, (out, column) in enumerate(zip(outs, columns)):
            at = pl.ds(column_of(column, side_ref), out.shape[2])
            outward.append(pltpu.make_async_copy(stage.at[part, :, at], out.at[part], sems.at[1 + k, g]))
            outward[-1].start()
    for copy in outward:
        copy.wait()


def cut(name, side, array, first, rows, parts):
    columns = array.shape[2]
    return pl.pallas_call(
        functools.partial(cut_kernel, first, [column for column, _ in parts]),
        in_specs=[INSMEM, ANY],
        out_specs=[ANY] * len(parts),
        out_shape=[pltpu.HBM((rows, 1, n), F32) for _, n in parts],
        scratch_shapes=[
            pltpu.VMEM((rows, 1, columns), F32),
            pltpu.SemaphoreType.DMA((1 + len(parts), GROUPS)),
        ],
        compiler_params=params(8),
        name=name,
    )(side, *hbm(array))


def column_of(column, side_ref):
    if isinstance(column, tuple):
        return pl.multiple_of(jnp.where(side_ref[1] == 1, column[0], column[1]), 128)
    return column


def cross_parts(columns):
    half, quarter = columns // 2, columns // 4
    return [(0, half), (half, quarter), ((half, 0), half), (3 * quarter, quarter)]


def cross_send(parts):
    def send(part, numbers, ends):
        pairs = []
        for k in range(3):
            for direction, number in ((0, k), (1, 2 - k)):
                if number in numbers:
                    pairs.append(ends(k)[direction])
        return lax.ppermute(part, "space", pairs)

    to_partner = lambda k: ((2 * k + 1, 2 * k), (2 * k + 2, 2 * k + 3))
    onward = lambda k: ((2 * k, 2 * k + 2), (2 * k + 3, 2 * k + 1))
    direct = lambda k: ((2 * k + 1, 2 * k + 2), (2 * k + 2, 2 * k + 1))
    straight = [send(part, numbers, direct) for part, numbers in zip(parts[2:], ((1, 2), (0, 2)))]
    relayed = [send(part, numbers, to_partner) for part, numbers in zip(parts[:2], ((0, 1), (0, 2)))]
    c, d, a, b = lax.optimization_barrier((*straight, *relayed))
    relayed, straight = [a, b], [c, d]
    passed = [send(part, numbers, onward) for part, numbers in zip(relayed, ((0, 1), (0, 2)))]
    return passed + straight


def cross_received(base, columns):
    a, b, c, d = range(base, base + 4)
    q = columns // 4
    return ((2, (c, 0), (a, 0)), (2, (c, q), (a, q)), (1, (c, 0), (b, 0)), (1, (c, q), (d, 0)))


def area(ref, row, rows, columns):
    return ref.at[pl.ds(row, rows), 0, columns] if len(ref.shape) == 3 else ref.at[pl.ds(row, rows), columns]


def weight_kernel(nblocks, band_ref, high_ref, low_ref):
    pair = pl.program_id(0)
    width = band_ref.shape[2]
    zero = jnp.zeros((width, width), F32)
    for o in range(2):
        for i in range(4):
            j = i - o
            value = band_ref[o, j] if 0 <= j <= 2 else zero
            if (o, j) == (0, 0):
                value = jnp.where(pair > 0, value, 0.0)
            if (o, j) == (1, 2):
                value = jnp.where(pair < nblocks // 2 - 1, value, 0.0)
            high, low = split(value)
            rows, columns = slice(o * width, (o + 1) * width), slice(i * width, (i + 1) * width)
            high_ref[0, rows, columns] = high
            low_ref[0, rows, columns] = low


def row_weights(band):
    nblocks, _, width, _ = band.shape
    shape = pltpu.HBM((nblocks // 2, 2 * width, 4 * width), BF16)
    out_spec = pl.BlockSpec((1, 2 * width, 4 * width), lambda t: (t, 0, 0))
    return pl.pallas_call(
        functools.partial(weight_kernel, nblocks),
        grid=(nblocks // 2,),
        in_specs=[pl.BlockSpec((2, 3, width, width), lambda t: (t, 0, 0, 0))],
        out_specs=(out_spec, out_spec),
        out_shape=(shape, shape),
        name="row_weights",
    )(*hbm(band))


def blur_kernel(plan, *refs):
    pieces, narrays, extra, final, split_out, units, groups, begun_at, joined = plan
    side_ref, refs = refs[0], refs[1:]
    arrays = refs[:narrays]
    band_ref, high_ref, low_ref, extra_ref = refs[narrays : narrays + 4]
    rest = refs[narrays + 4 :]
    if begun_at is not None:
        begun_ref, rest = rest[0], rest[1:]
    if final:
        weights_ref, rest = rest[0], rest[1:]
        all_weights = weights_ref[0]
        for k in range(1, weights_ref.shape[0]):
            all_weights += weights_ref[k]
        row_shape = (1, 2 * band_ref.shape[2])
        share = jnp.full(row_shape, weights_ref[side_ref[3]]) / jnp.full(row_shape, all_weights)
    nouts = (1 if joined else len(groups)) + 1 if final else 1 + len(split_out)
    outs = rest[:nouts]
    field, a_both, y_both, whigh, wlow, other = rest[nouts : nouts + 6]
    *results, in_sems, late_sems, out_sems = rest[nouts + 6 :]
    if begun_at is not None:
        *results, begun = results

    side = side_ref[0]
    nout, _, width, _ = band_ref.shape
    columns = field.shape[1]
    step = columns // GROUPS
    pairs = step // (2 * width)
    inside, late = [], {}

    def copy_in(u, k, place):
        _, row, rows, to = pieces[k]
        which, column = place
        start, stop = units[u]
        return pltpu.make_async_copy(
            area(arrays[which], pick(row, side), rows, pl.ds(column, stop - start)),
            field.at[pl.ds(pick(to, side), rows), pl.ds(start, stop - start)],
            in_sems.at[u, k],
        )

    def start_in(u, k):
        source = pieces[k][0]
        if isinstance(source, int):
            copy = copy_in(u, k, (source, units[u][0]))
        elif len(source[u]) == 2:
            copy = copy_in(u, k, source[u])
        else:
            number, this, other_one = source[u]
            pl.when(side_ref[2] == number)(copy_in(u, k, this).start)
            pl.when(side_ref[2] != number)(copy_in(u, k, other_one).start)
            return copy_in(u, k, other_one)
        copy.start()
        return copy

    for g in groups:
        at = pl.ds(g * step, step)
        some = pl.ds(g * pairs, pairs)
        late[g] = [
            pltpu.make_async_copy(high_ref.at[some], whigh.at[some], late_sems.at[g, 0]),
            pltpu.make_async_copy(low_ref.at[some], wlow.at[some], late_sems.at[g, 1]),
            pltpu.make_async_copy(
                area(extra_ref, pick(extra, side), other.shape[0], at), other.at[:, at], late_sems.at[g, 2]
            ),
        ]
    waiting = list(groups)
    for u in range(len(units)):
        inside.append([start_in(u, k) for k in range(len(pieces))])
        if begun_at is not None:
            start, stop = units[u]
            inside[u].append(
                pltpu.make_async_copy(
                    begun_ref.at[:, pl.ds(start - begun_at, stop - start)],
                    begun.at[:, pl.ds(start, stop - start)],
                    in_sems.at[u, len(pieces)],
                )
            )
            inside[u][-1].start()
        if u > 0 and waiting:
            for copy in late[waiting.pop(0)]:
                copy.start()
    for g in waiting:
        for copy in late[g]:
            copy.start()

    blocks = [(i, min(2, nout - i)) for i in range(0, nout, 2)]
    total = nout * width
    if begun_at is None:
        a_both[...] = jnp.zeros_like(a_both)
    else:
        for part, value in enumerate(split(jnp.where(side == 0, band_ref[0, 2], band_ref[0, 0]))):
            a_both[part * width : (part + 1) * width, :] = value
    for first, n in blocks if begun_at is None else ():
        for i in range(n):
            for j in range(3):
                for part, value in enumerate(split(band_ref[first + i, j])):
                    row = (2 * first + part * n + i) * width
                    a_both[row : row + width, (i + j) * width : (i + j + 1) * width] = value
    y_both[:, :width] = jnp.zeros((2 * total, width), BF16)
    y_both[:, columns + width :] = jnp.zeros((2 * total, width), BF16)

    def columns_pass(u):
        for copy in inside[u]:
            copy.wait()
        for i in range(units[u][0] // (2 * width), units[u][1] // (2 * width)):
            at = slice(i * 2 * width, (i + 1) * 2 * width)
            to = slice((2 * i + 1) * width, (2 * i + 3) * width)
            for first, n in blocks:
                k = width if begun_at is not None else (n + 2) * width
                a = a_both[2 * first * width : 2 * (first + n) * width, :k]
                y = dot3(a, split(field[first * width : first * width + k, at]), ((1,), (0,)))
                if begun_at is not None:
                    y += begun[:, at]
                for part, value in enumerate(split(y)):
                    row = part * total + first * width
                    y_both[row : row + n * width, to] = value

    def rows_pass(g):
        for copy in late[g]:
            copy.wait()
        for t in range(g * pairs, (g + 1) * pairs):
            source = slice(t * 2 * width, (t + 2) * 2 * width)
            at = slice(t * 2 * width, (t + 1) * 2 * width)
            value = dot3(y_both[:, source], (whigh[t], wlow[t]), ((1,), (1,)))
            if final:
                results[0][:, at] = value
                results[1][:, at] = share * jnp.log(other[:, at] * value)
            else:
                results[0][:, at] = other[:, at] / value
        at = pl.ds(g * step, step)
        place = pl.ds((g - groups[0]) * step, step)
        targets = [outs[-1].at[:, place]]
        if final:
            targets.append(outs[0].at[:, place] if joined else outs[groups.index(g)])
        copies = [
            pltpu.make_async_copy(src.at[:, at], dst, out_sems.at[g, k])
            for k, (src, dst) in enumerate(zip(results, targets))
        ]
        for k, (start, stop) in enumerate(split_out):
            if g * step < stop <= (g + 1) * step:
                part = results[0].at[:, pl.ds(start, stop - start)]
                copies.append(pltpu.make_async_copy(part, outs[k], out_sems.at[GROUPS, k]))
        for copy in copies:
            copy.start()
        return copies

    going = []
    waiting = list(groups)
    for u, (_, stop) in enumerate(units):
        columns_pass(u)
        while waiting and u > 0 and (stop == columns or (waiting[0] + 1) * step + width <= stop):
            going += rows_pass(waiting.pop(0))
    for copy in going:
        copy.wait()


def blur(
    name, side, arrays, pieces, bands, weights, other, extra,
    map_weights=None, pin=True, split_out=(), units=None, groups=tuple(range(GROUPS)), begun=None, joined=False,
):
    nout, _, width, _ = bands.shape
    npairs = weights[0].shape[0]
    columns = npairs * 2 * width
    rows, depth = nout * width, (nout + 2) * width if begun is None else width
    final = map_weights is not None
    nouts = 2 if final else 1
    kind = pltpu.HBM if pin else jax.ShapeDtypeStruct
    step = columns // GROUPS
    units = tuple((g * step, (g + 1) * step) for g in range(GROUPS)) if units is None else units
    parts = 1 if joined else len(groups)
    shapes = [kind((rows, len(groups) // parts * step), F32)] * (parts if final else 0)
    shapes += [pltpu.HBM((rows, stop - start), F32) for start, stop in split_out]
    shapes.append(pltpu.HBM((rows, len(groups) * step), F32))
    plan = (tuple(pieces), len(arrays), extra, final, split_out, units, groups, None if begun is None else begun[0], joined)
    work = 3 * 2 * rows * columns * (depth + 4 * width)
    moved = 4 * (depth + 3 * rows) * columns + npairs * 2 * 2 * 8 * width * width
    size = 4 * columns * (depth + (1 + nouts) * rows) + 4 * rows * columns + npairs * 2 * 2 * 8 * width * width
    result = pl.pallas_call(
        functools.partial(blur_kernel, plan),
        in_specs=[INSMEM] + [ANY] * len(arrays) + [INVMEM, ANY, ANY, ANY] + [ANY] * (begun is not None) + [INSMEM] * final,
        out_specs=[ANY] * len(shapes),
        out_shape=shapes,
        scratch_shapes=[
            pltpu.VMEM((depth, columns), F32),
            pltpu.VMEM((2 * rows, min(depth, 4 * width)), BF16),
            pltpu.VMEM((2 * rows, columns + 2 * width), BF16),
            pltpu.VMEM((npairs, 2 * width, 4 * width), BF16),
            pltpu.VMEM((npairs, 2 * width, 4 * width), BF16),
            pltpu.VMEM((rows, columns), F32),
        ]
        + [pltpu.VMEM((rows, columns), F32)] * (nouts + (begun is not None))
        + [
            pltpu.SemaphoreType.DMA((len(units), len(pieces) + (begun is not None))),
            pltpu.SemaphoreType.DMA((GROUPS, 3)),
            pltpu.SemaphoreType.DMA((GROUPS + 1, 2)),
        ],
        compiler_params=params(size // 2**20 + 6),
        cost_estimate=pl.CostEstimate(flops=work // 64, bytes_accessed=moved // 64, transcendentals=0),
        name=name,
    )(side, *arrays, bands, *hbm(*weights, other), *(hbm(begun[1]) if begun else []), *(hbm(map_weights) if final else []))
    return (result[:-1], result[-1]) if final else result if split_out else result[0]


def begin_kernel(beside_row, start, side_ref, own_ref, beside_ref, band_ref, out_ref, field, a_both, result, sems):
    width, columns = result.shape
    side = side_ref[0]
    at = pl.ds(start, columns)
    copies = [
        pltpu.make_async_copy(area(own_ref, 0, width, at), field.at[pl.ds(pick((width, 0), side), width)], sems.at[0]),
        pltpu.make_async_copy(
            area(beside_ref, pick(beside_row, side), width, at),
            field.at[pl.ds(pick((0, width), side), width)],
            sems.at[1],
        ),
    ]
    for copy in copies:
        copy.start()
    for j in range(2):
        for part, value in enumerate(split(jnp.where(side == 0, band_ref[0, j], band_ref[0, j + 1]))):
            a_both[part * width : (part + 1) * width, j * width : (j + 1) * width] = value
    for copy in copies:
        copy.wait()
    for i in range(columns // (2 * width)):
        tile = slice(i * 2 * width, (i + 1) * 2 * width)
        result[:, tile] = dot3(a_both[...], split(field[:, tile]), ((1,), (0,)))
    copy = pltpu.make_async_copy(result, out_ref, sems.at[2])
    copy.start()
    copy.wait()


def begin(name, side, own, beside, beside_row, bands, start):
    width, columns = own.shape[0], own.shape[1] - start
    return pl.pallas_call(
        functools.partial(begin_kernel, beside_row, start),
        in_specs=[INSMEM, ANY, ANY, INVMEM],
        out_specs=ANY,
        out_shape=pltpu.HBM((width, columns), F32),
        scratch_shapes=[
            pltpu.VMEM((2 * width, columns), F32),
            pltpu.VMEM((2 * width, 2 * width), BF16),
            pltpu.VMEM((width, columns), F32),
            pltpu.SemaphoreType.DMA((3,)),
        ],
        compiler_params=params(12),
        cost_estimate=pl.CostEstimate(flops=width * columns, bytes_accessed=width * columns, transcendentals=0),
        name=name,
    )(side, *hbm(own, beside), bands)


def raw_kernel(fresh, first, side_ref, *refs):
    own, peer, m_ref = refs[:GROUPS], refs[GROUPS : 2 * GROUPS], refs[2 * GROUPS]
    raw_ref, quotient_ref, mass_ref, quotient, sems = refs[-5:]
    tile = raw_ref.shape[0]
    at = pl.program_id(0)
    slot = lax.rem(at, 2)

    def copy(step, slot):
        row = pl.multiple_of(pick(first, side_ref[0]) + step * tile, tile)
        return pltpu.make_async_copy(quotient.at[slot], area(quotient_ref, row, tile, slice(None)), sems.at[slot])

    @pl.when(at >= 2)
    def _():
        copy(at - 2, slot).wait()

    mass = 0.0
    for g in range(GROUPS):
        raw = jnp.exp(own[g][...] + peer[g][...])
        step = raw.shape[1]
        raw_ref[:, g * step : (g + 1) * step] = raw
        mass += jnp.sum(raw)
        quotient[slot, :, g * step : (g + 1) * step] = raw / m_ref[:, g * step : (g + 1) * step]
    before = 0.0 if fresh else refs[2 * GROUPS + 3][...]
    mass_ref[...] = mass + jnp.where(at == 0, before, mass_ref[...])
    copy(at, slot).start()

    @pl.when(at == pl.num_programs(0) - 1)
    def _():
        copy(at - 1, 1 - slot).wait()
        copy(at, slot).wait()


def raw_rows(name, side, row, t, peers, m, rows_here, so_far):
    fresh = so_far is None
    rows, columns = m.shape
    tile = 32
    starts = [r // tile for r in row]
    part = pl.BlockSpec((tile, columns), lambda i, at: (i, 0))
    group = pl.BlockSpec((tile, columns // GROUPS), lambda i, at: (i, 0))
    return pl.pallas_call(
        functools.partial(raw_kernel, fresh, row),
        grid_spec=pltpu.PrefetchScalarGridSpec(
            num_scalar_prefetch=1,
            grid=(rows // tile,),
            in_specs=[group] * (2 * GROUPS) + [part] + ([] if fresh else [ANY, ANY, INVMEM]),
            out_specs=(
                pl.BlockSpec((tile, columns), lambda i, at: (jnp.where(at[0] == 0, *starts) + i, 0)),
                ANY,
                INVMEM,
            ),
            scratch_shapes=[pltpu.VMEM((2, tile, columns), F32), pltpu.SemaphoreType.DMA((2,))],
        ),
        out_shape=(
            pltpu.VMEM((rows_here, columns), F32),
            pltpu.VMEM((rows_here, 1, columns), F32),
            jax.ShapeDtypeStruct((1, 128), F32),
        ),
        input_output_aliases={} if fresh else {2 * GROUPS + 2: 0, 2 * GROUPS + 3: 1},
        compiler_params=params(16),
        cost_estimate=pl.CostEstimate(flops=m.size // 16, bytes_accessed=m.size // 4, transcendentals=0),
        name=name,
    )(side, *t, *peers, m, *([] if fresh else vmem(*so_far[:2]) + [so_far[2]]))


def raw_only_kernel(side_ref, *refs):
    *logs, _, before_ref, raw_ref, mass_ref = refs
    parts = len(logs) // 2
    mass = 0.0
    for g in range(parts):
        raw = jnp.exp(logs[g][...] + logs[parts + g][...])
        step = raw.shape[1]
        raw_ref[:, g * step : (g + 1) * step] = raw
        mass += jnp.sum(raw)
    mass_ref[...] = mass + jnp.where(pl.program_id(0) == 0, before_ref[...], mass_ref[...])


def piece_spec(tile, columns, row, column):
    starts = [r // tile for r in row]
    return pl.BlockSpec((tile, columns), lambda i, at: (jnp.where(at[0] == 0, *starts) + i, column // columns))


def raw_only(name, side, row, column, t, peers, raw_all, mass):
    rows, step = t[0].shape
    columns = len(t) * step
    tile = 64
    group = pl.BlockSpec((tile, step), lambda i, at: (i, 0))
    return pl.pallas_call(
        raw_only_kernel,
        grid_spec=pltpu.PrefetchScalarGridSpec(
            num_scalar_prefetch=1,
            grid=(rows // tile,),
            in_specs=[group] * (2 * len(t)) + [ANY, INVMEM],
            out_specs=(piece_spec(tile, columns, row, column), INVMEM),
        ),
        out_shape=(pltpu.VMEM(raw_all.shape, F32), jax.ShapeDtypeStruct(mass.shape, F32)),
        input_output_aliases={2 * len(t) + 1: 0},
        compiler_params=params(16),
        cost_estimate=pl.CostEstimate(flops=rows * columns // 16, bytes_accessed=rows * columns // 4, transcendentals=0),
        name=name,
    )(side, *t, *peers, *vmem(raw_all), mass)


def quotient_kernel(first, column, side_ref, raw_ref, m_ref, _, quotient_ref, quotient, sems):
    tile, columns = raw_ref.shape
    at = pl.program_id(0)
    row = pick(first, side_ref[0])
    quotient[at] = raw_ref[...] / m_ref[...]
    copies = [
        pltpu.make_async_copy(
            quotient.at[k], area(quotient_ref, row + k * tile, tile, pl.ds(column, columns)), sems.at[k]
        )
        for k in range(quotient.shape[0])
    ]
    for k, copy in enumerate(copies):
        pl.when(at == k)(copy.start)

    @pl.when(at == len(copies) - 1)
    def _():
        for copy in copies:
            copy.wait()


def quotient_part(name, side, row, column, raw_all, m, quotient_all):
    rows, columns = m.shape
    tile = 64
    return pl.pallas_call(
        functools.partial(quotient_kernel, row, column),
        grid_spec=pltpu.PrefetchScalarGridSpec(
            num_scalar_prefetch=1,
            grid=(rows // tile,),
            in_specs=[
                piece_spec(tile, columns, row, column),
                pl.BlockSpec((tile, columns), lambda i, at: (i, 0)),
                ANY,
            ],
            out_specs=ANY,
            scratch_shapes=[
                pltpu.VMEM((rows // tile, tile, columns), F32),
                pltpu.SemaphoreType.DMA((rows // tile,)),
            ],
        ),
        out_shape=pltpu.VMEM(quotient_all.shape, F32),
        input_output_aliases={3: 0},
        compiler_params=params(16),
        cost_estimate=pl.CostEstimate(flops=rows * columns // 16, bytes_accessed=rows * columns // 4, transcendentals=0),
        name=name,
    )(side, *vmem(raw_all), *hbm(m), *vmem(quotient_all))


def sum_kernel(a_ref, b_ref, out_ref):
    out_ref[...] = a_ref[...] + b_ref[...]


def mass_parts(mass, quotient):
    count = lax.axis_size("space")
    if count & (count - 1):
        return [lax.psum(mass, "space")], quotient
    parts = [mass]
    for bit in range(count.bit_length() - 1):
        if len(parts) == 2:
            if bit == 1:
                parts[1], quotient = lax.optimization_barrier((parts[1], quotient))
            parts = [
                pl.pallas_call(
                    sum_kernel,
                    in_specs=[INVMEM, INVMEM],
                    out_specs=INVMEM,
                    out_shape=jax.ShapeDtypeStruct(mass.shape, F32),
                    compiler_params=params(1),
                    name="mass",
                )(*parts)
            ]
        parts.append(lax.ppermute(parts[0], "space", [(i, i ^ (1 << bit)) for i in range(count)]))
    return parts, quotient


def output_kernel(total, raw_ref, quotient_ref, *refs):
    *masses, barycenter_ref, scaling_ref = refs
    mass = masses[0][...]
    for part in masses[1:]:
        mass += part[...]
    scale = total / mass
    width = scale.shape[1]
    for b in range(raw_ref.shape[1] // width):
        at = slice(b * width, (b + 1) * width)
        barycenter_ref[:, at] = raw_ref[:, at] * scale
    scaling_ref[...] = quotient_ref[...] * scale.reshape(1, 1, width)


def outputs(raw, quotient, masses):
    rows, columns = raw.shape
    tile = 32
    flat = pl.BlockSpec((tile, columns), lambda i: (i, 0))
    deep = pl.BlockSpec((tile,) + quotient.shape[1:], lambda i: (i, 0, 0))
    return pl.pallas_call(
        functools.partial(output_kernel, float(columns * columns)),
        grid=(rows // tile,),
        in_specs=[flat, deep] + [INVMEM] * len(masses),
        out_specs=(flat, deep),
        out_shape=(jax.ShapeDtypeStruct(raw.shape, F32), jax.ShapeDtypeStruct(quotient.shape, F32)),
        compiler_params=params(16),
        name="outputs",
    )(*vmem(raw, quotient), *masses)


def local(densities, scaling, weights, band):
    rows_here, maps_here, cols_all = densities.shape
    _, _, width, _ = band.shape
    nlocal = rows_here // width
    inner = max(nlocal - 2, 0)
    place = lax.axis_index("space")
    count = lax.axis_size("space")
    assert maps_here == 1 and lax.axis_size("member") == 2 and count % 2 == 0

    odd = place & 1
    middle = place >> 1
    numbers = [jnp.where(odd == 1, middle, 3 - middle), jnp.where(odd == 1, 2 - middle, middle - 1)]
    side = jnp.stack([odd, *numbers, lax.axis_index("member")])
    spread = count == 8 and nlocal > 1
    last = rows_here - width
    cross_row, near_row = (0, last), (last, 0)
    both = lambda pairs: pairs + [(b, a) for a, b in pairs]
    cross = functools.partial(
        lax.ppermute, axis_name="space", perm=both([(i, i + 1) for i in range(1, count - 1, 2)])
    )
    near = functools.partial(lax.ppermute, axis_name="space", perm=both([(i, i + 1) for i in range(0, count, 2)]))
    swap = functools.partial(lax.ppermute, axis_name="member", perm=[(0, 1), (1, 0)])

    def choose(choice):
        return jnp.where(odd == 0, *[c // width for c in choice]).astype(jnp.int32)

    near_columns = [(0, cols_all * 3 // 4), (cols_all * 3 // 4, cols_all // 4)]
    if spread:
        parts = cross_parts(cols_all)
        halves = cut("cut_cross_halves", side, scaling, cross_row, width, parts[0::2])
        quarters = cut("cut_cross_quarters", side, scaling, cross_row, width, parts[1::2])
        cross1 = cross_send([halves[0], quarters[0], halves[1], quarters[1]])
    else:
        cross1 = [cross(cut("cut_cross", side, scaling, cross_row, width, [(0, cols_all)])[0])]
    near1 = [near(part) for part in cut("cut_near", side, scaling, near_row, width, near_columns)]

    def near1_at(base):
        quarter = cols_all // GROUPS
        return tuple((base, g * quarter) if g < GROUPS - 1 else (base + 1, 0) for g in range(GROUPS))

    wts = row_weights(band)
    mine = place * nlocal
    band_at = lambda block, blocks: lax.dynamic_slice_in_dim(band, mine + block, blocks, 0)

    if inner > 0:
        inner_bands = band_at(1, inner)
        ratio_inner = blur(
            "ratio_inner", side, hbm(scaling), [(0, 0, rows_here, 0)], inner_bands, wts, densities, width
        )
        *cross1, ratio_inner = lax.optimization_barrier((*cross1, ratio_inner))
    if nlocal == 1:
        pieces = [(0, 0, width, width), (1, 0, width, (0, 2 * width)), (near1_at(2), 0, width, (2 * width, 0))]
        bands = band_at(0, 1)
        ratio = blur("ratio_only", side, [scaling, *cross1, *near1], pieces, bands, wts, densities, 0)
        cross2, near2 = cross(ratio), near(ratio)
    else:
        two = rows_here - 2 * width
        halo = cross_received(1, cols_all) if spread else 1
        pieces = [(0, (0, two), 2 * width, (width, 0)), (halo, 0, width, (0, 2 * width))]
        cross_bands = band_at(choose(cross_row), 1)
        ratio_cross = blur(
            "ratio_cross", side, hbm(scaling, *cross1), pieces, cross_bands, wts, densities, cross_row
        )
        ratio_cross, *near1 = lax.optimization_barrier((ratio_cross, *near1))
        cross2 = cross(ratio_cross)
        half, more = cols_all // 2, 2 * width
        pieces = [(0, (two, 0), 2 * width, (0, width)), (near1_at(1), 0, width, (2 * width, 0))]
        near_bands = band_at(choose(near_row), 1)
        *parts, ratio_near = blur(
            "ratio_near", side, hbm(scaling, *near1), pieces, near_bands, wts, densities, near_row,
            split_out=((0, half + more), (half + more, cols_all)),
        )
        near2 = [near(part) for part in parts]

    def finish(name, arrays, pieces, bands, row, weights, state):
        t, m = blur("logs_" + name, side, arrays, pieces, bands, wts, scaling, row, weights)
        return raw_rows(
            "raw_" + name, side, row, hbm(*t), [swap(part) for part in t], *hbm(m), rows_here, state
        )

    if nlocal == 1:
        pieces = [(0, 0, width, width), (1, 0, width, (0, 2 * width)), (2, 0, width, (2 * width, 0))]
        state = finish("only", [ratio, cross2, near2], pieces, bands, (0, 0), weights, None)
    else:
        state = None
        beside, beside_row = ratio_near, (0, 0)
        if inner > 0:
            arrays = hbm(ratio_inner, ratio_cross, ratio_near)
            pieces = [(0, 0, inner * width, width), (1, 0, width, cross_row), (2, 0, width, near_row)]
            state = finish("inner", arrays, pieces, inner_bands, (width, width), weights, None)
            weights, state = lax.optimization_barrier((weights, state))
            beside, beside_row = ratio_inner, (0, (inner - 1) * width)
        arrays = hbm(ratio_cross, beside) + [cross2]
        pieces = [(0, 0, width, width), (1, beside_row, width, (2 * width, 0)), (2, 0, width, (0, 2 * width))]
        state = finish("cross", arrays, pieces, cross_bands, cross_row, weights, state)
        weights, state = lax.optimization_barrier((weights, state))
        if inner == 0:
            beside = ratio_cross
        raw, quotient, mass = state
        step = cols_all // GROUPS
        first_units = tuple((g * step, (g + 1) * step) for g in range(GROUPS // 2)) + ((half, half + more),)
        later_units = ((half - more, half + more), (half + more, half + step + more), (half + step + more, cols_all))
        begun = begin("begin_near", side, ratio_near, beside, beside_row[::-1], near_bands, half - more)
        plans = [
            ("near_first", first_units, 0, [(2, start) for start, _ in first_units]),
            ("near_later", later_units, half, [(2, half - more)] + [(3, a - half - more) for a, _ in later_units[1:]]),
        ]
        for part, (name, units, column, halo) in enumerate(plans):
            arrays = hbm(ratio_near, beside) + near2[: part + 1]
            pieces = [
                (0, 0, width, width),
                (1, beside_row[::-1], width, (0, 2 * width)),
                (tuple(halo), 0, width, (2 * width, 0)),
            ]
            if part == 1:
                pieces = [(tuple(halo), 0, width, 0)]
            groups = tuple(g for g in range(GROUPS) if column <= g * step < column + half)
            t, m = blur(
                "logs_" + name, side, arrays, pieces, near_bands, wts, scaling, near_row, weights,
                pin=False, units=units, groups=groups, begun=(half - more, begun) if part == 1 else None, joined=part == 1,
            )
            raw, mass = raw_only("raw_" + name, side, near_row, column, t, [swap(part) for part in t], raw, mass)
            quotient = quotient_part("quotient_" + name, side, near_row, column, raw, m, quotient)
            if part == 0:
                weights, raw, mass, quotient = lax.optimization_barrier((weights, raw, mass, quotient))
        state = raw, quotient, mass

    raw, quotient, mass = state
    masses, quotient = mass_parts(mass, quotient)
    barycenter, new_scaling = outputs(raw, quotient.reshape(rows_here, cols_all // width, width), masses)
    return barycenter, new_scaling.reshape(rows_here, 1, cols_all)


def solution(mesh):
    return jax.shard_map(
        local,
        mesh=mesh,
        in_specs=(
            P("space", ("parts", "member"), None),
            P("space", ("parts", "member"), None),
            P("parts"),
            P(),
        ),
        out_specs=(P(("parts", "space"), None), P("space", ("parts", "member"), None)),
        check_vma=False,
    )
```
